32 devices in a mesh: batch: 8 (over z, core), seq: 4 (over y, x).
Axes of the slice: x: 2, y: 2, z: 4, core: 2. Of those that a mesh axis runs over, the one named last changes fastest.
Arguments:
- image_in: bfloat16 [1024, 8, 1152], P('seq', 'batch'), may hold values from -6 to 6
- cond_in: bfloat16 [78, 8, 1152], P(None, 'batch'), may hold values from -6 to 6
- skip_image: bfloat16 [1024, 8, 1152], P('seq', 'batch'), may hold values from -6 to 6
- skip_cond: bfloat16 [78, 8, 1152], P(None, 'batch'), may hold values from -6 to 6
- caption_len: int32 [8], P('batch'), may hold values from 1 to 77, as said below
- skip_weight: bfloat16 [2304, 1152], replicated, may hold values from -0.125 to 0.125
- skip_bias: float32 [1152], replicated, may hold values from -4 to 4
- first_gain: float32 [1152], replicated, may hold values from 0.5 to 1.5
- first_bias: float32 [1152], replicated, may hold values from -4 to 4
- qkv_weight: bfloat16 [1152, 3456], replicated, may hold values from -0.1875 to 0.1875
- proj_weight: bfloat16 [1152, 1152], replicated, may hold values from -3 to 3
- proj_bias: float32 [1152], replicated, may hold values from -4 to 4
- second_gain: float32 [1152], replicated, may hold values from 0.5 to 1.5
- second_bias: float32 [1152], replicated, may hold values from -4 to 4
- fc1_weight: bfloat16 [1152, 4608], replicated, may hold values from -0.1875 to 0.1875
- fc1_bias: float32 [4608], replicated, may hold values from -4 to 4
- fc2_weight: bfloat16 [4608, 1152], replicated, may hold values from -0.09375 to 0.09375
- fc2_bias: float32 [1152], replicated, may hold values from -4 to 4
- grad_image: bfloat16 [1024, 8, 1152], P('seq', 'batch'), may hold values from -6 to 6
- grad_cond: bfloat16 [78, 8, 1152], P(None, 'batch'), may hold values from -6 to 6
Outputs:
- out_image: float32 [1024, 8, 1152], P('seq', 'batch')
- out_cond: float32 [78, 8, 1152], P(None, 'batch')
- dgrad_image_in: float32 [1024, 8, 1152], P('seq', 'batch')
- dgrad_cond_in: float32 [78, 8, 1152], P(None, 'batch')
- dgrad_skip_image: float32 [1024, 8, 1152], P('seq', 'batch')
- dgrad_skip_cond: float32 [78, 8, 1152], P(None, 'batch')
- wgrad_skip_weight: float32 [2304, 1152], P('batch')
- wgrad_skip_bias: float32 [1152], P('batch')
- wgrad_first_gain: float32 [1152], P('batch')
- wgrad_first_bias: float32 [1152], P('batch')
- wgrad_qkv_weight: float32 [1152, 3456], P('batch')
- wgrad_proj_weight: float32 [1152, 1152], P('batch')
- wgrad_proj_bias: float32 [1152], P('batch')
- wgrad_second_gain: float32 [1152], P('batch')
- wgrad_second_bias: float32 [1152], P('batch')
- wgrad_fc1_weight: float32 [1152, 4608], P('batch')
- wgrad_fc1_bias: float32 [4608], P('batch')
- wgrad_fc2_weight: float32 [4608, 1152], P('batch')
- wgrad_fc2_bias: float32 [1152], P('batch')
The draws below stay inside these ranges and needn't reach their ends.
Inputs may be any that keep to these rules, and one draw needn't show every extreme that they name: `caption_len`: every item has at least one valid caption token; some item has all 77 valid and some item exactly one.
All inputs are finite; a program needn't handle non-finite values.
Results may differ from the reference program's by a relative error of at most 0.02.
Values may be sent and summed in bfloat16 or wider, within the bound.
A program may use at most 256 MiB of HBM per device.

```python
import math
import jax
import jax.numpy as jnp
from jax import lax

D = 1152
HEADS = 16
HEAD_DIM = 72
FF = 4608
CAP = 77
IMG = 1024
COND = 78
ITEMS = 8


def draw_caption_len(key, part):
    key = jax.random.fold_in(key, 7)
    key_lengths, key_place = jax.random.split(key)
    lengths = jax.random.randint(key_lengths, (ITEMS,), 1, CAP + 1)
    where_long = jax.random.randint(key_place, (), 0, ITEMS)
    lengths = lengths.at[where_long].set(CAP)
    lengths = lengths.at[(where_long + 1) % ITEMS].set(1)
    return lengths.astype(jnp.int32)


def level_of(key, shape, cuts, smallest, high):
    gain = 1.0
    for dim, blocks in cuts:
        steps = jax.random.uniform(jax.random.fold_in(jax.random.fold_in(key, 6), dim), (blocks,), jnp.float32, smallest / len(cuts), high / len(cuts))
        gain = gain * jnp.repeat(jnp.exp(steps), shape[dim] // blocks).reshape((-1,) + (1,) * (len(shape) - 1 - dim))
    return gain


def normal_values(rng, shape, scale, reach, cuts=(), kind=jnp.bfloat16):
    entries = jax.random.normal(rng, shape, jnp.float32) * scale
    if len(cuts) > 0:
        entries = level_of(rng, shape, cuts, -0.22, 0.18) * entries
    return jnp.clip(entries, min=-reach, max=reach).astype(kind)


def setup_inputs(seed: int = 0) -> dict:
    keys = jax.random.split(jax.random.key(seed), 21)
    image_in = normal_values(keys[0], (IMG, ITEMS, D), 1.0, 6.0, ((0, 4), (1, 8)))
    cond_in = normal_values(keys[1], (COND, ITEMS, D), 1.0, 6.0, ((1, 8),))
    skip_image = normal_values(keys[2], (IMG, ITEMS, D), 1.0, 6.0, ((0, 4), (1, 8)))
    skip_cond = normal_values(keys[3], (COND, ITEMS, D), 1.0, 6.0, ((1, 8),))
    caption_len = draw_caption_len(jax.random.fold_in(keys[20], 71), 0)
    skip_weight = normal_values(keys[5], (2 * D, D), (2 * D) ** -0.5, 0.125)
    skip_bias = normal_values(keys[6], (D,), 0.3, 4.0, (), jnp.float32)
    first_gain = jnp.clip(1.0 + 0.1 * jax.random.normal(keys[7], (D,), jnp.float32), 0.5, 1.5)
    first_bias = normal_values(keys[8], (D,), 0.3, 4.0, (), jnp.float32)
    qkv_weight = normal_values(keys[9], (D, 3 * D), D ** -0.5, 0.1875)
    proj_weight = normal_values(keys[10], (D, D), (max(D // 256, 1)) ** -0.5, 3.0)
    proj_bias = normal_values(keys[11], (D,), 0.3, 4.0, (), jnp.float32)
    second_gain = jnp.clip(1.0 + 0.1 * jax.random.normal(keys[12], (D,), jnp.float32), 0.5, 1.5)
    second_bias = normal_values(keys[13], (D,), 0.3, 4.0, (), jnp.float32)
    fc1_weight = normal_values(keys[14], (D, FF), D ** -0.5, 0.1875)
    fc1_bias = normal_values(keys[15], (FF,), 0.3, 4.0, (), jnp.float32)
    fc2_weight = normal_values(keys[16], (FF, D), FF ** -0.5, 0.09375)
    fc2_bias = normal_values(keys[17], (D,), 0.3, 4.0, (), jnp.float32)
    grad_image = normal_values(keys[18], (IMG, ITEMS, D), 1.0, 6.0, ((0, 4), (1, 8)))
    grad_cond = normal_values(keys[19], (COND, ITEMS, D), 1.0, 6.0, ((1, 8),))
    return dict(image_in=image_in, cond_in=cond_in, skip_image=skip_image, skip_cond=skip_cond, caption_len=caption_len, skip_weight=skip_weight, skip_bias=skip_bias, first_gain=first_gain, first_bias=first_bias, qkv_weight=qkv_weight, proj_weight=proj_weight, proj_bias=proj_bias, second_gain=second_gain, second_bias=second_bias, fc1_weight=fc1_weight, fc1_bias=fc1_bias, fc2_weight=fc2_weight, fc2_bias=fc2_bias, grad_image=grad_image, grad_cond=grad_cond)


@jax.custom_vjp
def low(v):
    return lax.optimization_barrier(v.astype(jnp.bfloat16)).astype(jnp.float32)

@jax.custom_vjp
def low_back(v):
    return v

def low_keep(v):
    return (low(v), None)

def low_pass(kept, grad):
    return (grad,)

def back_keep(v):
    return (v, None)

def back_low(kept, grad):
    return (low(grad),)
low.defvjp(low_keep, low_pass)
low_back.defvjp(back_keep, back_low)

def matmul(left, right):
    return jnp.dot(left, right, precision=lax.Precision.HIGHEST, preferred_element_type=jnp.float32)

def layer_norm(values, norm_gain, norm_shift):
    centre = values - lax.optimization_barrier(jnp.mean(values, axis=-1, keepdims=True))
    spread = lax.optimization_barrier(jnp.mean(centre * centre, axis=-1, keepdims=True))
    return centre * lax.rsqrt(spread + 1e-05) * norm_gain + norm_shift

def block_forward(params, values, skip_rows, valid):
    skip_weight, skip_bias, first_gain, first_bias, qkv_weight, proj_weight, proj_bias, second_gain, second_bias, fc1_weight, fc1_bias, fc2_weight, fc2_bias = params
    length = values.shape[0]
    score_scale = 1.0 / math.sqrt(HEAD_DIM)
    joined = jnp.concatenate([values, skip_rows], axis=-1)
    hidden = low_back(matmul(joined, skip_weight) + skip_bias)
    normed = low(layer_norm(hidden, first_gain, first_bias))
    triple = matmul(normed, qkv_weight)
    queries = low(low_back(triple[:, :D])).reshape(length, HEADS, HEAD_DIM)
    key_heads = low(low_back(triple[:, D:2 * D])).reshape(length, HEADS, HEAD_DIM)
    value_heads = low(low_back(triple[:, 2 * D:])).reshape(length, HEADS, HEAD_DIM)
    raw_scores = jnp.einsum('qhd,khd->hqk', queries, key_heads, precision=lax.Precision.HIGHEST)
    scores = jnp.where(valid[None, None, :], low_back(raw_scores) * score_scale, -1e+30)
    row_peak = lax.optimization_barrier(jnp.max(scores, axis=-1, keepdims=True))
    shifted = jnp.exp(scores - row_peak)
    attn_probs = low(shifted / lax.optimization_barrier(jnp.sum(shifted, axis=-1, keepdims=True)))
    context = jnp.einsum('hqk,khd->qhd', attn_probs, value_heads, precision=lax.Precision.HIGHEST)
    context = low(low_back(context.reshape(length, D)))
    branch = low_back(matmul(context, proj_weight) + proj_bias)
    middle = hidden + branch
    normed_two = low(layer_norm(middle, second_gain, second_bias))
    pre_gelu = low_back(matmul(normed_two, fc1_weight) + fc1_bias)
    active = low(jax.nn.gelu(pre_gelu, approximate=False))
    return middle + matmul(active, fc2_weight) + fc2_bias

def add_up(running, update):
    return running + update

def by_item(cond_part, image_part):
    return jnp.concatenate([jnp.transpose(cond_part, (1, 0, 2)), jnp.transpose(image_part, (1, 0, 2))], 1).astype(jnp.float32)

def reference(image_in, cond_in, skip_image, skip_cond, caption_len, skip_weight, skip_bias, first_gain, first_bias, qkv_weight, proj_weight, proj_bias, second_gain, second_bias, fc1_weight, fc1_bias, fc2_weight, fc2_bias, grad_image, grad_cond):
    params = tuple((array.astype(jnp.float32) for array in (skip_weight, skip_bias, first_gain, first_bias, qkv_weight, proj_weight, proj_bias, second_gain, second_bias, fc1_weight, fc1_bias, fc2_weight, fc2_bias)))
    inputs = by_item(cond_in, image_in)
    skips = by_item(skip_cond, skip_image)
    cotangents = by_item(grad_cond, grad_image)
    positions = jnp.arange(COND + IMG, dtype=jnp.int32)

    def one_item(totals, pieces):
        item_in, item_skip, item_cot, length = pieces
        valid = (positions <= length) | (positions >= COND)

        def forward(weights, values, skip_rows):
            return block_forward(weights, values, skip_rows, valid)
        result, pullback = jax.vjp(forward, params, item_in, item_skip)
        gradients, grad_in, grad_skip = pullback(item_cot)
        totals = jax.tree.map(add_up, totals, gradients)
        return (totals, (result, grad_in, grad_skip))
    zeros = jax.tree.map(jnp.zeros_like, params)
    totals, (results, grad_ins, grad_skips) = lax.scan(one_item, zeros, (inputs, skips, cotangents, caption_len.astype(jnp.int32)))

    def split_rows(stacked):
        return (jnp.transpose(stacked[:, COND:], (1, 0, 2)), jnp.transpose(stacked[:, :COND], (1, 0, 2)))
    out_image, out_cond = split_rows(results)
    dgrad_image_in, dgrad_cond_in = split_rows(grad_ins)
    dgrad_skip_image, dgrad_skip_cond = split_rows(grad_skips)
    return (out_image, out_cond, dgrad_image_in, dgrad_cond_in, dgrad_skip_image, dgrad_skip_cond, totals[0], totals[1], totals[2], totals[3], totals[4], totals[5], totals[6], totals[7], totals[8], totals[9], totals[10], totals[11], totals[12])
```

```python
import functools
import math

import jax
import jax.numpy as jnp
from jax import lax
from jax.experimental import pallas as pl
from jax.experimental.pallas import tpu as pltpu
from jax.sharding import PartitionSpec as P

HEADS = 16
HEAD_DIM = 72
LANES = 128
SLOTS = 128
F32 = jnp.float32
BF16 = jnp.bfloat16
VMEM_LIMIT = 60 * 1024 * 1024
SCALE = 1.0 / math.sqrt(HEAD_DIM)
SCALE2 = SCALE * math.log2(math.e)


def dot(left, right):
    return jnp.dot(left, right, preferred_element_type=F32)


def dot_nt(left, right):
    return lax.dot_general(left, right, (((1,), (1,)), ((), ())), preferred_element_type=F32)


def dot_tn(left, right):
    return lax.dot_general(left, right, (((0,), (0,)), ((), ())), preferred_element_type=F32)


def params():
    return pltpu.CompilerParams(vmem_limit_bytes=VMEM_LIMIT)


def cost(flops, nbytes):
    return pl.CostEstimate(flops=int(flops), bytes_accessed=int(nbytes), transcendentals=0)


def turned(value):
    return value.astype(F32).T.astype(BF16)


def normalize(values):
    centre = values - jnp.mean(values, axis=-1, keepdims=True)
    factor = lax.rsqrt(jnp.mean(centre * centre, axis=-1, keepdims=True) + 1e-5)
    return centre * factor, factor


def norm_back(upstream, scaled, factor, gain):
    inner = upstream * gain
    centred = inner - jnp.mean(inner, axis=-1, keepdims=True)
    return factor * (centred - scaled * jnp.mean(inner * scaled, axis=-1, keepdims=True))


def pre_kernel(x_ref, s_ref, w_ref, bias_ref, gain_ref, shift_ref, hidden_ref, normed_ref, turn_ref):
    width = x_ref.shape[1]
    hidden = dot(x_ref[...], w_ref[:width]) + dot(s_ref[...], w_ref[width:]) + bias_ref[...]
    hidden_ref[...] = hidden
    scaled, _ = normalize(hidden)
    normed_ref[...] = (scaled * gain_ref[...] + shift_ref[...]).astype(BF16)
    turn_ref[:width] = turned(x_ref[...])
    turn_ref[width:] = turned(s_ref[...])


def pre(x, s, w, bias, gain, shift):
    rows, width = x.shape
    return pl.pallas_call(
        pre_kernel,
        out_shape=(
            jax.ShapeDtypeStruct((rows, width), F32),
            jax.ShapeDtypeStruct((rows, width), BF16),
            jax.ShapeDtypeStruct((2 * width, rows), BF16),
        ),
        compiler_params=params(),
        cost_estimate=cost(4 * rows * width * width, 4 * width * width + 12 * rows * width),
        name="input_linear",
    )(x, s, w, bias, gain, shift)


def heads_weight_kernel(window, place_ref, w_ref, out_ref):
    heads = out_ref.shape[0]
    width = w_ref.shape[0]
    own = heads * HEAD_DIM
    keep = lax.broadcasted_iota(jnp.int32, (width, LANES), 1) < HEAD_DIM
    place = place_ref[0]
    for which in range(3):
        first = place * own + which * width
        start = jnp.minimum(first // LANES * LANES, 3 * width - window)
        value = w_ref[:, pl.ds(pl.multiple_of(start, LANES), window)].astype(F32)
        value = pltpu.roll(value, lax.rem(window - (first - start), window), 1)
        for head in range(heads):
            turned_back = value if head == 0 else pltpu.roll(value, window - head * HEAD_DIM, 1)
            out_ref[head, :, which * LANES : (which + 1) * LANES] = jnp.where(
                keep, turned_back[:, :LANES], 0.0
            ).astype(BF16)


def heads_weight(place, w, heads):
    width = w.shape[0]
    own = heads * HEAD_DIM
    offsets = [p * own % LANES for p in range(HEADS // heads)]
    window = (max(offsets) + own + LANES - 1) // LANES * LANES
    return pl.pallas_call(
        functools.partial(heads_weight_kernel, window),
        in_specs=[
            pl.BlockSpec(memory_space=pltpu.SMEM),
            pl.BlockSpec(memory_space=pltpu.VMEM),
        ],
        out_shape=jax.ShapeDtypeStruct((heads, width, 3 * LANES), BF16),
        compiler_params=params(),
        cost_estimate=cost(1e6, 2 * w.size + 6 * heads * width * LANES),
        name="heads_weight",
    )(place, w)


def attend_kernel(parts, normed_ref, w_ref, kbias_ref, qkv_ref, lse_ref, *rest):
    ctx_refs, (vt_ref, ot_ref) = rest[:parts], rest[parts:]
    head = pl.program_id(0)
    total = normed_ref.shape[0]
    rows = total // parts
    lane = lax.broadcasted_iota(jnp.int32, (1, LANES), 1)
    one = jnp.where(lane == HEAD_DIM, 1.0, 0.0)
    for part in range(parts):
        span = pl.ds(part * rows, rows)
        triple = dot(normed_ref[span], w_ref[0])
        qkv_ref[0, span, :LANES] = (triple[:, :LANES] + one).astype(BF16)
        qkv_ref[0, span, LANES : 2 * LANES] = (
            triple[:, LANES : 2 * LANES] + kbias_ref[span]
        ).astype(BF16)
        qkv_ref[0, span, 2 * LANES :] = triple[:, 2 * LANES :].astype(BF16)
        vt_ref[:, span] = turned(qkv_ref[0, span, 2 * LANES :])
    step = 3 * LANES if total % (3 * LANES) == 0 else LANES
    for start in range(0, total, step):
        query = qkv_ref[0, pl.ds(start, step), :LANES]
        scores = dot_nt(qkv_ref[0, :, LANES : 2 * LANES], query)
        peak = jnp.max(scores, axis=0, keepdims=True)
        shifted = jnp.exp2((scores - peak) * SCALE2)
        sums = jnp.sum(shifted, axis=0, keepdims=True)
        mixed = dot(vt_ref[...], shifted.astype(BF16)) / sums
        ot_ref[pl.ds(pl.multiple_of(head * HEAD_DIM, 8), HEAD_DIM), pl.ds(start, step)] = mixed[
            :HEAD_DIM
        ]
        lse_ref[0, :, pl.ds(start, step)] = peak * SCALE2 + jnp.log2(sums)

    @pl.when(head == pl.num_programs(0) - 1)
    def _():
        for part in range(parts):
            ctx_refs[part][...] = ot_ref[:, pl.ds(part * rows, rows)].T.astype(BF16)


def attend(parts, normed_all, w_heads, kbias):
    total, width = normed_all.shape
    heads = w_heads.shape[0]
    rows = total // parts
    own = heads * HEAD_DIM
    return pl.pallas_call(
        functools.partial(attend_kernel, parts),
        grid=(heads,),
        in_specs=[
            pl.BlockSpec((total, width), lambda h: (0, 0)),
            pl.BlockSpec((1, width, 3 * LANES), lambda h: (h, 0, 0)),
            pl.BlockSpec((total, LANES), lambda h: (0, 0)),
        ],
        out_specs=[
            pl.BlockSpec((1, total, 3 * LANES), lambda h: (h, 0, 0)),
            pl.BlockSpec((1, 1, total), lambda h: (h, 0, 0)),
        ]
        + [pl.BlockSpec((rows, own), lambda h: (0, 0))] * parts,
        out_shape=[
            jax.ShapeDtypeStruct((heads, total, 3 * LANES), BF16),
            jax.ShapeDtypeStruct((heads, 1, total), F32),
        ]
        + [jax.ShapeDtypeStruct((rows, own), BF16)] * parts,
        scratch_shapes=[pltpu.VMEM((LANES, total), BF16), pltpu.VMEM((own, total), F32)],
        compiler_params=params(),
        cost_estimate=cost(
            2 * heads * total * (width * 3 * LANES + 4 * LANES * total), 6 * total * width
        ),
        name="attend",
    )(normed_all, w_heads, kbias)


def attend_back_kernel(parts, *refs):
    d_refs = refs[:parts]
    (qkv_ref, lse_ref, w_ref, dt_ref, lead_ref, tail_ref) = refs[parts : parts + 6]
    (dot_all, dt_all, acc, dq_ref, dk_ref, dv_ref) = refs[parts + 6 :]
    head = pl.program_id(0)
    heads = pl.num_programs(0)
    total = qkv_ref.shape[1]
    rows = total // parts
    half = rows // 2
    own = dot_all.shape[0]

    @pl.when(head == 0)
    def _():
        for part in range(parts):
            dot_all[:, pl.ds(part * rows, rows)] = d_refs[part][...].astype(F32).T

    base = pl.multiple_of(head * HEAD_DIM, 8)
    upstream_t = jnp.concatenate(
        [dot_all[pl.ds(base, HEAD_DIM), :], jnp.zeros((LANES - HEAD_DIM, total), F32)], 0
    )
    upstream = upstream_t.T.astype(BF16)
    upstream_t = upstream_t.astype(BF16)
    key = qkv_ref[0, :, LANES : 2 * LANES]
    key_t = turned(key)
    value = qkv_ref[0, :, 2 * LANES :]
    step = 3 * LANES if total % (3 * LANES) == 0 else LANES
    for start in range(0, total, step):
        query = qkv_ref[0, pl.ds(start, step), :LANES]
        probs = jnp.exp2(dot_nt(key, query) * SCALE2 - lse_ref[0, :, pl.ds(start, step)])
        d_probs = dot(value, upstream_t[:, start : start + step])
        delta = jnp.sum(probs * d_probs, axis=0, keepdims=True)
        d_raw = (probs * (d_probs - delta) * SCALE).astype(BF16)
        d_value = dot(probs.astype(BF16), upstream[start : start + step])
        d_key = dot(d_raw, query)
        if start == 0:
            dv_ref[...] = d_value
            dk_ref[...] = d_key
        else:
            dv_ref[...] += d_value
            dk_ref[...] += d_key
        d_query = dot(key_t, d_raw)
        dt_all[pl.ds(base, HEAD_DIM), pl.ds(start, step)] = d_query[:HEAD_DIM]
        dq_ref[pl.ds(start, step)] = d_query.T
    dt_all[pl.ds(pl.multiple_of(own + base, 8), HEAD_DIM)] = dk_ref[...].T[:HEAD_DIM]
    dt_all[pl.ds(pl.multiple_of(2 * own + base, 8), HEAD_DIM)] = dv_ref[...].T[:HEAD_DIM]
    for part in range(parts):
        span = pl.ds(part * rows, rows)
        update = (
            dot_nt(dq_ref[span].astype(BF16), w_ref[0, :, :LANES])
            + dot_nt(dk_ref[span].astype(BF16), w_ref[0, :, LANES : 2 * LANES])
            + dot_nt(dv_ref[span].astype(BF16), w_ref[0, :, 2 * LANES :])
        )

        @pl.when(head == 0)
        def _():
            acc[span] = update

        @pl.when(head > 0)
        def _():
            acc[span] += update

    @pl.when(head == heads - 1)
    def _():
        dt_ref[...] = dt_all[...].astype(BF16)
        for part in range(parts):
            lead_ref[part] = acc[pl.ds(part * rows, half)].astype(BF16)
            tail_ref[part] = acc[pl.ds(part * rows + half, half)].astype(BF16)


def attend_back(parts, d_context, qkv, lse, w_heads):
    heads, total, _ = qkv.shape
    width = w_heads.shape[1]
    rows = total // parts
    own = heads * HEAD_DIM
    whole = lambda *shape: pl.BlockSpec(shape, lambda h: (0,) * len(shape))
    return pl.pallas_call(
        functools.partial(attend_back_kernel, parts),
        grid=(heads,),
        in_specs=[whole(rows, own)] * parts
        + [
            pl.BlockSpec((1, total, 3 * LANES), lambda h: (h, 0, 0)),
            pl.BlockSpec((1, 1, total), lambda h: (h, 0, 0)),
            pl.BlockSpec((1, width, 3 * LANES), lambda h: (h, 0, 0)),
        ],
        out_specs=[
            whole(3 * own, total),
            whole(parts, rows // 2, width),
            whole(parts, rows // 2, width),
        ],
        out_shape=[
            jax.ShapeDtypeStruct((3 * own, total), BF16),
            jax.ShapeDtypeStruct((parts, rows // 2, width), BF16),
            jax.ShapeDtypeStruct((parts, rows // 2, width), BF16),
        ],
        scratch_shapes=[
            pltpu.VMEM((own, total), F32),
            pltpu.VMEM((3 * own, total), F32),
            pltpu.VMEM((total, width), F32),
            pltpu.VMEM((total, LANES), F32),
            pltpu.VMEM((total, LANES), F32),
            pltpu.VMEM((total, LANES), F32),
        ],
        compiler_params=params(),
        cost_estimate=cost(
            2 * heads * total * (width * 3 * LANES + 10 * LANES * total), 12 * total * width
        ),
        name="attend_back",
    )(*d_context, qkv, lse, w_heads)


def mlp_kernel(parts, place_ref, *refs):
    ctx_refs = refs[:parts]
    (
        hidden_ref,
        cot_ref,
        proj_ref,
        vec_ref,
        fc1_ref,
        fc1_bias_ref,
        fc2_ref,
        out_ref,
        d_middle_ref,
        d_branch_ref,
        active_t_ref,
        d_pre_ref,
        normed_t_ref,
        ctx_t_ref,
        vec_out_ref,
        fc1_bias_out_ref,
    ) = refs[parts : parts + 16]
    d_ctx_refs = refs[parts + 16 : 2 * parts + 16]
    middle_ref, normed_ref, acc_out, acc_back, turn_ref = refs[2 * parts + 16 :]
    step = pl.program_id(0)
    place = place_ref[0]
    own = ctx_refs[0].shape[1]

    @pl.when(step == 0)
    def _():
        branch = vec_ref[0:1] + hidden_ref[...]
        for part in range(parts):
            at = pl.ds(pl.multiple_of((place ^ part) * own, 8), own)
            branch += dot(ctx_refs[part][...], proj_ref[at, :])
            turn_ref[at] = ctx_refs[part][...].astype(F32).T
        ctx_t_ref[...] = turn_ref[...].astype(BF16)
        middle_ref[...] = branch
        scaled, _ = normalize(branch)
        normed = (scaled * vec_ref[1:2] + vec_ref[2:3]).astype(BF16)
        normed_ref[...] = normed
        normed_t_ref[...] = turned(normed)

    before = dot(normed_ref[...], fc1_ref[...]) + fc1_bias_ref[...]
    cdf = 0.5 + 0.5 * lax.erf(before * math.sqrt(0.5))
    active = (before * cdf).astype(BF16)
    slope = cdf + before * (jnp.exp(-0.5 * before * before) * (1.0 / math.sqrt(2.0 * math.pi)))
    d_before = dot_nt(cot_ref[...], fc2_ref[...]) * slope
    fc1_bias_out_ref[...] = jnp.sum(d_before, axis=0, keepdims=True)
    d_low = d_before.astype(BF16)
    d_pre_ref[...] = d_low
    active_t_ref[...] = turned(active)
    forward = dot(active, fc2_ref[...])
    backward = dot_nt(d_low, fc1_ref[...])

    @pl.when(step == 0)
    def _():
        acc_out[...] = forward
        acc_back[...] = backward

    @pl.when(step > 0)
    def _():
        acc_out[...] += forward
        acc_back[...] += backward

    @pl.when(step == pl.num_programs(0) - 1)
    def _():
        middle = middle_ref[...]
        out_ref[...] = middle + acc_out[...] + vec_ref[3:4]
        scaled, factor = normalize(middle)
        upstream = acc_back[...]
        cot = cot_ref[...].astype(F32)
        d_middle = cot + norm_back(upstream, scaled, factor, vec_ref[1:2])
        d_middle_ref[...] = d_middle
        d_branch = d_middle.astype(BF16)
        d_branch_ref[...] = d_branch
        vec_out_ref[0:1] = jnp.sum(upstream * scaled, axis=0, keepdims=True)
        vec_out_ref[1:2] = jnp.sum(upstream, axis=0, keepdims=True)
        vec_out_ref[2:3] = jnp.sum(d_middle, axis=0, keepdims=True)
        vec_out_ref[3:4] = jnp.sum(cot, axis=0, keepdims=True)
        vec_out_ref[4:] = jnp.zeros((4, vec_out_ref.shape[1]), F32)
        for part in range(parts):
            at = pl.ds(pl.multiple_of((place ^ part) * own, 8), own)
            d_ctx_refs[part][...] = dot_nt(d_branch, proj_ref[at, :]).astype(BF16)


def mlp(parts, place, context, hidden, cot, proj, vecs, fc1, fc1_bias, fc2):
    rows, width = hidden.shape
    ff = fc1.shape[1]
    own = context[0].shape[1]
    chunk = width
    whole = lambda *shape: pl.BlockSpec(shape, lambda i, p: (0,) * len(shape))
    return pl.pallas_call(
        functools.partial(mlp_kernel, parts),
        grid_spec=pltpu.PrefetchScalarGridSpec(
            num_scalar_prefetch=1,
            grid=(ff // chunk,),
            in_specs=[whole(rows, own)] * parts
            + [
                whole(rows, width),
                whole(rows, width),
                whole(width, width),
                whole(8, width),
                pl.BlockSpec((width, chunk), lambda i, p: (0, i)),
                pl.BlockSpec((1, chunk), lambda i, p: (0, i)),
                pl.BlockSpec((chunk, width), lambda i, p: (i, 0)),
            ],
            out_specs=[
                whole(rows, width),
                whole(rows, width),
                whole(rows, width),
                pl.BlockSpec((chunk, rows), lambda i, p: (i, 0)),
                pl.BlockSpec((rows, chunk), lambda i, p: (0, i)),
                whole(width, rows),
                whole(width, rows),
                whole(8, width),
                pl.BlockSpec((1, chunk), lambda i, p: (0, i)),
            ]
            + [whole(rows, own)] * parts,
            scratch_shapes=[
                pltpu.VMEM((rows, width), F32),
                pltpu.VMEM((rows, width), BF16),
                pltpu.VMEM((rows, width), F32),
                pltpu.VMEM((rows, width), F32),
                pltpu.VMEM((width, rows), F32),
            ],
        ),
        out_shape=[
            jax.ShapeDtypeStruct((rows, width), F32),
            jax.ShapeDtypeStruct((rows, width), F32),
            jax.ShapeDtypeStruct((rows, width), BF16),
            jax.ShapeDtypeStruct((ff, rows), BF16),
            jax.ShapeDtypeStruct((rows, ff), BF16),
            jax.ShapeDtypeStruct((width, rows), BF16),
            jax.ShapeDtypeStruct((width, rows), BF16),
            jax.ShapeDtypeStruct((8, width), F32),
            jax.ShapeDtypeStruct((1, ff), F32),
        ]
        + [jax.ShapeDtypeStruct((rows, own), BF16)] * parts,
        compiler_params=params(),
        cost_estimate=cost(8 * rows * width * ff, 4 * width * ff + 24 * rows * width),
        name="feed_forward",
    )(place, *context, hidden, cot, proj, vecs, fc1, fc1_bias, fc2)


def post_kernel(lead_ref, tail_ref, hidden_ref, d_middle_ref, gain_ref, w_ref, din_ref, dskip_ref, low_ref, vec_ref):
    width = hidden_ref.shape[1]
    upstream = jnp.concatenate([lead_ref[...].astype(F32), tail_ref[...].astype(F32)], 0)
    scaled, factor = normalize(hidden_ref[...])
    d_hidden = d_middle_ref[...] + norm_back(upstream, scaled, factor, gain_ref[...])
    low = d_hidden.astype(BF16)
    low_ref[...] = low
    vec_ref[0:1] = jnp.sum(d_hidden, axis=0, keepdims=True)
    vec_ref[1:2] = jnp.sum(upstream * scaled, axis=0, keepdims=True)
    vec_ref[2:3] = jnp.sum(upstream, axis=0, keepdims=True)
    vec_ref[3:] = jnp.zeros((5, width), F32)
    din_ref[...] = dot_nt(low, w_ref[:width])
    dskip_ref[...] = dot_nt(low, w_ref[width:])


def post(lead, tail, hidden, d_middle, gain, w):
    rows, width = hidden.shape
    return pl.pallas_call(
        post_kernel,
        out_shape=(
            jax.ShapeDtypeStruct((rows, width), F32),
            jax.ShapeDtypeStruct((rows, width), F32),
            jax.ShapeDtypeStruct((rows, width), BF16),
            jax.ShapeDtypeStruct((8, width), F32),
        ),
        compiler_params=params(),
        cost_estimate=cost(4 * rows * width * width, 4 * width * width + 20 * rows * width),
        name="input_back",
    )(lead, tail, hidden, d_middle, gain, w)


def pair_kernel(count, where_ref, *refs):
    out_ref = refs[4 * count]
    at = 0
    for index in range(count):
        own_t, peer_t, own, peer = refs[4 * index : 4 * index + 4]
        size = own_t.shape[2]
        out_ref[0, pl.ds(at, size)] = (
            dot(own_t[0, 0], own[...]) + dot(peer_t[0], peer[...])
        ).astype(BF16)
        at += size


def pair_grads(where, groups):
    depth = groups[0][0].shape[0]
    width = groups[0][2].shape[1]
    in_specs, operands, height, flops = [], [], 0, 0
    for own_t, peer_t, own, peer in groups:
        size, rows = own_t.shape[2:]
        in_specs += [
            pl.BlockSpec((1, 1, size, rows), lambda z, w: (z, w[0], 0, 0)),
            pl.BlockSpec((1, size, rows), lambda z, w: (z, 0, 0)),
            pl.BlockSpec((rows, width), lambda z, w: (0, 0)),
            pl.BlockSpec((rows, width), lambda z, w: (0, 0)),
        ]
        operands += [own_t, peer_t, own, peer]
        height += size
        flops += 4 * depth * size * rows * width
    return pl.pallas_call(
        functools.partial(pair_kernel, len(groups)),
        grid_spec=pltpu.PrefetchScalarGridSpec(
            num_scalar_prefetch=1,
            grid=(depth,),
            in_specs=in_specs,
            out_specs=pl.BlockSpec((1, height, width), lambda z, w: (z, 0, 0)),
        ),
        out_shape=jax.ShapeDtypeStruct((depth, height, width), BF16),
        compiler_params=params(),
        cost_estimate=cost(flops, 4 * depth * height * width),
        name="pair_grads",
    )(where, *operands)


def column_kernel(where_ref, own_t, peer_t, own, peer, out_ref):
    for z in range(own_t.shape[0]):
        out_ref[0, z] = (dot(own_t[z, 0], own[...]) + dot(peer_t[z], peer[...])).astype(BF16)


def column_grads(where, parts, own_t, peer_t, own, peer):
    depth, _, size, rows = own_t.shape
    width = own.shape[1] // parts
    return pl.pallas_call(
        column_kernel,
        grid_spec=pltpu.PrefetchScalarGridSpec(
            num_scalar_prefetch=1,
            grid=(parts,),
            in_specs=[
                pl.BlockSpec((depth, 1, size, rows), lambda k, w: (0, w[0], 0, 0)),
                pl.BlockSpec((depth, size, rows), lambda k, w: (0, 0, 0)),
                pl.BlockSpec((rows, width), lambda k, w: (0, k ^ w[1])),
                pl.BlockSpec((rows, width), lambda k, w: (0, k ^ w[1])),
            ],
            out_specs=pl.BlockSpec((1, depth, size, width), lambda k, w: (k, 0, 0, 0)),
        ),
        out_shape=jax.ShapeDtypeStruct((parts, depth, size, width), BF16),
        compiler_params=params(),
        cost_estimate=cost(
            4 * parts * depth * size * rows * width, 4 * parts * depth * size * width
        ),
        name="column_grads",
    )(where, own_t, peer_t, own, peer)


def heads_kernel(normed_ref, dt_ref, out_ref):
    out_ref[...] = lax.dot_general(
        normed_ref[...], dt_ref[...], (((0,), (1,)), ((), ())), preferred_element_type=F32
    ).astype(BF16)


def heads_grads(normed_all, d_triple_t):
    total, width = normed_all.shape
    wide = d_triple_t.shape[0]
    return pl.pallas_call(
        heads_kernel,
        out_shape=jax.ShapeDtypeStruct((width, wide), BF16),
        compiler_params=params(),
        cost_estimate=cost(2 * total * width * wide, 2 * total * (width + wide)),
        name="heads_grads",
    )(normed_all, d_triple_t)


def columns_kernel(place_ref, *refs):
    out_ref = refs[-1]
    size = refs[0].shape[1]
    for k in range(len(refs) - 1):
        at = pl.multiple_of((place_ref[0] ^ k) * size, LANES)
        out_ref[:, pl.ds(at, size)] = refs[k][...].astype(F32)


def put_columns(place, pieces):
    height, size = pieces[0].shape
    count = len(pieces)
    return pl.pallas_call(
        columns_kernel,
        in_specs=[pl.BlockSpec(memory_space=pltpu.SMEM)]
        + [pl.BlockSpec(memory_space=pltpu.VMEM)] * count,
        out_shape=jax.ShapeDtypeStruct((height, count * size), F32),
        compiler_params=params(),
        cost_estimate=cost(1e6, 6 * count * height * size),
        name="put_columns",
    )(place, *pieces)


def head_columns_kernel(place_ref, *refs):
    out_ref = refs[-1]
    count = len(refs) - 1
    size = refs[0].shape[1] // 3
    for j in range(count):
        value = refs[0][...]
        for k in range(1, count):
            value = jnp.where((place_ref[0] ^ k) == j, refs[k][...], value)
        value = value.astype(F32)
        for which in range(3):
            at = (which * count + j) * size
            out_ref[:, at : at + size] = value[:, which * size : (which + 1) * size]


def put_heads(place, pieces):
    height, size = pieces[0].shape
    count = len(pieces)
    return pl.pallas_call(
        head_columns_kernel,
        in_specs=[pl.BlockSpec(memory_space=pltpu.SMEM)]
        + [pl.BlockSpec(memory_space=pltpu.VMEM)] * count,
        out_shape=jax.ShapeDtypeStruct((height, count * size), F32),
        compiler_params=params(),
        cost_estimate=cost(1e6, 6 * count * height * size),
        name="put_heads",
    )(place, *pieces)


def across(value, size, bit):
    return lax.ppermute(value, "seq", [(i, i ^ bit) for i in range(size)])


def other_core(value, size):
    return lax.ppermute(value, "batch", [(i, i ^ 1) for i in range(size)])


def plus(*terms):
    total = terms[0].astype(F32)
    for term in terms[1:]:
        total = total + term.astype(F32)
    return total.astype(BF16)


def bits_of(size):
    return [1 << i for i in range(size.bit_length() - 1)]


def everywhere(value, size):
    if size != 4:
        return [value] + [across(value, size, k) for k in range(1, size)]
    half = value.shape[0] // 2
    near, far = across(value, size, 1), across(value, size, 2)
    lead, tail = across(near[:half], size, 2), across(far[half:], size, 1)
    return [value, near, far, jnp.concatenate([lead, tail], 0)]


def scattered(value, size, bits):
    left = list(range(size))
    for bit in bits:
        keep = [i for i, k in enumerate(left) if not k & bit]
        send = [i for i, k in enumerate(left) if k & bit]
        pick = lambda which: jnp.concatenate([value[i : i + 1] for i in which], 0)
        value = plus(pick(keep), across(pick(send), size, bit))
        left = [left[i] for i in keep]
    return value[0]


def summed(value, size):
    half = (value.shape[0] // 2 + 7) // 8 * 8
    bits = bits_of(size)
    done = []
    for piece, order in ((value[:half], bits), (value[half:], bits[::-1])):
        for bit in order:
            piece = plus(piece, across(piece, size, bit))
        done.append(piece)
    return jnp.concatenate(done, 0)


def down_the_line(value, size, at):
    depth = value.shape[0]
    pick = lambda index: lax.dynamic_index_in_dim(
        value, jnp.clip(index, 0, depth - 1), 0, keepdims=False
    )
    up = down = None
    for t in range(depth - 1):
        send_up = pick(depth - 1 - t + at)
        send_down = pick(t - (depth - 1 - at))
        if t:
            send_up, send_down = plus(send_up, up), plus(send_down, down)
        up = lax.ppermute(
            send_up,
            "batch",
            [(2 * z + c, 2 * z + 2 + c) for z in range(depth - 1) if z <= t for c in (0, 1)],
        )
        down = lax.ppermute(
            send_down,
            "batch",
            [
                (2 * z + c, 2 * z - 2 + c)
                for z in range(1, depth)
                if z >= depth - 1 - t
                for c in (0, 1)
            ],
        )
    return plus(pick(at), up, down)


MESH = pl.DeviceIdType.MESH


def flip(value, k):
    if k == 0:
        return value
    if k == 1:
        return value + 1 - 2 * (value % 2)
    if k == 2:
        return value + 2 - 4 * (value // 2)
    return 3 - value


def add_rows(into, other):
    if len(into.shape) > 2:
        for i in range(into.shape[0]):
            add_rows(into.at[i], other.at[i])
        return
    tile = 16

    def body(i, carry):
        at = pl.ds(pl.multiple_of(i * tile, tile), tile)
        into[at] = (into[at].astype(F32) + other[at].astype(F32)).astype(BF16)
        return carry

    lax.fori_loop(0, into.shape[0] // tile, body, 0)


class Wires:
    def __init__(self, send_sems, recv_sems):
        self.send_sems, self.recv_sems, self.made = send_sems, recv_sems, []

    def copy(self, src, dst, device, when=None):
        index = len(self.made)
        made = Wire(
            pltpu.make_async_remote_copy(
                src_ref=src,
                dst_ref=dst,
                send_sem=self.send_sems.at[index],
                recv_sem=self.recv_sems.at[index],
                device_id=device,
                device_id_type=MESH,
            ),
            when,
        )
        self.made.append(made)
        return made

    def drain(self):
        for wire in self.made:
            if wire.when is None:
                wire.copy.wait_send()
            else:
                pl.when(wire.when)(wire.copy.wait_send)


class Wire:
    def __init__(self, copy, when):
        self.copy, self.when = copy, when
        self.start, self.arrive = copy.start, copy.wait_recv


class Line:
    def __init__(self, wires, depth, chip, up_to, down_to, own, up_in, down_in, begun=False):
        self.depth, self.chip, self.own, self.begun = depth, chip, own, begun
        self.up_in, self.down_in = up_in, down_in
        last = depth - 1
        self.up = {
            d: wires.copy(
                own(d),
                up_in.at[d - 1],
                up_to,
                (chip < d) & (chip > 0) if begun and d == last else chip < d,
            )
            for d in range(1, depth)
        }
        self.down = {
            d: wires.copy(
                own(d),
                down_in.at[d],
                down_to,
                (chip > d) & (chip < last) if begun and d == 0 else chip > d,
            )
            for d in range(last)
        }

    def hop(self, t):
        last = self.depth - 1
        for d in range(1, self.depth):
            z = d - (last - t)
            if 0 <= z < d:

                @pl.when(self.chip == z)
                def _():
                    if z > 0 and not (self.begun and t == 1):
                        self.up[d].arrive()
                        add_rows(self.own(d), self.up_in.at[d - 1])
                    self.up[d].start()

                @pl.when(self.chip == last - z)
                def _():
                    if z > 0 and not (self.begun and t == 1):
                        self.down[last - d].arrive()
                        add_rows(self.own(last - d), self.down_in.at[last - d])
                    self.down[last - d].start()

    def finish(self):
        for d in range(self.depth):

            @pl.when(self.chip == d)
            def _():
                if d > 0:
                    self.up[d].arrive()
                    add_rows(self.own(d), self.up_in.at[d - 1])
                if d < self.depth - 1:
                    self.down[d].arrive()
                    add_rows(self.own(d), self.down_in.at[d])


class Square:
    def __init__(self, wires, to, own, in_one, in_two, src=None, begun=False):
        self.own, self.in_one, self.in_two = own, in_one, in_two
        src = src or own
        self.one, self.two = [], []
        for h, (f, g) in enumerate(((1, 2), (2, 1))):
            if not begun:
                self.one.append(
                    (
                        wires.copy(src(h, 3), in_one.at[h, 1], to[f]),
                        wires.copy(src(h, f), in_one.at[h, 0], to[f]),
                    )
                )
        for h, (f, g) in enumerate(((1, 2), (2, 1))):
            self.two.append(wires.copy(own(h, g), in_two.at[h], to[g]))

    def start(self):
        for i in range(2):
            for h in range(2):
                self.one[h][i].start()

    def middle(self):
        for h, g in ((0, 2), (1, 1)):
            self.one[h][0].arrive()
            add_rows(self.own(h, g), self.in_one.at[h, 1])
            self.two[h].start()
        for h in range(2):
            self.one[h][1].arrive()
            add_rows(self.own(h, 0), self.in_one.at[h, 0])

    def finish(self):
        for h in range(2):
            self.two[h].arrive()
            add_rows(self.own(h, 0), self.in_two.at[h])


class Spread:
    def __init__(self, wires, to, slots):
        rows = slots.shape[1]
        cut = (rows // 2 + 15) // 16 * 16
        self.near = wires.copy(slots.at[0], slots.at[1], to[1])
        self.far = wires.copy(slots.at[0], slots.at[2], to[2])
        lead, tail = pl.ds(0, cut), pl.ds(cut, rows - cut)
        self.lead = wires.copy(slots.at[1, lead], slots.at[3, lead], to[2])
        self.tail = wires.copy(slots.at[2, tail], slots.at[3, tail], to[1])

    def start(self):
        self.near.start()
        self.far.start()

    def relay(self):
        self.near.arrive()
        self.lead.start()
        self.far.arrive()
        self.tail.start()

    def finish(self):
        self.lead.arrive()
        self.tail.arrive()


def reduce_kernel(
    late_hbm,
    up_hbm,
    down_hbm,
    first_a_hbm,
    first_b_hbm,
    lead_hbm,
    tail_hbm,
    normed_hbm,
    dt_hbm,
    joined_hbm,
    joined_peer_hbm,
    hidden_hbm,
    d_middle_hbm,
    w_hbm,
    gain_ref,
    vec_two_ref,
    fc1_bias_ref,
    g_late_hbm,
    g_first_hbm,
    g_heads_hbm,
    g_skip_hbm,
    din_hbm,
    dskip_hbm,
    cond_ref,
    vec_ref,
    l_own,
    l_up,
    l_down,
    f_own,
    f_in,
    f_up,
    f_down,
    f_all,
    q_own,
    q_sum,
    q_up,
    q_down,
    q_all,
    s_own,
    s_one,
    s_two,
    s_z,
    s_up,
    s_down,
    s_all,
    d_own,
    d_one,
    d_two,
    p_one,
    p_two,
    p_all,
    low_ref,
    low_peer,
    c_all,
    v_own,
    v_in,
    send_sems,
    recv_sems,
    local_sems,
):
    depth, late_rows, width = late_hbm.shape
    rows = hidden_hbm.shape[0]
    half = rows // 2
    mid = depth // 2
    slots = c_all.shape[1]
    place = lax.axis_index("seq")
    index = lax.axis_index("batch")
    chip, core = index // 2, index % 2
    last = depth - 1
    to = {1: (index, flip(place, 1)), 2: (index, flip(place, 2)), 3: (index, flip(place, 3))}
    other = (index + 1 - 2 * core, place)
    up_to, down_to = (index + 2, place), (index - 2, place)

    barrier = pltpu.get_barrier_semaphore()
    for device in (to[1], to[2], to[3], other):
        pl.semaphore_signal(barrier, inc=1, device_id=device, device_id_type=MESH)

    @pl.when(chip < last)
    def _():
        pl.semaphore_signal(barrier, inc=1, device_id=up_to, device_id_type=MESH)

    @pl.when(chip > 0)
    def _():
        pl.semaphore_signal(barrier, inc=1, device_id=down_to, device_id_type=MESH)

    pl.semaphore_wait(barrier, 4 + jnp.minimum(chip, 1) + jnp.minimum(last - chip, 1))

    wires = Wires(send_sems, recv_sems)
    taken = [0]

    def local(src, dst):
        taken[0] += 1
        copy = pltpu.make_async_copy(src, dst, local_sems.at[taken[0] - 1])
        copy.start()
        return copy

    d_hbm = (lead_hbm, tail_hbm)
    norm_sum = Square(
        wires,
        to,
        lambda h, k: d_own.at[h, (0, 1, 1, None)[k]],
        d_one,
        d_two,
        src=lambda h, k: d_hbm[h].at[k],
    )
    norm_sum.start()
    d_loads = [
        local(d_hbm[h].at[k], d_own.at[h, i]) for h, ks in ((0, (0, 2)), (1, (0, 1))) for i, k in enumerate(ks)
    ]
    l_loads = [local(late_hbm.at[z], l_own.at[z, pl.ds(0, late_rows)]) for z in range(depth)]
    f_loads = [local(first_a_hbm, f_own.at[0]), local(first_b_hbm, f_own.at[1])]

    l_line = Line(
        wires,
        depth,
        chip,
        up_to,
        down_to,
        lambda d: l_own.at[d, pl.ds(0, late_rows)],
        l_up,
        l_down,
        begun=True,
    )
    for copy in l_loads:
        copy.wait()
    l_own[:, late_rows:] = jnp.zeros((depth, l_own.shape[1] - late_rows, width), BF16)
    up_sem, down_sem = local_sems.at[taken[0]], local_sems.at[taken[0] + 1]
    taken[0] += 2

    @pl.when(chip == 1)
    def _():
        copy = pltpu.make_async_copy(up_hbm, l_up.at[last - 1], up_sem)
        copy.start()
        copy.wait()
        add_rows(l_own.at[last, pl.ds(0, late_rows)], l_up.at[last - 1])

    @pl.when(chip == last - 1)
    def _():
        copy = pltpu.make_async_copy(down_hbm, l_down.at[0], down_sem)
        copy.start()
        copy.wait()
        add_rows(l_own.at[0, pl.ds(0, late_rows)], l_down.at[0])

    l_line.hop(1)

    def heads_part(normed, dt):
        loads = [local(normed_hbm, normed), local(dt_hbm, dt)]
        for copy in loads:
            copy.wait()
        height = normed.shape[1] // (2 * depth)
        step = 3 * LANES
        for part in range(normed.shape[1] // step):
            grads = lax.dot_general(
                normed[:, part * step : (part + 1) * step],
                dt[...],
                (((0,), (1,)), ((), ())),
                preferred_element_type=F32,
            ).astype(BF16)
            q_own[pl.ds(part * step, step)] = grads

    pl.run_scoped(
        heads_part, pltpu.VMEM(normed_hbm.shape, BF16), pltpu.VMEM(dt_hbm.shape, BF16)
    )
    height = q_sum.shape[1]
    q_swap = [
        wires.copy(
            q_own.at[pl.ds(pl.multiple_of((2 * z + 1 - core) * height, 16), height)],
            q_sum.at[z],
            other,
        )
        for z in range(depth)
    ]
    for wire in q_swap:
        wire.start()

    for copy in d_loads:
        copy.wait()
    norm_sum.middle()

    for copy in f_loads:
        copy.wait()
    f_two = [
        wires.copy(f_own.at[h, 1], f_in.at[h], to[2 - h]) for h in range(2)
    ]
    for wire in f_two:
        wire.start()
    for z, wire in enumerate(q_swap):
        wire.arrive()
        add_rows(q_sum.at[z], q_own.at[pl.ds(pl.multiple_of((2 * z + core) * height, 16), height)])
    q_line = Line(wires, depth, chip, up_to, down_to, lambda d: q_sum.at[d], q_up, q_down)
    q_line.hop(0)

    norm_sum.finish()
    low_swap = wires.copy(low_ref, low_peer, other)
    v_swap = wires.copy(v_own.at[0], v_in.at[0], other)

    def back_part(hidden, d_middle):
        loads = [local(hidden_hbm, hidden), local(d_middle_hbm, d_middle)]
        for copy in loads:
            copy.wait()
        upstream = jnp.concatenate(
            [d_own[0, 0].astype(F32), d_own[1, 0].astype(F32)], 0
        )
        scaled, factor = normalize(hidden[...])
        d_hidden = d_middle[...] + norm_back(upstream, scaled, factor, gain_ref[...])
        low_ref[...] = d_hidden.astype(BF16)
        low_swap.start()
        v_own[0] = jnp.zeros(v_own.shape[1:], F32)
        v_own[0, 0:1] = jnp.sum(d_hidden, axis=0, keepdims=True)
        v_own[0, 1:2] = jnp.sum(upstream * scaled, axis=0, keepdims=True)
        v_own[0, 2:3] = jnp.sum(upstream, axis=0, keepdims=True)
        v_own[0, 3:7] = vec_two_ref[0:4]
        v_own[0, 8:12] = fc1_bias_ref[...]
        v_swap.start()

    pl.run_scoped(back_part, pltpu.VMEM(hidden_hbm.shape, F32), pltpu.VMEM(hidden_hbm.shape, F32))

    low_swap.arrive()

    def skip_part(joined, peer):
        loads = [local(joined_hbm.at[:, core], joined), local(joined_peer_hbm, peer)]
        for copy in loads:
            copy.wait()
        chunk = joined.shape[1] // 4
        for z in range(depth):
            grads = dot(joined[z], low_ref[...]) + dot(peer[z], low_peer[...])
            for j in range(4):
                piece = grads[j * chunk : (j + 1) * chunk]
                piece = jnp.concatenate(
                    [piece, jnp.zeros((s_own.shape[2] - chunk, width), F32)], 0
                )
                s_own[flip(place, j), z] = piece.astype(BF16)

    pl.run_scoped(
        skip_part,
        pltpu.VMEM(joined_peer_hbm.shape, BF16),
        pltpu.VMEM(joined_peer_hbm.shape, BF16),
    )
    s_sum = Square(
        wires, to, lambda h, k: s_own.at[k, pl.ds(h * mid, mid)], s_one, s_two
    )
    s_sum.start()

    c_go = [wires.copy(c_all.at[0], c_all.at[k], to[k]) for k in (1, 2, 3)]

    def rows_part(w, stage):
        copy = local(w_hbm.at[pl.ds(0, width)], w)
        copy.wait()
        stage[...] = dot_nt(low_ref[...], w[...])
        c_all[0, :, :width] = stage[:slots].astype(BF16)
        copy = local(w_hbm.at[pl.ds(width, width)], w)
        out = local(stage, din_hbm)
        copy.wait()
        out.wait()
        stage[...] = dot_nt(low_ref[...], w[...])
        c_all[0, :, width:] = stage[:slots].astype(BF16)
        for wire in c_go:
            wire.start()
        local(stage, dskip_hbm).wait()

    pl.run_scoped(rows_part, pltpu.VMEM((width, width), BF16), pltpu.VMEM((rows, width), F32))

    v_swap.arrive()
    v_own[1] = v_own[0] + v_in[0]
    v_up = wires.copy(v_own.at[2], v_in.at[1], up_to, chip < last)
    v_down = wires.copy(v_own.at[3], v_in.at[2], down_to, chip > 0)

    for h in range(2):
        f_two[h].arrive()
        add_rows(f_own.at[h, 0], f_in.at[h])
    f_line = Line(
        wires,
        depth,
        chip,
        up_to,
        down_to,
        lambda d: f_own.at[d // mid, 0, d % mid],
        f_up,
        f_down,
    )
    f_line.hop(0)
    l_line.hop(2)
    q_line.hop(1)
    s_sum.middle()
    f_line.hop(1)
    for t in range(3, last):
        l_line.hop(t)
    for t in range(2, last):
        q_line.hop(t)
    s_sum.finish()
    for d in range(depth):
        s_z[d] = s_own[0, d]
    s_line = Line(wires, depth, chip, up_to, down_to, lambda d: s_z.at[d], s_up, s_down)
    s_line.hop(0)
    for t in range(2, last):
        f_line.hop(t)
    q_line.finish()
    q_all[0] = q_sum[chip]
    q_go = Spread(wires, to, q_all)
    q_go.start()

    v_own[2] = v_own[1]
    v_own[3] = v_own[1]

    @pl.when(chip > 0)
    def _():
        v_up.arrive()
        v_own[2] = v_own[1] + v_in[1]

    @pl.when(chip < last)
    def _():
        v_up.start()

    @pl.when(chip < last)
    def _():
        v_down.arrive()
        v_own[3] = v_own[1] + v_in[2]

    @pl.when(chip > 0)
    def _():
        v_down.start()

    v_own[4] = v_own[2] + v_own[3] - v_own[1]
    v_near = wires.copy(v_own.at[4], v_in.at[3], to[1])
    v_near.start()
    s_line.hop(1)

    l_line.finish()
    chunk = p_all.shape[1]
    part = chunk // 2

    def p_rows(h, k):
        at = pl.multiple_of(flip(place, k) * chunk + h * part, 16)
        return l_own.at[chip, pl.ds(at, part)]

    p_sum = Square(wires, to, p_rows, p_one, p_two)
    p_sum.start()
    f_line.finish()
    f_all[0] = f_own[chip // mid, 0, chip % mid]
    f_go = Spread(wires, to, f_all)
    q_go.relay()
    f_go.start()
    for t in range(2, last):
        s_line.hop(t)
    p_sum.middle()
    v_near.arrive()
    v_own[5] = v_own[4] + v_in[3]
    v_far = wires.copy(v_own.at[5], v_in.at[4], to[2])
    v_far.start()
    s_line.finish()
    s_all[0] = s_z[chip]
    s_go = Spread(wires, to, s_all)
    s_go.start()
    p_sum.finish()
    p_all[0, pl.ds(0, part)] = p_rows(0, 0)[...]
    p_all[0, pl.ds(part, part)] = p_rows(1, 0)[...]
    p_go = Spread(wires, to, p_all)
    p_go.start()
    f_go.relay()
    q_go.finish()

    def heads_out(stage):
        size = q_all.shape[2] // 3
        for j in range(4):
            value = q_all[flip(place, j)].astype(F32)
            for which in range(3):
                at = (which * 4 + j) * size
                stage[:, at : at + size] = value[:, which * size : (which + 1) * size]
        local(stage, g_heads_hbm).wait()

    pl.run_scoped(heads_out, pltpu.VMEM(g_heads_hbm.shape, F32))
    for wire in c_go:
        wire.arrive()
    for j in range(4):
        cond_ref[j * slots : (j + 1) * slots] = c_all[flip(place, j)].astype(F32)
    v_far.arrive()
    vec_ref[...] = v_own[5] + v_in[4]
    s_go.relay()
    p_go.relay()
    f_go.finish()

    def first_out(stage):
        for j in range(4):
            stage[:, j * width : (j + 1) * width] = f_all[flip(place, j)].astype(F32)
        local(stage, g_first_hbm).wait()

    pl.run_scoped(first_out, pltpu.VMEM(g_first_hbm.shape, F32))
    s_go.finish()

    def skip_out(stage):
        size = stage.shape[0] // 4
        for j in range(4):
            stage[j * size : (j + 1) * size] = s_all[flip(place, j), :size].astype(F32)
        local(stage, g_skip_hbm).wait()

    pl.run_scoped(skip_out, pltpu.VMEM(g_skip_hbm.shape, F32))
    p_go.finish()

    def late_out(stage):
        for j in range(4):
            stage[j * chunk : (j + 1) * chunk] = p_all[flip(place, j)].astype(F32)
        local(stage.at[pl.ds(0, late_rows)], g_late_hbm).wait()

    pl.run_scoped(late_out, pltpu.VMEM((4 * chunk, width), F32))
    wires.drain()


def reduce_all(
    late, up, down, first_a, first_b, lead, tail, normed_all, d_triple_t, joined, joined_peer,
    hidden, d_middle, w, gain, vec_two, fc1_bias_grad, slots,
):
    depth, late_rows, width = late.shape
    rows = hidden.shape[0]
    mid = depth // 2
    batch = 2 * depth
    small = first_a.shape[2]
    own = d_triple_t.shape[0]
    chunk = (-(-late_rows // 4) + 31) // 32 * 32
    skip_chunk = (joined.shape[2] // 4 + 15) // 16 * 16
    half = rows // 2
    v = lambda *shape: pltpu.VMEM(shape, BF16)
    ends = depth - 1
    scratch = [
        v(depth, 4 * chunk, width), v(ends, late_rows, width), v(ends, late_rows, width),
        v(2, 2, mid, small, width), v(2, mid, small, width), v(ends, small, width), v(ends, small, width),
        v(4, small, width),
        v(width, own), v(depth, small, own), v(ends, small, own), v(ends, small, own), v(4, small, own),
        v(4, depth, skip_chunk, width), v(2, 2, mid, skip_chunk, width), v(2, mid, skip_chunk, width),
        v(depth, skip_chunk, width), v(ends, skip_chunk, width), v(ends, skip_chunk, width),
        v(4, skip_chunk, width),
        v(2, 2, half, width), v(2, 2, half, width), v(2, half, width),
        v(2, 2, chunk // 2, width), v(2, chunk // 2, width), v(4, chunk, width),
        v(rows, width), v(rows, width), v(4, slots, 2 * width),
        pltpu.VMEM((6, 16, width), F32), pltpu.VMEM((5, 16, width), F32),
        pltpu.SemaphoreType.DMA((96,)), pltpu.SemaphoreType.DMA((96,)), pltpu.SemaphoreType.DMA((64,)),
    ]
    hbm = pl.BlockSpec(memory_space=pl.ANY)
    vmem = pl.BlockSpec(memory_space=pltpu.VMEM)
    f = lambda *shape: jax.ShapeDtypeStruct(shape, F32)
    return pl.pallas_call(
        reduce_kernel,
        in_specs=[hbm] * 14 + [vmem] * 3,
        out_specs=[hbm] * 6 + [vmem] * 2,
        out_shape=[
            f(late_rows, width),
            f(small, 4 * width),
            f(small, 4 * own),
            f(joined.shape[2], width),
            f(rows, width),
            f(rows, width),
            f(4 * slots, 2 * width),
            f(16, width),
        ],
        scratch_shapes=scratch,
        compiler_params=pltpu.CompilerParams(
            vmem_limit_bytes=VMEM_LIMIT, collective_id=0, has_side_effects=True
        ),
        cost_estimate=cost(1e10, 1e8),
        name="reduce_all",
    )(
        late, up, down, first_a, first_b, lead, tail, normed_all, d_triple_t, joined, joined_peer,
        hidden, d_middle, w, gain, vec_two, fc1_bias_grad.reshape(-1, width),
    )


def per_device(
    batch,
    parts,
    image_in,
    cond_in,
    skip_image,
    skip_cond,
    caption_len,
    skip_weight,
    skip_bias,
    first_gain,
    first_bias,
    qkv_weight,
    proj_weight,
    proj_bias,
    second_gain,
    second_bias,
    fc1_weight,
    fc1_bias,
    fc2_weight,
    fc2_bias,
    grad_image,
    grad_cond,
):
    conds = cond_in.shape[0]
    width = image_in.shape[2]
    images = image_in.shape[0]
    ff = fc1_weight.shape[1]
    slots = SLOTS // parts
    rows = slots + images
    total = rows * parts
    heads = HEADS // parts
    depth = batch // 2
    place = lax.axis_index("seq")
    index = lax.axis_index("batch")
    core, chip = index % 2, index // 2
    where = jnp.stack([core, place]).astype(jnp.int32)

    def own_rows(cond, image):
        padded = jnp.pad(cond[:, 0], ((0, SLOTS - conds), (0, 0)))
        lead = lax.dynamic_slice_in_dim(padded, place * slots, slots, 0)
        return jnp.concatenate([lead, image[:, 0]], 0)

    x = own_rows(cond_in, image_in)
    s = own_rows(skip_cond, skip_image)
    cot = own_rows(grad_cond, grad_image)

    hidden, normed, joined_t = pre(
        x, s, skip_weight, skip_bias[None], first_gain[None], first_bias[None]
    )
    normed_all = jnp.concatenate(everywhere(normed, parts), 0)
    own = heads * HEAD_DIM
    w_heads = heads_weight(where[1:], qkv_weight, heads)
    order = place ^ jnp.arange(parts, dtype=jnp.int32)
    position = order[:, None] * slots + jnp.arange(rows, dtype=jnp.int32)[None]
    valid = (jnp.arange(rows)[None] >= slots) | (position <= caption_len[0])
    kbias = jnp.where(
        (jnp.arange(LANES) == HEAD_DIM)[None] & ~valid.reshape(total, 1), F32(-1e30), F32(0)
    )
    qkv, lse, *ctx_parts = attend(parts, normed_all, w_heads, kbias)
    context = [ctx_parts[0]] + [across(ctx_parts[k], parts, k) for k in range(1, parts)]

    zero = jnp.zeros_like(proj_bias)
    vecs = jnp.stack([proj_bias, second_gain, second_bias, fc2_bias, zero, zero, zero, zero])
    (
        out,
        d_middle,
        d_branch,
        active_t,
        d_pre,
        normed2_t,
        ctx_t,
        vec_two,
        fc1_bias_grad,
        *d_ctx_parts,
    ) = mlp(
        parts,
        where[1:],
        context,
        hidden,
        cot,
        proj_weight,
        vecs,
        fc1_weight,
        fc1_bias[None],
        fc2_weight,
    )
    d_context = [d_ctx_parts[0]] + [across(d_ctx_parts[k], parts, k) for k in range(1, parts)]

    def by_core(turned_rows):
        blocks = turned_rows.reshape(depth, 2, -1, rows)
        send = lax.dynamic_index_in_dim(blocks, 1 - core, 1, keepdims=False)
        return blocks, other_core(send, batch)

    active_b, active_p = by_core(active_t)
    normed2_b, normed2_p = by_core(normed2_t)
    ctx_b, ctx_p = by_core(ctx_t)
    joined_b, joined_p = by_core(joined_t)
    cot_p, d_pre_p, d_branch_p = (other_core(v, batch) for v in (cot, d_pre, d_branch))
    late = pair_grads(
        where, [(active_b, active_p, cot, cot_p), (ctx_b, ctx_p, d_branch, d_branch_p)]
    )
    by_columns = (ff // parts) % LANES == 0
    fast = parts == 4 and depth == 4 and by_columns
    if by_columns:
        first = column_grads(where, parts, normed2_b, normed2_p, d_pre, d_pre_p)
        late, first, d_context = lax.optimization_barrier((late, first, d_context))
        middle = depth // 2
    if fast:
        up = lax.ppermute(late[-1], "batch", [(c, 2 + c) for c in (0, 1)])
        down = lax.ppermute(late[0], "batch", [(batch - 2 + c, batch - 4 + c) for c in (0, 1)])
        first_a = (first[0::2, :middle], across(first[1::2, :middle], parts, 1))
        first_b = (first[:2, middle:], across(first[2:, middle:], parts, 2))
    elif by_columns:
        first = jnp.concatenate(
            [
                scattered(first[:, :middle], parts, bits_of(parts)),
                scattered(first[:, middle:], parts, bits_of(parts)[::-1]),
            ],
            0,
        )
    if not by_columns:
        first = pair_grads(where, [(normed2_b, normed2_p, d_pre, d_pre_p)])
    def all_conds(lead):
        pieces = [lead] + [across(lead, parts, k) for k in range(1, parts)]
        full = jnp.zeros((SLOTS, lead.shape[1]), F32)
        for k in range(parts):
            full = lax.dynamic_update_slice_in_dim(
                full, pieces[k].astype(F32), (place ^ k) * slots, 0
            )
        return full[:conds, None]

    d_triple_t, d_lead, d_tail = attend_back(parts, d_context, qkv, lse, w_heads)
    if fast:
        d_lead, d_tail, d_triple_t, up, down, first_a, first_b = lax.optimization_barrier(
            (d_lead, d_tail, d_triple_t, up, down, first_a, first_b)
        )
        g_late, wgrad_fc1, wgrad_qkv, wgrad_skip, d_in, d_skip, d_cond, vec = reduce_all(
            late, up, down, plus(*first_a), plus(*first_b), d_lead, d_tail, normed_all,
            d_triple_t, joined_b, joined_p, hidden, d_middle, skip_weight, first_gain[None],
            vec_two, fc1_bias_grad, slots,
        )
        fc2_rows = ff // batch
        share = lambda v: lax.dynamic_slice_in_dim(v, index * (v.size // batch), v.size // batch, 0)
        vec = [share(vec[i]) for i in (0, 1, 2, 5, 3, 4)] + [share(vec[8:12].reshape(-1)), share(vec[6])]
        return (
            out[slots:, None],
            all_conds(out[:slots].astype(BF16)),
            d_in[slots:, None],
            d_cond[:conds, None, :width],
            d_skip[slots:, None],
            d_cond[:conds, None, width:],
            wgrad_skip,
            vec[0],
            vec[1],
            vec[2],
            wgrad_qkv,
            g_late[fc2_rows:],
            vec[3],
            vec[4],
            vec[5],
            wgrad_fc1,
            vec[6],
            g_late[:fc2_rows],
            vec[7],
        )

    d_lead = scattered(d_lead, parts, bits_of(parts))
    d_tail = scattered(d_tail, parts, bits_of(parts)[::-1])
    heads_grad = heads_grads(normed_all, d_triple_t).reshape(depth, 2, -1, 3 * own)
    heads_grad = plus(
        lax.dynamic_index_in_dim(heads_grad, core, 1, keepdims=False),
        other_core(lax.dynamic_index_in_dim(heads_grad, 1 - core, 1, keepdims=False), batch),
    )
    heads_grad = everywhere(down_the_line(heads_grad, batch, chip), parts)
    wgrad_qkv = put_heads(where[1:], heads_grad)

    d_in, d_skip, d_low, vec_one = post(
        d_lead, d_tail, hidden, d_middle, first_gain[None], skip_weight
    )
    d_low_p = other_core(d_low, batch)
    last = pair_grads(where, [(joined_b, joined_p, d_low, d_low_p)])

    late = down_the_line(late, batch, chip)
    first = down_the_line(first, batch, chip)
    late = summed(late, parts)
    if by_columns:
        fc1_cols = everywhere(first, parts)
        wgrad_fc1 = put_columns(where[1:], fc1_cols)
    else:
        wgrad_fc1 = summed(first, parts).astype(F32)

    vectors = [
        vec_one[0],
        vec_one[1],
        vec_one[2],
        vec_two[2],
        vec_two[0],
        vec_two[1],
        fc1_bias_grad[0],
        vec_two[3],
    ]
    sizes = [v.shape[0] // batch for v in vectors]
    packed = jnp.concatenate([v.reshape(batch, -1) for v in vectors], 1)
    packed = packed.reshape(depth, 2, -1)
    packed = lax.dynamic_index_in_dim(packed, core, 1, keepdims=False) + other_core(
        lax.dynamic_index_in_dim(packed, 1 - core, 1, keepdims=False), batch
    )
    packed = jnp.pad(packed, ((0, 0), (0, 16 * width - packed.shape[1]))).reshape(depth, 16, width)
    last = jnp.concatenate([last, packed.astype(BF16)], 1)
    last = summed(down_the_line(last, batch, chip), parts)
    skip_rows = 2 * width // batch
    wgrad_skip = last[:skip_rows].astype(F32)
    flat = last[skip_rows:].reshape(-1).astype(F32)
    vector_out, at = [], 0
    for size in sizes:
        vector_out.append(flat[at : at + size])
        at += size
    fc2_rows = ff // batch
    wgrad_fc2 = late[:fc2_rows].astype(F32)
    wgrad_proj = late[fc2_rows:].astype(F32)

    out_cond = all_conds(out[:slots].astype(BF16))
    d_cond = all_conds(jnp.concatenate([d_in[:slots], d_skip[:slots]], 1).astype(BF16))
    return (
        out[slots:, None],
        out_cond,
        d_in[slots:, None],
        d_cond[:, :, :width],
        d_skip[slots:, None],
        d_cond[:, :, width:],
        wgrad_skip,
        vector_out[0],
        vector_out[1],
        vector_out[2],
        wgrad_qkv,
        wgrad_proj,
        vector_out[3],
        vector_out[4],
        vector_out[5],
        wgrad_fc1,
        vector_out[6],
        wgrad_fc2,
        vector_out[7],
    )


def solution(mesh):
    tokens, conds, shared = P("seq", "batch", None), P(None, "batch", None), P()
    return jax.shard_map(
        functools.partial(per_device, mesh.shape["batch"], mesh.shape["seq"]),
        mesh=mesh,
        in_specs=(tokens, conds, tokens, conds, P("batch")) + (shared,) * 13 + (tokens, conds),
        out_specs=(tokens, conds) * 3
        + (
            P("batch", None),
            P("batch"),
            P("batch"),
            P("batch"),
            P("batch", None),
            P("batch", None),
            P("batch"),
            P("batch"),
            P("batch"),
            P("batch", None),
            P("batch"),
            P("batch", None),
            P("batch"),
        ),
        check_vma=False,
    )
```

```python
import functools
import math

import jax
import jax.numpy as jnp
from jax import lax
from jax.experimental import pallas as pl
from jax.experimental.pallas import tpu as pltpu
from jax.sharding import PartitionSpec as P

HEADS = 16
HEAD_DIM = 72
LANES = 128
SLOTS = 128
F32 = jnp.float32
BF16 = jnp.bfloat16
VMEM_LIMIT = 60 * 1024 * 1024
SCALE = 1.0 / math.sqrt(HEAD_DIM)
SCALE2 = SCALE * math.log2(math.e)


def dot(left, right):
    return jnp.dot(left, right, preferred_element_type=F32)


def dot_nt(left, right):
    return lax.dot_general(left, right, (((1,), (1,)), ((), ())), preferred_element_type=F32)


def dot_tn(left, right):
    return lax.dot_general(left, right, (((0,), (0,)), ((), ())), preferred_element_type=F32)


def params():
    return pltpu.CompilerParams(vmem_limit_bytes=VMEM_LIMIT)


def cost(flops, nbytes):
    return pl.CostEstimate(flops=int(flops), bytes_accessed=int(nbytes), transcendentals=0)


def turned(value):
    return value.astype(F32).T.astype(BF16)


def normalize(values):
    centre = values - jnp.mean(values, axis=-1, keepdims=True)
    factor = lax.rsqrt(jnp.mean(centre * centre, axis=-1, keepdims=True) + 1e-5)
    return centre * factor, factor


def norm_back(upstream, scaled, factor, gain):
    inner = upstream * gain
    centred = inner - jnp.mean(inner, axis=-1, keepdims=True)
    return factor * (centred - scaled * jnp.mean(inner * scaled, axis=-1, keepdims=True))


def pre_kernel(x_ref, s_ref, w_ref, bias_ref, gain_ref, shift_ref, hidden_ref, normed_ref, turn_ref):
    width = x_ref.shape[1]
    hidden = dot(x_ref[...], w_ref[:width]) + dot(s_ref[...], w_ref[width:]) + bias_ref[...]
    hidden_ref[...] = hidden
    scaled, _ = normalize(hidden)
    normed_ref[...] = (scaled * gain_ref[...] + shift_ref[...]).astype(BF16)
    turn_ref[:width] = turned(x_ref[...])
    turn_ref[width:] = turned(s_ref[...])


def pre(x, s, w, bias, gain, shift):
    rows, width = x.shape
    return pl.pallas_call(
        pre_kernel,
        out_shape=(
            jax.ShapeDtypeStruct((rows, width), F32),
            jax.ShapeDtypeStruct((rows, width), BF16),
            jax.ShapeDtypeStruct((2 * width, rows), BF16),
        ),
        compiler_params=params(),
        cost_estimate=cost(4 * rows * width * width, 4 * width * width + 12 * rows * width),
        name="input_linear",
    )(x, s, w, bias, gain, shift)


def heads_weight_kernel(window, place_ref, w_ref, out_ref):
    heads = out_ref.shape[0]
    width = w_ref.shape[0]
    own = heads * HEAD_DIM
    keep = lax.broadcasted_iota(jnp.int32, (width, LANES), 1) < HEAD_DIM
    place = place_ref[0]
    for which in range(3):
        first = place * own + which * width
        start = jnp.minimum(first // LANES * LANES, 3 * width - window)
        value = w_ref[:, pl.ds(pl.multiple_of(start, LANES), window)].astype(F32)
        value = pltpu.roll(value, lax.rem(window - (first - start), window), 1)
        for head in range(heads):
            turned_back = value if head == 0 else pltpu.roll(value, window - head * HEAD_DIM, 1)
            out_ref[head, :, which * LANES : (which + 1) * LANES] = jnp.where(
                keep, turned_back[:, :LANES], 0.0
            ).astype(BF16)


def heads_weight(place, w, heads):
    width = w.shape[0]
    own = heads * HEAD_DIM
    offsets = [p * own % LANES for p in range(HEADS // heads)]
    window = (max(offsets) + own + LANES - 1) // LANES * LANES
    return pl.pallas_call(
        functools.partial(heads_weight_kernel, window),
        in_specs=[
            pl.BlockSpec(memory_space=pltpu.SMEM),
            pl.BlockSpec(memory_space=pltpu.VMEM),
        ],
        out_shape=jax.ShapeDtypeStruct((heads, width, 3 * LANES), BF16),
        compiler_params=params(),
        cost_estimate=cost(1e6, 2 * w.size + 6 * heads * width * LANES),
        name="heads_weight",
    )(place, w)


def attend_kernel(parts, normed_ref, w_ref, kbias_ref, qkv_ref, lse_ref, *rest):
    ctx_refs, (vt_ref, ot_ref) = rest[:parts], rest[parts:]
    head = pl.program_id(0)
    total = normed_ref.shape[0]
    rows = total // parts
    lane = lax.broadcasted_iota(jnp.int32, (1, LANES), 1)
    one = jnp.where(lane == HEAD_DIM, 1.0, 0.0)
    for part in range(parts):
        span = pl.ds(part * rows, rows)
        triple = dot(normed_ref[span], w_ref[0])
        qkv_ref[0, span, :LANES] = (triple[:, :LANES] + one).astype(BF16)
        qkv_ref[0, span, LANES : 2 * LANES] = (
            triple[:, LANES : 2 * LANES] + kbias_ref[span]
        ).astype(BF16)
        qkv_ref[0, span, 2 * LANES :] = triple[:, 2 * LANES :].astype(BF16)
        vt_ref[:, span] = turned(qkv_ref[0, span, 2 * LANES :])
    step = 3 * LANES if total % (3 * LANES) == 0 else LANES
    for start in range(0, total, step):
        query = qkv_ref[0, pl.ds(start, step), :LANES]
        scores = dot_nt(qkv_ref[0, :, LANES : 2 * LANES], query)
        peak = jnp.max(scores, axis=0, keepdims=True)
        shifted = jnp.exp2((scores - peak) * SCALE2)
        sums = jnp.sum(shifted, axis=0, keepdims=True)
        mixed = dot(vt_ref[...], shifted.astype(BF16)) / sums
        ot_ref[pl.ds(pl.multiple_of(head * HEAD_DIM, 8), HEAD_DIM), pl.ds(start, step)] = mixed[
            :HEAD_DIM
        ]
        lse_ref[0, :, pl.ds(start, step)] = peak * SCALE2 + jnp.log2(sums)

    @pl.when(head == pl.num_programs(0) - 1)
    def _():
        for part in range(parts):
            ctx_refs[part][...] = ot_ref[:, pl.ds(part * rows, rows)].T.astype(BF16)


def attend(parts, normed_all, w_heads, kbias):
    total, width = normed_all.shape
    heads = w_heads.shape[0]
    rows = total // parts
    own = heads * HEAD_DIM
    return pl.pallas_call(
        functools.partial(attend_kernel, parts),
        grid=(heads,),
        in_specs=[
            pl.BlockSpec((total, width), lambda h: (0, 0)),
            pl.BlockSpec((1, width, 3 * LANES), lambda h: (h, 0, 0)),
            pl.BlockSpec((total, LANES), lambda h: (0, 0)),
        ],
        out_specs=[
            pl.BlockSpec((1, total, 3 * LANES), lambda h: (h, 0, 0)),
            pl.BlockSpec((1, 1, total), lambda h: (h, 0, 0)),
        ]
        + [pl.BlockSpec((rows, own), lambda h: (0, 0))] * parts,
        out_shape=[
            jax.ShapeDtypeStruct((heads, total, 3 * LANES), BF16),
            jax.ShapeDtypeStruct((heads, 1, total), F32),
        ]
        + [jax.ShapeDtypeStruct((rows, own), BF16)] * parts,
        scratch_shapes=[pltpu.VMEM((LANES, total), BF16), pltpu.VMEM((own, total), F32)],
        compiler_params=params(),
        cost_estimate=cost(
            2 * heads * total * (width * 3 * LANES + 4 * LANES * total), 6 * total * width
        ),
        name="attend",
    )(normed_all, w_heads, kbias)


def attend_back_kernel(parts, *refs):
    d_refs = refs[:parts]
    (qkv_ref, lse_ref, w_ref, dt_ref, lead_ref, tail_ref) = refs[parts : parts + 6]
    (dot_all, dt_all, acc, dq_ref, dk_ref, dv_ref) = refs[parts + 6 :]
    head = pl.program_id(0)
    heads = pl.num_programs(0)
    total = qkv_ref.shape[1]
    rows = total // parts
    half = rows // 2
    own = dot_all.shape[0]

    @pl.when(head == 0)
    def _():
        for part in range(parts):
            dot_all[:, pl.ds(part * rows, rows)] = d_refs[part][...].astype(F32).T

    base = pl.multiple_of(head * HEAD_DIM, 8)
    upstream_t = jnp.concatenate(
        [dot_all[pl.ds(base, HEAD_DIM), :], jnp.zeros((LANES - HEAD_DIM, total), F32)], 0
    )
    upstream = upstream_t.T.astype(BF16)
    upstream_t = upstream_t.astype(BF16)
    key = qkv_ref[0, :, LANES : 2 * LANES]
    key_t = turned(key)
    value = qkv_ref[0, :, 2 * LANES :]
    step = 3 * LANES if total % (3 * LANES) == 0 else LANES
    for start in range(0, total, step):
        query = qkv_ref[0, pl.ds(start, step), :LANES]
        probs = jnp.exp2(dot_nt(key, query) * SCALE2 - lse_ref[0, :, pl.ds(start, step)])
        d_probs = dot(value, upstream_t[:, start : start + step])
        delta = jnp.sum(probs * d_probs, axis=0, keepdims=True)
        d_raw = (probs * (d_probs - delta) * SCALE).astype(BF16)
        d_value = dot(probs.astype(BF16), upstream[start : start + step])
        d_key = dot(d_raw, query)
        if start == 0:
            dv_ref[...] = d_value
            dk_ref[...] = d_key
        else:
            dv_ref[...] += d_value
            dk_ref[...] += d_key
        d_query = dot(key_t, d_raw)
        dt_all[pl.ds(base, HEAD_DIM), pl.ds(start, step)] = d_query[:HEAD_DIM]
        dq_ref[pl.ds(start, step)] = d_query.T
    dt_all[pl.ds(pl.multiple_of(own + base, 8), HEAD_DIM)] = dk_ref[...].T[:HEAD_DIM]
    dt_all[pl.ds(pl.multiple_of(2 * own + base, 8), HEAD_DIM)] = dv_ref[...].T[:HEAD_DIM]
    for part in range(parts):
        span = pl.ds(part * rows, rows)
        update = (
            dot_nt(dq_ref[span].astype(BF16), w_ref[0, :, :LANES])
            + dot_nt(dk_ref[span].astype(BF16), w_ref[0, :, LANES : 2 * LANES])
            + dot_nt(dv_ref[span].astype(BF16), w_ref[0, :, 2 * LANES :])
        )

        @pl.when(head == 0)
        def _():
            acc[span] = update

        @pl.when(head > 0)
        def _():
            acc[span] += update

    @pl.when(head == heads - 1)
    def _():
        dt_ref[...] = dt_all[...].astype(BF16)
        for part in range(parts):
            lead_ref[part] = acc[pl.ds(part * rows, half)].astype(BF16)
            tail_ref[part] = acc[pl.ds(part * rows + half, half)].astype(BF16)


def attend_back(parts, d_context, qkv, lse, w_heads):
    heads, total, _ = qkv.shape
    width = w_heads.shape[1]
    rows = total // parts
    own = heads * HEAD_DIM
    whole = lambda *shape: pl.BlockSpec(shape, lambda h: (0,) * len(shape))
    return pl.pallas_call(
        functools.partial(attend_back_kernel, parts),
        grid=(heads,),
        in_specs=[whole(rows, own)] * parts
        + [
            pl.BlockSpec((1, total, 3 * LANES), lambda h: (h, 0, 0)),
            pl.BlockSpec((1, 1, total), lambda h: (h, 0, 0)),
            pl.BlockSpec((1, width, 3 * LANES), lambda h: (h, 0, 0)),
        ],
        out_specs=[
            whole(3 * own, total),
            whole(parts, rows // 2, width),
            whole(parts, rows // 2, width),
        ],
        out_shape=[
            jax.ShapeDtypeStruct((3 * own, total), BF16),
            jax.ShapeDtypeStruct((parts, rows // 2, width), BF16),
            jax.ShapeDtypeStruct((parts, rows // 2, width), BF16),
        ],
        scratch_shapes=[
            pltpu.VMEM((own, total), F32),
            pltpu.VMEM((3 * own, total), F32),
            pltpu.VMEM((total, width), F32),
            pltpu.VMEM((total, LANES), F32),
            pltpu.VMEM((total, LANES), F32),
            pltpu.VMEM((total, LANES), F32),
        ],
        compiler_params=params(),
        cost_estimate=cost(
            2 * heads * total * (width * 3 * LANES + 10 * LANES * total), 12 * total * width
        ),
        name="attend_back",
    )(*d_context, qkv, lse, w_heads)


def mlp_kernel(parts, place_ref, *refs):
    ctx_refs = refs[:parts]
    (
        hidden_ref,
        cot_ref,
        proj_ref,
        vec_ref,
        fc1_ref,
        fc1_bias_ref,
        fc2_ref,
        out_ref,
        d_middle_ref,
        d_branch_ref,
        active_t_ref,
        d_pre_ref,
        normed_t_ref,
        ctx_t_ref,
        vec_out_ref,
        fc1_bias_out_ref,
    ) = refs[parts : parts + 16]
    d_ctx_refs = refs[parts + 16 : 2 * parts + 16]
    middle_ref, normed_ref, acc_out, acc_back, turn_ref = refs[2 * parts + 16 :]
    step = pl.program_id(0)
    place = place_ref[0]
    own = ctx_refs[0].shape[1]

    @pl.when(step == 0)
    def _():
        branch = vec_ref[0:1] + hidden_ref[...]
        for part in range(parts):
            at = pl.ds(pl.multiple_of((place ^ part) * own, 8), own)
            branch += dot(ctx_refs[part][...], proj_ref[at, :])
            turn_ref[at] = ctx_refs[part][...].astype(F32).T
        ctx_t_ref[...] = turn_ref[...].astype(BF16)
        middle_ref[...] = branch
        scaled, _ = normalize(branch)
        normed = (scaled * vec_ref[1:2] + vec_ref[2:3]).astype(BF16)
        normed_ref[...] = normed
        normed_t_ref[...] = turned(normed)

    before = dot(normed_ref[...], fc1_ref[...]) + fc1_bias_ref[...]
    cdf = 0.5 + 0.5 * lax.erf(before * math.sqrt(0.5))
    active = (before * cdf).astype(BF16)
    slope = cdf + before * (jnp.exp(-0.5 * before * before) * (1.0 / math.sqrt(2.0 * math.pi)))
    d_before = dot_nt(cot_ref[...], fc2_ref[...]) * slope
    fc1_bias_out_ref[...] = jnp.sum(d_before, axis=0, keepdims=True)
    d_low = d_before.astype(BF16)
    d_pre_ref[...] = d_low
    active_t_ref[...] = turned(active)
    forward = dot(active, fc2_ref[...])
    backward = dot_nt(d_low, fc1_ref[...])

    @pl.when(step == 0)
    def _():
        acc_out[...] = forward
        acc_back[...] = backward

    @pl.when(step > 0)
    def _():
        acc_out[...] += forward
        acc_back[...] += backward

    @pl.when(step == pl.num_programs(0) - 1)
    def _():
        middle = middle_ref[...]
        out_ref[...] = middle + acc_out[...] + vec_ref[3:4]
        scaled, factor = normalize(middle)
        upstream = acc_back[...]
        cot = cot_ref[...].astype(F32)
        d_middle = cot + norm_back(upstream, scaled, factor, vec_ref[1:2])
        d_middle_ref[...] = d_middle
        d_branch = d_middle.astype(BF16)
        d_branch_ref[...] = d_branch
        vec_out_ref[0:1] = jnp.sum(upstream * scaled, axis=0, keepdims=True)
        vec_out_ref[1:2] = jnp.sum(upstream, axis=0, keepdims=True)
        vec_out_ref[2:3] = jnp.sum(d_middle, axis=0, keepdims=True)
        vec_out_ref[3:4] = jnp.sum(cot, axis=0, keepdims=True)
        vec_out_ref[4:] = jnp.zeros((4, vec_out_ref.shape[1]), F32)
        for part in range(parts):
            at = pl.ds(pl.multiple_of((place ^ part) * own, 8), own)
            d_ctx_refs[part][...] = dot_nt(d_branch, proj_ref[at, :]).astype(BF16)


def mlp(parts, place, context, hidden, cot, proj, vecs, fc1, fc1_bias, fc2):
    rows, width = hidden.shape
    ff = fc1.shape[1]
    own = context[0].shape[1]
    chunk = width
    whole = lambda *shape: pl.BlockSpec(shape, lambda i, p: (0,) * len(shape))
    return pl.pallas_call(
        functools.partial(mlp_kernel, parts),
        grid_spec=pltpu.PrefetchScalarGridSpec(
            num_scalar_prefetch=1,
            grid=(ff // chunk,),
            in_specs=[whole(rows, own)] * parts
            + [
                whole(rows, width),
                whole(rows, width),
                whole(width, width),
                whole(8, width),
                pl.BlockSpec((width, chunk), lambda i, p: (0, i)),
                pl.BlockSpec((1, chunk), lambda i, p: (0, i)),
                pl.BlockSpec((chunk, width), lambda i, p: (i, 0)),
            ],
            out_specs=[
                whole(rows, width),
                whole(rows, width),
                whole(rows, width),
                pl.BlockSpec((chunk, rows), lambda i, p: (i, 0)),
                pl.BlockSpec((rows, chunk), lambda i, p: (0, i)),
                whole(width, rows),
                whole(width, rows),
                whole(8, width),
                pl.BlockSpec((1, chunk), lambda i, p: (0, i)),
            ]
            + [whole(rows, own)] * parts,
            scratch_shapes=[
                pltpu.VMEM((rows, width), F32),
                pltpu.VMEM((rows, width), BF16),
                pltpu.VMEM((rows, width), F32),
                pltpu.VMEM((rows, width), F32),
                pltpu.VMEM((width, rows), F32),
            ],
        ),
        out_shape=[
            jax.ShapeDtypeStruct((rows, width), F32),
            jax.ShapeDtypeStruct((rows, width), F32),
            jax.ShapeDtypeStruct((rows, width), BF16),
            jax.ShapeDtypeStruct((ff, rows), BF16),
            jax.ShapeDtypeStruct((rows, ff), BF16),
            jax.ShapeDtypeStruct((width, rows), BF16),
            jax.ShapeDtypeStruct((width, rows), BF16),
            jax.ShapeDtypeStruct((8, width), F32),
            jax.ShapeDtypeStruct((1, ff), F32),
        ]
        + [jax.ShapeDtypeStruct((rows, own), BF16)] * parts,
        compiler_params=params(),
        cost_estimate=cost(8 * rows * width * ff, 4 * width * ff + 24 * rows * width),
        name="feed_forward",
    )(place, *context, hidden, cot, proj, vecs, fc1, fc1_bias, fc2)


def post_kernel(lead_ref, tail_ref, hidden_ref, d_middle_ref, gain_ref, w_ref, din_ref, dskip_ref, low_ref, vec_ref):
    width = hidden_ref.shape[1]
    upstream = jnp.concatenate([lead_ref[...].astype(F32), tail_ref[...].astype(F32)], 0)
    scaled, factor = normalize(hidden_ref[...])
    d_hidden = d_middle_ref[...] + norm_back(upstream, scaled, factor, gain_ref[...])
    low = d_hidden.astype(BF16)
    low_ref[...] = low
    vec_ref[0:1] = jnp.sum(d_hidden, axis=0, keepdims=True)
    vec_ref[1:2] = jnp.sum(upstream * scaled, axis=0, keepdims=True)
    vec_ref[2:3] = jnp.sum(upstream, axis=0, keepdims=True)
    vec_ref[3:] = jnp.zeros((5, width), F32)
    din_ref[...] = dot_nt(low, w_ref[:width])
    dskip_ref[...] = dot_nt(low, w_ref[width:])


def post(lead, tail, hidden, d_middle, gain, w):
    rows, width = hidden.shape
    return pl.pallas_call(
        post_kernel,
        out_shape=(
            jax.ShapeDtypeStruct((rows, width), F32),
            jax.ShapeDtypeStruct((rows, width), F32),
            jax.ShapeDtypeStruct((rows, width), BF16),
            jax.ShapeDtypeStruct((8, width), F32),
        ),
        compiler_params=params(),
        cost_estimate=cost(4 * rows * width * width, 4 * width * width + 20 * rows * width),
        name="input_back",
    )(lead, tail, hidden, d_middle, gain, w)


def pair_kernel(count, where_ref, *refs):
    out_ref = refs[4 * count]
    at = 0
    for index in range(count):
        own_t, peer_t, own, peer = refs[4 * index : 4 * index + 4]
        size = own_t.shape[2]
        out_ref[0, pl.ds(at, size)] = (
            dot(own_t[0, 0], own[...]) + dot(peer_t[0], peer[...])
        ).astype(BF16)
        at += size


def pair_grads(where, groups):
    depth = groups[0][0].shape[0]
    width = groups[0][2].shape[1]
    in_specs, operands, height, flops = [], [], 0, 0
    for own_t, peer_t, own, peer in groups:
        size, rows = own_t.shape[2:]
        in_specs += [
            pl.BlockSpec((1, 1, size, rows), lambda z, w: (z, w[0], 0, 0)),
            pl.BlockSpec((1, size, rows), lambda z, w: (z, 0, 0)),
            pl.BlockSpec((rows, width), lambda z, w: (0, 0)),
            pl.BlockSpec((rows, width), lambda z, w: (0, 0)),
        ]
        operands += [own_t, peer_t, own, peer]
        height += size
        flops += 4 * depth * size * rows * width
    return pl.pallas_call(
        functools.partial(pair_kernel, len(groups)),
        grid_spec=pltpu.PrefetchScalarGridSpec(
            num_scalar_prefetch=1,
            grid=(depth,),
            in_specs=in_specs,
            out_specs=pl.BlockSpec((1, height, width), lambda z, w: (z, 0, 0)),
        ),
        out_shape=jax.ShapeDtypeStruct((depth, height, width), BF16),
        compiler_params=params(),
        cost_estimate=cost(flops, 4 * depth * height * width),
        name="pair_grads",
    )(where, *operands)


def column_kernel(where_ref, own_t, peer_t, own, peer, out_ref):
    for z in range(own_t.shape[0]):
        out_ref[0, z] = (dot(own_t[z, 0], own[...]) + dot(peer_t[z], peer[...])).astype(BF16)


def column_grads(where, parts, own_t, peer_t, own, peer):
    depth, _, size, rows = own_t.shape
    width = own.shape[1] // parts
    return pl.pallas_call(
        column_kernel,
        grid_spec=pltpu.PrefetchScalarGridSpec(
            num_scalar_prefetch=1,
            grid=(parts,),
            in_specs=[
                pl.BlockSpec((depth, 1, size, rows), lambda k, w: (0, w[0], 0, 0)),
                pl.BlockSpec((depth, size, rows), lambda k, w: (0, 0, 0)),
                pl.BlockSpec((rows, width), lambda k, w: (0, k ^ w[1])),
                pl.BlockSpec((rows, width), lambda k, w: (0, k ^ w[1])),
            ],
            out_specs=pl.BlockSpec((1, depth, size, width), lambda k, w: (k, 0, 0, 0)),
        ),
        out_shape=jax.ShapeDtypeStruct((parts, depth, size, width), BF16),
        compiler_params=params(),
        cost_estimate=cost(
            4 * parts * depth * size * rows * width, 4 * parts * depth * size * width
        ),
        name="column_grads",
    )(where, own_t, peer_t, own, peer)


def heads_kernel(normed_ref, dt_ref, out_ref):
    out_ref[...] = lax.dot_general(
        normed_ref[...], dt_ref[...], (((0,), (1,)), ((), ())), preferred_element_type=F32
    ).astype(BF16)


def heads_grads(normed_all, d_triple_t):
    total, width = normed_all.shape
    wide = d_triple_t.shape[0]
    return pl.pallas_call(
        heads_kernel,
        out_shape=jax.ShapeDtypeStruct((width, wide), BF16),
        compiler_params=params(),
        cost_estimate=cost(2 * total * width * wide, 2 * total * (width + wide)),
        name="heads_grads",
    )(normed_all, d_triple_t)


def columns_kernel(place_ref, *refs):
    out_ref = refs[-1]
    size = refs[0].shape[1]
    for k in range(len(refs) - 1):
        at = pl.multiple_of((place_ref[0] ^ k) * size, LANES)
        out_ref[:, pl.ds(at, size)] = refs[k][...].astype(F32)


def put_columns(place, pieces):
    height, size = pieces[0].shape
    count = len(pieces)
    return pl.pallas_call(
        columns_kernel,
        in_specs=[pl.BlockSpec(memory_space=pltpu.SMEM)]
        + [pl.BlockSpec(memory_space=pltpu.VMEM)] * count,
        out_shape=jax.ShapeDtypeStruct((height, count * size), F32),
        compiler_params=params(),
        cost_estimate=cost(1e6, 6 * count * height * size),
        name="put_columns",
    )(place, *pieces)


def head_columns_kernel(place_ref, *refs):
    out_ref = refs[-1]
    count = len(refs) - 1
    size = refs[0].shape[1] // 3
    for j in range(count):
        value = refs[0][...]
        for k in range(1, count):
            value = jnp.where((place_ref[0] ^ k) == j, refs[k][...], value)
        value = value.astype(F32)
        for which in range(3):
            at = (which * count + j) * size
            out_ref[:, at : at + size] = value[:, which * size : (which + 1) * size]


def put_heads(place, pieces):
    height, size = pieces[0].shape
    count = len(pieces)
    return pl.pallas_call(
        head_columns_kernel,
        in_specs=[pl.BlockSpec(memory_space=pltpu.SMEM)]
        + [pl.BlockSpec(memory_space=pltpu.VMEM)] * count,
        out_shape=jax.ShapeDtypeStruct((height, count * size), F32),
        compiler_params=params(),
        cost_estimate=cost(1e6, 6 * count * height * size),
        name="put_heads",
    )(place, *pieces)


def across(value, size, bit):
    return lax.ppermute(value, "seq", [(i, i ^ bit) for i in range(size)])


def other_core(value, size):
    return lax.ppermute(value, "batch", [(i, i ^ 1) for i in range(size)])


def plus(*terms):
    total = terms[0].astype(F32)
    for term in terms[1:]:
        total = total + term.astype(F32)
    return total.astype(BF16)


def bits_of(size):
    return [1 << i for i in range(size.bit_length() - 1)]


def everywhere(value, size):
    if size != 4:
        return [value] + [across(value, size, k) for k in range(1, size)]
    half = value.shape[0] // 2
    near, far = across(value, size, 1), across(value, size, 2)
    lead, tail = across(near[:half], size, 2), across(far[half:], size, 1)
    return [value, near, far, jnp.concatenate([lead, tail], 0)]


def scattered(value, size, bits):
    left = list(range(size))
    for bit in bits:
        keep = [i for i, k in enumerate(left) if not k & bit]
        send = [i for i, k in enumerate(left) if k & bit]
        pick = lambda which: jnp.concatenate([value[i : i + 1] for i in which], 0)
        value = plus(pick(keep), across(pick(send), size, bit))
        left = [left[i] for i in keep]
    return value[0]


def summed(value, size):
    half = (value.shape[0] // 2 + 7) // 8 * 8
    bits = bits_of(size)
    done = []
    for piece, order in ((value[:half], bits), (value[half:], bits[::-1])):
        for bit in order:
            piece = plus(piece, across(piece, size, bit))
        done.append(piece)
    return jnp.concatenate(done, 0)


def down_the_line(value, size, at):
    depth = value.shape[0]
    pick = lambda index: lax.dynamic_index_in_dim(
        value, jnp.clip(index, 0, depth - 1), 0, keepdims=False
    )
    up = down = None
    for t in range(depth - 1):
        send_up = pick(depth - 1 - t + at)
        send_down = pick(t - (depth - 1 - at))
        if t:
            send_up, send_down = plus(send_up, up), plus(send_down, down)
        up = lax.ppermute(
            send_up,
            "batch",
            [(2 * z + c, 2 * z + 2 + c) for z in range(depth - 1) if z <= t for c in (0, 1)],
        )
        down = lax.ppermute(
            send_down,
            "batch",
            [
                (2 * z + c, 2 * z - 2 + c)
                for z in range(1, depth)
                if z >= depth - 1 - t
                for c in (0, 1)
            ],
        )
    return plus(pick(at), up, down)


MESH = pl.DeviceIdType.MESH


def flip(value, k):
    if k == 0:
        return value
    if k == 1:
        return value + 1 - 2 * (value % 2)
    if k == 2:
        return value + 2 - 4 * (value // 2)
    return 3 - value


def add_rows(into, other):
    if len(into.shape) > 2:
        for i in range(into.shape[0]):
            add_rows(into.at[i], other.at[i])
        return
    tile = 16

    def body(i, carry):
        at = pl.ds(pl.multiple_of(i * tile, tile), tile)
        into[at] = (into[at].astype(F32) + other[at].astype(F32)).astype(BF16)
        return carry

    lax.fori_loop(0, into.shape[0] // tile, body, 0)


class Wires:
    def __init__(self, send_sems, recv_sems):
        self.send_sems, self.recv_sems, self.made = send_sems, recv_sems, []

    def copy(self, src, dst, device, when=None):
        index = len(self.made)
        made = Wire(
            pltpu.make_async_remote_copy(
                src_ref=src,
                dst_ref=dst,
                send_sem=self.send_sems.at[index],
                recv_sem=self.recv_sems.at[index],
                device_id=device,
                device_id_type=MESH,
            ),
            when,
        )
        self.made.append(made)
        return made

    def drain(self):
        for wire in self.made:
            if wire.when is None:
                wire.copy.wait_send()
            else:
                pl.when(wire.when)(wire.copy.wait_send)


class Wire:
    def __init__(self, copy, when):
        self.copy, self.when = copy, when
        self.start, self.arrive = copy.start, copy.wait_recv


class Line:
    def __init__(self, wires, depth, chip, up_to, down_to, own, up_in, down_in, begun=False):
        self.depth, self.chip, self.own, self.begun = depth, chip, own, begun
        self.up_in, self.down_in = up_in, down_in
        last = depth - 1
        self.up = {
            d: wires.copy(
                own(d),
                up_in.at[d - 1],
                up_to,
                (chip < d) & (chip > 0) if begun and d == last else chip < d,
            )
            for d in range(1, depth)
        }
        self.down = {
            d: wires.copy(
                own(d),
                down_in.at[d],
                down_to,
                (chip > d) & (chip < last) if begun and d == 0 else chip > d,
            )
            for d in range(last)
        }

    def hop(self, t):
        last = self.depth - 1
        for d in range(1, self.depth):
            z = d - (last - t)
            if 0 <= z < d:

                @pl.when(self.chip == z)
                def _():
                    if z > 0 and not (self.begun and t == 1):
                        self.up[d].arrive()
                        add_rows(self.own(d), self.up_in.at[d - 1])
                    self.up[d].start()

                @pl.when(self.chip == last - z)
                def _():
                    if z > 0 and not (self.begun and t == 1):
                        self.down[last - d].arrive()
                        add_rows(self.own(last - d), self.down_in.at[last - d])
                    self.down[last - d].start()

    def finish(self):
        for d in range(self.depth):

            @pl.when(self.chip == d)
            def _():
                if d > 0:
                    self.up[d].arrive()
                    add_rows(self.own(d), self.up_in.at[d - 1])
                if d < self.depth - 1:
                    self.down[d].arrive()
                    add_rows(self.own(d), self.down_in.at[d])


class Square:
    def __init__(self, wires, to, own, in_one, in_two, src=None, begun=False):
        self.own, self.in_one, self.in_two = own, in_one, in_two
        src = src or own
        self.one, self.two = [], []
        for h, (f, g) in enumerate(((1, 2), (2, 1))):
            if not begun:
                self.one.append(
                    (
                        wires.copy(src(h, 3), in_one.at[h, 1], to[f]),
                        wires.copy(src(h, f), in_one.at[h, 0], to[f]),
                    )
                )
        for h, (f, g) in enumerate(((1, 2), (2, 1))):
            self.two.append(wires.copy(own(h, g), in_two.at[h], to[g]))

    def start(self):
        for i in range(2):
            for h in range(2):
                self.one[h][i].start()

    def middle(self):
        for h, g in ((0, 2), (1, 1)):
            self.one[h][0].arrive()
            add_rows(self.own(h, g), self.in_one.at[h, 1])
            self.two[h].start()
        for h in range(2):
            self.one[h][1].arrive()
            add_rows(self.own(h, 0), self.in_one.at[h, 0])

    def finish(self):
        for h in range(2):
            self.two[h].arrive()
            add_rows(self.own(h, 0), self.in_two.at[h])


class Spread:
    def __init__(self, wires, to, slots, src=None):
        rows = slots.shape[1]
        cut = (rows // 2 + 15) // 16 * 16
        src = slots.at[0] if src is None else src
        lead, tail = pl.ds(0, cut), pl.ds(cut, rows - cut)
        self.near = [wires.copy(src.at[p], slots.at[1, p], to[1]) for p in (lead, tail)]
        self.far = [wires.copy(src.at[p], slots.at[2, p], to[2]) for p in (tail, lead)]
        self.lead = wires.copy(slots.at[1, lead], slots.at[3, lead], to[2])
        self.tail = wires.copy(slots.at[2, tail], slots.at[3, tail], to[1])

    def start(self):
        for i in range(2):
            self.near[i].start()
            self.far[i].start()

    def relay(self):
        self.near[0].arrive()
        self.lead.start()
        self.far[0].arrive()
        self.tail.start()

    def finish(self):
        self.near[1].arrive()
        self.far[1].arrive()
        self.lead.arrive()
        self.tail.arrive()


def reduce_kernel(
    late_hbm,
    up_hbm,
    down_hbm,
    first_hbm,
    f_one_hbm,
    lead_hbm,
    tail_hbm,
    normed_hbm,
    dt_hbm,
    joined_hbm,
    joined_peer_hbm,
    hidden_hbm,
    d_middle_hbm,
    w_hbm,
    gain_ref,
    vec_two_ref,
    fc1_bias_ref,
    p_all,
    f_all,
    q_all,
    s_all,
    c_all,
    din_hbm,
    dskip_hbm,
    vec_ref,
    l_own,
    l_up,
    l_down,
    f_own,
    f_one,
    f_in,
    f_up,
    f_down,
    q_own,
    q_sum,
    q_up,
    q_down,
    s_own,
    s_one,
    s_two,
    s_z,
    s_up,
    s_down,
    d_own,
    d_one,
    d_two,
    p_one,
    p_two,
    low_ref,
    low_peer,
    c_own,
    v_own,
    v_in,
    send_sems,
    recv_sems,
    local_sems,
):
    depth, late_rows, width = late_hbm.shape
    rows = hidden_hbm.shape[0]
    half = rows // 2
    mid = depth // 2
    slots = c_own.shape[0]
    place = lax.axis_index("seq")
    index = lax.axis_index("batch")
    chip, core = index // 2, index % 2
    last = depth - 1
    to = {1: (index, flip(place, 1)), 2: (index, flip(place, 2)), 3: (index, flip(place, 3))}
    other = (index + 1 - 2 * core, place)
    up_to, down_to = (index + 2, place), (index - 2, place)

    barrier = pltpu.get_barrier_semaphore()
    for device in (to[1], to[2], to[3], other):
        pl.semaphore_signal(barrier, inc=1, device_id=device, device_id_type=MESH)

    @pl.when(chip < last)
    def _():
        pl.semaphore_signal(barrier, inc=1, device_id=up_to, device_id_type=MESH)

    @pl.when(chip > 0)
    def _():
        pl.semaphore_signal(barrier, inc=1, device_id=down_to, device_id_type=MESH)

    pl.semaphore_wait(barrier, 4 + jnp.minimum(chip, 1) + jnp.minimum(last - chip, 1))

    wires = Wires(send_sems, recv_sems)
    taken = [0]

    def local(src, dst):
        taken[0] += 1
        copy = pltpu.make_async_copy(src, dst, local_sems.at[taken[0] - 1])
        copy.start()
        return copy

    keeps = []

    d_hbm = (lead_hbm, tail_hbm)
    norm_sum = Square(
        wires,
        to,
        lambda h, k: d_own.at[h, (0, 1, 1, None)[k]],
        d_one,
        d_two,
        src=lambda h, k: d_hbm[h].at[k],
    )
    norm_sum.start()
    d_loads = [
        local(d_hbm[h].at[k], d_own.at[h, i]) for h, ks in ((0, (0, 2)), (1, (0, 1))) for i, k in enumerate(ks)
    ]
    l_loads = [local(late_hbm.at[z], l_own.at[z, pl.ds(0, late_rows)]) for z in range(depth)]
    f_loads = [
        local(first_hbm.at[h, k], f_own.at[h, i]) for h, ks in ((0, (0, 2)), (1, (0, 1))) for i, k in enumerate(ks)
    ] + [local(f_one_hbm, f_one)]

    l_line = Line(
        wires,
        depth,
        chip,
        up_to,
        down_to,
        lambda d: l_own.at[d, pl.ds(0, late_rows)],
        l_up,
        l_down,
        begun=True,
    )
    for copy in l_loads:
        copy.wait()
    l_own[:, late_rows:] = jnp.zeros((depth, l_own.shape[1] - late_rows, width), BF16)
    up_sem, down_sem = local_sems.at[taken[0]], local_sems.at[taken[0] + 1]
    taken[0] += 2

    @pl.when(chip == 1)
    def _():
        copy = pltpu.make_async_copy(up_hbm, l_up.at[last - 1], up_sem)
        copy.start()
        copy.wait()
        add_rows(l_own.at[last, pl.ds(0, late_rows)], l_up.at[last - 1])

    @pl.when(chip == last - 1)
    def _():
        copy = pltpu.make_async_copy(down_hbm, l_down.at[0], down_sem)
        copy.start()
        copy.wait()
        add_rows(l_own.at[0, pl.ds(0, late_rows)], l_down.at[0])

    l_line.hop(1)

    def heads_part(normed, dt):
        loads = [local(normed_hbm, normed), local(dt_hbm, dt)]
        for copy in loads:
            copy.wait()
        height = normed.shape[1] // (2 * depth)
        step = 3 * LANES
        for part in range(normed.shape[1] // step):
            grads = lax.dot_general(
                normed[:, part * step : (part + 1) * step],
                dt[...],
                (((0,), (1,)), ((), ())),
                preferred_element_type=F32,
            ).astype(BF16)
            q_own[pl.ds(part * step, step)] = grads

    pl.run_scoped(
        heads_part, pltpu.VMEM(normed_hbm.shape, BF16), pltpu.VMEM(dt_hbm.shape, BF16)
    )
    height = q_sum.shape[1]
    q_swap = [
        wires.copy(
            q_own.at[pl.ds(pl.multiple_of((2 * z + 1 - core) * height, 16), height)],
            q_sum.at[z],
            other,
        )
        for z in range(depth)
    ]
    for wire in q_swap:
        wire.start()

    for copy in d_loads:
        copy.wait()
    norm_sum.middle()

    for copy in f_loads:
        copy.wait()
    for h in range(2):
        add_rows(f_own.at[h, 1], f_one.at[h, 1])
    f_two = [
        wires.copy(f_own.at[h, 1], f_in.at[h], to[2 - h]) for h in range(2)
    ]
    for wire in f_two:
        wire.start()
    for h in range(2):
        add_rows(f_own.at[h, 0], f_one.at[h, 0])
    for z, wire in enumerate(q_swap):
        wire.arrive()
        add_rows(q_sum.at[z], q_own.at[pl.ds(pl.multiple_of((2 * z + core) * height, 16), height)])
    q_line = Line(wires, depth, chip, up_to, down_to, lambda d: q_sum.at[d], q_up, q_down)
    q_line.hop(0)

    norm_sum.finish()
    low_swap = wires.copy(low_ref, low_peer, other)
    v_swap = wires.copy(v_own.at[0], v_in.at[0], other)

    def back_part(hidden, d_middle):
        loads = [local(hidden_hbm, hidden), local(d_middle_hbm, d_middle)]
        for copy in loads:
            copy.wait()
        upstream = jnp.concatenate(
            [d_own[0, 0].astype(F32), d_own[1, 0].astype(F32)], 0
        )
        scaled, factor = normalize(hidden[...])
        d_hidden = d_middle[...] + norm_back(
            upstream, scaled, factor, gain_ref[...].reshape(1, -1)
        )
        low_ref[...] = d_hidden.astype(BF16)
        low_swap.start()
        v_own[0] = jnp.zeros(v_own.shape[1:], F32)
        v_own[0, 0:1] = jnp.sum(d_hidden, axis=0, keepdims=True)
        v_own[0, 1:2] = jnp.sum(upstream * scaled, axis=0, keepdims=True)
        v_own[0, 2:3] = jnp.sum(upstream, axis=0, keepdims=True)
        v_own[0, 3:7] = vec_two_ref[0:4]
        v_own[0, 8:12] = fc1_bias_ref[...]
        v_swap.start()

    pl.run_scoped(back_part, pltpu.VMEM(hidden_hbm.shape, F32), pltpu.VMEM(hidden_hbm.shape, F32))

    low_swap.arrive()

    def skip_part(joined, peer):
        loads = [local(joined_hbm, joined), local(joined_peer_hbm, peer)]
        for copy in loads:
            copy.wait()
        chunk = joined.shape[1] // 4
        for z in range(depth):
            grads = dot(joined[z], low_ref[...]) + dot(peer[z], low_peer[...])
            for j in range(4):
                piece = grads[j * chunk : (j + 1) * chunk]
                piece = jnp.concatenate(
                    [piece, jnp.zeros((s_own.shape[2] - chunk, width), F32)], 0
                )
                s_own[flip(place, j), z] = piece.astype(BF16)

    pl.run_scoped(
        skip_part,
        pltpu.VMEM(joined_peer_hbm.shape, BF16),
        pltpu.VMEM(joined_peer_hbm.shape, BF16),
    )
    s_sum = Square(
        wires, to, lambda h, k: s_own.at[k, pl.ds(h * mid, mid)], s_one, s_two
    )
    s_sum.start()

    c_go = [wires.copy(c_own, c_all.at[k], to[k]) for k in (1, 2, 3)]

    images = rows - slots

    def rows_part(w, stage):
        copy = local(w_hbm.at[pl.ds(0, width)], w)
        copy.wait()
        stage[...] = dot_nt(low_ref[...], w[...])
        c_own[:, :width] = stage[images:].astype(BF16)
        copy = local(w_hbm.at[pl.ds(width, width)], w)
        out = local(stage.at[pl.ds(0, images)], din_hbm)
        copy.wait()
        out.wait()
        stage[...] = dot_nt(low_ref[...], w[...])
        c_own[:, width:] = stage[images:].astype(BF16)
        for wire in c_go:
            wire.start()
        local(stage.at[pl.ds(0, images)], dskip_hbm).wait()

    pl.run_scoped(rows_part, pltpu.VMEM((width, width), BF16), pltpu.VMEM((rows, width), F32))
    keeps.append(local(c_own, c_all.at[0]))

    v_swap.arrive()
    v_own[1] = v_own[0] + v_in[0]
    v_up = wires.copy(v_own.at[2], v_in.at[1], up_to, chip < last)
    v_down = wires.copy(v_own.at[3], v_in.at[2], down_to, chip > 0)

    for h in range(2):
        f_two[h].arrive()
        add_rows(f_own.at[h, 0], f_in.at[h])
    f_line = Line(
        wires,
        depth,
        chip,
        up_to,
        down_to,
        lambda d: f_own.at[d // mid, 0, d % mid],
        f_up,
        f_down,
    )
    f_line.hop(0)
    l_line.hop(2)
    q_line.hop(1)
    s_sum.middle()
    f_line.hop(1)
    for t in range(3, last):
        l_line.hop(t)
    for t in range(2, last):
        q_line.hop(t)
    s_sum.finish()
    for d in range(depth):
        s_z[d] = s_own[0, d]
    s_line = Line(wires, depth, chip, up_to, down_to, lambda d: s_z.at[d], s_up, s_down)
    s_line.hop(0)
    for t in range(2, last):
        f_line.hop(t)
    q_line.finish()
    q_go = Spread(wires, to, q_all, q_sum.at[chip])
    q_go.start()
    keeps.append(local(q_sum.at[chip], q_all.at[0]))

    v_own[2] = v_own[1]
    v_own[3] = v_own[1]

    @pl.when(chip > 0)
    def _():
        v_up.arrive()
        v_own[2] = v_own[1] + v_in[1]

    @pl.when(chip < last)
    def _():
        v_up.start()

    @pl.when(chip < last)
    def _():
        v_down.arrive()
        v_own[3] = v_own[1] + v_in[2]

    @pl.when(chip > 0)
    def _():
        v_down.start()

    v_own[4] = v_own[2] + v_own[3] - v_own[1]
    v_near = wires.copy(v_own.at[4], v_in.at[3], to[1])
    v_near.start()
    s_line.hop(1)

    l_line.finish()
    chunk = p_all.shape[1]
    part = chunk // 2

    def p_rows(h, k):
        at = pl.multiple_of(flip(place, k) * chunk + h * part, 16)
        return l_own.at[chip, pl.ds(at, part)]

    p_sum = Square(wires, to, p_rows, p_one, p_two)
    p_sum.start()
    f_line.finish()
    f_mine = f_own.at[chip // mid, 0, chip % mid]
    f_go = Spread(wires, to, f_all, f_mine)
    keeps.append(local(f_mine, f_all.at[0]))
    q_go.relay()
    f_go.start()
    for t in range(2, last):
        s_line.hop(t)
    p_sum.middle()
    v_near.arrive()
    v_own[5] = v_own[4] + v_in[3]
    v_far = wires.copy(v_own.at[5], v_in.at[4], to[2])
    v_far.start()
    s_line.finish()
    s_go = Spread(wires, to, s_all, s_z.at[chip])
    keeps.append(local(s_z.at[chip], s_all.at[0]))
    s_go.start()
    p_sum.finish()
    p_mine = l_own.at[chip, pl.ds(pl.multiple_of(place * chunk, 16), chunk)]
    p_go = Spread(wires, to, p_all, p_mine)
    p_go.start()
    keeps.append(local(p_mine, p_all.at[0]))
    f_go.relay()
    q_go.finish()

    for wire in c_go:
        wire.arrive()
    v_far.arrive()
    vec_ref[...] = v_own[5] + v_in[4]
    s_go.relay()
    p_go.relay()
    f_go.finish()
    s_go.finish()
    p_go.finish()
    for copy in keeps:
        copy.wait()
    wires.drain()


def reduce_all(
    late, up, down, first, f_one, lead, tail, normed_all, d_triple_t, joined, joined_peer,
    hidden, d_middle, w, gain, vec_two, fc1_bias_grad,
):
    depth, late_rows, width = late.shape
    rows = hidden.shape[0]
    slots = SLOTS // 4
    images = rows - slots
    mid = depth // 2
    batch = 2 * depth
    small = first.shape[3]
    own = d_triple_t.shape[0]
    chunk = (-(-late_rows // 4) + 31) // 32 * 32
    skip_rows = joined.shape[1]
    skip_chunk = (skip_rows // 4 + 15) // 16 * 16
    half = rows // 2
    v = lambda *shape: pltpu.VMEM(shape, BF16)
    ends = depth - 1
    scratch = [
        v(depth, 4 * chunk, width), v(ends, late_rows, width), v(ends, late_rows, width),
        v(2, 2, mid, small, width), v(2, 2, mid, small, width), v(2, mid, small, width),
        v(ends, small, width), v(ends, small, width),
        v(width, own), v(depth, small, own), v(ends, small, own), v(ends, small, own),
        v(4, depth, skip_chunk, width), v(2, 2, mid, skip_chunk, width), v(2, mid, skip_chunk, width),
        v(depth, skip_chunk, width), v(ends, skip_chunk, width), v(ends, skip_chunk, width),
        v(2, 2, half, width), v(2, 2, half, width), v(2, half, width),
        v(2, 2, chunk // 2, width), v(2, chunk // 2, width),
        v(rows, width), v(rows, width), v(slots, 2 * width),
        pltpu.VMEM((6, 16, width), F32), pltpu.VMEM((5, 16, width), F32),
        pltpu.SemaphoreType.DMA((96,)), pltpu.SemaphoreType.DMA((96,)), pltpu.SemaphoreType.DMA((64,)),
    ]
    hbm = pl.BlockSpec(memory_space=pl.ANY)
    vmem = pl.BlockSpec(memory_space=pltpu.VMEM)
    f = lambda *shape: jax.ShapeDtypeStruct(shape, F32)
    b = lambda *shape: jax.ShapeDtypeStruct(shape, BF16)
    return pl.pallas_call(
        reduce_kernel,
        in_specs=[hbm] * 14 + [vmem] * 3,
        out_specs=[hbm] * 7 + [vmem],
        out_shape=[
            b(4, chunk, width),
            b(4, small, width),
            b(4, small, own),
            b(4, skip_chunk, width),
            b(4, slots, 2 * width),
            f(images, width),
            f(images, width),
            f(16, width),
        ],
        scratch_shapes=scratch,
        compiler_params=pltpu.CompilerParams(
            vmem_limit_bytes=VMEM_LIMIT, collective_id=0, has_side_effects=True
        ),
        cost_estimate=cost(1e10, 1e8),
        name="reduce_all",
    )(
        late, up, down, first, f_one, lead, tail, normed_all, d_triple_t, joined, joined_peer,
        hidden, d_middle, w, gain, vec_two, fc1_bias_grad,
    )


def ends_of(place, index, depth):
    chip, core = index // 2, index % 2
    to = {k: (index, flip(place, k)) for k in (1, 2, 3)}
    return to, (index + 1 - 2 * core, place), (index + 2, place), (index - 2, place)


def greet(devices, chip=None, depth=0, up_to=None, down_to=None):
    barrier = pltpu.get_barrier_semaphore()
    for device in devices:
        pl.semaphore_signal(barrier, inc=1, device_id=device, device_id_type=MESH)
    if chip is None:
        pl.semaphore_wait(barrier, len(devices))
        return

    @pl.when(chip < depth - 1)
    def _():
        pl.semaphore_signal(barrier, inc=1, device_id=up_to, device_id_type=MESH)

    @pl.when(chip > 0)
    def _():
        pl.semaphore_signal(barrier, inc=1, device_id=down_to, device_id_type=MESH)

    pl.semaphore_wait(
        barrier, len(devices) + jnp.minimum(chip, 1) + jnp.minimum(depth - 1 - chip, 1)
    )


class Locals:
    def __init__(self, sems):
        self.sems, self.taken = sems, 0

    def copy(self, src, dst):
        self.taken += 1
        return pltpu.make_async_copy(src, dst, self.sems.at[self.taken - 1])

    def start(self, src, dst):
        copy = self.copy(src, dst)
        copy.start()
        return copy


def own_slots(cond_ref, pad_ref, place, slots):
    pad_ref[...] = jnp.zeros(pad_ref.shape, BF16)
    pad_ref[0 : cond_ref.shape[0]] = cond_ref[...]
    return pad_ref[pl.ds(pl.multiple_of(place * slots, 16), slots)]


def start_kernel(
    window,
    x_ref,
    x_cond_ref,
    s_ref,
    s_cond_ref,
    w_ref,
    bias_ref,
    gain_ref,
    shift_ref,
    qkv_w_hbm,
    hidden_ref,
    normed_hbm,
    heads_ref,
    joined_hbm,
    peer_hbm,
    pad_ref,
    x_all,
    s_all,
    normed_ref,
    joined_ref,
    qkv_w_ref,
    send_sems,
    recv_sems,
    local_sems,
):
    images, width = x_ref.shape
    slots = x_all.shape[0] - images
    place, index = lax.axis_index("seq"), lax.axis_index("batch")
    core = index % 2
    to, other, _, _ = ends_of(place, index, 0)
    greet([to[1], to[2], other])
    wires, moves = Wires(send_sems, recv_sems), Locals(local_sems)
    w_load = moves.start(qkv_w_hbm, qkv_w_ref)
    for ref, cond, whole in ((x_ref, x_cond_ref, x_all), (s_ref, s_cond_ref, s_all)):
        whole[:images] = ref[...]
        whole[images:] = own_slots(cond, pad_ref, place, slots)
    hidden = (
        dot(x_all[...], w_ref[:width]) + dot(s_all[...], w_ref[width:]) + bias_ref[...].reshape(1, -1)
    )
    hidden_ref[...] = hidden
    scaled, _ = normalize(hidden)
    normed_ref[...] = (
        scaled * gain_ref[...].reshape(1, -1) + shift_ref[...].reshape(1, -1)
    ).astype(BF16)
    spread = Spread(wires, to, normed_hbm, normed_ref)
    spread.start()
    own = moves.start(normed_ref, normed_hbm.at[0])

    size = joined_ref.shape[2]
    per = width // size
    for which, whole in enumerate((x_all, s_all)):
        flat = turned(whole[...])
        for i in range(per):
            block = which * per + i
            joined_ref[block // 2, block % 2] = flat[i * size : (i + 1) * size]
    swap = wires.copy(joined_ref.at[:, 1 - core], peer_hbm, other)
    swap.start()
    keep = moves.start(joined_ref.at[:, core], joined_hbm)
    spread.relay()
    w_load.wait()

    heads = heads_ref.shape[0]
    width_own = heads * HEAD_DIM
    real = lax.broadcasted_iota(jnp.int32, (width, LANES), 1) < HEAD_DIM
    for which in range(3):
        first = place * width_own + which * width
        start = jnp.minimum(first // LANES * LANES, 3 * width - window)
        value = qkv_w_ref[:, pl.ds(pl.multiple_of(start, LANES), window)].astype(F32)
        value = pltpu.roll(value, lax.rem(window - (first - start), window), 1)
        for head in range(heads):
            shifted = value if head == 0 else pltpu.roll(value, window - head * HEAD_DIM, 1)
            heads_ref[head, :, which * LANES : (which + 1) * LANES] = jnp.where(
                real, shifted[:, :LANES], 0.0
            ).astype(BF16)
    spread.finish()
    own.wait()
    keep.wait()
    swap.arrive()
    wires.drain()


def start_stage(depth, x, x_cond, s, s_cond, w, bias, gain, shift, qkv_w):
    images, width = x.shape
    slots = SLOTS // 4
    rows = images + slots
    heads = HEADS // 4
    own = heads * HEAD_DIM
    window = (max(p * own % LANES for p in range(4)) + own + LANES - 1) // LANES * LANES
    block = 2 * width // (2 * depth)
    vmem, hbm = pl.BlockSpec(memory_space=pltpu.VMEM), pl.BlockSpec(memory_space=pl.ANY)
    b = lambda *shape: jax.ShapeDtypeStruct(shape, BF16)
    v = lambda *shape: pltpu.VMEM(shape, BF16)
    return pl.pallas_call(
        functools.partial(start_kernel, window),
        in_specs=[vmem] * 8 + [hbm],
        out_specs=[vmem, hbm, vmem, hbm, hbm],
        out_shape=[
            jax.ShapeDtypeStruct((rows, width), F32),
            b(4, rows, width),
            b(heads, width, 3 * LANES),
            b(depth, block, rows),
            b(depth, block, rows),
        ],
        scratch_shapes=[
            v(SLOTS, width), v(rows, width), v(rows, width), v(rows, width),
            v(depth, 2, block, rows), v(width, 3 * width),
            pltpu.SemaphoreType.DMA((8,)), pltpu.SemaphoreType.DMA((8,)), pltpu.SemaphoreType.DMA((4,)),
        ],
        compiler_params=pltpu.CompilerParams(
            vmem_limit_bytes=VMEM_LIMIT, collective_id=1, has_side_effects=True
        ),
        cost_estimate=cost(4 * rows * width * width, 12 * width * width),
        name="start_stage",
    )(x, x_cond, s, s_cond, w, bias, gain, shift, qkv_w)


def attend_send_kernel(
    length_ref, normed_ref, w_ref, qkv_ref, lse_ref, ctx_hbm, vt_ref, ot_ref, go_ref,
    send_sems, recv_sems, local_sems,
):
    head = pl.program_id(0)
    heads = HEADS // 4
    total = normed_ref.shape[0]
    rows = total // 4
    slots = SLOTS // 4
    place, index = lax.axis_index("seq"), lax.axis_index("batch")
    to, _, _, _ = ends_of(place, index, 0)
    half = heads // 2 * HEAD_DIM
    wires, moves = Wires(send_sems, recv_sems), Locals(local_sems)
    go = [
        [
            wires.copy(
                go_ref.at[k, pl.ds(i * half, half)], ctx_hbm.at[k, pl.ds(i * half, half)], to[k]
            )
            for k in (3, 1, 2)
        ]
        for i in range(2)
    ]
    keep = moves.copy(go_ref.at[0], ctx_hbm.at[0])

    @pl.when(head == 0)
    def _():
        greet([to[1], to[2], to[3]])

    lane = lax.broadcasted_iota(jnp.int32, (1, LANES), 1)
    one = jnp.where(lane == HEAD_DIM, 1.0, 0.0)
    slot = lax.broadcasted_iota(jnp.int32, (slots, LANES), 0)
    lanes = lax.broadcasted_iota(jnp.int32, (slots, LANES), 1)
    for part in range(4):
        span = pl.ds(part * rows, rows)
        triple = dot(normed_ref[span], w_ref[0])
        qkv_ref[0, span, :LANES] = (triple[:, :LANES] + one).astype(BF16)
        qkv_ref[0, span, 2 * LANES :] = triple[:, 2 * LANES :].astype(BF16)
        hidden = flip(place, part) * slots + slot > length_ref[0]
        bias = jnp.where(hidden & (lanes == HEAD_DIM), -1e30, 0.0)
        key = triple[:, LANES : 2 * LANES]
        qkv_ref[0, pl.ds(part * rows, rows - slots), LANES : 2 * LANES] = key[: rows - slots].astype(BF16)
        qkv_ref[0, pl.ds(part * rows + rows - slots, slots), LANES : 2 * LANES] = (
            key[rows - slots :] + bias
        ).astype(BF16)
        vt_ref[:, span] = turned(qkv_ref[0, span, 2 * LANES :])
    step = 3 * LANES
    for start in range(0, total, step):
        query = qkv_ref[0, pl.ds(start, step), :LANES]
        scores = dot_nt(qkv_ref[0, :, LANES : 2 * LANES], query)
        peak = jnp.max(scores, axis=0, keepdims=True)
        shifted = jnp.exp2((scores - peak) * SCALE2)
        sums = jnp.sum(shifted, axis=0, keepdims=True)
        mixed = dot(vt_ref[...], shifted.astype(BF16)) / sums
        ot_ref[pl.ds(pl.multiple_of(head * HEAD_DIM, 8), HEAD_DIM), pl.ds(start, step)] = mixed[
            :HEAD_DIM
        ]
        lse_ref[0, :, pl.ds(start, step)] = peak * SCALE2 + jnp.log2(sums)

    for i in range(2):

        @pl.when(head == (i + 1) * heads // 2 - 1)
        def _():
            for part in (3, 1, 2, 0):
                go_ref[part, pl.ds(i * half, half)] = ot_ref[
                    pl.ds(i * half, half), pl.ds(part * rows, rows)
                ].astype(BF16)
            for wire in go[i]:
                wire.start()

    @pl.when(head == heads - 1)
    def _():
        keep.start()
        for i in range(2):
            for wire in go[i]:
                wire.arrive()
        keep.wait()
        wires.drain()


def attend_send(length, normed_all, w_heads):
    total, width = normed_all.shape
    heads = w_heads.shape[0]
    rows = total // 4
    own = heads * HEAD_DIM
    return pl.pallas_call(
        attend_send_kernel,
        grid=(heads,),
        in_specs=[
            pl.BlockSpec(memory_space=pltpu.SMEM),
            pl.BlockSpec((total, width), lambda h: (0, 0)),
            pl.BlockSpec((1, width, 3 * LANES), lambda h: (h, 0, 0)),
        ],
        out_specs=[
            pl.BlockSpec((1, total, 3 * LANES), lambda h: (h, 0, 0)),
            pl.BlockSpec((1, 1, total), lambda h: (h, 0, 0)),
            pl.BlockSpec(memory_space=pl.ANY),
        ],
        out_shape=[
            jax.ShapeDtypeStruct((heads, total, 3 * LANES), BF16),
            jax.ShapeDtypeStruct((heads, 1, total), F32),
            jax.ShapeDtypeStruct((4, own, rows), BF16),
        ],
        scratch_shapes=[
            pltpu.VMEM((LANES, total), BF16),
            pltpu.VMEM((own, total), F32),
            pltpu.VMEM((4, own, rows), BF16),
            pltpu.SemaphoreType.DMA((6,)),
            pltpu.SemaphoreType.DMA((6,)),
            pltpu.SemaphoreType.DMA((1,)),
        ],
        compiler_params=pltpu.CompilerParams(
            vmem_limit_bytes=VMEM_LIMIT, collective_id=2, has_side_effects=True
        ),
        cost_estimate=cost(
            2 * heads * total * (width * 3 * LANES + 4 * LANES * total), 6 * total * width
        ),
        name="attend_send",
    )(length, normed_all, w_heads)


def both(own_t, peer_t, own, peer):
    rows = own_t.shape[-1]
    cut = rows // 256 * 256
    total = dot(own_t[:, :cut], own[:cut]) + dot(peer_t[:, :cut], peer[:cut])
    ends_t = jnp.concatenate([own_t[:, cut:], peer_t[:, cut:]], 1)
    return total + dot(ends_t, jnp.concatenate([own[cut:], peer[cut:]], 0))


def middle_kernel(
    ctx_t_ref,
    hidden_ref,
    cot_ref,
    cot_cond_ref,
    proj_ref,
    proj_bias_ref,
    gain_ref,
    shift_ref,
    fc2_bias_ref,
    fc1_bias_ref,
    fc1_hbm,
    fc2_hbm,
    out_hbm,
    c_all,
    d_middle_ref,
    late_hbm,
    first_hbm,
    d_ctx_hbm,
    vec_ref,
    fc1_vec_ref,
    pad_ref,
    cot_all,
    cot_peer,
    fc1_ref,
    fc2_ref,
    normed_ref,
    middle_ref,
    acc_out,
    acc_back,
    normed_t,
    normed_t_peer,
    ctx_two,
    ctx_peer,
    active_t,
    active_peer,
    d_pre,
    d_pre_peer,
    d_branch_ref,
    d_branch_peer,
    d_go,
    late_stage,
    first_stage,
    proj_stage,
    c_own,
    send_sems,
    recv_sems,
    local_sems,
):
    images, width = cot_ref.shape
    rows = hidden_ref.shape[0]
    slots = rows - images
    depth, _, small, _ = normed_t.shape
    large = active_t.shape[2]
    chunk = fc1_ref.shape[2]
    chunks = fc1_hbm.shape[1] // chunk
    own = ctx_t_ref.shape[1]
    mid = depth // 2
    place, index = lax.axis_index("seq"), lax.axis_index("batch")
    core = index % 2
    to, other, _, _ = ends_of(place, index, depth)
    moves = Locals(local_sems)

    def load(f):
        span = pl.ds(f * chunk, chunk)
        return (
            moves.start(fc1_hbm.at[:, span], fc1_ref.at[f % 2]),
            moves.start(fc2_hbm.at[span], fc2_ref.at[f % 2]),
        )

    loads = [load(0), load(1)]
    greet([to[1], to[2], to[3], other])
    wires = Wires(send_sems, recv_sems)
    cot_all[:images] = cot_ref[...]
    cot_all[images:] = own_slots(cot_cond_ref, pad_ref, place, slots)
    cot_swap = wires.copy(cot_all, cot_peer, other)
    cot_swap.start()

    branch = proj_bias_ref[...].reshape(1, -1) + hidden_ref[...]
    for k in range(4):
        at = pl.ds(pl.multiple_of(flip(place, k) * own, 16), own)
        branch += dot(turned(ctx_t_ref[k]), proj_ref[at, :])
        for i in range(2):
            ctx_two[flip(place, k), i] = ctx_t_ref[k, i * small : (i + 1) * small]
    ctx_swap = wires.copy(ctx_two.at[:, 1 - core], ctx_peer, other)
    ctx_swap.start()
    middle_ref[...] = branch
    scaled, _ = normalize(branch)
    gain = gain_ref[...].reshape(1, -1)
    normed = scaled * gain + shift_ref[...].reshape(1, -1)
    normed_ref[...] = normed.astype(BF16)
    flat = normed.T.astype(BF16)
    for b in range(2 * depth):
        normed_t[b // 2, b % 2] = flat[b * small : (b + 1) * small]
    normed_swap = wires.copy(normed_t.at[:, 1 - core], normed_t_peer, other)
    normed_swap.start()

    swaps, outs = [], []

    def grads(f):
        for wire in swaps[f]:
            wire.arrive()
        if f == 0:
            cot_swap.arrive()
            normed_swap.arrive()
        if f >= 2:
            for copy in outs[f - 2]:
                copy.wait()
        late_stage[f % 2] = both(
            active_t[f, core], active_peer[f], cot_all[...], cot_peer[...]
        ).astype(BF16)
        done = [moves.start(late_stage.at[f % 2], late_hbm.at[f, pl.ds(0, large)])]
        first_stage[f % 2] = (
            both(
                normed_t[:, core].reshape(depth * small, rows),
                normed_t_peer[...].reshape(depth * small, rows),
                d_pre[f],
                d_pre_peer[f],
            )
            .astype(BF16)
            .reshape(2, mid, small, width)
        )
        for h in range(2):
            done.append(moves.start(first_stage.at[f % 2, h], first_hbm.at[h, flip(place, f)]))
        outs.append(done)

    for f in range(chunks):
        for copy in loads[f]:
            copy.wait()
        fc1, fc2 = fc1_ref.at[f % 2], fc2_ref.at[f % 2]
        bias = fc1_bias_ref[f * chunk : (f + 1) * chunk].reshape(1, -1)
        before = dot(normed_ref[...], fc1[...]) + bias
        cdf = 0.5 + 0.5 * lax.erf(before * math.sqrt(0.5))
        active = before * cdf
        slope = cdf + before * (jnp.exp(-0.5 * before * before) * (1.0 / math.sqrt(2.0 * math.pi)))
        d_before = dot_nt(cot_all[...], fc2[...]) * slope
        fc1_vec_ref[f : f + 1] = jnp.sum(d_before, axis=0, keepdims=True)
        d_pre[f] = d_before.astype(BF16)
        flat = active.T.astype(BF16)
        for i in range(2):
            active_t[f, i] = flat[i * large : (i + 1) * large]
        swaps.append(
            [
                wires.copy(active_t.at[f, 1 - core], active_peer.at[f], other),
                wires.copy(d_pre.at[f], d_pre_peer.at[f], other),
            ]
        )
        for wire in swaps[f]:
            wire.start()
        forward = dot(active.astype(BF16), fc2[...])
        backward = dot_nt(d_pre[f], fc1[...])
        if f == 0:
            acc_out[...] = forward
            acc_back[...] = backward
        else:
            acc_out[...] += forward
            acc_back[...] += backward
        if f + 2 < chunks:
            loads.append(load(f + 2))
        if f >= 1 and f < chunks - 1:
            grads(f - 1)

    middle = middle_ref[...]
    scaled, factor = normalize(middle)
    upstream = acc_back[...]
    cot = cot_all[...].astype(F32)
    d_middle = cot + norm_back(upstream, scaled, factor, gain)
    d_middle_ref[...] = d_middle
    d_branch_ref[...] = d_middle.astype(BF16)
    branch_swap = wires.copy(d_branch_ref, d_branch_peer, other)
    branch_swap.start()
    go = {}
    for k in (3, 1, 2, 0):
        at = pl.ds(pl.multiple_of(flip(place, k) * own, 16), own)
        d_go[k] = dot_nt(d_branch_ref[...], proj_ref[at, :]).astype(BF16)
        if k:
            go[k] = wires.copy(d_go.at[k], d_ctx_hbm.at[k], to[k])
            go[k].start()
    keep = moves.start(d_go.at[0], d_ctx_hbm.at[0])
    acc_out[...] = middle + acc_out[...] + fc2_bias_ref[...].reshape(1, -1)
    image_out = moves.start(acc_out.at[pl.ds(0, images)], out_hbm)
    c_own[...] = acc_out[images:].astype(BF16)
    c_go = [wires.copy(c_own, c_all.at[k], to[k]) for k in (3, 1, 2)]
    c_keep = moves.start(c_own, c_all.at[0])
    for wire in c_go:
        wire.start()
    vec_ref[0:1] = jnp.sum(upstream * scaled, axis=0, keepdims=True)
    vec_ref[1:2] = jnp.sum(upstream, axis=0, keepdims=True)
    vec_ref[2:3] = jnp.sum(d_middle, axis=0, keepdims=True)
    vec_ref[3:4] = jnp.sum(cot, axis=0, keepdims=True)
    vec_ref[4:] = jnp.zeros((4, width), F32)
    for f in range(max(chunks - 2, 0), chunks):
        grads(f)
    ctx_swap.arrive()
    branch_swap.arrive()
    proj_stage[...] = (
        both(
            ctx_two[:, core].reshape(depth * small, rows),
            ctx_peer[...].reshape(depth * small, rows),
            d_branch_ref[...],
            d_branch_peer[...],
        )
        .astype(BF16)
        .reshape(depth, small, width)
    )
    proj_out = moves.start(proj_stage, late_hbm.at[:, pl.ds(large, small)])
    for wire in c_go:
        wire.arrive()
    for wire in go.values():
        wire.arrive()
    for copy in [keep, image_out, c_keep, proj_out] + [c for done in outs[-2:] for c in done]:
        copy.wait()
    wires.drain()


def middle_stage(depth, ctx_t, hidden, cot, cot_cond, proj, proj_bias, gain, shift, fc2_bias, fc1_bias, fc1, fc2):
    rows, width = hidden.shape
    images = cot.shape[0]
    slots = rows - images
    ff = fc1.shape[1]
    small, large = width // (2 * depth), ff // (2 * depth)
    own = ctx_t.shape[1]
    chunk = 2 * large
    mid = depth // 2
    vmem, hbm = pl.BlockSpec(memory_space=pltpu.VMEM), pl.BlockSpec(memory_space=pl.ANY)
    f = lambda *shape: jax.ShapeDtypeStruct(shape, F32)
    b = lambda *shape: jax.ShapeDtypeStruct(shape, BF16)
    v = lambda *shape: pltpu.VMEM(shape, BF16)
    return pl.pallas_call(
        middle_kernel,
        in_specs=[vmem] * 10 + [hbm] * 2,
        out_specs=[hbm, hbm, vmem, hbm, hbm, hbm, vmem, vmem],
        out_shape=[
            f(images, width),
            b(4, slots, width),
            f(rows, width),
            b(depth, large + small, width),
            b(2, 4, mid, small, width),
            b(4, rows, own),
            f(8, width),
            f(ff // width, width),
        ],
        scratch_shapes=[
            v(SLOTS, width), v(rows, width), v(rows, width),
            v(2, width, chunk), v(2, chunk, width),
            v(rows, width), pltpu.VMEM((rows, width), F32),
            pltpu.VMEM((rows, width), F32), pltpu.VMEM((rows, width), F32),
            v(depth, 2, small, rows), v(depth, small, rows),
            v(depth, 2, small, rows), v(depth, small, rows),
            v(depth, 2, large, rows), v(depth, large, rows),
            v(depth, rows, chunk), v(depth, rows, chunk),
            v(rows, width), v(rows, width),
            v(4, rows, own),
            v(2, large, width), v(2, 2, mid, small, width), v(depth, small, width),
            v(slots, width),
            pltpu.SemaphoreType.DMA((24,)), pltpu.SemaphoreType.DMA((24,)), pltpu.SemaphoreType.DMA((32,)),
        ],
        compiler_params=pltpu.CompilerParams(
            vmem_limit_bytes=VMEM_LIMIT, collective_id=3, has_side_effects=True
        ),
        cost_estimate=cost(12 * rows * width * ff, 8 * width * ff),
        name="middle_stage",
    )(ctx_t, hidden, cot, cot_cond, proj, proj_bias, gain, shift, fc2_bias, fc1_bias, fc1, fc2)


def attend_back_send_kernel(
    d_ref, qkv_ref, lse_ref, w_ref, late_hbm, first_hbm,
    dt_ref, lead_ref, tail_ref, up_hbm, down_hbm, f_in_hbm,
    dot_all, dt_all, acc, dq_ref, dk_ref, dv_ref, send_sems, recv_sems,
):
    head = pl.program_id(0)
    depth = late_hbm.shape[0]
    place, index = lax.axis_index("seq"), lax.axis_index("batch")
    chip = index // 2
    to, _, up_to, down_to = ends_of(place, index, depth)
    wires = Wires(send_sems, recv_sems)
    up = wires.copy(late_hbm.at[depth - 1], up_hbm, up_to, chip == 0)
    down = wires.copy(late_hbm.at[0], down_hbm, down_to, chip == depth - 1)
    square = [
        wires.copy(first_hbm.at[h, k], f_in_hbm.at[h, i], to[h + 1])
        for h, i, k in ((0, 1, 3), (1, 1, 3), (0, 0, 1), (1, 0, 2))
    ]

    @pl.when(head == 0)
    def _():
        greet([to[1], to[2]], chip, depth, up_to, down_to)
        pl.when(chip == 0)(up.start)
        pl.when(chip == depth - 1)(down.start)
        for wire in square:
            wire.start()

    attend_back_kernel(
        4, *[d_ref.at[k] for k in range(4)], qkv_ref, lse_ref, w_ref, dt_ref, lead_ref, tail_ref,
        dot_all, dt_all, acc, dq_ref, dk_ref, dv_ref,
    )

    @pl.when(head == pl.num_programs(0) - 1)
    def _():
        for wire in square:
            wire.arrive()
        pl.when(chip == 1)(up.arrive)
        pl.when(chip == depth - 2)(down.arrive)
        wires.drain()


def attend_back_send(d_context, qkv, lse, w_heads, late, first):
    heads, total, _ = qkv.shape
    width = w_heads.shape[1]
    rows = total // 4
    own = heads * HEAD_DIM
    whole = lambda *shape: pl.BlockSpec(shape, lambda h: (0,) * len(shape))
    hbm = pl.BlockSpec(memory_space=pl.ANY)
    b = lambda *shape: jax.ShapeDtypeStruct(shape, BF16)
    return pl.pallas_call(
        attend_back_send_kernel,
        grid=(heads,),
        in_specs=[
            whole(4, rows, own),
            pl.BlockSpec((1, total, 3 * LANES), lambda h: (h, 0, 0)),
            pl.BlockSpec((1, 1, total), lambda h: (h, 0, 0)),
            pl.BlockSpec((1, width, 3 * LANES), lambda h: (h, 0, 0)),
            hbm,
            hbm,
        ],
        out_specs=[
            whole(3 * own, total),
            whole(4, rows // 2, width),
            whole(4, rows // 2, width),
            hbm,
            hbm,
            hbm,
        ],
        out_shape=[
            b(3 * own, total),
            b(4, rows // 2, width),
            b(4, rows // 2, width),
            b(*late.shape[1:]),
            b(*late.shape[1:]),
            b(2, 2, *first.shape[2:]),
        ],
        scratch_shapes=[
            pltpu.VMEM((own, total), F32),
            pltpu.VMEM((3 * own, total), F32),
            pltpu.VMEM((total, width), F32),
            pltpu.VMEM((total, LANES), F32),
            pltpu.VMEM((total, LANES), F32),
            pltpu.VMEM((total, LANES), F32),
            pltpu.SemaphoreType.DMA((6,)),
            pltpu.SemaphoreType.DMA((6,)),
        ],
        compiler_params=pltpu.CompilerParams(
            vmem_limit_bytes=VMEM_LIMIT, collective_id=4, has_side_effects=True
        ),
        cost_estimate=cost(
            2 * heads * total * (width * 3 * LANES + 10 * LANES * total), 12 * total * width
        ),
        name="attend_back_send",
    )(d_context, qkv, lse, w_heads, late, first)


def finish_kernel(
    p_hbm, f_hbm, q_hbm, s_hbm, c_hbm, out_c_hbm, vec_ref, out_hbm, din_hbm, dskip_hbm,
    g_fc2_hbm, g_proj_hbm, g_first_hbm, g_heads_hbm, g_skip_hbm,
    o_out, o_din, o_dskip, o_out_cond, o_din_cond, o_dskip_cond,
    v0, v1, v2, v3, v4, v5, v6, fc1_vec_ref,
    p_in, f_in, q_in, s_in, c_in, out_c_in, p_st, f_st, q_st, s_st, cond_st, rows_st, sems,
):
    width = out_hbm.shape[1]
    place, index = lax.axis_index("seq"), lax.axis_index("batch")
    batch = lax.axis_size("batch")
    moves = Locals(sems)
    loads = [
        moves.start(src, dst)
        for src, dst in (
            (p_hbm, p_in), (f_hbm, f_in), (q_hbm, q_in), (s_hbm, s_in), (c_hbm, c_in),
            (out_c_hbm, out_c_in),
        )
    ]
    rows_in = [
        moves.start(src, rows_st.at[i]) for i, src in enumerate((out_hbm, din_hbm, dskip_hbm))
    ]
    done = []
    for i, dst in enumerate((o_out, o_din, o_dskip)):
        rows_in[i].wait()
        done.append(moves.start(rows_st.at[i], dst.at[:, 0]))
    loads[0].wait()
    chunk = p_in.shape[1]
    for j in range(4):
        p_st[j * chunk : (j + 1) * chunk] = p_in[flip(place, j)].astype(F32)
    size = g_fc2_hbm.shape[0]
    done.append(moves.start(p_st.at[pl.ds(0, size)], g_fc2_hbm))
    done.append(moves.start(p_st.at[pl.ds(size, g_proj_hbm.shape[0])], g_proj_hbm))
    loads[1].wait()
    for j in range(4):
        f_st[:, j * width : (j + 1) * width] = f_in[flip(place, j)].astype(F32)
    done.append(moves.start(f_st, g_first_hbm))
    loads[2].wait()
    size = q_in.shape[2] // 3
    for j in range(4):
        value = q_in[flip(place, j)].astype(F32)
        for which in range(3):
            at = (which * 4 + j) * size
            q_st[:, at : at + size] = value[:, which * size : (which + 1) * size]
    done.append(moves.start(q_st, g_heads_hbm))
    loads[3].wait()
    size = s_st.shape[0] // 4
    for j in range(4):
        s_st[j * size : (j + 1) * size] = s_in[flip(place, j), :size].astype(F32)
    done.append(moves.start(s_st, g_skip_hbm))
    for copy in loads[4:]:
        copy.wait()
    slots = c_in.shape[1]
    for j in range(4):
        span = slice(j * slots, (j + 1) * slots)
        piece = c_in[flip(place, j)].astype(F32)
        cond_st[0, span] = out_c_in[flip(place, j)].astype(F32)
        cond_st[1, span] = piece[:, :width]
        cond_st[2, span] = piece[:, width:]
    conds = o_out_cond.shape[0]
    for i, ref in enumerate((o_out_cond, o_din_cond, o_dskip_cond)):
        ref[:, 0] = cond_st[i, :conds]
    share = width // batch
    vectors = vec_ref[...]
    rolled = pltpu.roll(vectors, lax.rem(width - index * share, width), 1)
    for row, ref in zip((0, 1, 2, 5, 3, 4, 6), (v0, v1, v2, v3, v4, v5, v6)):
        ref[...] = rolled[row, :share]
    share = 4 * width // batch
    per = width // share
    vector = vec_ref[pl.ds(8 + index // per, 1)]
    vector = pltpu.roll(vector, lax.rem(width - index % per * share, width), 1)
    fc1_vec_ref[...] = vector[0, :share]
    for copy in done:
        copy.wait()


def finish_stage(batch, conds, slots_of, out_c, vec, out, d_image, d_skip):
    p_all, f_all, q_all, s_all, c_all = slots_of
    images, width = out.shape
    small = f_all.shape[1]
    skip_rows = 2 * width // batch
    large = 4 * width // batch
    slots = c_all.shape[1]
    vmem, hbm = pl.BlockSpec(memory_space=pltpu.VMEM), pl.BlockSpec(memory_space=pl.ANY)
    f = lambda *shape: jax.ShapeDtypeStruct(shape, F32)
    like = lambda a: pltpu.VMEM(a.shape, a.dtype)
    vf = lambda *shape: pltpu.VMEM(shape, F32)
    return pl.pallas_call(
        finish_kernel,
        in_specs=[hbm] * 6 + [vmem] + [hbm] * 3,
        out_specs=[hbm] * 8 + [vmem] * 11,
        out_shape=[
            f(large, width), f(small, width), f(small, 4 * width), f(small, 4 * q_all.shape[2]),
            f(skip_rows, width), f(images, 1, width), f(images, 1, width), f(images, 1, width),
            f(conds, 1, width), f(conds, 1, width), f(conds, 1, width),
        ]
        + [f(width // batch)] * 7
        + [f(large)],
        scratch_shapes=[
            like(p_all), like(f_all), like(q_all), like(s_all), like(c_all), like(out_c),
            vf(4 * p_all.shape[1], width), vf(small, 4 * width), vf(small, 4 * q_all.shape[2]),
            vf(skip_rows, width), vf(3, 4 * slots, width), vf(3, images, width),
            pltpu.SemaphoreType.DMA((20,)),
        ],
        compiler_params=params(),
        cost_estimate=cost(1e6, 2e7),
        name="finish_stage",
    )(*slots_of, out_c, vec, out, d_image, d_skip)


def per_device(
    batch,
    parts,
    image_in,
    cond_in,
    skip_image,
    skip_cond,
    caption_len,
    skip_weight,
    skip_bias,
    first_gain,
    first_bias,
    qkv_weight,
    proj_weight,
    proj_bias,
    second_gain,
    second_bias,
    fc1_weight,
    fc1_bias,
    fc2_weight,
    fc2_bias,
    grad_image,
    grad_cond,
):
    conds = cond_in.shape[0]
    width = image_in.shape[2]
    images = image_in.shape[0]
    ff = fc1_weight.shape[1]
    slots = SLOTS // parts
    rows = slots + images
    total = rows * parts
    heads = HEADS // parts
    depth = batch // 2
    place = lax.axis_index("seq")
    index = lax.axis_index("batch")
    core, chip = index % 2, index // 2
    where = jnp.stack([core, place]).astype(jnp.int32)

    fast = parts == 4 and depth == 4 and (ff // parts) % LANES == 0
    if fast:
        hidden, normed_all, w_heads, joined, joined_peer = start_stage(
            depth, image_in[:, 0], cond_in[:, 0], skip_image[:, 0], skip_cond[:, 0],
            skip_weight, skip_bias, first_gain, first_bias, qkv_weight,
        )
        normed_all = normed_all.reshape(total, width)
        qkv, lse, ctx_t = attend_send(caption_len, normed_all, w_heads)
        out, out_c, d_middle, late, first, d_ctx, vec_two, fc1_vec = middle_stage(
            depth, ctx_t, hidden, grad_image[:, 0], grad_cond[:, 0], proj_weight, proj_bias,
            second_gain, second_bias, fc2_bias, fc1_bias, fc1_weight, fc2_weight,
        )
        d_triple_t, lead, tail, up, down, f_one = attend_back_send(
            d_ctx, qkv, lse, w_heads, late, first
        )
        *slots_of, d_image, d_skip, vec = reduce_all(
            late, up, down, first, f_one, lead, tail, normed_all, d_triple_t, joined,
            joined_peer, hidden, d_middle, skip_weight, first_gain, vec_two, fc1_vec,
        )
        (
            wgrad_fc2, wgrad_proj, wgrad_fc1, wgrad_qkv, wgrad_skip, out_image, d_image, d_skip,
            out_cond, d_cond, d_skip_cond, *vec,
        ) = finish_stage(batch, conds, slots_of, out_c, vec, out, d_image, d_skip)
        return (
            out_image, out_cond, d_image, d_cond, d_skip, d_skip_cond, wgrad_skip, vec[0],
            vec[1], vec[2], wgrad_qkv, wgrad_proj, vec[3], vec[4], vec[5], wgrad_fc1, vec[7],
            wgrad_fc2, vec[6],
        )

    def own_rows(cond, image):
        padded = jnp.pad(cond[:, 0], ((0, SLOTS - conds), (0, 0)))
        lead = lax.dynamic_slice_in_dim(padded, place * slots, slots, 0)
        return jnp.concatenate([lead, image[:, 0]], 0)

    x = own_rows(cond_in, image_in)
    s = own_rows(skip_cond, skip_image)
    cot = own_rows(grad_cond, grad_image)

    hidden, normed, joined_t = pre(
        x, s, skip_weight, skip_bias[None], first_gain[None], first_bias[None]
    )
    normed_all = jnp.concatenate(everywhere(normed, parts), 0)
    own = heads * HEAD_DIM
    w_heads = heads_weight(where[1:], qkv_weight, heads)
    order = place ^ jnp.arange(parts, dtype=jnp.int32)
    position = order[:, None] * slots + jnp.arange(rows, dtype=jnp.int32)[None]
    valid = (jnp.arange(rows)[None] >= slots) | (position <= caption_len[0])
    kbias = jnp.where(
        (jnp.arange(LANES) == HEAD_DIM)[None] & ~valid.reshape(total, 1), F32(-1e30), F32(0)
    )
    qkv, lse, *ctx_parts = attend(parts, normed_all, w_heads, kbias)
    context = [ctx_parts[0]] + [across(ctx_parts[k], parts, k) for k in range(1, parts)]

    zero = jnp.zeros_like(proj_bias)
    vecs = jnp.stack([proj_bias, second_gain, second_bias, fc2_bias, zero, zero, zero, zero])
    (
        out,
        d_middle,
        d_branch,
        active_t,
        d_pre,
        normed2_t,
        ctx_t,
        vec_two,
        fc1_bias_grad,
        *d_ctx_parts,
    ) = mlp(
        parts,
        where[1:],
        context,
        hidden,
        cot,
        proj_weight,
        vecs,
        fc1_weight,
        fc1_bias[None],
        fc2_weight,
    )
    d_context = [d_ctx_parts[0]] + [across(d_ctx_parts[k], parts, k) for k in range(1, parts)]

    def by_core(turned_rows):
        blocks = turned_rows.reshape(depth, 2, -1, rows)
        send = lax.dynamic_index_in_dim(blocks, 1 - core, 1, keepdims=False)
        return blocks, other_core(send, batch)

    active_b, active_p = by_core(active_t)
    normed2_b, normed2_p = by_core(normed2_t)
    ctx_b, ctx_p = by_core(ctx_t)
    joined_b, joined_p = by_core(joined_t)
    cot_p, d_pre_p, d_branch_p = (other_core(v, batch) for v in (cot, d_pre, d_branch))
    late = pair_grads(
        where, [(active_b, active_p, cot, cot_p), (ctx_b, ctx_p, d_branch, d_branch_p)]
    )
    by_columns = (ff // parts) % LANES == 0
    if by_columns:
        first = column_grads(where, parts, normed2_b, normed2_p, d_pre, d_pre_p)
        late, first, d_context = lax.optimization_barrier((late, first, d_context))
        middle = depth // 2
    if by_columns:
        first = jnp.concatenate(
            [
                scattered(first[:, :middle], parts, bits_of(parts)),
                scattered(first[:, middle:], parts, bits_of(parts)[::-1]),
            ],
            0,
        )
    if not by_columns:
        first = pair_grads(where, [(normed2_b, normed2_p, d_pre, d_pre_p)])
    def all_conds(lead):
        pieces = [lead] + [across(lead, parts, k) for k in range(1, parts)]
        full = jnp.zeros((SLOTS, lead.shape[1]), F32)
        for k in range(parts):
            full = lax.dynamic_update_slice_in_dim(
                full, pieces[k].astype(F32), (place ^ k) * slots, 0
            )
        return full[:conds, None]

    d_triple_t, d_lead, d_tail = attend_back(parts, d_context, qkv, lse, w_heads)
    d_lead = scattered(d_lead, parts, bits_of(parts))
    d_tail = scattered(d_tail, parts, bits_of(parts)[::-1])
    heads_grad = heads_grads(normed_all, d_triple_t).reshape(depth, 2, -1, 3 * own)
    heads_grad = plus(
        lax.dynamic_index_in_dim(heads_grad, core, 1, keepdims=False),
        other_core(lax.dynamic_index_in_dim(heads_grad, 1 - core, 1, keepdims=False), batch),
    )
    heads_grad = everywhere(down_the_line(heads_grad, batch, chip), parts)
    wgrad_qkv = put_heads(where[1:], heads_grad)

    d_in, d_skip, d_low, vec_one = post(
        d_lead, d_tail, hidden, d_middle, first_gain[None], skip_weight
    )
    d_low_p = other_core(d_low, batch)
    last = pair_grads(where, [(joined_b, joined_p, d_low, d_low_p)])

    late = down_the_line(late, batch, chip)
    first = down_the_line(first, batch, chip)
    late = summed(late, parts)
    if by_columns:
        fc1_cols = everywhere(first, parts)
        wgrad_fc1 = put_columns(where[1:], fc1_cols)
    else:
        wgrad_fc1 = summed(first, parts).astype(F32)

    vectors = [
        vec_one[0],
        vec_one[1],
        vec_one[2],
        vec_two[2],
        vec_two[0],
        vec_two[1],
        fc1_bias_grad[0],
        vec_two[3],
    ]
    sizes = [v.shape[0] // batch for v in vectors]
    packed = jnp.concatenate([v.reshape(batch, -1) for v in vectors], 1)
    packed = packed.reshape(depth, 2, -1)
    packed = lax.dynamic_index_in_dim(packed, core, 1, keepdims=False) + other_core(
        lax.dynamic_index_in_dim(packed, 1 - core, 1, keepdims=False), batch
    )
    packed = jnp.pad(packed, ((0, 0), (0, 16 * width - packed.shape[1]))).reshape(depth, 16, width)
    last = jnp.concatenate([last, packed.astype(BF16)], 1)
    last = summed(down_the_line(last, batch, chip), parts)
    skip_rows = 2 * width // batch
    wgrad_skip = last[:skip_rows].astype(F32)
    flat = last[skip_rows:].reshape(-1).astype(F32)
    vector_out, at = [], 0
    for size in sizes:
        vector_out.append(flat[at : at + size])
        at += size
    fc2_rows = ff // batch
    wgrad_fc2 = late[:fc2_rows].astype(F32)
    wgrad_proj = late[fc2_rows:].astype(F32)

    out_cond = all_conds(out[:slots].astype(BF16))
    d_cond = all_conds(jnp.concatenate([d_in[:slots], d_skip[:slots]], 1).astype(BF16))
    return (
        out[slots:, None],
        out_cond,
        d_in[slots:, None],
        d_cond[:, :, :width],
        d_skip[slots:, None],
        d_cond[:, :, width:],
        wgrad_skip,
        vector_out[0],
        vector_out[1],
        vector_out[2],
        wgrad_qkv,
        wgrad_proj,
        vector_out[3],
        vector_out[4],
        vector_out[5],
        wgrad_fc1,
        vector_out[6],
        wgrad_fc2,
        vector_out[7],
    )


def solution(mesh):
    tokens, conds, shared = P("seq", "batch", None), P(None, "batch", None), P()
    return jax.shard_map(
        functools.partial(per_device, mesh.shape["batch"], mesh.shape["seq"]),
        mesh=mesh,
        in_specs=(tokens, conds, tokens, conds, P("batch")) + (shared,) * 13 + (tokens, conds),
        out_specs=(tokens, conds) * 3
        + (
            P("batch", None),
            P("batch"),
            P("batch"),
            P("batch"),
            P("batch", None),
            P("batch", None),
            P("batch"),
            P("batch"),
            P("batch"),
            P("batch", None),
            P("batch"),
            P("batch", None),
            P("batch"),
        ),
        check_vma=False,
    )
```

```python
import functools
import math

import jax
import jax.numpy as jnp
from jax import lax
from jax.experimental import pallas as pl
from jax.experimental.pallas import tpu as pltpu
from jax.sharding import PartitionSpec as P

HEADS = 16
HEAD_DIM = 72
LANES = 128
SLOTS = 128
F32 = jnp.float32
BF16 = jnp.bfloat16
VMEM_LIMIT = 60 * 1024 * 1024
SCALE = 1.0 / math.sqrt(HEAD_DIM)
SCALE2 = SCALE * math.log2(math.e)


def dot(left, right):
    return jnp.dot(left, right, preferred_element_type=F32)


def dot_nt(left, right):
    return lax.dot_general(left, right, (((1,), (1,)), ((), ())), preferred_element_type=F32)


def dot_tn(left, right):
    return lax.dot_general(left, right, (((0,), (0,)), ((), ())), preferred_element_type=F32)


def params():
    return pltpu.CompilerParams(vmem_limit_bytes=VMEM_LIMIT)


def cost(flops, nbytes):
    return pl.CostEstimate(flops=int(flops), bytes_accessed=int(nbytes), transcendentals=0)


def turned(value):
    return value.astype(F32).T.astype(BF16)


def normalize(values):
    centre = values - jnp.mean(values, axis=-1, keepdims=True)
    factor = lax.rsqrt(jnp.mean(centre * centre, axis=-1, keepdims=True) + 1e-5)
    return centre * factor, factor


def norm_back(upstream, scaled, factor, gain):
    inner = upstream * gain
    centred = inner - jnp.mean(inner, axis=-1, keepdims=True)
    return factor * (centred - scaled * jnp.mean(inner * scaled, axis=-1, keepdims=True))


def pre_kernel(x_ref, s_ref, w_ref, bias_ref, gain_ref, shift_ref, hidden_ref, normed_ref, turn_ref):
    width = x_ref.shape[1]
    hidden = dot(x_ref[...], w_ref[:width]) + dot(s_ref[...], w_ref[width:]) + bias_ref[...]
    hidden_ref[...] = hidden
    scaled, _ = normalize(hidden)
    normed_ref[...] = (scaled * gain_ref[...] + shift_ref[...]).astype(BF16)
    turn_ref[:width] = turned(x_ref[...])
    turn_ref[width:] = turned(s_ref[...])


def pre(x, s, w, bias, gain, shift):
    rows, width = x.shape
    return pl.pallas_call(
        pre_kernel,
        out_shape=(
            jax.ShapeDtypeStruct((rows, width), F32),
            jax.ShapeDtypeStruct((rows, width), BF16),
            jax.ShapeDtypeStruct((2 * width, rows), BF16),
        ),
        compiler_params=params(),
        cost_estimate=cost(4 * rows * width * width, 4 * width * width + 12 * rows * width),
        name="input_linear",
    )(x, s, w, bias, gain, shift)


def heads_weight_kernel(window, place_ref, w_ref, out_ref):
    heads = out_ref.shape[0]
    width = w_ref.shape[0]
    own = heads * HEAD_DIM
    keep = lax.broadcasted_iota(jnp.int32, (width, LANES), 1) < HEAD_DIM
    place = place_ref[0]
    for which in range(3):
        first = place * own + which * width
        start = jnp.minimum(first // LANES * LANES, 3 * width - window)
        value = w_ref[:, pl.ds(pl.multiple_of(start, LANES), window)].astype(F32)
        value = pltpu.roll(value, lax.rem(window - (first - start), window), 1)
        for head in range(heads):
            turned_back = value if head == 0 else pltpu.roll(value, window - head * HEAD_DIM, 1)
            out_ref[head, :, which * LANES : (which + 1) * LANES] = jnp.where(
                keep, turned_back[:, :LANES], 0.0
            ).astype(BF16)


def heads_weight(place, w, heads):
    width = w.shape[0]
    own = heads * HEAD_DIM
    offsets = [p * own % LANES for p in range(HEADS // heads)]
    window = (max(offsets) + own + LANES - 1) // LANES * LANES
    return pl.pallas_call(
        functools.partial(heads_weight_kernel, window),
        in_specs=[
            pl.BlockSpec(memory_space=pltpu.SMEM),
            pl.BlockSpec(memory_space=pltpu.VMEM),
        ],
        out_shape=jax.ShapeDtypeStruct((heads, width, 3 * LANES), BF16),
        compiler_params=params(),
        cost_estimate=cost(1e6, 2 * w.size + 6 * heads * width * LANES),
        name="heads_weight",
    )(place, w)


def attend_kernel(parts, normed_ref, w_ref, kbias_ref, qkv_ref, lse_ref, *rest):
    ctx_refs, (vt_ref, ot_ref) = rest[:parts], rest[parts:]
    head = pl.program_id(0)
    total = normed_ref.shape[0]
    rows = total // parts
    lane = lax.broadcasted_iota(jnp.int32, (1, LANES), 1)
    one = jnp.where(lane == HEAD_DIM, 1.0, 0.0)
    for part in range(parts):
        span = pl.ds(part * rows, rows)
        triple = dot(normed_ref[span], w_ref[0])
        qkv_ref[0, span, :LANES] = (triple[:, :LANES] + one).astype(BF16)
        qkv_ref[0, span, LANES : 2 * LANES] = (
            triple[:, LANES : 2 * LANES] + kbias_ref[span]
        ).astype(BF16)
        qkv_ref[0, span, 2 * LANES :] = triple[:, 2 * LANES :].astype(BF16)
        vt_ref[:, span] = turned(qkv_ref[0, span, 2 * LANES :])
    step = 3 * LANES if total % (3 * LANES) == 0 else LANES
    for start in range(0, total, step):
        query = qkv_ref[0, pl.ds(start, step), :LANES]
        scores = dot_nt(qkv_ref[0, :, LANES : 2 * LANES], query)
        peak = jnp.max(scores, axis=0, keepdims=True)
        shifted = jnp.exp2((scores - peak) * SCALE2)
        sums = jnp.sum(shifted, axis=0, keepdims=True)
        mixed = dot(vt_ref[...], shifted.astype(BF16)) / sums
        ot_ref[pl.ds(pl.multiple_of(head * HEAD_DIM, 8), HEAD_DIM), pl.ds(start, step)] = mixed[
            :HEAD_DIM
        ]
        lse_ref[0, :, pl.ds(start, step)] = peak * SCALE2 + jnp.log2(sums)

    @pl.when(head == pl.num_programs(0) - 1)
    def _():
        for part in range(parts):
            ctx_refs[part][...] = ot_ref[:, pl.ds(part * rows, rows)].T.astype(BF16)


def attend(parts, normed_all, w_heads, kbias):
    total, width = normed_all.shape
    heads = w_heads.shape[0]
    rows = total // parts
    own = heads * HEAD_DIM
    return pl.pallas_call(
        functools.partial(attend_kernel, parts),
        grid=(heads,),
        in_specs=[
            pl.BlockSpec((total, width), lambda h: (0, 0)),
            pl.BlockSpec((1, width, 3 * LANES), lambda h: (h, 0, 0)),
            pl.BlockSpec((total, LANES), lambda h: (0, 0)),
        ],
        out_specs=[
            pl.BlockSpec((1, total, 3 * LANES), lambda h: (h, 0, 0)),
            pl.BlockSpec((1, 1, total), lambda h: (h, 0, 0)),
        ]
        + [pl.BlockSpec((rows, own), lambda h: (0, 0))] * parts,
        out_shape=[
            jax.ShapeDtypeStruct((heads, total, 3 * LANES), BF16),
            jax.ShapeDtypeStruct((heads, 1, total), F32),
        ]
        + [jax.ShapeDtypeStruct((rows, own), BF16)] * parts,
        scratch_shapes=[pltpu.VMEM((LANES, total), BF16), pltpu.VMEM((own, total), F32)],
        compiler_params=params(),
        cost_estimate=cost(
            2 * heads * total * (width * 3 * LANES + 4 * LANES * total), 6 * total * width
        ),
        name="attend",
    )(normed_all, w_heads, kbias)


def attend_back_kernel(parts, *refs):
    d_refs = refs[:parts]
    (qkv_ref, lse_ref, w_ref, dt_ref, lead_ref, tail_ref) = refs[parts : parts + 6]
    (dot_all, dt_all, acc, dq_ref, dk_ref, dv_ref) = refs[parts + 6 :]
    head = pl.program_id(0)
    heads = pl.num_programs(0)
    total = qkv_ref.shape[1]
    rows = total // parts
    half = rows // 2
    own = dot_all.shape[0]

    @pl.when(head == 0)
    def _():
        for part in range(parts):
            dot_all[:, pl.ds(part * rows, rows)] = d_refs[part][...].astype(F32).T

    base = pl.multiple_of(head * HEAD_DIM, 8)
    upstream_t = jnp.concatenate(
        [dot_all[pl.ds(base, HEAD_DIM), :], jnp.zeros((LANES - HEAD_DIM, total), F32)], 0
    )
    upstream = upstream_t.T.astype(BF16)
    upstream_t = upstream_t.astype(BF16)
    key = qkv_ref[0, :, LANES : 2 * LANES]
    key_t = turned(key)
    value = qkv_ref[0, :, 2 * LANES :]
    step = 3 * LANES if total % (3 * LANES) == 0 else LANES
    for start in range(0, total, step):
        query = qkv_ref[0, pl.ds(start, step), :LANES]
        probs = jnp.exp2(dot_nt(key, query) * SCALE2 - lse_ref[0, :, pl.ds(start, step)])
        d_probs = dot(value, upstream_t[:, start : start + step])
        delta = jnp.sum(probs * d_probs, axis=0, keepdims=True)
        d_raw = (probs * (d_probs - delta) * SCALE).astype(BF16)
        d_value = dot(probs.astype(BF16), upstream[start : start + step])
        d_key = dot(d_raw, query)
        if start == 0:
            dv_ref[...] = d_value
            dk_ref[...] = d_key
        else:
            dv_ref[...] += d_value
            dk_ref[...] += d_key
        d_query = dot(key_t, d_raw)
        dt_all[pl.ds(base, HEAD_DIM), pl.ds(start, step)] = d_query[:HEAD_DIM]
        dq_ref[pl.ds(start, step)] = d_query.T
    dt_all[pl.ds(pl.multiple_of(own + base, 8), HEAD_DIM)] = dk_ref[...].T[:HEAD_DIM]
    dt_all[pl.ds(pl.multiple_of(2 * own + base, 8), HEAD_DIM)] = dv_ref[...].T[:HEAD_DIM]
    for part in range(parts):
        span = pl.ds(part * rows, rows)
        update = (
            dot_nt(dq_ref[span].astype(BF16), w_ref[0, :, :LANES])
            + dot_nt(dk_ref[span].astype(BF16), w_ref[0, :, LANES : 2 * LANES])
            + dot_nt(dv_ref[span].astype(BF16), w_ref[0, :, 2 * LANES :])
        )

        @pl.when(head == 0)
        def _():
            acc[span] = update

        @pl.when(head > 0)
        def _():
            acc[span] += update

    @pl.when(head == heads - 1)
    def _():
        dt_ref[...] = dt_all[...].astype(BF16)
        for part in range(parts):
            lead_ref[part] = acc[pl.ds(part * rows, half)].astype(BF16)
            tail_ref[part] = acc[pl.ds(part * rows + half, half)].astype(BF16)


def attend_back(parts, d_context, qkv, lse, w_heads):
    heads, total, _ = qkv.shape
    width = w_heads.shape[1]
    rows = total // parts
    own = heads * HEAD_DIM
    whole = lambda *shape: pl.BlockSpec(shape, lambda h: (0,) * len(shape))
    return pl.pallas_call(
        functools.partial(attend_back_kernel, parts),
        grid=(heads,),
        in_specs=[whole(rows, own)] * parts
        + [
            pl.BlockSpec((1, total, 3 * LANES), lambda h: (h, 0, 0)),
            pl.BlockSpec((1, 1, total), lambda h: (h, 0, 0)),
            pl.BlockSpec((1, width, 3 * LANES), lambda h: (h, 0, 0)),
        ],
        out_specs=[
            whole(3 * own, total),
            whole(parts, rows // 2, width),
            whole(parts, rows // 2, width),
        ],
        out_shape=[
            jax.ShapeDtypeStruct((3 * own, total), BF16),
            jax.ShapeDtypeStruct((parts, rows // 2, width), BF16),
            jax.ShapeDtypeStruct((parts, rows // 2, width), BF16),
        ],
        scratch_shapes=[
            pltpu.VMEM((own, total), F32),
            pltpu.VMEM((3 * own, total), F32),
            pltpu.VMEM((total, width), F32),
            pltpu.VMEM((total, LANES), F32),
            pltpu.VMEM((total, LANES), F32),
            pltpu.VMEM((total, LANES), F32),
        ],
        compiler_params=params(),
        cost_estimate=cost(
            2 * heads * total * (width * 3 * LANES + 10 * LANES * total), 12 * total * width
        ),
        name="attend_back",
    )(*d_context, qkv, lse, w_heads)


def mlp_kernel(parts, place_ref, *refs):
    ctx_refs = refs[:parts]
    (
        hidden_ref,
        cot_ref,
        proj_ref,
        vec_ref,
        fc1_ref,
        fc1_bias_ref,
        fc2_ref,
        out_ref,
        d_middle_ref,
        d_branch_ref,
        active_t_ref,
        d_pre_ref,
        normed_t_ref,
        ctx_t_ref,
        vec_out_ref,
        fc1_bias_out_ref,
    ) = refs[parts : parts + 16]
    d_ctx_refs = refs[parts + 16 : 2 * parts + 16]
    middle_ref, normed_ref, acc_out, acc_back, turn_ref = refs[2 * parts + 16 :]
    step = pl.program_id(0)
    place = place_ref[0]
    own = ctx_refs[0].shape[1]

    @pl.when(step == 0)
    def _():
        branch = vec_ref[0:1] + hidden_ref[...]
        for part in range(parts):
            at = pl.ds(pl.multiple_of((place ^ part) * own, 8), own)
            branch += dot(ctx_refs[part][...], proj_ref[at, :])
            turn_ref[at] = ctx_refs[part][...].astype(F32).T
        ctx_t_ref[...] = turn_ref[...].astype(BF16)
        middle_ref[...] = branch
        scaled, _ = normalize(branch)
        normed = (scaled * vec_ref[1:2] + vec_ref[2:3]).astype(BF16)
        normed_ref[...] = normed
        normed_t_ref[...] = turned(normed)

    before = dot(normed_ref[...], fc1_ref[...]) + fc1_bias_ref[...]
    cdf = 0.5 + 0.5 * lax.erf(before * math.sqrt(0.5))
    active = (before * cdf).astype(BF16)
    slope = cdf + before * (jnp.exp(-0.5 * before * before) * (1.0 / math.sqrt(2.0 * math.pi)))
    d_before = dot_nt(cot_ref[...], fc2_ref[...]) * slope
    fc1_bias_out_ref[...] = jnp.sum(d_before, axis=0, keepdims=True)
    d_low = d_before.astype(BF16)
    d_pre_ref[...] = d_low
    active_t_ref[...] = turned(active)
    forward = dot(active, fc2_ref[...])
    backward = dot_nt(d_low, fc1_ref[...])

    @pl.when(step == 0)
    def _():
        acc_out[...] = forward
        acc_back[...] = backward

    @pl.when(step > 0)
    def _():
        acc_out[...] += forward
        acc_back[...] += backward

    @pl.when(step == pl.num_programs(0) - 1)
    def _():
        middle = middle_ref[...]
        out_ref[...] = middle + acc_out[...] + vec_ref[3:4]
        scaled, factor = normalize(middle)
        upstream = acc_back[...]
        cot = cot_ref[...].astype(F32)
        d_middle = cot + norm_back(upstream, scaled, factor, vec_ref[1:2])
        d_middle_ref[...] = d_middle
        d_branch = d_middle.astype(BF16)
        d_branch_ref[...] = d_branch
        vec_out_ref[0:1] = jnp.sum(upstream * scaled, axis=0, keepdims=True)
        vec_out_ref[1:2] = jnp.sum(upstream, axis=0, keepdims=True)
        vec_out_ref[2:3] = jnp.sum(d_middle, axis=0, keepdims=True)
        vec_out_ref[3:4] = jnp.sum(cot, axis=0, keepdims=True)
        vec_out_ref[4:] = jnp.zeros((4, vec_out_ref.shape[1]), F32)
        for part in range(parts):
            at = pl.ds(pl.multiple_of((place ^ part) * own, 8), own)
            d_ctx_refs[part][...] = dot_nt(d_branch, proj_ref[at, :]).astype(BF16)


def mlp(parts, place, context, hidden, cot, proj, vecs, fc1, fc1_bias, fc2):
    rows, width = hidden.shape
    ff = fc1.shape[1]
    own = context[0].shape[1]
    chunk = width
    whole = lambda *shape: pl.BlockSpec(shape, lambda i, p: (0,) * len(shape))
    return pl.pallas_call(
        functools.partial(mlp_kernel, parts),
        grid_spec=pltpu.PrefetchScalarGridSpec(
            num_scalar_prefetch=1,
            grid=(ff // chunk,),
            in_specs=[whole(rows, own)] * parts
            + [
                whole(rows, width),
                whole(rows, width),
                whole(width, width),
                whole(8, width),
                pl.BlockSpec((width, chunk), lambda i, p: (0, i)),
                pl.BlockSpec((1, chunk), lambda i, p: (0, i)),
                pl.BlockSpec((chunk, width), lambda i, p: (i, 0)),
            ],
            out_specs=[
                whole(rows, width),
                whole(rows, width),
                whole(rows, width),
                pl.BlockSpec((chunk, rows), lambda i, p: (i, 0)),
                pl.BlockSpec((rows, chunk), lambda i, p: (0, i)),
                whole(width, rows),
                whole(width, rows),
                whole(8, width),
                pl.BlockSpec((1, chunk), lambda i, p: (0, i)),
            ]
            + [whole(rows, own)] * parts,
            scratch_shapes=[
                pltpu.VMEM((rows, width), F32),
                pltpu.VMEM((rows, width), BF16),
                pltpu.VMEM((rows, width), F32),
                pltpu.VMEM((rows, width), F32),
                pltpu.VMEM((width, rows), F32),
            ],
        ),
        out_shape=[
            jax.ShapeDtypeStruct((rows, width), F32),
            jax.ShapeDtypeStruct((rows, width), F32),
            jax.ShapeDtypeStruct((rows, width), BF16),
            jax.ShapeDtypeStruct((ff, rows), BF16),
            jax.ShapeDtypeStruct((rows, ff), BF16),
            jax.ShapeDtypeStruct((width, rows), BF16),
            jax.ShapeDtypeStruct((width, rows), BF16),
            jax.ShapeDtypeStruct((8, width), F32),
            jax.ShapeDtypeStruct((1, ff), F32),
        ]
        + [jax.ShapeDtypeStruct((rows, own), BF16)] * parts,
        compiler_params=params(),
        cost_estimate=cost(8 * rows * width * ff, 4 * width * ff + 24 * rows * width),
        name="feed_forward",
    )(place, *context, hidden, cot, proj, vecs, fc1, fc1_bias, fc2)


def post_kernel(lead_ref, tail_ref, hidden_ref, d_middle_ref, gain_ref, w_ref, din_ref, dskip_ref, low_ref, vec_ref):
    width = hidden_ref.shape[1]
    upstream = jnp.concatenate([lead_ref[...].astype(F32), tail_ref[...].astype(F32)], 0)
    scaled, factor = normalize(hidden_ref[...])
    d_hidden = d_middle_ref[...] + norm_back(upstream, scaled, factor, gain_ref[...])
    low = d_hidden.astype(BF16)
    low_ref[...] = low
    vec_ref[0:1] = jnp.sum(d_hidden, axis=0, keepdims=True)
    vec_ref[1:2] = jnp.sum(upstream * scaled, axis=0, keepdims=True)
    vec_ref[2:3] = jnp.sum(upstream, axis=0, keepdims=True)
    vec_ref[3:] = jnp.zeros((5, width), F32)
    din_ref[...] = dot_nt(low, w_ref[:width])
    dskip_ref[...] = dot_nt(low, w_ref[width:])


def post(lead, tail, hidden, d_middle, gain, w):
    rows, width = hidden.shape
    return pl.pallas_call(
        post_kernel,
        out_shape=(
            jax.ShapeDtypeStruct((rows, width), F32),
            jax.ShapeDtypeStruct((rows, width), F32),
            jax.ShapeDtypeStruct((rows, width), BF16),
            jax.ShapeDtypeStruct((8, width), F32),
        ),
        compiler_params=params(),
        cost_estimate=cost(4 * rows * width * width, 4 * width * width + 20 * rows * width),
        name="input_back",
    )(lead, tail, hidden, d_middle, gain, w)


def pair_kernel(count, where_ref, *refs):
    out_ref = refs[4 * count]
    at = 0
    for index in range(count):
        own_t, peer_t, own, peer = refs[4 * index : 4 * index + 4]
        size = own_t.shape[2]
        out_ref[0, pl.ds(at, size)] = (
            dot(own_t[0, 0], own[...]) + dot(peer_t[0], peer[...])
        ).astype(BF16)
        at += size


def pair_grads(where, groups):
    depth = groups[0][0].shape[0]
    width = groups[0][2].shape[1]
    in_specs, operands, height, flops = [], [], 0, 0
    for own_t, peer_t, own, peer in groups:
        size, rows = own_t.shape[2:]
        in_specs += [
            pl.BlockSpec((1, 1, size, rows), lambda z, w: (z, w[0], 0, 0)),
            pl.BlockSpec((1, size, rows), lambda z, w: (z, 0, 0)),
            pl.BlockSpec((rows, width), lambda z, w: (0, 0)),
            pl.BlockSpec((rows, width), lambda z, w: (0, 0)),
        ]
        operands += [own_t, peer_t, own, peer]
        height += size
        flops += 4 * depth * size * rows * width
    return pl.pallas_call(
        functools.partial(pair_kernel, len(groups)),
        grid_spec=pltpu.PrefetchScalarGridSpec(
            num_scalar_prefetch=1,
            grid=(depth,),
            in_specs=in_specs,
            out_specs=pl.BlockSpec((1, height, width), lambda z, w: (z, 0, 0)),
        ),
        out_shape=jax.ShapeDtypeStruct((depth, height, width), BF16),
        compiler_params=params(),
        cost_estimate=cost(flops, 4 * depth * height * width),
        name="pair_grads",
    )(where, *operands)


def column_kernel(where_ref, own_t, peer_t, own, peer, out_ref):
    for z in range(own_t.shape[0]):
        out_ref[0, z] = (dot(own_t[z, 0], own[...]) + dot(peer_t[z], peer[...])).astype(BF16)


def column_grads(where, parts, own_t, peer_t, own, peer):
    depth, _, size, rows = own_t.shape
    width = own.shape[1] // parts
    return pl.pallas_call(
        column_kernel,
        grid_spec=pltpu.PrefetchScalarGridSpec(
            num_scalar_prefetch=1,
            grid=(parts,),
            in_specs=[
                pl.BlockSpec((depth, 1, size, rows), lambda k, w: (0, w[0], 0, 0)),
                pl.BlockSpec((depth, size, rows), lambda k, w: (0, 0, 0)),
                pl.BlockSpec((rows, width), lambda k, w: (0, k ^ w[1])),
                pl.BlockSpec((rows, width), lambda k, w: (0, k ^ w[1])),
            ],
            out_specs=pl.BlockSpec((1, depth, size, width), lambda k, w: (k, 0, 0, 0)),
        ),
        out_shape=jax.ShapeDtypeStruct((parts, depth, size, width), BF16),
        compiler_params=params(),
        cost_estimate=cost(
            4 * parts * depth * size * rows * width, 4 * parts * depth * size * width
        ),
        name="column_grads",
    )(where, own_t, peer_t, own, peer)


def heads_kernel(normed_ref, dt_ref, out_ref):
    out_ref[...] = lax.dot_general(
        normed_ref[...], dt_ref[...], (((0,), (1,)), ((), ())), preferred_element_type=F32
    ).astype(BF16)


def heads_grads(normed_all, d_triple_t):
    total, width = normed_all.shape
    wide = d_triple_t.shape[0]
    return pl.pallas_call(
        heads_kernel,
        out_shape=jax.ShapeDtypeStruct((width, wide), BF16),
        compiler_params=params(),
        cost_estimate=cost(2 * total * width * wide, 2 * total * (width + wide)),
        name="heads_grads",
    )(normed_all, d_triple_t)


def columns_kernel(place_ref, *refs):
    out_ref = refs[-1]
    size = refs[0].shape[1]
    for k in range(len(refs) - 1):
        at = pl.multiple_of((place_ref[0] ^ k) * size, LANES)
        out_ref[:, pl.ds(at, size)] = refs[k][...].astype(F32)


def put_columns(place, pieces):
    height, size = pieces[0].shape
    count = len(pieces)
    return pl.pallas_call(
        columns_kernel,
        in_specs=[pl.BlockSpec(memory_space=pltpu.SMEM)]
        + [pl.BlockSpec(memory_space=pltpu.VMEM)] * count,
        out_shape=jax.ShapeDtypeStruct((height, count * size), F32),
        compiler_params=params(),
        cost_estimate=cost(1e6, 6 * count * height * size),
        name="put_columns",
    )(place, *pieces)


def head_columns_kernel(place_ref, *refs):
    out_ref = refs[-1]
    count = len(refs) - 1
    size = refs[0].shape[1] // 3
    for j in range(count):
        value = refs[0][...]
        for k in range(1, count):
            value = jnp.where((place_ref[0] ^ k) == j, refs[k][...], value)
        value = value.astype(F32)
        for which in range(3):
            at = (which * count + j) * size
            out_ref[:, at : at + size] = value[:, which * size : (which + 1) * size]


def put_heads(place, pieces):
    height, size = pieces[0].shape
    count = len(pieces)
    return pl.pallas_call(
        head_columns_kernel,
        in_specs=[pl.BlockSpec(memory_space=pltpu.SMEM)]
        + [pl.BlockSpec(memory_space=pltpu.VMEM)] * count,
        out_shape=jax.ShapeDtypeStruct((height, count * size), F32),
        compiler_params=params(),
        cost_estimate=cost(1e6, 6 * count * height * size),
        name="put_heads",
    )(place, *pieces)


def across(value, size, bit):
    return lax.ppermute(value, "seq", [(i, i ^ bit) for i in range(size)])


def other_core(value, size):
    return lax.ppermute(value, "batch", [(i, i ^ 1) for i in range(size)])


def plus(*terms):
    total = terms[0].astype(F32)
    for term in terms[1:]:
        total = total + term.astype(F32)
    return total.astype(BF16)


def bits_of(size):
    return [1 << i for i in range(size.bit_length() - 1)]


def everywhere(value, size):
    if size != 4:
        return [value] + [across(value, size, k) for k in range(1, size)]
    half = value.shape[0] // 2
    near, far = across(value, size, 1), across(value, size, 2)
    lead, tail = across(near[:half], size, 2), across(far[half:], size, 1)
    return [value, near, far, jnp.concatenate([lead, tail], 0)]


def scattered(value, size, bits):
    left = list(range(size))
    for bit in bits:
        keep = [i for i, k in enumerate(left) if not k & bit]
        send = [i for i, k in enumerate(left) if k & bit]
        pick = lambda which: jnp.concatenate([value[i : i + 1] for i in which], 0)
        value = plus(pick(keep), across(pick(send), size, bit))
        left = [left[i] for i in keep]
    return value[0]


def summed(value, size):
    half = (value.shape[0] // 2 + 7) // 8 * 8
    bits = bits_of(size)
    done = []
    for piece, order in ((value[:half], bits), (value[half:], bits[::-1])):
        for bit in order:
            piece = plus(piece, across(piece, size, bit))
        done.append(piece)
    return jnp.concatenate(done, 0)


def down_the_line(value, size, at):
    depth = value.shape[0]
    pick = lambda index: lax.dynamic_index_in_dim(
        value, jnp.clip(index, 0, depth - 1), 0, keepdims=False
    )
    up = down = None
    for t in range(depth - 1):
        send_up = pick(depth - 1 - t + at)
        send_down = pick(t - (depth - 1 - at))
        if t:
            send_up, send_down = plus(send_up, up), plus(send_down, down)
        up = lax.ppermute(
            send_up,
            "batch",
            [(2 * z + c, 2 * z + 2 + c) for z in range(depth - 1) if z <= t for c in (0, 1)],
        )
        down = lax.ppermute(
            send_down,
            "batch",
            [
                (2 * z + c, 2 * z - 2 + c)
                for z in range(1, depth)
                if z >= depth - 1 - t
                for c in (0, 1)
            ],
        )
    return plus(pick(at), up, down)


MESH = pl.DeviceIdType.MESH
AWAY = (1, 3, 2, 0)


def flip(value, k):
    if k == 0:
        return value
    if k == 1:
        return value + 1 - 2 * (value % 2)
    if k == 2:
        return value + 2 - 4 * (value // 2)
    return 3 - value


def add_rows(into, other):
    if len(into.shape) > 2:
        for i in range(into.shape[0]):
            add_rows(into.at[i], other.at[i])
        return
    tile = 16

    def body(i, carry):
        at = pl.ds(pl.multiple_of(i * tile, tile), tile)
        into[at] = (into[at].astype(F32) + other[at].astype(F32)).astype(BF16)
        return carry

    lax.fori_loop(0, into.shape[0] // tile, body, 0)


class Wires:
    def __init__(self, send_sems, recv_sems):
        self.send_sems, self.recv_sems, self.made = send_sems, recv_sems, []
        self.limit = send_sems.shape[0]

    def copy(self, src, dst, device, when=None):
        index = len(self.made)
        assert index < self.limit
        made = Wire(
            pltpu.make_async_remote_copy(
                src_ref=src,
                dst_ref=dst,
                send_sem=self.send_sems.at[index],
                recv_sem=self.recv_sems.at[index],
                device_id=device,
                device_id_type=MESH,
            ),
            when,
        )
        self.made.append(made)
        return made

    def by_core(self, core, src, dst, device, when=None):
        index = len(self.made)
        assert index + 1 < self.limit
        self.made.append(None)
        pick = lambda which: pltpu.make_async_remote_copy(
            src_ref=src,
            dst_ref=dst,
            send_sem=self.send_sems.at[index],
            recv_sem=self.recv_sems.at[index + which],
            device_id=device,
            device_id_type=MESH,
        )
        made = Wire(pick(core), when)
        made.arrive = lambda: [pick(which).wait_recv() for which in (0, 1)]
        self.made.append(made)
        return made

    def drain(self):
        for wire in [w for w in self.made if w is not None]:
            if wire.when is None:
                wire.copy.wait_send()
            else:
                pl.when(wire.when)(wire.copy.wait_send)


class Wire:
    def __init__(self, copy, when):
        self.copy, self.when = copy, when
        self.start, self.arrive = copy.start, copy.wait_recv


class Line:
    def __init__(self, wires, depth, chip, up_to, down_to, own, up_in, down_in, begun=False):
        self.depth, self.chip, self.own, self.begun = depth, chip, own, begun
        self.up_in, self.down_in = up_in, down_in
        last = depth - 1
        self.up = {
            d: wires.copy(
                own(d),
                up_in.at[d - 1],
                up_to,
                (chip < d) & (chip > 0) if begun and d == last else chip < d,
            )
            for d in range(1, depth)
        }
        self.down = {
            d: wires.copy(
                own(d),
                down_in.at[d],
                down_to,
                (chip > d) & (chip < last) if begun and d == 0 else chip > d,
            )
            for d in range(last)
        }

    def hop(self, t):
        last = self.depth - 1
        for d in range(1, self.depth):
            z = d - (last - t)
            if 0 <= z < d:

                @pl.when(self.chip == z)
                def _():
                    if z > 0 and not (self.begun and t == 1):
                        self.up[d].arrive()
                        add_rows(self.own(d), self.up_in.at[d - 1])
                    self.up[d].start()

                @pl.when(self.chip == last - z)
                def _():
                    if z > 0 and not (self.begun and t == 1):
                        self.down[last - d].arrive()
                        add_rows(self.own(last - d), self.down_in.at[last - d])
                    self.down[last - d].start()

    def finish(self):
        for d in range(self.depth):

            @pl.when(self.chip == d)
            def _():
                if d > 0:
                    self.up[d].arrive()
                    add_rows(self.own(d), self.up_in.at[d - 1])
                if d < self.depth - 1:
                    self.down[d].arrive()
                    add_rows(self.own(d), self.down_in.at[d])


class Square:
    def __init__(self, wires, to, own, in_one, in_two, src=None, begun=False):
        self.own, self.in_one, self.in_two = own, in_one, in_two
        src = src or own
        self.one, self.two = [], []
        for h, (f, g) in enumerate(((1, 2), (2, 1))):
            if not begun:
                self.one.append(
                    (
                        wires.copy(src(h, 3), in_one[h].at[1], to[f]),
                        wires.copy(src(h, f), in_one[h].at[0], to[f]),
                    )
                )
        for h, (f, g) in enumerate(((1, 2), (2, 1))):
            self.two.append(wires.copy(own(h, g), in_two[h], to[g]))

    def start(self):
        for i in range(2):
            for h in range(2):
                self.one[h][i].start()

    def middle(self):
        for h, g in ((0, 2), (1, 1)):
            self.one[h][0].arrive()
            add_rows(self.own(h, g), self.in_one[h].at[1])
            self.two[h].start()
        for h in range(2):
            self.one[h][1].arrive()
            add_rows(self.own(h, 0), self.in_one[h].at[0])

    def finish(self):
        for h in range(2):
            self.two[h].arrive()
            add_rows(self.own(h, 0), self.in_two[h])


class Spread:
    def __init__(self, wires, to, slots, src=None):
        rows = slots.shape[1]
        cut = (rows // 2 + 15) // 16 * 16
        src = slots.at[0] if src is None else src
        lead, tail = pl.ds(0, cut), pl.ds(cut, rows - cut)
        self.near = [wires.copy(src.at[p], slots.at[1, p], to[1]) for p in (lead, tail)]
        self.far = [wires.copy(src.at[p], slots.at[2, p], to[2]) for p in (tail, lead)]
        self.lead = wires.copy(slots.at[1, lead], slots.at[3, lead], to[2])
        self.tail = wires.copy(slots.at[2, tail], slots.at[3, tail], to[1])

    def start(self):
        for i in range(2):
            self.near[i].start()
            self.far[i].start()

    def relay(self):
        self.near[0].arrive()
        self.lead.start()
        self.far[0].arrive()
        self.tail.start()

    def finish(self):
        self.near[1].arrive()
        self.far[1].arrive()
        self.lead.arrive()
        self.tail.arrive()


class Pair:
    def __init__(self, wires, to, halves, ins):
        self.halves, self.ins, self.wires, self.to, self.step = halves, ins, wires, to, 0
        self.sent = [
            [wires.copy(halves[h][i], ins[h].at[i], to[(1, 2)[(h + i) % 2]]) for h in range(2)]
            for i in range(2)
        ]

    def start(self):
        for wire in self.sent[0]:
            wire.start()

    def middle(self):
        for h in range(2):
            self.sent[0][h].arrive()
            one, two = self.halves[h][0], self.halves[h][1]
            two[...] = (one[...].astype(F32) + self.ins[h][0].astype(F32)).astype(BF16)
            self.sent[1][h].start()

    def finish(self):
        for h in range(2):
            self.sent[1][h].arrive()
            two, three = self.halves[h][1], self.halves[h][2]
            three[...] = (two[...].astype(F32) + self.ins[h][1].astype(F32)).astype(BF16)


def reduce_kernel(
    late_hbm,
    lead_hbm,
    tail_hbm,
    normed_hbm,
    dt_hbm,
    joined_hbm,
    joined_peer_hbm,
    hidden_hbm,
    d_middle_hbm,
    w_hbm,
    normed_x,
    normed_peer,
    normed_cond_x,
    normed_cond_peer,
    d_pre_x,
    active_near,
    active_x,
    active_cond_near,
    active_cond_x,
    cot_hbm,
    cot_z,
    cot_zz,
    cot_far,
    cot_peer,
    gain_ref,
    vec_two_ref,
    fc1_bias_ref,
    p_all,
    f_all,
    g_all,
    q_all,
    s_all,
    c_all,
    din_hbm,
    dskip_hbm,
    vec_ref,
    left_one,
    right_one,
    left_two,
    right_two,
    cond_rows,
    cond_flat,
    active_cond,
    f_own,
    f_up,
    f_down,
    g_own,
    g_lead_one,
    g_tail_one,
    g_lead_two,
    g_tail_two,
    l_own,
    l_up,
    l_down,
    q_own,
    q_sum,
    q_up,
    q_down,
    s_own,
    s_one,
    s_two,
    s_z,
    s_up,
    s_down,
    d_own,
    d_one,
    d_two,
    p_lead,
    p_tail,
    p_lead_in,
    p_tail_in,
    low_ref,
    low_peer,
    c_own,
    v_own,
    v_in,
    send_sems,
    recv_sems,
    local_sems,
):
    rows, width = hidden_hbm.shape
    depth = f_own.shape[0]
    mid = depth // 2
    slots = c_own.shape[0]
    images = rows - slots
    place, index = lax.axis_index("seq"), lax.axis_index("batch")
    chip, core = index // 2, index % 2
    last = depth - 1
    to, other, up_to, down_to = ends_of(place, index, depth)
    greet([to[1], to[2], to[3], other], chip, depth, up_to, down_to)
    wires = Wires(send_sems, recv_sems)
    taken = [0]

    def local(src, dst):
        taken[0] += 1
        copy = pltpu.make_async_copy(src, dst, local_sems.at[taken[0] - 1])
        copy.start()
        return copy

    keeps = []

    d_hbm = (lead_hbm, tail_hbm)
    norm_sum = Square(
        wires,
        to,
        lambda h, k: d_own.at[h, (0, 1, 1, None)[k]],
        [d_one.at[h] for h in range(2)],
        [d_two.at[h] for h in range(2)],
        src=lambda h, k: d_hbm[h].at[k],
    )
    norm_sum.start()

    l_load = local(late_hbm, l_own)
    l_line = Line(wires, depth, chip, up_to, down_to, lambda d: l_own.at[d], l_up, l_down)

    img, cnd = pl.ds(0, images), pl.ds(images, slots)

    def cut(g):
        return pl.ds(pl.multiple_of(g * images, images), images)

    def end(g):
        return pl.ds(pl.multiple_of(8 * images + g * slots, slots), slots)

    loads_two, loads_able = [], []
    for i in range(depth):
        source = (chip + depth - AWAY[i]) % depth
        for c in range(2):
            g = source * 2 + c
            left = active_near.at[i, c] if i < 2 else active_x.at[i - 2, c]
            ends = active_cond_near.at[i, c] if i < 2 else active_cond_x.at[i - 2, c]
            loads_two.append(local(left, left_two.at[:, :, cut(g)]))
            loads_two.append(local(ends, active_cond.at[g]))
    held = [cot_hbm, cot_z.at[0], cot_z.at[1], cot_zz.at[0], cot_zz.at[1], cot_far]
    for away, picks in ((0, (0, 0)), (1, (1, 2)), (2, (3, 4)), (3, (5, 5))):
        for which in range(2):
            if away == 0 and which == 1:
                continue
            z = chip - away if which == 0 else chip + away
            able = (z >= 0) & (z <= last)
            for ref, c in ((held[picks[which]], core), (cot_peer.at[picks[which]], 1 - core)):
                g = jnp.clip(z, 0, last) * 2 + c
                for src, dst in ((img, cut(g)), (cnd, end(g))):
                    sem = local_sems.at[taken[0]]
                    taken[0] += 1
                    copy = pltpu.make_async_copy(ref.at[src], right_two.at[dst], sem)
                    pl.when(able)(copy.start)
                    loads_able.append((able, copy))
    swaps_one = []
    for k in range(4):
        swaps_one.append(wires.copy(d_pre_x.at[k, img], right_one.at[cut(4 + k)], other))
        swaps_one.append(wires.copy(d_pre_x.at[k, cnd], right_one.at[end(4 + k)], other))
    for wire in swaps_one:
        wire.start()
    loads_one = []
    for k in range(4):
        for g, left, cond in (
            (k, normed_x.at[k, :, core], normed_cond_x.at[k]),
            (4 + k, normed_peer.at[k], normed_cond_peer.at[k]),
        ):
            loads_one.append(local(left, left_one.at[:, :, cut(g)]))
            loads_one.append(local(cond, cond_rows.at[pl.ds(g * slots, slots)]))
        loads_one.append(local(d_pre_x.at[k, img], right_one.at[cut(k)]))
        loads_one.append(local(d_pre_x.at[k, cnd], right_one.at[end(k)]))
    d_loads = [
        local(d_hbm[h].at[k], d_own.at[h, i]) for h, ks in ((0, (0, 2)), (1, (0, 1))) for i, k in enumerate(ks)
    ]
    p_cut = p_lead.shape[1]
    l_load.wait()
    l_line.hop(0)

    for copy in loads_two:
        copy.wait()
    for able, copy in loads_able:
        pl.when(able)(copy.wait)
    small = f_own.shape[1]
    for j in range(4):
        left_two[j, :, 8 * images :] = jnp.concatenate(
            [active_cond[g, :, j * slots : (j + 1) * slots] for g in range(8)], 1
        )
        g_own[j] = dot(left_two[j], right_two[...]).astype(BF16)
    g_cut = g_lead_one.shape[1]
    g_sum = Square(
        wires,
        to,
        lambda h, k: g_own.at[flip(place, k), (pl.ds(0, g_cut), pl.ds(g_cut, small - g_cut))[h]],
        (g_lead_one, g_tail_one),
        (g_lead_two, g_tail_two),
    )

    for copy in loads_one:
        copy.wait()
    flat = turned(cond_rows[...])
    for b in range(2 * depth):
        cond_flat[b // 2, b % 2] = flat[b * small : (b + 1) * small]
    for z in range(depth):
        left_one[z, :, 8 * images :] = cond_flat[z, core]
    for wire in swaps_one:
        wire.arrive()
    for z in range(depth):
        f_own[z] = dot(left_one[z], right_one[...]).astype(BF16)
    f_line = Line(wires, depth, chip, up_to, down_to, lambda d: f_own.at[d], f_up, f_down)
    f_line.hop(0)
    for copy in d_loads:
        copy.wait()
    norm_sum.middle()
    g_sum.start()

    def heads_part(normed, dt):
        loads = [local(normed_hbm, normed), local(dt_hbm, dt)]
        for copy in loads:
            copy.wait()
        step = 3 * LANES
        for part in range(normed.shape[1] // step):
            grads = lax.dot_general(
                normed[:, part * step : (part + 1) * step],
                dt[...],
                (((0,), (1,)), ((), ())),
                preferred_element_type=F32,
            ).astype(BF16)
            q_own[pl.ds(part * step, step)] = grads

    pl.run_scoped(
        heads_part, pltpu.VMEM(normed_hbm.shape, BF16), pltpu.VMEM(dt_hbm.shape, BF16)
    )
    height = q_sum.shape[1]
    q_swap = [
        wires.copy(
            q_own.at[pl.ds(pl.multiple_of((2 * z + 1 - core) * height, 16), height)],
            q_sum.at[z],
            other,
        )
        for z in range(depth)
    ]
    for wire in q_swap:
        wire.start()

    norm_sum.finish()
    low_swap = wires.copy(low_ref, low_peer, other)
    v_swap = wires.copy(v_own.at[0], v_in.at[0], other)

    def back_part(hidden, d_middle):
        loads = [local(hidden_hbm, hidden), local(d_middle_hbm, d_middle)]
        for copy in loads:
            copy.wait()
        upstream = jnp.concatenate(
            [d_own[0, 0].astype(F32), d_own[1, 0].astype(F32)], 0
        )
        scaled, factor = normalize(hidden[...])
        d_hidden = d_middle[...] + norm_back(
            upstream, scaled, factor, gain_ref[...].reshape(1, -1)
        )
        low_ref[...] = d_hidden.astype(BF16)
        low_swap.start()
        v_own[0] = jnp.zeros(v_own.shape[1:], F32)
        v_own[0, 0:1] = jnp.sum(d_hidden, axis=0, keepdims=True)
        v_own[0, 1:2] = jnp.sum(upstream * scaled, axis=0, keepdims=True)
        v_own[0, 2:3] = jnp.sum(upstream, axis=0, keepdims=True)
        v_own[0, 3:7] = vec_two_ref[0:4]
        v_own[0, 8:12] = fc1_bias_ref[...]
        v_swap.start()

    pl.run_scoped(back_part, pltpu.VMEM(hidden_hbm.shape, F32), pltpu.VMEM(hidden_hbm.shape, F32))
    for z, wire in enumerate(q_swap):
        wire.arrive()
        add_rows(q_sum.at[z], q_own.at[pl.ds(pl.multiple_of((2 * z + core) * height, 16), height)])
    q_line = Line(wires, depth, chip, up_to, down_to, lambda d: q_sum.at[d], q_up, q_down)
    l_line.hop(1)
    f_line.hop(1)
    q_line.hop(0)

    low_swap.arrive()

    def skip_part(joined, peer):
        loads = [local(joined_hbm, joined), local(joined_peer_hbm, peer)]
        for copy in loads:
            copy.wait()
        chunk = joined.shape[1] // 4
        for z in range(depth):
            grads = both(joined[z], peer[z], low_ref[...], low_peer[...])
            for j in range(4):
                piece = grads[j * chunk : (j + 1) * chunk]
                piece = jnp.concatenate(
                    [piece, jnp.zeros((s_own.shape[2] - chunk, width), F32)], 0
                )
                s_own[flip(place, j), z] = piece.astype(BF16)

    pl.run_scoped(
        skip_part,
        pltpu.VMEM(joined_peer_hbm.shape, BF16),
        pltpu.VMEM(joined_peer_hbm.shape, BF16),
    )
    s_sum = Square(
        wires,
        to,
        lambda h, k: s_own.at[k, pl.ds(h * mid, mid)],
        [s_one.at[h] for h in range(2)],
        [s_two.at[h] for h in range(2)],
    )
    s_sum.start()
    g_sum.middle()
    for t in range(2, last):
        l_line.hop(t)
        f_line.hop(t)

    c_go = [wires.copy(c_own, c_all.at[k], to[k]) for k in (1, 2, 3)]

    def rows_part(w, stage):
        copy = local(w_hbm.at[pl.ds(0, width)], w)
        copy.wait()
        stage[...] = dot_nt(low_ref[...], w[...])
        c_own[:, :width] = stage[images:].astype(BF16)
        copy = local(w_hbm.at[pl.ds(width, width)], w)
        out = local(stage.at[pl.ds(0, images)], din_hbm)
        copy.wait()
        out.wait()
        stage[...] = dot_nt(low_ref[...], w[...])
        c_own[:, width:] = stage[images:].astype(BF16)
        for wire in c_go:
            wire.start()
        local(stage.at[pl.ds(0, images)], dskip_hbm).wait()

    pl.run_scoped(rows_part, pltpu.VMEM((width, width), BF16), pltpu.VMEM((rows, width), F32))
    keeps.append(local(c_own, c_all.at[0]))

    v_swap.arrive()
    v_own[1] = v_own[0] + v_in[0]
    v_own[2] = v_own[1]
    v_own[3] = v_own[1]
    v_up = wires.copy(v_own.at[2], v_in.at[1], up_to, chip < last)
    v_down = wires.copy(v_own.at[3], v_in.at[2], down_to, chip > 0)
    q_line.hop(1)
    for t in range(2, last):
        q_line.hop(t)
    s_sum.middle()
    g_sum.finish()
    g_go = Spread(wires, to, g_all, g_own.at[place])
    g_go.start()
    keeps.append(local(g_own.at[place], g_all.at[0]))
    f_line.finish()
    f_go = Spread(wires, to, f_all, f_own.at[chip])
    f_go.start()
    keeps.append(local(f_own.at[chip], f_all.at[0]))
    s_sum.finish()
    for d in range(depth):
        s_z[d] = s_own[0, d]
    s_line = Line(wires, depth, chip, up_to, down_to, lambda d: s_z.at[d], s_up, s_down)
    s_line.hop(0)

    @pl.when(chip > 0)
    def _():
        v_up.arrive()
        v_own[2] = v_own[1] + v_in[1]

    @pl.when(chip < last)
    def _():
        v_up.start()

    @pl.when(chip < last)
    def _():
        v_down.arrive()
        v_own[3] = v_own[1] + v_in[2]

    @pl.when(chip > 0)
    def _():
        v_down.start()

    v_own[4] = v_own[2] + v_own[3] - v_own[1]
    v_near = wires.copy(v_own.at[4], v_in.at[3], to[1])
    v_near.start()
    s_line.hop(1)
    l_line.finish()
    p_lead[0] = l_own[chip, :p_cut]
    p_tail[0] = l_own[chip, p_cut:]
    p_sum = Pair(
        wires,
        to,
        [[ref.at[i] for i in range(3)] for ref in (p_lead, p_tail)],
        (p_lead_in, p_tail_in),
    )
    p_sum.start()
    q_line.finish()
    q_go = Spread(wires, to, q_all, q_sum.at[chip])
    q_go.start()
    keeps.append(local(q_sum.at[chip], q_all.at[0]))
    f_go.relay()
    for t in range(2, last):
        s_line.hop(t)
    p_sum.middle()
    v_near.arrive()
    v_own[5] = v_own[4] + v_in[3]
    v_far = wires.copy(v_own.at[5], v_in.at[4], to[2])
    v_far.start()
    s_line.finish()
    s_go = Spread(wires, to, s_all, s_z.at[chip])
    s_go.start()
    keeps.append(local(s_z.at[chip], s_all.at[0]))
    g_go.relay()
    q_go.relay()
    p_sum.finish()
    keeps.append(local(p_lead.at[2], p_all.at[pl.ds(0, p_cut)]))
    keeps.append(local(p_tail.at[2], p_all.at[pl.ds(p_cut, p_tail.shape[1])]))
    for wire in c_go:
        wire.arrive()
    v_far.arrive()
    vec_ref[...] = v_own[5] + v_in[4]
    s_go.relay()
    f_go.finish()
    g_go.finish()
    q_go.finish()
    s_go.finish()
    for copy in keeps:
        copy.wait()
    wires.drain()


def reduce_all(
    late, lead, tail, normed_all, d_triple_t, joined, joined_peer, hidden, d_middle, w, feeds,
    gain, vec_two, fc1_bias_grad,
):
    depth, small, width = late.shape
    rows = hidden.shape[0]
    slots = SLOTS // 4
    images = rows - slots
    mid = depth // 2
    own = d_triple_t.shape[0]
    skip_rows = joined.shape[1]
    skip_chunk = (skip_rows // 4 + 15) // 16 * 16
    half = rows // 2
    cut = (small // 2 + 15) // 16 * 16
    v = lambda *shape: pltpu.VMEM(shape, BF16)
    ends = depth - 1
    scratch = [
        v(depth, small, 8 * rows), v(8 * rows, width), v(depth, small, 8 * rows), v(8 * rows, width),
        v(8 * slots, width), v(depth, 2, small, 8 * slots), v(8, small, 4 * slots),
        v(depth, small, width), v(ends, small, width), v(ends, small, width),
        v(4, small, width), v(2, cut, width), v(2, small - cut, width), v(cut, width), v(small - cut, width),
        v(depth, small, width), v(ends, small, width), v(ends, small, width),
        v(width, own), v(depth, small, own), v(ends, small, own), v(ends, small, own),
        v(4, depth, skip_chunk, width), v(2, 2, mid, skip_chunk, width), v(2, mid, skip_chunk, width),
        v(depth, skip_chunk, width), v(ends, skip_chunk, width), v(ends, skip_chunk, width),
        v(2, 2, half, width), v(2, 2, half, width), v(2, half, width),
        v(3, cut, width), v(3, small - cut, width), v(2, cut, width), v(2, small - cut, width),
        v(rows, width), v(rows, width), v(slots, 2 * width),
        pltpu.VMEM((6, 16, width), F32), pltpu.VMEM((5, 16, width), F32),
        pltpu.SemaphoreType.DMA((128,)), pltpu.SemaphoreType.DMA((128,)), pltpu.SemaphoreType.DMA((128,)),
    ]
    hbm = pl.BlockSpec(memory_space=pl.ANY)
    vmem = pl.BlockSpec(memory_space=pltpu.VMEM)
    f = lambda *shape: jax.ShapeDtypeStruct(shape, F32)
    b = lambda *shape: jax.ShapeDtypeStruct(shape, BF16)
    return pl.pallas_call(
        reduce_kernel,
        in_specs=[hbm] * 24 + [vmem] * 3,
        out_specs=[hbm] * 8 + [vmem],
        out_shape=[
            b(small, width),
            b(4, small, width),
            b(4, small, width),
            b(4, small, own),
            b(4, skip_chunk, width),
            b(4, slots, 2 * width),
            f(images, width),
            f(images, width),
            f(16, width),
        ],
        scratch_shapes=scratch,
        compiler_params=pltpu.CompilerParams(
            vmem_limit_bytes=VMEM_LIMIT, collective_id=0, has_side_effects=True
        ),
        cost_estimate=cost(1e10, 1e8),
        name="reduce_all",
    )(
        late, lead, tail, normed_all, d_triple_t, joined, joined_peer, hidden, d_middle, w, *feeds,
        gain, vec_two, fc1_bias_grad,
    )


def ends_of(place, index, depth):
    chip, core = index // 2, index % 2
    to = {k: (index, flip(place, k)) for k in (1, 2, 3)}
    return to, (index + 1 - 2 * core, place), (index + 2, place), (index - 2, place)


def line_of(place, index, depth):
    chip = index // 2
    return [((chip + i) % depth * 2 + c, place) for i in range(1, depth) for c in (0, 1)]


def arrive_by_core(wires, core):
    for c in range(2):

        @pl.when(core == c)
        def _():
            wires[2 * c].arrive()
            wires[2 * c + 1].arrive()


class Hop:
    def __init__(self, wires, depth, chip, up_to, down_to, t, src_up, src_down, dst_up, dst_down):
        last = depth - 1
        self.up = wires.copy(src_up, dst_up, up_to, (chip < last) & (chip >= t))
        self.down = wires.copy(src_down, dst_down, down_to, (chip > 0) & (chip <= last - t))
        self.from_up = (chip > 0) & (chip - 1 >= t)
        self.from_down = (chip < last) & (chip + 1 <= last - t)

    def start(self):
        pl.when(self.up.when)(self.up.start)
        pl.when(self.down.when)(self.down.start)

    def arrive(self):
        pl.when(self.from_up)(self.up.arrive)
        pl.when(self.from_down)(self.down.arrive)


def greet(devices, chip=None, depth=0, up_to=None, down_to=None):
    barrier = pltpu.get_barrier_semaphore()
    for device in devices:
        pl.semaphore_signal(barrier, inc=1, device_id=device, device_id_type=MESH)
    if chip is None:
        pl.semaphore_wait(barrier, len(devices))
        return

    @pl.when(chip < depth - 1)
    def _():
        pl.semaphore_signal(barrier, inc=1, device_id=up_to, device_id_type=MESH)

    @pl.when(chip > 0)
    def _():
        pl.semaphore_signal(barrier, inc=1, device_id=down_to, device_id_type=MESH)

    pl.semaphore_wait(
        barrier, len(devices) + jnp.minimum(chip, 1) + jnp.minimum(depth - 1 - chip, 1)
    )


class Locals:
    def __init__(self, sems):
        self.sems, self.taken = sems, 0

    def copy(self, src, dst):
        self.taken += 1
        assert self.taken <= self.sems.shape[0]
        return pltpu.make_async_copy(src, dst, self.sems.at[self.taken - 1])

    def start(self, src, dst):
        copy = self.copy(src, dst)
        copy.start()
        return copy


def own_slots(cond_ref, pad_ref, place, slots):
    pad_ref[...] = jnp.zeros(pad_ref.shape, BF16)
    pad_ref[0 : cond_ref.shape[0]] = cond_ref[...]
    return pad_ref[pl.ds(pl.multiple_of(place * slots, 16), slots)]


def start_kernel(
    window,
    length_ref,
    x_ref,
    x_cond_ref,
    s_ref,
    s_cond_ref,
    cot_ref,
    cot_cond_ref,
    w_ref,
    bias_ref,
    gain_ref,
    shift_ref,
    qkv_w_hbm,
    hidden_ref,
    normed_hbm,
    heads_ref,
    qkv_ref,
    joined_hbm,
    peer_hbm,
    cot_all,
    cot_z,
    pad_ref,
    x_all,
    s_all,
    normed_all,
    joined_ref,
    qkv_w_ref,
    send_sems,
    recv_sems,
    local_sems,
):
    images, width = x_ref.shape
    slots = x_all.shape[0] - images
    place, index = lax.axis_index("seq"), lax.axis_index("batch")
    core = index % 2
    chip = index // 2
    depth = joined_hbm.shape[0]
    to, other, up_to, down_to = ends_of(place, index, depth)
    greet([to[1], to[2], other], chip, depth, up_to, down_to)
    wires, moves = Wires(send_sems, recv_sems), Locals(local_sems)
    w_load = moves.start(qkv_w_hbm, qkv_w_ref)
    cot_all[:images] = cot_ref[...]
    cot_all[images:] = own_slots(cot_cond_ref, pad_ref, place, slots)
    cot_go = Hop(
        wires, depth, chip, up_to, down_to, 0, cot_all, cot_all, cot_z.at[0], cot_z.at[1]
    )
    cot_go.start()
    for ref, cond, whole in ((x_ref, x_cond_ref, x_all), (s_ref, s_cond_ref, s_all)):
        whole[:images] = ref[...]
        whole[images:] = own_slots(cond, pad_ref, place, slots)
    hidden = (
        dot(x_all[...], w_ref[:width]) + dot(s_all[...], w_ref[width:]) + bias_ref[...].reshape(1, -1)
    )
    hidden_ref[...] = hidden
    scaled, _ = normalize(hidden)
    normed_all[0] = (
        scaled * gain_ref[...].reshape(1, -1) + shift_ref[...].reshape(1, -1)
    ).astype(BF16)
    spread = Spread(wires, to, normed_all)
    spread.start()

    size = joined_ref.shape[2]
    per = width // size
    for which, whole in enumerate((x_all, s_all)):
        flat = turned(whole[...])
        for i in range(per):
            block = which * per + i
            joined_ref[block // 2, block % 2] = flat[i * size : (i + 1) * size]
    swap = wires.copy(joined_ref.at[:, 1 - core], peer_hbm, other)
    swap.start()
    keep = moves.start(joined_ref.at[:, core], joined_hbm)
    heads = qkv_ref.shape[0]
    width_own = heads * HEAD_DIM
    real = lax.broadcasted_iota(jnp.int32, (width, LANES), 1) < HEAD_DIM

    def weights(which):
        first = place * width_own + which * width
        start = jnp.minimum(first // LANES * LANES, 3 * width - window)
        value = qkv_w_ref[:, pl.ds(pl.multiple_of(start, LANES), window)].astype(F32)
        value = pltpu.roll(value, lax.rem(window - (first - start), window), 1)
        for head in range(heads):
            shifted = value if head == 0 else pltpu.roll(value, window - head * HEAD_DIM, 1)
            at = (3 * head + which) * LANES
            heads_ref[:, at : at + LANES] = jnp.where(real, shifted[:, :LANES], 0.0).astype(BF16)

    rows = normed_all.shape[1]
    lane = lax.broadcasted_iota(jnp.int32, (1, LANES), 1)
    one = jnp.where(lane == HEAD_DIM, 1.0, 0.0)
    slot = lax.broadcasted_iota(jnp.int32, (slots, LANES), 0)
    lanes = lax.broadcasted_iota(jnp.int32, (slots, LANES), 1)

    def project(part):
        hidden_key = flip(place, part) * slots + slot > length_ref[0]
        bias = jnp.where(hidden_key & (lanes == HEAD_DIM), -1e30, 0.0)
        base = part * rows
        for head in range(heads):
            triple = dot(
                normed_all[part], heads_ref[:, 3 * head * LANES : 3 * (head + 1) * LANES]
            )
            qkv_ref[head, base : base + rows, :LANES] = (triple[:, :LANES] + one).astype(BF16)
            key = triple[:, LANES : 2 * LANES]
            qkv_ref[head, base : base + images, LANES : 2 * LANES] = key[:images].astype(BF16)
            qkv_ref[head, base + images : base + rows, LANES : 2 * LANES] = (
                key[images:] + bias
            ).astype(BF16)
            qkv_ref[head, base : base + rows, 2 * LANES :] = triple[:, 2 * LANES :].astype(BF16)

    w_load.wait()
    weights(0)
    spread.relay()
    weights(1)
    weights(2)
    project(0)
    spread.near[1].arrive()
    project(1)
    spread.far[1].arrive()
    project(2)
    spread.lead.arrive()
    spread.tail.arrive()
    project(3)
    out = moves.start(normed_all, normed_hbm)
    keep.wait()
    cot_go.arrive()
    swap.arrive()
    out.wait()
    wires.drain()


def start_stage(depth, length, x, x_cond, s, s_cond, cot, cot_cond, w, bias, gain, shift, qkv_w):
    images, width = x.shape
    slots = SLOTS // 4
    rows = images + slots
    heads = HEADS // 4
    own = heads * HEAD_DIM
    window = (max(p * own % LANES for p in range(4)) + own + LANES - 1) // LANES * LANES
    block = 2 * width // (2 * depth)
    vmem, hbm = pl.BlockSpec(memory_space=pltpu.VMEM), pl.BlockSpec(memory_space=pl.ANY)
    b = lambda *shape: jax.ShapeDtypeStruct(shape, BF16)
    v = lambda *shape: pltpu.VMEM(shape, BF16)
    return pl.pallas_call(
        functools.partial(start_kernel, window),
        in_specs=[pl.BlockSpec(memory_space=pltpu.SMEM)] + [vmem] * 10 + [hbm],
        out_specs=[vmem, hbm, vmem, vmem, hbm, hbm, vmem, hbm],
        out_shape=[
            jax.ShapeDtypeStruct((rows, width), F32),
            b(4, rows, width),
            b(width, heads * 3 * LANES),
            b(heads, 4 * rows, 3 * LANES),
            b(depth, block, rows),
            b(depth, block, rows),
            b(rows, width),
            b(2, rows, width),
        ],
        scratch_shapes=[
            v(SLOTS, width), v(rows, width), v(rows, width), v(4, rows, width),
            v(depth, 2, block, rows), v(width, 3 * width),
            pltpu.SemaphoreType.DMA((32,)), pltpu.SemaphoreType.DMA((32,)), pltpu.SemaphoreType.DMA((16,)),
        ],
        compiler_params=pltpu.CompilerParams(
            vmem_limit_bytes=VMEM_LIMIT, collective_id=1, has_side_effects=True
        ),
        cost_estimate=cost(12 * rows * width * width, 12 * width * width),
        name="start_stage",
    )(length, x, x_cond, s, s_cond, cot, cot_cond, w, bias, gain, shift, qkv_w)


def attend_send_kernel(
    qkv_ref, cot_z, lse_ref, ctx_hbm, cot_zz, vt_ref, ot_ref, go_ref,
    send_sems, recv_sems, local_sems,
):
    head = pl.program_id(0)
    heads = HEADS // 4
    total = qkv_ref.shape[1]
    rows = total // 4
    place, index = lax.axis_index("seq"), lax.axis_index("batch")
    depth = lax.axis_size("batch") // 2
    chip = index // 2
    to, _, up_to, down_to = ends_of(place, index, depth)
    half = heads // 2 * HEAD_DIM
    wires, moves = Wires(send_sems, recv_sems), Locals(local_sems)
    go = [
        [
            wires.copy(
                go_ref.at[k, pl.ds(i * half, half)], ctx_hbm.at[k, pl.ds(i * half, half)], to[k]
            )
            for k in (3, 1, 2)
        ]
        for i in range(2)
    ]
    keep = moves.copy(go_ref.at[0], ctx_hbm.at[0])
    hop = Hop(
        wires, depth, chip, up_to, down_to, 1, cot_z.at[0], cot_z.at[1], cot_zz.at[0], cot_zz.at[1]
    )

    @pl.when(head == 0)
    def _():
        greet([to[1], to[2], to[3]], chip, depth, up_to, down_to)
        hop.start()

    vt_ref[...] = turned(qkv_ref[0, :, 2 * LANES :])
    step = 3 * LANES
    for start in range(0, total, step):
        query = qkv_ref[0, pl.ds(start, step), :LANES]
        scores = dot_nt(qkv_ref[0, :, LANES : 2 * LANES], query)
        peak = jnp.max(scores, axis=0, keepdims=True)
        shifted = jnp.exp2((scores - peak) * SCALE2)
        sums = jnp.sum(shifted, axis=0, keepdims=True)
        mixed = dot(vt_ref[...], shifted.astype(BF16)) / sums
        ot_ref[pl.ds(pl.multiple_of(head * HEAD_DIM, 8), HEAD_DIM), pl.ds(start, step)] = mixed[
            :HEAD_DIM
        ]
        lse_ref[0, :, pl.ds(start, step)] = peak * SCALE2 + jnp.log2(sums)

    for i in range(2):

        @pl.when(head == (i + 1) * heads // 2 - 1)
        def _():
            for part in (3, 1, 2, 0):
                go_ref[part, pl.ds(i * half, half)] = ot_ref[
                    pl.ds(i * half, half), pl.ds(part * rows, rows)
                ].astype(BF16)
            for wire in go[i]:
                wire.start()

    @pl.when(head == heads - 1)
    def _():
        keep.start()
        for i in range(2):
            for wire in go[i]:
                wire.arrive()
        keep.wait()
        hop.arrive()
        wires.drain()


def attend_send(qkv, cot_z):
    heads, total, _ = qkv.shape
    rows, width = cot_z.shape[1:]
    own = heads * HEAD_DIM
    hbm = pl.BlockSpec(memory_space=pl.ANY)
    return pl.pallas_call(
        attend_send_kernel,
        grid=(heads,),
        in_specs=[pl.BlockSpec((1, total, 3 * LANES), lambda h: (h, 0, 0)), hbm],
        out_specs=[pl.BlockSpec((1, 1, total), lambda h: (h, 0, 0)), hbm, hbm],
        out_shape=[
            jax.ShapeDtypeStruct((heads, 1, total), F32),
            jax.ShapeDtypeStruct((4, own, rows), BF16),
            jax.ShapeDtypeStruct((2, rows, width), BF16),
        ],
        scratch_shapes=[
            pltpu.VMEM((LANES, total), BF16),
            pltpu.VMEM((own, total), F32),
            pltpu.VMEM((4, own, rows), BF16),
            pltpu.SemaphoreType.DMA((16,)),
            pltpu.SemaphoreType.DMA((16,)),
            pltpu.SemaphoreType.DMA((2,)),
        ],
        compiler_params=pltpu.CompilerParams(
            vmem_limit_bytes=VMEM_LIMIT, collective_id=2, has_side_effects=True
        ),
        cost_estimate=cost(8 * heads * total * LANES * total, 6 * total * width),
        name="attend_send",
    )(qkv, cot_z)


def both(own_t, peer_t, own, peer):
    rows = own_t.shape[-1]
    cut = rows // 256 * 256
    total = dot(own_t[:, :cut], own[:cut]) + dot(peer_t[:, :cut], peer[:cut])
    ends_t = jnp.concatenate([own_t[:, cut:], peer_t[:, cut:]], 1)
    return total + dot(ends_t, jnp.concatenate([own[cut:], peer[cut:]], 0))


def middle_kernel(
    ctx_t_ref,
    hidden_ref,
    cot_ref,
    proj_ref,
    proj_bias_ref,
    gain_ref,
    shift_ref,
    fc2_bias_ref,
    fc1_bias_ref,
    cot_zz,
    fc1_hbm,
    fc2_hbm,
    out_hbm,
    c_all,
    d_middle_ref,
    late_hbm,
    d_ctx_hbm,
    vec_ref,
    fc1_vec_ref,
    normed_x,
    normed_cond_x,
    d_pre_go,
    active_go,
    active_cond_go,
    active_near,
    active_cond_near,
    cot_far,
    fc1_ref,
    fc2_ref,
    bias_ref,
    normed_ref,
    middle_ref,
    acc_out,
    acc_back,
    normed_t,
    ctx_two,
    ctx_peer,
    active_t,
    active_pack,
    d_pre,
    d_branch_ref,
    d_branch_peer,
    d_go,
    proj_stage,
    c_own,
    send_sems,
    recv_sems,
    local_sems,
):
    rows, width = cot_ref.shape
    slots = c_own.shape[0]
    images = rows - slots
    depth, _, small, _ = ctx_two.shape
    chunk = fc1_ref.shape[2]
    own = ctx_t_ref.shape[1]
    quarter = chunk // 8
    place, index = lax.axis_index("seq"), lax.axis_index("batch")
    chip, core = index // 2, index % 2
    to, other, up_to, down_to = ends_of(place, index, depth)
    moves = Locals(local_sems)

    def load(i):
        span = pl.ds(pl.multiple_of((chip + AWAY[i]) % depth * chunk, LANES), chunk)
        return (
            moves.start(fc1_hbm.at[:, span], fc1_ref.at[i % 2]),
            moves.start(fc2_hbm.at[span], fc2_ref.at[i % 2]),
        )

    loads = [load(0), load(1)]
    greet([to[1], to[2], to[3], other] + line_of(place, index, depth))
    wires = Wires(send_sems, recv_sems)
    hop = Hop(
        wires, depth, chip, up_to, down_to, 2, cot_zz.at[0], cot_zz.at[1], cot_far, cot_far
    )
    hop.start()
    for f in range(4):
        bias_ref[f : f + 1] = fc1_bias_ref[f * chunk : (f + 1) * chunk].reshape(1, -1)

    branch = proj_bias_ref[...].reshape(1, -1) + hidden_ref[...]
    for k in range(4):
        at = pl.ds(pl.multiple_of(flip(place, k) * own, 16), own)
        branch += dot(turned(ctx_t_ref[k]), proj_ref[at, :])
        for i in range(2):
            ctx_two[flip(place, k), i] = ctx_t_ref[k, i * small : (i + 1) * small]
    ctx_swap = wires.copy(ctx_two.at[:, 1 - core], ctx_peer, other)
    ctx_swap.start()
    middle_ref[...] = branch
    scaled, _ = normalize(branch)
    gain = gain_ref[...].reshape(1, -1)
    normed = scaled * gain + shift_ref[...].reshape(1, -1)
    normed_ref[...] = normed.astype(BF16)
    normed_t[...] = normed[:images].T.astype(BF16)
    normed_go = Spread(wires, to, normed_x, normed_t)
    normed_go.start()
    keeps = [
        moves.start(normed_t, normed_x.at[0]),
        moves.start(normed_ref.at[pl.ds(images, slots)], normed_cond_x.at[0]),
    ]
    cond_go = [
        wires.copy(normed_ref.at[pl.ds(images, slots)], normed_cond_x.at[k], to[k]) for k in (1, 2, 3)
    ]
    for wire in cond_go:
        wire.start()

    near = []
    for i in range(4):
        f = (chip + AWAY[i]) % depth
        for copy in loads[i]:
            copy.wait()
        fc1, fc2 = fc1_ref.at[i % 2], fc2_ref.at[i % 2]
        before = dot(normed_ref[...], fc1[...]) + bias_ref[pl.ds(f, 1)]
        cdf = 0.5 + 0.5 * lax.erf(before * math.sqrt(0.5))
        active = before * cdf
        slope = cdf + before * (jnp.exp(-0.5 * before * before) * (1.0 / math.sqrt(2.0 * math.pi)))
        d_before = dot_nt(cot_ref[...], fc2[...]) * slope
        fc1_vec_ref[pl.ds(f, 1)] = jnp.sum(d_before, axis=0, keepdims=True)
        d_pre[i] = d_before.astype(BF16)
        keeps.append(moves.start(d_pre.at[i], d_pre_go.at[f]))
        flat = active.T
        for c in range(2):
            for j in range(4):
                piece = flat[(c * 4 + j) * quarter : (c * 4 + j + 1) * quarter]
                active_t[i, c, j] = piece[:, :images].astype(BF16)
            active_pack[i, c] = jnp.concatenate(
                [flat[(c * 4 + j) * quarter : (c * 4 + j + 1) * quarter, images:] for j in range(4)], 1
            ).astype(BF16)
        if i < 2:
            for c in range(2):
                device = (f * 2 + c, place)
                near.append(
                    wires.by_core(core, active_t.at[i, c], active_near.at[i, core], device)
                )
                near.append(
                    wires.by_core(core, active_pack.at[i, c], active_cond_near.at[i, core], device)
                )
            for wire in near[4 * i :]:
                wire.start()
        else:
            keeps.append(moves.start(active_t.at[i], active_go.at[i - 2]))
            keeps.append(moves.start(active_pack.at[i], active_cond_go.at[i - 2]))
        forward = dot(active.astype(BF16), fc2[...])
        backward = dot_nt(d_pre[i], fc1[...])
        if i == 0:
            acc_out[...] = forward
            acc_back[...] = backward
        else:
            acc_out[...] += forward
            acc_back[...] += backward
        if i + 2 < 4:
            loads.append(load(i + 2))
        if i == 1:
            normed_go.relay()

    middle = middle_ref[...]
    scaled, factor = normalize(middle)
    upstream = acc_back[...]
    cot = cot_ref[...].astype(F32)
    d_middle = cot + norm_back(upstream, scaled, factor, gain)
    d_middle_ref[...] = d_middle
    d_branch_ref[...] = d_middle.astype(BF16)
    branch_swap = wires.copy(d_branch_ref, d_branch_peer, other)
    branch_swap.start()
    go = []
    for k in (3, 1, 2, 0):
        at = pl.ds(pl.multiple_of(flip(place, k) * own, 16), own)
        d_go[k] = dot_nt(d_branch_ref[...], proj_ref[at, :]).astype(BF16)
        if k:
            go.append(wires.copy(d_go.at[k], d_ctx_hbm.at[k], to[k]))
            go[-1].start()
    keeps.append(moves.start(d_go.at[0], d_ctx_hbm.at[0]))
    acc_out[...] = middle + acc_out[...] + fc2_bias_ref[...].reshape(1, -1)
    keeps.append(moves.start(acc_out.at[pl.ds(0, images)], out_hbm))
    c_own[...] = acc_out[images:].astype(BF16)
    c_go = [wires.copy(c_own, c_all.at[k], to[k]) for k in (3, 1, 2)]
    keeps.append(moves.start(c_own, c_all.at[0]))
    for wire in c_go:
        wire.start()
    vec_ref[0:1] = jnp.sum(upstream * scaled, axis=0, keepdims=True)
    vec_ref[1:2] = jnp.sum(upstream, axis=0, keepdims=True)
    vec_ref[2:3] = jnp.sum(d_middle, axis=0, keepdims=True)
    vec_ref[3:4] = jnp.sum(cot, axis=0, keepdims=True)
    vec_ref[4:] = jnp.zeros((4, width), F32)
    ctx_swap.arrive()
    branch_swap.arrive()
    proj_stage[...] = (
        both(
            ctx_two[:, core].reshape(depth * small, rows),
            ctx_peer[...].reshape(depth * small, rows),
            d_branch_ref[...],
            d_branch_peer[...],
        )
        .astype(BF16)
        .reshape(depth, small, width)
    )
    keeps.append(moves.start(proj_stage, late_hbm))
    for wire in c_go + cond_go + go:
        wire.arrive()
    hop.arrive()
    for i in range(2):
        arrive_by_core(near[4 * i : 4 * i + 4], core)
    normed_go.finish()
    for copy in keeps:
        copy.wait()
    wires.drain()


def middle_stage(
    depth, ctx_t, hidden, cot, proj, proj_bias, gain, shift, fc2_bias, fc1_bias, cot_zz, fc1, fc2
):
    rows, width = hidden.shape
    slots = SLOTS // 4
    images = rows - slots
    ff = fc1.shape[1]
    small = width // (2 * depth)
    own = ctx_t.shape[1]
    chunk = ff // 4
    quarter = chunk // 8
    vmem, hbm = pl.BlockSpec(memory_space=pltpu.VMEM), pl.BlockSpec(memory_space=pl.ANY)
    f = lambda *shape: jax.ShapeDtypeStruct(shape, F32)
    b = lambda *shape: jax.ShapeDtypeStruct(shape, BF16)
    v = lambda *shape: pltpu.VMEM(shape, BF16)
    vf = lambda *shape: pltpu.VMEM(shape, F32)
    return pl.pallas_call(
        middle_kernel,
        in_specs=[vmem] * 9 + [hbm] * 3,
        out_specs=[hbm, hbm, vmem, hbm, hbm, vmem, vmem] + [hbm] * 8,
        out_shape=[
            f(images, width),
            b(4, slots, width),
            f(rows, width),
            b(depth, small, width),
            b(4, rows, own),
            f(8, width),
            f(4, chunk),
            b(4, width, images),
            b(4, slots, width),
            b(4, rows, chunk),
            b(2, 2, 4, quarter, images),
            b(2, 2, quarter, 4 * slots),
            b(2, 2, 4, quarter, images),
            b(2, 2, quarter, 4 * slots),
            b(rows, width),
        ],
        scratch_shapes=[
            v(2, width, chunk), v(2, chunk, width), vf(4, chunk),
            v(rows, width), vf(rows, width), vf(rows, width), vf(rows, width),
            v(width, images),
            v(depth, 2, small, rows), v(depth, small, rows),
            v(4, 2, 4, quarter, images), v(4, 2, quarter, 4 * slots),
            v(4, rows, chunk),
            v(rows, width), v(rows, width),
            v(4, rows, own),
            v(depth, small, width),
            v(slots, width),
            pltpu.SemaphoreType.DMA((48,)), pltpu.SemaphoreType.DMA((48,)), pltpu.SemaphoreType.DMA((48,)),
        ],
        compiler_params=pltpu.CompilerParams(
            vmem_limit_bytes=VMEM_LIMIT, collective_id=3, has_side_effects=True
        ),
        cost_estimate=cost(8 * rows * width * ff, 8 * width * ff),
        name="middle_stage",
    )(ctx_t, hidden, cot, proj, proj_bias, gain, shift, fc2_bias, fc1_bias, cot_zz, fc1, fc2)


def attend_back_send_kernel(
    d_ref, qkv_ref, lse_ref, w_ref,
    normed_x, normed_cond_x, d_pre_go, active_go, active_cond_go, cot_hbm, cot_z, cot_zz, cot_far,
    dt_ref, lead_ref, tail_ref,
    normed_peer, normed_cond_peer, d_pre_x, active_x, active_cond_x, cot_peer,
    dot_all, dt_all, d_all, dk_ref, dv_ref, send_sems, recv_sems, local_sems,
):
    head = pl.program_id(0)
    depth = lax.axis_size("batch") // 2
    place, index = lax.axis_index("seq"), lax.axis_index("batch")
    chip, core = index // 2, index % 2
    to, other, _, _ = ends_of(place, index, depth)
    wires, moves = Wires(send_sems, recv_sems), Locals(local_sems)
    links = [wires.copy(d_pre_go.at[flip(place, k)], d_pre_x.at[k], to[k]) for k in (3, 1, 2)]
    far = []
    for c in range(2):
        device = ((chip + AWAY[2]) % depth * 2 + c, place)
        far.append(wires.by_core(core, active_go.at[0, c], active_x.at[0, core], device))
        far.append(wires.by_core(core, active_cond_go.at[0, c], active_cond_x.at[0, core], device))
    links += [
        wires.copy(active_go.at[1, 1 - core], active_x.at[1, core], other),
        wires.copy(active_cond_go.at[1, 1 - core], active_cond_x.at[1, core], other),
        wires.copy(normed_x.at[:, :, 1 - core], normed_peer, other),
        wires.copy(normed_cond_x, normed_cond_peer, other),
        wires.copy(cot_hbm, cot_peer.at[0], other),
        wires.copy(cot_z, cot_peer.at[pl.ds(1, 2)], other),
        wires.copy(cot_zz, cot_peer.at[pl.ds(3, 2)], other),
        wires.copy(cot_far, cot_peer.at[5], other),
    ]
    keeps = [
        moves.copy(d_pre_go.at[place], d_pre_x.at[0]),
        moves.copy(active_go.at[1, core], active_x.at[1, core]),
        moves.copy(active_cond_go.at[1, core], active_cond_x.at[1, core]),
    ]

    @pl.when(head == 0)
    def _():
        greet([to[1], to[2], to[3], other] + line_of(place, index, depth))
        for wire in links + far:
            wire.start()
        for copy in keeps:
            copy.start()

    total = qkv_ref.shape[1]
    rows = total // 4
    half = rows // 2
    own = dot_all.shape[0]

    @pl.when(head == 0)
    def _():
        for part in range(4):
            dot_all[:, pl.ds(part * rows, rows)] = d_ref[part].astype(F32).T

    base = pl.multiple_of(head * HEAD_DIM, 8)
    upstream_t = jnp.concatenate(
        [dot_all[pl.ds(base, HEAD_DIM), :], jnp.zeros((LANES - HEAD_DIM, total), F32)], 0
    )
    upstream = upstream_t.T.astype(BF16)
    upstream_t = upstream_t.astype(BF16)
    key = qkv_ref[0, :, LANES : 2 * LANES]
    key_t = turned(key)
    value = qkv_ref[0, :, 2 * LANES :]
    lane = pl.multiple_of(head * 3 * LANES, LANES)
    step = 3 * LANES
    for start in range(0, total, step):
        query = qkv_ref[0, pl.ds(start, step), :LANES]
        probs = jnp.exp2(dot_nt(key, query) * SCALE2 - lse_ref[0, :, pl.ds(start, step)])
        d_probs = dot(value, upstream_t[:, start : start + step])
        delta = jnp.sum(probs * d_probs, axis=0, keepdims=True)
        d_raw = (probs * (d_probs - delta)).astype(BF16)
        d_value = dot(probs.astype(BF16), upstream[start : start + step])
        d_key = dot(d_raw, query)
        if start == 0:
            dv_ref[...] = d_value
            dk_ref[...] = d_key
        else:
            dv_ref[...] += d_value
            dk_ref[...] += d_key
        d_query = dot(key_t, d_raw) * SCALE
        dt_all[pl.ds(base, HEAD_DIM), pl.ds(start, step)] = d_query[:HEAD_DIM]
        d_all[pl.ds(start, step), pl.ds(lane, LANES)] = d_query.T.astype(BF16)
    d_key = dk_ref[...] * SCALE
    d_value = dv_ref[...]
    dt_all[pl.ds(pl.multiple_of(own + base, 8), HEAD_DIM)] = d_key.T[:HEAD_DIM]
    dt_all[pl.ds(pl.multiple_of(2 * own + base, 8), HEAD_DIM)] = d_value.T[:HEAD_DIM]
    d_all[:, pl.ds(pl.multiple_of(lane + LANES, LANES), LANES)] = d_key.astype(BF16)
    d_all[:, pl.ds(pl.multiple_of(lane + 2 * LANES, LANES), LANES)] = d_value.astype(BF16)

    @pl.when(head == pl.num_programs(0) - 1)
    def _():
        for part in (3, 1, 2, 0):
            update = dot_nt(d_all[pl.ds(part * rows, rows)], w_ref[...])
            lead_ref[part] = update[:half].astype(BF16)
            tail_ref[part] = update[half:].astype(BF16)
        dt_ref[...] = dt_all[...].astype(BF16)

    @pl.when(head == pl.num_programs(0) - 1)
    def _():
        for wire in links:
            wire.arrive()
        arrive_by_core(far, core)
        for copy in keeps:
            copy.wait()
        wires.drain()


def attend_back_send(
    d_context, qkv, lse, w_heads, normed_x, normed_cond_x, d_pre_go, active_go, active_cond_go,
    cot, cot_z, cot_zz, cot_far,
):
    heads, total, _ = qkv.shape
    width = w_heads.shape[0]
    rows = total // 4
    own = heads * HEAD_DIM
    whole = lambda *shape: pl.BlockSpec(shape, lambda h: (0,) * len(shape))
    hbm = pl.BlockSpec(memory_space=pl.ANY)
    b = lambda *shape: jax.ShapeDtypeStruct(shape, BF16)
    v = lambda *shape: pltpu.VMEM(shape, BF16)
    shape = normed_x.shape
    return pl.pallas_call(
        attend_back_send_kernel,
        grid=(heads,),
        in_specs=[
            whole(4, rows, own),
            pl.BlockSpec((1, total, 3 * LANES), lambda h: (h, 0, 0)),
            pl.BlockSpec((1, 1, total), lambda h: (h, 0, 0)),
            whole(*w_heads.shape),
        ]
        + [hbm] * 9,
        out_specs=[
            whole(3 * own, total),
            whole(4, rows // 2, width),
            whole(4, rows // 2, width),
        ]
        + [hbm] * 6,
        out_shape=[
            b(3 * own, total),
            b(4, rows // 2, width),
            b(4, rows // 2, width),
            b(shape[0], shape[1], *shape[3:]),
            b(*normed_cond_x.shape),
            b(*d_pre_go.shape),
            b(*active_go.shape),
            b(*active_cond_go.shape),
            b(6, *cot.shape),
        ],
        scratch_shapes=[
            pltpu.VMEM((own, total), F32),
            pltpu.VMEM((3 * own, total), F32),
            pltpu.VMEM((total, heads * 3 * LANES), BF16),
            pltpu.VMEM((total, LANES), F32),
            pltpu.VMEM((total, LANES), F32),
            pltpu.SemaphoreType.DMA((48,)),
            pltpu.SemaphoreType.DMA((48,)),
            pltpu.SemaphoreType.DMA((8,)),
        ],
        compiler_params=pltpu.CompilerParams(
            vmem_limit_bytes=VMEM_LIMIT, collective_id=4, has_side_effects=True
        ),
        cost_estimate=cost(
            2 * heads * total * (width * 3 * LANES + 10 * LANES * total), 12 * total * width
        ),
        name="attend_back_send",
    )(
        d_context, qkv, lse, w_heads, normed_x, normed_cond_x, d_pre_go, active_go, active_cond_go,
        cot, cot_z, cot_zz, cot_far,
    )


def finish_kernel(
    p_hbm, f_hbm, g_hbm, q_hbm, s_hbm, c_hbm, out_c_hbm, vec_ref, out_hbm, din_hbm, dskip_hbm,
    g_fc2_hbm, g_proj_hbm, g_first_hbm, g_heads_hbm, g_skip_hbm,
    o_out, o_din, o_dskip, o_out_cond, o_din_cond, o_dskip_cond,
    v0, v1, v2, v3, v4, v5, v6, fc1_vec_ref,
    p_in, f_in, g_in, q_in, s_in, c_in, out_c_in, p_st, f_st, g_st, q_st, s_st, cond_st, rows_st, sems,
):
    width = out_hbm.shape[1]
    place, index = lax.axis_index("seq"), lax.axis_index("batch")
    batch = lax.axis_size("batch")
    moves = Locals(sems)
    loads = [
        moves.start(src, dst)
        for src, dst in (
            (f_hbm, f_in), (g_hbm, g_in), (q_hbm, q_in), (s_hbm, s_in), (p_hbm, p_in), (c_hbm, c_in),
            (out_c_hbm, out_c_in),
        )
    ]
    rows_in = [
        moves.start(src, rows_st.at[i]) for i, src in enumerate((out_hbm, din_hbm, dskip_hbm))
    ]
    done = []
    for i, dst in enumerate((o_out, o_din, o_dskip)):
        rows_in[i].wait()
        done.append(moves.start(rows_st.at[i], dst.at[:, 0]))
    loads[0].wait()
    for j in range(4):
        f_st[:, j * width : (j + 1) * width] = f_in[flip(place, j)].astype(F32)
    done.append(moves.start(f_st, g_first_hbm))
    loads[1].wait()
    small = g_in.shape[1]
    for j in range(4):
        g_st[j * small : (j + 1) * small] = g_in[flip(place, j)].astype(F32)
    done.append(moves.start(g_st, g_fc2_hbm))
    loads[2].wait()
    size = q_in.shape[2] // 3
    for j in range(4):
        value = q_in[flip(place, j)].astype(F32)
        for which in range(3):
            at = (which * 4 + j) * size
            q_st[:, at : at + size] = value[:, which * size : (which + 1) * size]
    done.append(moves.start(q_st, g_heads_hbm))
    loads[3].wait()
    size = s_st.shape[0] // 4
    for j in range(4):
        s_st[j * size : (j + 1) * size] = s_in[flip(place, j), :size].astype(F32)
    done.append(moves.start(s_st, g_skip_hbm))
    for copy in loads[4:]:
        copy.wait()
    p_st[...] = p_in[...].astype(F32)
    done.append(moves.start(p_st, g_proj_hbm))
    slots = c_in.shape[1]
    for j in range(4):
        span = slice(j * slots, (j + 1) * slots)
        piece = c_in[flip(place, j)].astype(F32)
        cond_st[0, span] = out_c_in[flip(place, j)].astype(F32)
        cond_st[1, span] = piece[:, :width]
        cond_st[2, span] = piece[:, width:]
    conds = o_out_cond.shape[0]
    for i, ref in enumerate((o_out_cond, o_din_cond, o_dskip_cond)):
        ref[:, 0] = cond_st[i, :conds]
    share = width // batch
    vectors = vec_ref[...]
    rolled = pltpu.roll(vectors, lax.rem(width - index * share, width), 1)
    for row, ref in zip((0, 1, 2, 5, 3, 4, 6), (v0, v1, v2, v3, v4, v5, v6)):
        ref[...] = rolled[row, :share]
    share = 4 * width // batch
    per = width // share
    vector = vec_ref[pl.ds(8 + index // per, 1)]
    vector = pltpu.roll(vector, lax.rem(width - index % per * share, width), 1)
    fc1_vec_ref[...] = vector[0, :share]
    for copy in done:
        copy.wait()


def finish_stage(batch, conds, slots_of, out_c, vec, out, d_image, d_skip):
    p_all, f_all, g_all, q_all, s_all, c_all = slots_of
    images, width = out.shape
    small = f_all.shape[1]
    skip_rows = 2 * width // batch
    large = 4 * width // batch
    slots = c_all.shape[1]
    vmem, hbm = pl.BlockSpec(memory_space=pltpu.VMEM), pl.BlockSpec(memory_space=pl.ANY)
    f = lambda *shape: jax.ShapeDtypeStruct(shape, F32)
    like = lambda a: pltpu.VMEM(a.shape, a.dtype)
    vf = lambda *shape: pltpu.VMEM(shape, F32)
    return pl.pallas_call(
        finish_kernel,
        in_specs=[hbm] * 7 + [vmem] + [hbm] * 3,
        out_specs=[hbm] * 8 + [vmem] * 11,
        out_shape=[
            f(large, width), f(small, width), f(small, 4 * width), f(small, 4 * q_all.shape[2]),
            f(skip_rows, width), f(images, 1, width), f(images, 1, width), f(images, 1, width),
            f(conds, 1, width), f(conds, 1, width), f(conds, 1, width),
        ]
        + [f(width // batch)] * 7
        + [f(large)],
        scratch_shapes=[
            like(p_all), like(f_all), like(g_all), like(q_all), like(s_all), like(c_all), like(out_c),
            vf(small, width), vf(small, 4 * width), vf(large, width), vf(small, 4 * q_all.shape[2]),
            vf(skip_rows, width), vf(3, 4 * slots, width), vf(3, images, width),
            pltpu.SemaphoreType.DMA((24,)),
        ],
        compiler_params=params(),
        cost_estimate=cost(1e6, 2e7),
        name="finish_stage",
    )(*slots_of, out_c, vec, out, d_image, d_skip)


def per_device(
    batch,
    parts,
    image_in,
    cond_in,
    skip_image,
    skip_cond,
    caption_len,
    skip_weight,
    skip_bias,
    first_gain,
    first_bias,
    qkv_weight,
    proj_weight,
    proj_bias,
    second_gain,
    second_bias,
    fc1_weight,
    fc1_bias,
    fc2_weight,
    fc2_bias,
    grad_image,
    grad_cond,
):
    conds = cond_in.shape[0]
    width = image_in.shape[2]
    images = image_in.shape[0]
    ff = fc1_weight.shape[1]
    slots = SLOTS // parts
    rows = slots + images
    total = rows * parts
    heads = HEADS // parts
    depth = batch // 2
    place = lax.axis_index("seq")
    index = lax.axis_index("batch")
    core, chip = index % 2, index // 2
    where = jnp.stack([core, place]).astype(jnp.int32)

    fast = parts == 4 and depth == 4 and (ff // parts) % LANES == 0
    if fast:
        hidden, normed_all, w_heads, qkv, joined, joined_peer, cot, cot_z = start_stage(
            depth, caption_len, image_in[:, 0], cond_in[:, 0], skip_image[:, 0], skip_cond[:, 0],
            grad_image[:, 0], grad_cond[:, 0], skip_weight, skip_bias, first_gain, first_bias,
            qkv_weight,
        )
        normed_all = normed_all.reshape(total, width)
        lse, ctx_t, cot_zz = attend_send(qkv, cot_z)
        (
            out, out_c, d_middle, late, d_ctx, vec_two, fc1_vec, normed_x, normed_cond_x, d_pre_go,
            active_go, active_cond_go, active_near, active_cond_near, cot_far,
        ) = middle_stage(
            depth, ctx_t, hidden, cot, proj_weight, proj_bias, second_gain, second_bias, fc2_bias,
            fc1_bias, cot_zz, fc1_weight, fc2_weight,
        )
        normed_x = normed_x.reshape(4, depth, 2, width // batch, images)
        (
            d_triple_t, lead, tail, normed_peer, normed_cond_peer, d_pre_x, active_x, active_cond_x,
            cot_peer,
        ) = attend_back_send(
            d_ctx, qkv, lse, w_heads, normed_x, normed_cond_x, d_pre_go, active_go, active_cond_go,
            cot, cot_z, cot_zz, cot_far,
        )
        feeds = (
            normed_x, normed_peer, normed_cond_x, normed_cond_peer, d_pre_x, active_near, active_x,
            active_cond_near, active_cond_x, cot, cot_z, cot_zz, cot_far, cot_peer,
        )
        *slots_of, d_image, d_skip, vec = reduce_all(
            late, lead, tail, normed_all, d_triple_t, joined, joined_peer, hidden, d_middle,
            skip_weight, feeds, first_gain, vec_two, fc1_vec,
        )
        (
            wgrad_fc2, wgrad_proj, wgrad_fc1, wgrad_qkv, wgrad_skip, out_image, d_image, d_skip,
            out_cond, d_cond, d_skip_cond, *vec,
        ) = finish_stage(batch, conds, slots_of, out_c, vec, out, d_image, d_skip)
        return (
            out_image, out_cond, d_image, d_cond, d_skip, d_skip_cond, wgrad_skip, vec[0],
            vec[1], vec[2], wgrad_qkv, wgrad_proj, vec[3], vec[4], vec[5], wgrad_fc1, vec[7],
            wgrad_fc2, vec[6],
        )

    def own_rows(cond, image):
        padded = jnp.pad(cond[:, 0], ((0, SLOTS - conds), (0, 0)))
        lead = lax.dynamic_slice_in_dim(padded, place * slots, slots, 0)
        return jnp.concatenate([lead, image[:, 0]], 0)

    x = own_rows(cond_in, image_in)
    s = own_rows(skip_cond, skip_image)
    cot = own_rows(grad_cond, grad_image)

    hidden, normed, joined_t = pre(
        x, s, skip_weight, skip_bias[None], first_gain[None], first_bias[None]
    )
    normed_all = jnp.concatenate(everywhere(normed, parts), 0)
    own = heads * HEAD_DIM
    w_heads = heads_weight(where[1:], qkv_weight, heads)
    order = place ^ jnp.arange(parts, dtype=jnp.int32)
    position = order[:, None] * slots + jnp.arange(rows, dtype=jnp.int32)[None]
    valid = (jnp.arange(rows)[None] >= slots) | (position <= caption_len[0])
    kbias = jnp.where(
        (jnp.arange(LANES) == HEAD_DIM)[None] & ~valid.reshape(total, 1), F32(-1e30), F32(0)
    )
    qkv, lse, *ctx_parts = attend(parts, normed_all, w_heads, kbias)
    context = [ctx_parts[0]] + [across(ctx_parts[k], parts, k) for k in range(1, parts)]

    zero = jnp.zeros_like(proj_bias)
    vecs = jnp.stack([proj_bias, second_gain, second_bias, fc2_bias, zero, zero, zero, zero])
    (
        out,
        d_middle,
        d_branch,
        active_t,
        d_pre,
        normed2_t,
        ctx_t,
        vec_two,
        fc1_bias_grad,
        *d_ctx_parts,
    ) = mlp(
        parts,
        where[1:],
        context,
        hidden,
        cot,
        proj_weight,
        vecs,
        fc1_weight,
        fc1_bias[None],
        fc2_weight,
    )
    d_context = [d_ctx_parts[0]] + [across(d_ctx_parts[k], parts, k) for k in range(1, parts)]

    def by_core(turned_rows):
        blocks = turned_rows.reshape(depth, 2, -1, rows)
        send = lax.dynamic_index_in_dim(blocks, 1 - core, 1, keepdims=False)
        return blocks, other_core(send, batch)

    active_b, active_p = by_core(active_t)
    normed2_b, normed2_p = by_core(normed2_t)
    ctx_b, ctx_p = by_core(ctx_t)
    joined_b, joined_p = by_core(joined_t)
    cot_p, d_pre_p, d_branch_p = (other_core(v, batch) for v in (cot, d_pre, d_branch))
    late = pair_grads(
        where, [(active_b, active_p, cot, cot_p), (ctx_b, ctx_p, d_branch, d_branch_p)]
    )
    by_columns = (ff // parts) % LANES == 0
    if by_columns:
        first = column_grads(where, parts, normed2_b, normed2_p, d_pre, d_pre_p)
        late, first, d_context = lax.optimization_barrier((late, first, d_context))
        middle = depth // 2
    if by_columns:
        first = jnp.concatenate(
            [
                scattered(first[:, :middle], parts, bits_of(parts)),
                scattered(first[:, middle:], parts, bits_of(parts)[::-1]),
            ],
            0,
        )
    if not by_columns:
        first = pair_grads(where, [(normed2_b, normed2_p, d_pre, d_pre_p)])
    def all_conds(lead):
        pieces = [lead] + [across(lead, parts, k) for k in range(1, parts)]
        full = jnp.zeros((SLOTS, lead.shape[1]), F32)
        for k in range(parts):
            full = lax.dynamic_update_slice_in_dim(
                full, pieces[k].astype(F32), (place ^ k) * slots, 0
            )
        return full[:conds, None]

    d_triple_t, d_lead, d_tail = attend_back(parts, d_context, qkv, lse, w_heads)
    d_lead = scattered(d_lead, parts, bits_of(parts))
    d_tail = scattered(d_tail, parts, bits_of(parts)[::-1])
    heads_grad = heads_grads(normed_all, d_triple_t).reshape(depth, 2, -1, 3 * own)
    heads_grad = plus(
        lax.dynamic_index_in_dim(heads_grad, core, 1, keepdims=False),
        other_core(lax.dynamic_index_in_dim(heads_grad, 1 - core, 1, keepdims=False), batch),
    )
    heads_grad = everywhere(down_the_line(heads_grad, batch, chip), parts)
    wgrad_qkv = put_heads(where[1:], heads_grad)

    d_in, d_skip, d_low, vec_one = post(
        d_lead, d_tail, hidden, d_middle, first_gain[None], skip_weight
    )
    d_low_p = other_core(d_low, batch)
    last = pair_grads(where, [(joined_b, joined_p, d_low, d_low_p)])

    late = down_the_line(late, batch, chip)
    first = down_the_line(first, batch, chip)
    late = summed(late, parts)
    if by_columns:
        fc1_cols = everywhere(first, parts)
        wgrad_fc1 = put_columns(where[1:], fc1_cols)
    else:
        wgrad_fc1 = summed(first, parts).astype(F32)

    vectors = [
        vec_one[0],
        vec_one[1],
        vec_one[2],
        vec_two[2],
        vec_two[0],
        vec_two[1],
        fc1_bias_grad[0],
        vec_two[3],
    ]
    sizes = [v.shape[0] // batch for v in vectors]
    packed = jnp.concatenate([v.reshape(batch, -1) for v in vectors], 1)
    packed = packed.reshape(depth, 2, -1)
    packed = lax.dynamic_index_in_dim(packed, core, 1, keepdims=False) + other_core(
        lax.dynamic_index_in_dim(packed, 1 - core, 1, keepdims=False), batch
    )
    packed = jnp.pad(packed, ((0, 0), (0, 16 * width - packed.shape[1]))).reshape(depth, 16, width)
    last = jnp.concatenate([last, packed.astype(BF16)], 1)
    last = summed(down_the_line(last, batch, chip), parts)
    skip_rows = 2 * width // batch
    wgrad_skip = last[:skip_rows].astype(F32)
    flat = last[skip_rows:].reshape(-1).astype(F32)
    vector_out, at = [], 0
    for size in sizes:
        vector_out.append(flat[at : at + size])
        at += size
    fc2_rows = ff // batch
    wgrad_fc2 = late[:fc2_rows].astype(F32)
    wgrad_proj = late[fc2_rows:].astype(F32)

    out_cond = all_conds(out[:slots].astype(BF16))
    d_cond = all_conds(jnp.concatenate([d_in[:slots], d_skip[:slots]], 1).astype(BF16))
    return (
        out[slots:, None],
        out_cond,
        d_in[slots:, None],
        d_cond[:, :, :width],
        d_skip[slots:, None],
        d_cond[:, :, width:],
        wgrad_skip,
        vector_out[0],
        vector_out[1],
        vector_out[2],
        wgrad_qkv,
        wgrad_proj,
        vector_out[3],
        vector_out[4],
        vector_out[5],
        wgrad_fc1,
        vector_out[6],
        wgrad_fc2,
        vector_out[7],
    )


def solution(mesh):
    tokens, conds, shared = P("seq", "batch", None), P(None, "batch", None), P()
    return jax.shard_map(
        functools.partial(per_device, mesh.shape["batch"], mesh.shape["seq"]),
        mesh=mesh,
        in_specs=(tokens, conds, tokens, conds, P("batch")) + (shared,) * 13 + (tokens, conds),
        out_specs=(tokens, conds) * 3
        + (
            P("batch", None),
            P("batch"),
            P("batch"),
            P("batch"),
            P("batch", None),
            P("batch", None),
            P("batch"),
            P("batch"),
            P("batch"),
            P("batch", None),
            P("batch"),
            P("batch", None),
            P("batch"),
        ),
        check_vma=False,
    )
```

```python
import functools
import math

import jax
import jax.numpy as jnp
from jax import lax
from jax.experimental import pallas as pl
from jax.experimental.pallas import tpu as pltpu
from jax.sharding import PartitionSpec as P

HEADS = 16
HEAD_DIM = 72
LANES = 128
SLOTS = 128
F32 = jnp.float32
BF16 = jnp.bfloat16
VMEM_LIMIT = 60 * 1024 * 1024
SCALE = 1.0 / math.sqrt(HEAD_DIM)
SCALE2 = SCALE * math.log2(math.e)


def dot(left, right):
    return jnp.dot(left, right, preferred_element_type=F32)


def dot_nt(left, right):
    return lax.dot_general(left, right, (((1,), (1,)), ((), ())), preferred_element_type=F32)


def dot_tn(left, right):
    return lax.dot_general(left, right, (((0,), (0,)), ((), ())), preferred_element_type=F32)


def params():
    return pltpu.CompilerParams(vmem_limit_bytes=VMEM_LIMIT)


def cost(flops, nbytes):
    return pl.CostEstimate(flops=int(flops), bytes_accessed=int(nbytes), transcendentals=0)


def turned(value):
    return value.astype(F32).T.astype(BF16)


def normalize(values):
    centre = values - jnp.mean(values, axis=-1, keepdims=True)
    factor = lax.rsqrt(jnp.mean(centre * centre, axis=-1, keepdims=True) + 1e-5)
    return centre * factor, factor


def norm_back(upstream, scaled, factor, gain):
    inner = upstream * gain
    centred = inner - jnp.mean(inner, axis=-1, keepdims=True)
    return factor * (centred - scaled * jnp.mean(inner * scaled, axis=-1, keepdims=True))


def pre_kernel(x_ref, s_ref, w_ref, bias_ref, gain_ref, shift_ref, hidden_ref, normed_ref, turn_ref):
    width = x_ref.shape[1]
    hidden = dot(x_ref[...], w_ref[:width]) + dot(s_ref[...], w_ref[width:]) + bias_ref[...]
    hidden_ref[...] = hidden
    scaled, _ = normalize(hidden)
    normed_ref[...] = (scaled * gain_ref[...] + shift_ref[...]).astype(BF16)
    turn_ref[:width] = turned(x_ref[...])
    turn_ref[width:] = turned(s_ref[...])


def pre(x, s, w, bias, gain, shift):
    rows, width = x.shape
    return pl.pallas_call(
        pre_kernel,
        out_shape=(
            jax.ShapeDtypeStruct((rows, width), F32),
            jax.ShapeDtypeStruct((rows, width), BF16),
            jax.ShapeDtypeStruct((2 * width, rows), BF16),
        ),
        compiler_params=params(),
        cost_estimate=cost(4 * rows * width * width, 4 * width * width + 12 * rows * width),
        name="input_linear",
    )(x, s, w, bias, gain, shift)


def heads_weight_kernel(window, place_ref, w_ref, out_ref):
    heads = out_ref.shape[0]
    width = w_ref.shape[0]
    own = heads * HEAD_DIM
    keep = lax.broadcasted_iota(jnp.int32, (width, LANES), 1) < HEAD_DIM
    place = place_ref[0]
    for which in range(3):
        first = place * own + which * width
        start = jnp.minimum(first // LANES * LANES, 3 * width - window)
        value = w_ref[:, pl.ds(pl.multiple_of(start, LANES), window)].astype(F32)
        value = pltpu.roll(value, lax.rem(window - (first - start), window), 1)
        for head in range(heads):
            turned_back = value if head == 0 else pltpu.roll(value, window - head * HEAD_DIM, 1)
            out_ref[head, :, which * LANES : (which + 1) * LANES] = jnp.where(
                keep, turned_back[:, :LANES], 0.0
            ).astype(BF16)


def heads_weight(place, w, heads):
    width = w.shape[0]
    own = heads * HEAD_DIM
    offsets = [p * own % LANES for p in range(HEADS // heads)]
    window = (max(offsets) + own + LANES - 1) // LANES * LANES
    return pl.pallas_call(
        functools.partial(heads_weight_kernel, window),
        in_specs=[
            pl.BlockSpec(memory_space=pltpu.SMEM),
            pl.BlockSpec(memory_space=pltpu.VMEM),
        ],
        out_shape=jax.ShapeDtypeStruct((heads, width, 3 * LANES), BF16),
        compiler_params=params(),
        cost_estimate=cost(1e6, 2 * w.size + 6 * heads * width * LANES),
        name="heads_weight",
    )(place, w)


def attend_kernel(parts, normed_ref, w_ref, kbias_ref, qkv_ref, lse_ref, *rest):
    ctx_refs, (vt_ref, ot_ref) = rest[:parts], rest[parts:]
    head = pl.program_id(0)
    total = normed_ref.shape[0]
    rows = total // parts
    lane = lax.broadcasted_iota(jnp.int32, (1, LANES), 1)
    one = jnp.where(lane == HEAD_DIM, 1.0, 0.0)
    for part in range(parts):
        span = pl.ds(part * rows, rows)
        triple = dot(normed_ref[span], w_ref[0])
        qkv_ref[0, span, :LANES] = (triple[:, :LANES] + one).astype(BF16)
        qkv_ref[0, span, LANES : 2 * LANES] = (
            triple[:, LANES : 2 * LANES] + kbias_ref[span]
        ).astype(BF16)
        qkv_ref[0, span, 2 * LANES :] = triple[:, 2 * LANES :].astype(BF16)
        vt_ref[:, span] = turned(qkv_ref[0, span, 2 * LANES :])
    step = 3 * LANES if total % (3 * LANES) == 0 else LANES
    for start in range(0, total, step):
        query = qkv_ref[0, pl.ds(start, step), :LANES]
        scores = dot_nt(qkv_ref[0, :, LANES : 2 * LANES], query)
        peak = jnp.max(scores, axis=0, keepdims=True)
        shifted = jnp.exp2((scores - peak) * SCALE2)
        sums = jnp.sum(shifted, axis=0, keepdims=True)
        mixed = dot(vt_ref[...], shifted.astype(BF16)) / sums
        ot_ref[pl.ds(pl.multiple_of(head * HEAD_DIM, 8), HEAD_DIM), pl.ds(start, step)] = mixed[
            :HEAD_DIM
        ]
        lse_ref[0, :, pl.ds(start, step)] = peak * SCALE2 + jnp.log2(sums)

    @pl.when(head == pl.num_programs(0) - 1)
    def _():
        for part in range(parts):
            ctx_refs[part][...] = ot_ref[:, pl.ds(part * rows, rows)].T.astype(BF16)


def attend(parts, normed_all, w_heads, kbias):
    total, width = normed_all.shape
    heads = w_heads.shape[0]
    rows = total // parts
    own = heads * HEAD_DIM
    return pl.pallas_call(
        functools.partial(attend_kernel, parts),
        grid=(heads,),
        in_specs=[
            pl.BlockSpec((total, width), lambda h: (0, 0)),
            pl.BlockSpec((1, width, 3 * LANES), lambda h: (h, 0, 0)),
            pl.BlockSpec((total, LANES), lambda h: (0, 0)),
        ],
        out_specs=[
            pl.BlockSpec((1, total, 3 * LANES), lambda h: (h, 0, 0)),
            pl.BlockSpec((1, 1, total), lambda h: (h, 0, 0)),
        ]
        + [pl.BlockSpec((rows, own), lambda h: (0, 0))] * parts,
        out_shape=[
            jax.ShapeDtypeStruct((heads, total, 3 * LANES), BF16),
            jax.ShapeDtypeStruct((heads, 1, total), F32),
        ]
        + [jax.ShapeDtypeStruct((rows, own), BF16)] * parts,
        scratch_shapes=[pltpu.VMEM((LANES, total), BF16), pltpu.VMEM((own, total), F32)],
        compiler_params=params(),
        cost_estimate=cost(
            2 * heads * total * (width * 3 * LANES + 4 * LANES * total), 6 * total * width
        ),
        name="attend",
    )(normed_all, w_heads, kbias)


def attend_back_kernel(parts, *refs):
    d_refs = refs[:parts]
    (qkv_ref, lse_ref, w_ref, dt_ref, lead_ref, tail_ref) = refs[parts : parts + 6]
    (dot_all, dt_all, acc, dq_ref, dk_ref, dv_ref) = refs[parts + 6 :]
    head = pl.program_id(0)
    heads = pl.num_programs(0)
    total = qkv_ref.shape[1]
    rows = total // parts
    half = rows // 2
    own = dot_all.shape[0]

    @pl.when(head == 0)
    def _():
        for part in range(parts):
            dot_all[:, pl.ds(part * rows, rows)] = d_refs[part][...].astype(F32).T

    base = pl.multiple_of(head * HEAD_DIM, 8)
    upstream_t = jnp.concatenate(
        [dot_all[pl.ds(base, HEAD_DIM), :], jnp.zeros((LANES - HEAD_DIM, total), F32)], 0
    )
    upstream = upstream_t.T.astype(BF16)
    upstream_t = upstream_t.astype(BF16)
    key = qkv_ref[0, :, LANES : 2 * LANES]
    key_t = turned(key)
    value = qkv_ref[0, :, 2 * LANES :]
    step = 3 * LANES if total % (3 * LANES) == 0 else LANES
    for start in range(0, total, step):
        query = qkv_ref[0, pl.ds(start, step), :LANES]
        probs = jnp.exp2(dot_nt(key, query) * SCALE2 - lse_ref[0, :, pl.ds(start, step)])
        d_probs = dot(value, upstream_t[:, start : start + step])
        delta = jnp.sum(probs * d_probs, axis=0, keepdims=True)
        d_raw = (probs * (d_probs - delta) * SCALE).astype(BF16)
        d_value = dot(probs.astype(BF16), upstream[start : start + step])
        d_key = dot(d_raw, query)
        if start == 0:
            dv_ref[...] = d_value
            dk_ref[...] = d_key
        else:
            dv_ref[...] += d_value
            dk_ref[...] += d_key
        d_query = dot(key_t, d_raw)
        dt_all[pl.ds(base, HEAD_DIM), pl.ds(start, step)] = d_query[:HEAD_DIM]
        dq_ref[pl.ds(start, step)] = d_query.T
    dt_all[pl.ds(pl.multiple_of(own + base, 8), HEAD_DIM)] = dk_ref[...].T[:HEAD_DIM]
    dt_all[pl.ds(pl.multiple_of(2 * own + base, 8), HEAD_DIM)] = dv_ref[...].T[:HEAD_DIM]
    for part in range(parts):
        span = pl.ds(part * rows, rows)
        update = (
            dot_nt(dq_ref[span].astype(BF16), w_ref[0, :, :LANES])
            + dot_nt(dk_ref[span].astype(BF16), w_ref[0, :, LANES : 2 * LANES])
            + dot_nt(dv_ref[span].astype(BF16), w_ref[0, :, 2 * LANES :])
        )

        @pl.when(head == 0)
        def _():
            acc[span] = update

        @pl.when(head > 0)
        def _():
            acc[span] += update

    @pl.when(head == heads - 1)
    def _():
        dt_ref[...] = dt_all[...].astype(BF16)
        for part in range(parts):
            lead_ref[part] = acc[pl.ds(part * rows, half)].astype(BF16)
            tail_ref[part] = acc[pl.ds(part * rows + half, half)].astype(BF16)


def attend_back(parts, d_context, qkv, lse, w_heads):
    heads, total, _ = qkv.shape
    width = w_heads.shape[1]
    rows = total // parts
    own = heads * HEAD_DIM
    whole = lambda *shape: pl.BlockSpec(shape, lambda h: (0,) * len(shape))
    return pl.pallas_call(
        functools.partial(attend_back_kernel, parts),
        grid=(heads,),
        in_specs=[whole(rows, own)] * parts
        + [
            pl.BlockSpec((1, total, 3 * LANES), lambda h: (h, 0, 0)),
            pl.BlockSpec((1, 1, total), lambda h: (h, 0, 0)),
            pl.BlockSpec((1, width, 3 * LANES), lambda h: (h, 0, 0)),
        ],
        out_specs=[
            whole(3 * own, total),
            whole(parts, rows // 2, width),
            whole(parts, rows // 2, width),
        ],
        out_shape=[
            jax.ShapeDtypeStruct((3 * own, total), BF16),
            jax.ShapeDtypeStruct((parts, rows // 2, width), BF16),
            jax.ShapeDtypeStruct((parts, rows // 2, width), BF16),
        ],
        scratch_shapes=[
            pltpu.VMEM((own, total), F32),
            pltpu.VMEM((3 * own, total), F32),
            pltpu.VMEM((total, width), F32),
            pltpu.VMEM((total, LANES), F32),
            pltpu.VMEM((total, LANES), F32),
            pltpu.VMEM((total, LANES), F32),
        ],
        compiler_params=params(),
        cost_estimate=cost(
            2 * heads * total * (width * 3 * LANES + 10 * LANES * total), 12 * total * width
        ),
        name="attend_back",
    )(*d_context, qkv, lse, w_heads)


def mlp_kernel(parts, place_ref, *refs):
    ctx_refs = refs[:parts]
    (
        hidden_ref,
        cot_ref,
        proj_ref,
        vec_ref,
        fc1_ref,
        fc1_bias_ref,
        fc2_ref,
        out_ref,
        d_middle_ref,
        d_branch_ref,
        active_t_ref,
        d_pre_ref,
        normed_t_ref,
        ctx_t_ref,
        vec_out_ref,
        fc1_bias_out_ref,
    ) = refs[parts : parts + 16]
    d_ctx_refs = refs[parts + 16 : 2 * parts + 16]
    middle_ref, normed_ref, acc_out, acc_back, turn_ref = refs[2 * parts + 16 :]
    step = pl.program_id(0)
    place = place_ref[0]
    own = ctx_refs[0].shape[1]

    @pl.when(step == 0)
    def _():
        branch = vec_ref[0:1] + hidden_ref[...]
        for part in range(parts):
            at = pl.ds(pl.multiple_of((place ^ part) * own, 8), own)
            branch += dot(ctx_refs[part][...], proj_ref[at, :])
            turn_ref[at] = ctx_refs[part][...].astype(F32).T
        ctx_t_ref[...] = turn_ref[...].astype(BF16)
        middle_ref[...] = branch
        scaled, _ = normalize(branch)
        normed = (scaled * vec_ref[1:2] + vec_ref[2:3]).astype(BF16)
        normed_ref[...] = normed
        normed_t_ref[...] = turned(normed)

    before = dot(normed_ref[...], fc1_ref[...]) + fc1_bias_ref[...]
    cdf = 0.5 + 0.5 * lax.erf(before * math.sqrt(0.5))
    active = (before * cdf).astype(BF16)
    slope = cdf + before * (jnp.exp(-0.5 * before * before) * (1.0 / math.sqrt(2.0 * math.pi)))
    d_before = dot_nt(cot_ref[...], fc2_ref[...]) * slope
    fc1_bias_out_ref[...] = jnp.sum(d_before, axis=0, keepdims=True)
    d_low = d_before.astype(BF16)
    d_pre_ref[...] = d_low
    active_t_ref[...] = turned(active)
    forward = dot(active, fc2_ref[...])
    backward = dot_nt(d_low, fc1_ref[...])

    @pl.when(step == 0)
    def _():
        acc_out[...] = forward
        acc_back[...] = backward

    @pl.when(step > 0)
    def _():
        acc_out[...] += forward
        acc_back[...] += backward

    @pl.when(step == pl.num_programs(0) - 1)
    def _():
        middle = middle_ref[...]
        out_ref[...] = middle + acc_out[...] + vec_ref[3:4]
        scaled, factor = normalize(middle)
        upstream = acc_back[...]
        cot = cot_ref[...].astype(F32)
        d_middle = cot + norm_back(upstream, scaled, factor, vec_ref[1:2])
        d_middle_ref[...] = d_middle
        d_branch = d_middle.astype(BF16)
        d_branch_ref[...] = d_branch
        vec_out_ref[0:1] = jnp.sum(upstream * scaled, axis=0, keepdims=True)
        vec_out_ref[1:2] = jnp.sum(upstream, axis=0, keepdims=True)
        vec_out_ref[2:3] = jnp.sum(d_middle, axis=0, keepdims=True)
        vec_out_ref[3:4] = jnp.sum(cot, axis=0, keepdims=True)
        vec_out_ref[4:] = jnp.zeros((4, vec_out_ref.shape[1]), F32)
        for part in range(parts):
            at = pl.ds(pl.multiple_of((place ^ part) * own, 8), own)
            d_ctx_refs[part][...] = dot_nt(d_branch, proj_ref[at, :]).astype(BF16)


def mlp(parts, place, context, hidden, cot, proj, vecs, fc1, fc1_bias, fc2):
    rows, width = hidden.shape
    ff = fc1.shape[1]
    own = context[0].shape[1]
    chunk = width
    whole = lambda *shape: pl.BlockSpec(shape, lambda i, p: (0,) * len(shape))
    return pl.pallas_call(
        functools.partial(mlp_kernel, parts),
        grid_spec=pltpu.PrefetchScalarGridSpec(
            num_scalar_prefetch=1,
            grid=(ff // chunk,),
            in_specs=[whole(rows, own)] * parts
            + [
                whole(rows, width),
                whole(rows, width),
                whole(width, width),
                whole(8, width),
                pl.BlockSpec((width, chunk), lambda i, p: (0, i)),
                pl.BlockSpec((1, chunk), lambda i, p: (0, i)),
                pl.BlockSpec((chunk, width), lambda i, p: (i, 0)),
            ],
            out_specs=[
                whole(rows, width),
                whole(rows, width),
                whole(rows, width),
                pl.BlockSpec((chunk, rows), lambda i, p: (i, 0)),
                pl.BlockSpec((rows, chunk), lambda i, p: (0, i)),
                whole(width, rows),
                whole(width, rows),
                whole(8, width),
                pl.BlockSpec((1, chunk), lambda i, p: (0, i)),
            ]
            + [whole(rows, own)] * parts,
            scratch_shapes=[
                pltpu.VMEM((rows, width), F32),
                pltpu.VMEM((rows, width), BF16),
                pltpu.VMEM((rows, width), F32),
                pltpu.VMEM((rows, width), F32),
                pltpu.VMEM((width, rows), F32),
            ],
        ),
        out_shape=[
            jax.ShapeDtypeStruct((rows, width), F32),
            jax.ShapeDtypeStruct((rows, width), F32),
            jax.ShapeDtypeStruct((rows, width), BF16),
            jax.ShapeDtypeStruct((ff, rows), BF16),
            jax.ShapeDtypeStruct((rows, ff), BF16),
            jax.ShapeDtypeStruct((width, rows), BF16),
            jax.ShapeDtypeStruct((width, rows), BF16),
            jax.ShapeDtypeStruct((8, width), F32),
            jax.ShapeDtypeStruct((1, ff), F32),
        ]
        + [jax.ShapeDtypeStruct((rows, own), BF16)] * parts,
        compiler_params=params(),
        cost_estimate=cost(8 * rows * width * ff, 4 * width * ff + 24 * rows * width),
        name="feed_forward",
    )(place, *context, hidden, cot, proj, vecs, fc1, fc1_bias, fc2)


def post_kernel(lead_ref, tail_ref, hidden_ref, d_middle_ref, gain_ref, w_ref, din_ref, dskip_ref, low_ref, vec_ref):
    width = hidden_ref.shape[1]
    upstream = jnp.concatenate([lead_ref[...].astype(F32), tail_ref[...].astype(F32)], 0)
    scaled, factor = normalize(hidden_ref[...])
    d_hidden = d_middle_ref[...] + norm_back(upstream, scaled, factor, gain_ref[...])
    low = d_hidden.astype(BF16)
    low_ref[...] = low
    vec_ref[0:1] = jnp.sum(d_hidden, axis=0, keepdims=True)
    vec_ref[1:2] = jnp.sum(upstream * scaled, axis=0, keepdims=True)
    vec_ref[2:3] = jnp.sum(upstream, axis=0, keepdims=True)
    vec_ref[3:] = jnp.zeros((5, width), F32)
    din_ref[...] = dot_nt(low, w_ref[:width])
    dskip_ref[...] = dot_nt(low, w_ref[width:])


def post(lead, tail, hidden, d_middle, gain, w):
    rows, width = hidden.shape
    return pl.pallas_call(
        post_kernel,
        out_shape=(
            jax.ShapeDtypeStruct((rows, width), F32),
            jax.ShapeDtypeStruct((rows, width), F32),
            jax.ShapeDtypeStruct((rows, width), BF16),
            jax.ShapeDtypeStruct((8, width), F32),
        ),
        compiler_params=params(),
        cost_estimate=cost(4 * rows * width * width, 4 * width * width + 20 * rows * width),
        name="input_back",
    )(lead, tail, hidden, d_middle, gain, w)


def pair_kernel(count, where_ref, *refs):
    out_ref = refs[4 * count]
    at = 0
    for index in range(count):
        own_t, peer_t, own, peer = refs[4 * index : 4 * index + 4]
        size = own_t.shape[2]
        out_ref[0, pl.ds(at, size)] = (
            dot(own_t[0, 0], own[...]) + dot(peer_t[0], peer[...])
        ).astype(BF16)
        at += size


def pair_grads(where, groups):
    depth = groups[0][0].shape[0]
    width = groups[0][2].shape[1]
    in_specs, operands, height, flops = [], [], 0, 0
    for own_t, peer_t, own, peer in groups:
        size, rows = own_t.shape[2:]
        in_specs += [
            pl.BlockSpec((1, 1, size, rows), lambda z, w: (z, w[0], 0, 0)),
            pl.BlockSpec((1, size, rows), lambda z, w: (z, 0, 0)),
            pl.BlockSpec((rows, width), lambda z, w: (0, 0)),
            pl.BlockSpec((rows, width), lambda z, w: (0, 0)),
        ]
        operands += [own_t, peer_t, own, peer]
        height += size
        flops += 4 * depth * size * rows * width
    return pl.pallas_call(
        functools.partial(pair_kernel, len(groups)),
        grid_spec=pltpu.PrefetchScalarGridSpec(
            num_scalar_prefetch=1,
            grid=(depth,),
            in_specs=in_specs,
            out_specs=pl.BlockSpec((1, height, width), lambda z, w: (z, 0, 0)),
        ),
        out_shape=jax.ShapeDtypeStruct((depth, height, width), BF16),
        compiler_params=params(),
        cost_estimate=cost(flops, 4 * depth * height * width),
        name="pair_grads",
    )(where, *operands)


def column_kernel(where_ref, own_t, peer_t, own, peer, out_ref):
    for z in range(own_t.shape[0]):
        out_ref[0, z] = (dot(own_t[z, 0], own[...]) + dot(peer_t[z], peer[...])).astype(BF16)


def column_grads(where, parts, own_t, peer_t, own, peer):
    depth, _, size, rows = own_t.shape
    width = own.shape[1] // parts
    return pl.pallas_call(
        column_kernel,
        grid_spec=pltpu.PrefetchScalarGridSpec(
            num_scalar_prefetch=1,
            grid=(parts,),
            in_specs=[
                pl.BlockSpec((depth, 1, size, rows), lambda k, w: (0, w[0], 0, 0)),
                pl.BlockSpec((depth, size, rows), lambda k, w: (0, 0, 0)),
                pl.BlockSpec((rows, width), lambda k, w: (0, k ^ w[1])),
                pl.BlockSpec((rows, width), lambda k, w: (0, k ^ w[1])),
            ],
            out_specs=pl.BlockSpec((1, depth, size, width), lambda k, w: (k, 0, 0, 0)),
        ),
        out_shape=jax.ShapeDtypeStruct((parts, depth, size, width), BF16),
        compiler_params=params(),
        cost_estimate=cost(
            4 * parts * depth * size * rows * width, 4 * parts * depth * size * width
        ),
        name="column_grads",
    )(where, own_t, peer_t, own, peer)


def heads_kernel(normed_ref, dt_ref, out_ref):
    out_ref[...] = lax.dot_general(
        normed_ref[...], dt_ref[...], (((0,), (1,)), ((), ())), preferred_element_type=F32
    ).astype(BF16)


def heads_grads(normed_all, d_triple_t):
    total, width = normed_all.shape
    wide = d_triple_t.shape[0]
    return pl.pallas_call(
        heads_kernel,
        out_shape=jax.ShapeDtypeStruct((width, wide), BF16),
        compiler_params=params(),
        cost_estimate=cost(2 * total * width * wide, 2 * total * (width + wide)),
        name="heads_grads",
    )(normed_all, d_triple_t)


def columns_kernel(place_ref, *refs):
    out_ref = refs[-1]
    size = refs[0].shape[1]
    for k in range(len(refs) - 1):
        at = pl.multiple_of((place_ref[0] ^ k) * size, LANES)
        out_ref[:, pl.ds(at, size)] = refs[k][...].astype(F32)


def put_columns(place, pieces):
    height, size = pieces[0].shape
    count = len(pieces)
    return pl.pallas_call(
        columns_kernel,
        in_specs=[pl.BlockSpec(memory_space=pltpu.SMEM)]
        + [pl.BlockSpec(memory_space=pltpu.VMEM)] * count,
        out_shape=jax.ShapeDtypeStruct((height, count * size), F32),
        compiler_params=params(),
        cost_estimate=cost(1e6, 6 * count * height * size),
        name="put_columns",
    )(place, *pieces)


def head_columns_kernel(place_ref, *refs):
    out_ref = refs[-1]
    count = len(refs) - 1
    size = refs[0].shape[1] // 3
    for j in range(count):
        value = refs[0][...]
        for k in range(1, count):
            value = jnp.where((place_ref[0] ^ k) == j, refs[k][...], value)
        value = value.astype(F32)
        for which in range(3):
            at = (which * count + j) * size
            out_ref[:, at : at + size] = value[:, which * size : (which + 1) * size]


def put_heads(place, pieces):
    height, size = pieces[0].shape
    count = len(pieces)
    return pl.pallas_call(
        head_columns_kernel,
        in_specs=[pl.BlockSpec(memory_space=pltpu.SMEM)]
        + [pl.BlockSpec(memory_space=pltpu.VMEM)] * count,
        out_shape=jax.ShapeDtypeStruct((height, count * size), F32),
        compiler_params=params(),
        cost_estimate=cost(1e6, 6 * count * height * size),
        name="put_heads",
    )(place, *pieces)


def across(value, size, bit):
    return lax.ppermute(value, "seq", [(i, i ^ bit) for i in range(size)])


def other_core(value, size):
    return lax.ppermute(value, "batch", [(i, i ^ 1) for i in range(size)])


def plus(*terms):
    total = terms[0].astype(F32)
    for term in terms[1:]:
        total = total + term.astype(F32)
    return total.astype(BF16)


def bits_of(size):
    return [1 << i for i in range(size.bit_length() - 1)]


def everywhere(value, size):
    if size != 4:
        return [value] + [across(value, size, k) for k in range(1, size)]
    half = value.shape[0] // 2
    near, far = across(value, size, 1), across(value, size, 2)
    lead, tail = across(near[:half], size, 2), across(far[half:], size, 1)
    return [value, near, far, jnp.concatenate([lead, tail], 0)]


def scattered(value, size, bits):
    left = list(range(size))
    for bit in bits:
        keep = [i for i, k in enumerate(left) if not k & bit]
        send = [i for i, k in enumerate(left) if k & bit]
        pick = lambda which: jnp.concatenate([value[i : i + 1] for i in which], 0)
        value = plus(pick(keep), across(pick(send), size, bit))
        left = [left[i] for i in keep]
    return value[0]


def summed(value, size):
    half = (value.shape[0] // 2 + 7) // 8 * 8
    bits = bits_of(size)
    done = []
    for piece, order in ((value[:half], bits), (value[half:], bits[::-1])):
        for bit in order:
            piece = plus(piece, across(piece, size, bit))
        done.append(piece)
    return jnp.concatenate(done, 0)


def down_the_line(value, size, at):
    depth = value.shape[0]
    pick = lambda index: lax.dynamic_index_in_dim(
        value, jnp.clip(index, 0, depth - 1), 0, keepdims=False
    )
    up = down = None
    for t in range(depth - 1):
        send_up = pick(depth - 1 - t + at)
        send_down = pick(t - (depth - 1 - at))
        if t:
            send_up, send_down = plus(send_up, up), plus(send_down, down)
        up = lax.ppermute(
            send_up,
            "batch",
            [(2 * z + c, 2 * z + 2 + c) for z in range(depth - 1) if z <= t for c in (0, 1)],
        )
        down = lax.ppermute(
            send_down,
            "batch",
            [
                (2 * z + c, 2 * z - 2 + c)
                for z in range(1, depth)
                if z >= depth - 1 - t
                for c in (0, 1)
            ],
        )
    return plus(pick(at), up, down)


MESH = pl.DeviceIdType.MESH
AWAY = (1, 3, 2, 0)


def flip(value, k):
    if k == 0:
        return value
    if k == 1:
        return value + 1 - 2 * (value % 2)
    if k == 2:
        return value + 2 - 4 * (value // 2)
    return 3 - value


def add_rows(into, other):
    if len(into.shape) > 2:
        for i in range(into.shape[0]):
            add_rows(into.at[i], other.at[i])
        return
    tile = 16

    def body(i, carry):
        at = pl.ds(pl.multiple_of(i * tile, tile), tile)
        into[at] = (into[at].astype(F32) + other[at].astype(F32)).astype(BF16)
        return carry

    lax.fori_loop(0, into.shape[0] // tile, body, 0)


class Wires:
    def __init__(self, send_sems, recv_sems):
        self.send_sems, self.recv_sems, self.made = send_sems, recv_sems, []
        self.limit = send_sems.shape[0]

    def copy(self, src, dst, device, when=None):
        index = len(self.made)
        assert index < self.limit
        made = Wire(
            pltpu.make_async_remote_copy(
                src_ref=src,
                dst_ref=dst,
                send_sem=self.send_sems.at[index],
                recv_sem=self.recv_sems.at[index],
                device_id=device,
                device_id_type=MESH,
            ),
            when,
        )
        self.made.append(made)
        return made

    def by_core(self, core, src, dst, device, when=None):
        index = len(self.made)
        assert index + 1 < self.limit
        self.made.append(None)
        pick = lambda which: pltpu.make_async_remote_copy(
            src_ref=src,
            dst_ref=dst,
            send_sem=self.send_sems.at[index],
            recv_sem=self.recv_sems.at[index + which],
            device_id=device,
            device_id_type=MESH,
        )
        made = Wire(pick(core), when)
        made.arrive = lambda: [pick(which).wait_recv() for which in (0, 1)]
        self.made.append(made)
        return made

    def drain(self):
        for wire in [w for w in self.made if w is not None]:
            if wire.when is None:
                wire.copy.wait_send()
            else:
                pl.when(wire.when)(wire.copy.wait_send)


class Wire:
    def __init__(self, copy, when):
        self.copy, self.when = copy, when
        self.start, self.arrive = copy.start, copy.wait_recv


class Line:
    def __init__(self, wires, depth, chip, up_to, down_to, own, up_in, down_in, begun=False):
        self.depth, self.chip, self.own, self.begun = depth, chip, own, begun
        self.up_in, self.down_in = up_in, down_in
        last = depth - 1
        self.up = {
            d: wires.copy(
                own(d),
                up_in.at[d - 1],
                up_to,
                (chip < d) & (chip > 0) if begun and d == last else chip < d,
            )
            for d in range(1, depth)
        }
        self.down = {
            d: wires.copy(
                own(d),
                down_in.at[d],
                down_to,
                (chip > d) & (chip < last) if begun and d == 0 else chip > d,
            )
            for d in range(last)
        }

    def hop(self, t):
        last = self.depth - 1
        for d in range(1, self.depth):
            z = d - (last - t)
            if 0 <= z < d:

                @pl.when(self.chip == z)
                def _():
                    if z > 0 and not (self.begun and t == 1):
                        self.up[d].arrive()
                        add_rows(self.own(d), self.up_in.at[d - 1])
                    self.up[d].start()

                @pl.when(self.chip == last - z)
                def _():
                    if z > 0 and not (self.begun and t == 1):
                        self.down[last - d].arrive()
                        add_rows(self.own(last - d), self.down_in.at[last - d])
                    self.down[last - d].start()

    def finish(self):
        for d in range(self.depth):

            @pl.when(self.chip == d)
            def _():
                if d > 0:
                    self.up[d].arrive()
                    add_rows(self.own(d), self.up_in.at[d - 1])
                if d < self.depth - 1:
                    self.down[d].arrive()
                    add_rows(self.own(d), self.down_in.at[d])


class Square:
    def __init__(self, wires, to, own, in_one, in_two, src=None, begun=False):
        self.own, self.in_one, self.in_two = own, in_one, in_two
        src = src or own
        self.one, self.two = [], []
        for h, (f, g) in enumerate(((1, 2), (2, 1))):
            if not begun:
                self.one.append(
                    (
                        wires.copy(src(h, 3), in_one[h].at[1], to[f]),
                        wires.copy(src(h, f), in_one[h].at[0], to[f]),
                    )
                )
        for h, (f, g) in enumerate(((1, 2), (2, 1))):
            self.two.append(wires.copy(own(h, g), in_two[h], to[g]))

    def start(self):
        for i in range(2):
            for h in range(2):
                self.one[h][i].start()

    def middle(self):
        for h, g in ((0, 2), (1, 1)):
            self.one[h][0].arrive()
            add_rows(self.own(h, g), self.in_one[h].at[1])
            self.two[h].start()
        for h in range(2):
            self.one[h][1].arrive()
            add_rows(self.own(h, 0), self.in_one[h].at[0])

    def finish(self):
        for h in range(2):
            self.two[h].arrive()
            add_rows(self.own(h, 0), self.in_two[h])


class Spread:
    def __init__(self, wires, to, slots, src=None):
        rows = slots.shape[1]
        cut = (rows // 2 + 15) // 16 * 16
        src = slots.at[0] if src is None else src
        lead, tail = pl.ds(0, cut), pl.ds(cut, rows - cut)
        self.near = [wires.copy(src.at[p], slots.at[1, p], to[1]) for p in (lead, tail)]
        self.far = [wires.copy(src.at[p], slots.at[2, p], to[2]) for p in (tail, lead)]
        self.lead = wires.copy(slots.at[1, lead], slots.at[3, lead], to[2])
        self.tail = wires.copy(slots.at[2, tail], slots.at[3, tail], to[1])

    def start(self):
        for i in range(2):
            self.near[i].start()
            self.far[i].start()

    def relay(self):
        self.near[0].arrive()
        self.lead.start()
        self.far[0].arrive()
        self.tail.start()

    def finish(self):
        self.near[1].arrive()
        self.far[1].arrive()
        self.lead.arrive()
        self.tail.arrive()


class Pair:
    def __init__(self, wires, to, halves, ins):
        self.halves, self.ins, self.wires, self.to, self.step = halves, ins, wires, to, 0
        self.sent = [
            [wires.copy(halves[h][i], ins[h].at[i], to[(1, 2)[(h + i) % 2]]) for h in range(2)]
            for i in range(2)
        ]

    def start(self):
        for wire in self.sent[0]:
            wire.start()

    def middle(self):
        for h in range(2):
            self.sent[0][h].arrive()
            one, two = self.halves[h][0], self.halves[h][1]
            two[...] = (one[...].astype(F32) + self.ins[h][0].astype(F32)).astype(BF16)
            self.sent[1][h].start()

    def finish(self):
        for h in range(2):
            self.sent[1][h].arrive()
            two, three = self.halves[h][1], self.halves[h][2]
            three[...] = (two[...].astype(F32) + self.ins[h][1].astype(F32)).astype(BF16)


def reduce_kernel(
    late_hbm,
    lead_hbm,
    tail_hbm,
    normed_hbm,
    dt_hbm,
    joined_hbm,
    joined_peer_hbm,
    hidden_hbm,
    d_middle_hbm,
    w_hbm,
    normed_x,
    normed_peer,
    normed_cond_x,
    normed_cond_peer,
    d_pre_go,
    d_pre_x,
    active_go,
    active_near,
    active_x,
    active_cond_go,
    active_cond_near,
    active_cond_x,
    cot_hbm,
    cot_z,
    cot_zz,
    cot_far,
    cot_peer,
    gain_ref,
    vec_two_ref,
    fc1_bias_ref,
    p_all,
    f_all,
    g_all,
    q_all,
    s_all,
    c_all,
    din_hbm,
    dskip_hbm,
    vec_ref,
    left_one,
    right_one,
    left_two,
    right_two,
    cond_rows,
    cond_flat,
    active_cond,
    f_own,
    f_up,
    f_down,
    g_own,
    g_lead_one,
    g_tail_one,
    g_lead_two,
    g_tail_two,
    l_own,
    l_up,
    l_down,
    q_own,
    q_sum,
    q_up,
    q_down,
    s_own,
    s_one,
    s_two,
    s_z,
    s_up,
    s_down,
    d_own,
    d_one,
    d_two,
    p_lead,
    p_tail,
    p_lead_in,
    p_tail_in,
    low_ref,
    low_peer,
    c_own,
    hidden_ref,
    d_middle_ref,
    joined_ref,
    joined_peer_ref,
    v_own,
    v_in,
    send_sems,
    recv_sems,
    local_sems,
):
    rows, width = hidden_hbm.shape
    depth = f_own.shape[0]
    mid = depth // 2
    slots = c_own.shape[0]
    images = rows - slots
    place, index = lax.axis_index("seq"), lax.axis_index("batch")
    chip, core = index // 2, index % 2
    last = depth - 1
    to, other, up_to, down_to = ends_of(place, index, depth)
    greet([to[1], to[2], to[3], other], chip, depth, up_to, down_to)
    wires = Wires(send_sems, recv_sems)
    taken = [0]

    def local(src, dst):
        taken[0] += 1
        copy = pltpu.make_async_copy(src, dst, local_sems.at[taken[0] - 1])
        copy.start()
        return copy

    keeps = []

    d_hbm = (lead_hbm, tail_hbm)
    norm_sum = Square(
        wires,
        to,
        lambda h, k: d_own.at[h, (0, 1, 1, None)[k]],
        [d_one.at[h] for h in range(2)],
        [d_two.at[h] for h in range(2)],
        src=lambda h, k: d_hbm[h].at[k],
    )
    norm_sum.start()

    l_load = local(late_hbm, l_own)
    l_line = Line(wires, depth, chip, up_to, down_to, lambda d: l_own.at[d], l_up, l_down)

    img, cnd = pl.ds(0, images), pl.ds(images, slots)

    def cut(g):
        return pl.ds(pl.multiple_of(g * images, images), images)

    def end(g):
        return pl.ds(pl.multiple_of(8 * images + g * slots, slots), slots)

    loads_two, loads_able = [], []
    for i in range(depth):
        source = (chip + depth - AWAY[i]) % depth
        for c in range(2):
            g = source * 2 + c
            left = active_near.at[i, c] if i < 2 else active_x.at[i - 2, c]
            ends = active_cond_near.at[i, c] if i < 2 else active_cond_x.at[i - 2, c]
            if i < 3:
                loads_two.append(local(left, left_two.at[:, :, cut(g)]))
                loads_two.append(local(ends, active_cond.at[g]))
    g = chip * 2 + core
    loads_two.append(local(active_go.at[1, core], left_two.at[:, :, cut(g)]))
    loads_two.append(local(active_cond_go.at[1, core], active_cond.at[g]))
    g = chip * 2 + 1 - core
    loads_two.append(local(active_x.at[1, 1 - core], left_two.at[:, :, cut(g)]))
    loads_two.append(local(active_cond_x.at[1, 1 - core], active_cond.at[g]))
    held = [cot_hbm, cot_z.at[0], cot_z.at[1], cot_zz.at[0], cot_zz.at[1], cot_far]
    for away, picks in ((0, (0, 0)), (1, (1, 2)), (2, (3, 4)), (3, (5, 5))):
        for which in range(2):
            if away == 0 and which == 1:
                continue
            z = chip - away if which == 0 else chip + away
            able = (z >= 0) & (z <= last)
            for ref, c in ((held[picks[which]], core), (cot_peer.at[picks[which]], 1 - core)):
                g = jnp.clip(z, 0, last) * 2 + c
                for src, dst in ((img, cut(g)), (cnd, end(g))):
                    sem = local_sems.at[taken[0]]
                    taken[0] += 1
                    copy = pltpu.make_async_copy(ref.at[src], right_two.at[dst], sem)
                    pl.when(able)(copy.start)
                    loads_able.append((able, copy))
    swaps_one = []
    d_pre_of = lambda k, part: d_pre_x.at[k - 1, part] if k else d_pre_go.at[place, part]
    for k in range(4):
        swaps_one.append(wires.copy(d_pre_of(k, img), right_one.at[cut(4 + k)], other))
        swaps_one.append(wires.copy(d_pre_of(k, cnd), right_one.at[end(4 + k)], other))
    for wire in swaps_one:
        wire.start()
    loads_one = []
    for k in range(4):
        for g, left, cond in (
            (k, normed_x.at[k, :, core], normed_cond_x.at[k]),
            (4 + k, normed_peer.at[k], normed_cond_peer.at[k]),
        ):
            loads_one.append(local(left, left_one.at[:, :, cut(g)]))
            loads_one.append(local(cond, cond_rows.at[pl.ds(g * slots, slots)]))
        loads_one.append(local(d_pre_of(k, img), right_one.at[cut(k)]))
        loads_one.append(local(d_pre_of(k, cnd), right_one.at[end(k)]))
    d_loads = [
        local(d_hbm[h].at[k], d_own.at[h, i]) for h, ks in ((0, (0, 2)), (1, (0, 1))) for i, k in enumerate(ks)
    ]
    p_cut = p_lead.shape[1]
    h_loads = [local(hidden_hbm, hidden_ref), local(d_middle_hbm, d_middle_ref)]
    j_loads = [local(joined_hbm, joined_ref), local(joined_peer_hbm, joined_peer_ref)]
    l_load.wait()
    l_line.hop(0)

    for copy in loads_two:
        copy.wait()
    for able, copy in loads_able:
        pl.when(able)(copy.wait)
    small = f_own.shape[1]
    for j in range(4):
        left_two[j, :, 8 * images :] = jnp.concatenate(
            [active_cond[g, :, j * slots : (j + 1) * slots] for g in range(8)], 1
        )
    g_own[...] = (
        dot(left_two[...].reshape(4 * small, 8 * rows), right_two[...])
        .astype(BF16)
        .reshape(4, small, width)
    )
    l_line.hop(1)
    g_cut = g_lead_one.shape[1]
    g_sum = Square(
        wires,
        to,
        lambda h, k: g_own.at[flip(place, k), (pl.ds(0, g_cut), pl.ds(g_cut, small - g_cut))[h]],
        (g_lead_one, g_tail_one),
        (g_lead_two, g_tail_two),
    )

    for copy in loads_one:
        copy.wait()
    flat = turned(cond_rows[...])
    for b in range(2 * depth):
        cond_flat[b // 2, b % 2] = flat[b * small : (b + 1) * small]
    for z in range(depth):
        left_one[z, :, 8 * images :] = cond_flat[z, core]
    for wire in swaps_one:
        wire.arrive()
    f_own[...] = (
        dot(left_one[...].reshape(depth * small, 8 * rows), right_one[...])
        .astype(BF16)
        .reshape(depth, small, width)
    )
    f_line = Line(wires, depth, chip, up_to, down_to, lambda d: f_own.at[d], f_up, f_down)
    f_line.hop(0)
    for copy in d_loads:
        copy.wait()
    norm_sum.middle()
    for t in range(2, last):
        l_line.hop(t)

    def heads_part(normed, dt):
        loads = [local(normed_hbm, normed), local(dt_hbm, dt)]
        for copy in loads:
            copy.wait()
        step = 3 * LANES
        for part in range(normed.shape[1] // step):
            grads = lax.dot_general(
                normed[:, part * step : (part + 1) * step],
                dt[...],
                (((0,), (1,)), ((), ())),
                preferred_element_type=F32,
            ).astype(BF16)
            q_own[pl.ds(part * step, step)] = grads

    pl.run_scoped(
        heads_part, pltpu.VMEM(normed_hbm.shape, BF16), pltpu.VMEM(dt_hbm.shape, BF16)
    )
    height = q_sum.shape[1]
    q_swap = [
        wires.copy(
            q_own.at[pl.ds(pl.multiple_of((2 * z + 1 - core) * height, 16), height)],
            q_sum.at[z],
            other,
        )
        for z in range(depth)
    ]
    for wire in q_swap:
        wire.start()

    norm_sum.finish()
    low_swap = wires.copy(low_ref, low_peer, other)
    v_swap = wires.copy(v_own.at[0], v_in.at[0], other)
    for copy in h_loads:
        copy.wait()
    upstream = jnp.concatenate([d_own[0, 0].astype(F32), d_own[1, 0].astype(F32)], 0)
    scaled, factor = normalize(hidden_ref[...])
    d_hidden = d_middle_ref[...] + norm_back(
        upstream, scaled, factor, gain_ref[...].reshape(1, -1)
    )
    low_ref[...] = d_hidden.astype(BF16)
    low_swap.start()
    l_line.finish()
    p_lead[0] = l_own[chip, :p_cut]
    p_tail[0] = l_own[chip, p_cut:]
    p_sum = Pair(
        wires,
        to,
        [[ref.at[i] for i in range(3)] for ref in (p_lead, p_tail)],
        (p_lead_in, p_tail_in),
    )
    p_sum.start()
    g_sum.start()
    v_own[0] = jnp.zeros(v_own.shape[1:], F32)
    v_own[0, 0:1] = jnp.sum(d_hidden, axis=0, keepdims=True)
    v_own[0, 1:2] = jnp.sum(upstream * scaled, axis=0, keepdims=True)
    v_own[0, 2:3] = jnp.sum(upstream, axis=0, keepdims=True)
    v_own[0, 3:7] = vec_two_ref[0:4]
    v_own[0, 8:12] = fc1_bias_ref[...]
    v_swap.start()
    f_line.hop(1)
    for z, wire in enumerate(q_swap):
        wire.arrive()
        add_rows(q_sum.at[z], q_own.at[pl.ds(pl.multiple_of((2 * z + core) * height, 16), height)])
    q_line = Line(wires, depth, chip, up_to, down_to, lambda d: q_sum.at[d], q_up, q_down)
    q_line.hop(0)

    for copy in j_loads:
        copy.wait()
    low_swap.arrive()
    block = joined_ref.shape[1]
    chunk = block // 4
    grads = both(
        joined_ref[...].reshape(depth * block, rows),
        joined_peer_ref[...].reshape(depth * block, rows),
        low_ref[...],
        low_peer[...],
    )
    for h in range(mid):
        for j in range(4):
            at = [(2 * h + i) * block + j * chunk for i in range(2)]
            piece = jnp.concatenate([grads[a : a + chunk] for a in at], 0)
            s_own[flip(place, j), h] = piece.astype(BF16)
    s_sum = Square(
        wires,
        to,
        lambda h, k: s_own.at[k, h],
        [s_one.at[h] for h in range(2)],
        [s_two.at[h] for h in range(2)],
    )
    s_sum.start()
    for t in range(2, last):
        f_line.hop(t)
    p_sum.middle()

    c_go = Spread(wires, to, c_all, c_own)

    def rows_part(which, out_hbm):
        def run(w, stage):
            copy = local(w_hbm.at[pl.ds(which * width, width)], w)
            copy.wait()
            stage[...] = dot_nt(low_ref[...], w[...])
            c_own[:, which * width : (which + 1) * width] = stage[images:].astype(BF16)
            local(stage.at[pl.ds(0, images)], out_hbm).wait()

        pl.run_scoped(run, pltpu.VMEM((width, width), BF16), pltpu.VMEM((rows, width), F32))

    rows_part(0, din_hbm)
    q_line.hop(1)
    g_sum.middle()
    rows_part(1, dskip_hbm)
    keeps.append(local(c_own, c_all.at[0]))
    for t in range(2, last):
        q_line.hop(t)

    v_swap.arrive()
    v_own[1] = v_own[0] + v_in[0]
    v_own[2] = v_own[1]
    v_own[3] = v_own[1]
    v_up = wires.copy(v_own.at[2], v_in.at[1], up_to, chip < last)
    v_down = wires.copy(v_own.at[3], v_in.at[2], down_to, chip > 0)
    s_sum.middle()
    g_sum.finish()
    f_line.finish()
    s_sum.finish()
    room = s_z.shape[1]
    for h in range(mid):
        value = s_own[0, h].astype(F32)
        for i in range(2):
            s_z[2 * h + i] = jnp.concatenate(
                [value[i * chunk : (i + 1) * chunk], jnp.zeros((room - chunk, width), F32)], 0
            ).astype(BF16)
    s_line = Line(wires, depth, chip, up_to, down_to, lambda d: s_z.at[d], s_up, s_down)
    s_line.hop(0)
    g_go = Spread(wires, to, g_all, g_own.at[place])
    g_go.start()
    f_go = Spread(wires, to, f_all, f_own.at[chip])
    f_go.start()
    c_go.start()
    keeps.append(local(g_own.at[place], g_all.at[0]))
    keeps.append(local(f_own.at[chip], f_all.at[0]))

    @pl.when(chip > 0)
    def _():
        v_up.arrive()
        v_own[2] = v_own[1] + v_in[1]

    @pl.when(chip < last)
    def _():
        v_up.start()

    @pl.when(chip < last)
    def _():
        v_down.arrive()
        v_own[3] = v_own[1] + v_in[2]

    @pl.when(chip > 0)
    def _():
        v_down.start()

    v_own[4] = v_own[2] + v_own[3] - v_own[1]
    v_near = wires.copy(v_own.at[4], v_in.at[3], to[1])
    v_near.start()
    s_line.hop(1)
    q_line.finish()
    q_go = Spread(wires, to, q_all, q_sum.at[chip])
    q_go.start()
    keeps.append(local(q_sum.at[chip], q_all.at[0]))
    for t in range(2, last):
        s_line.hop(t)
    c_go.relay()
    g_go.relay()
    f_go.relay()
    v_near.arrive()
    v_own[5] = v_own[4] + v_in[3]
    v_far = wires.copy(v_own.at[5], v_in.at[4], to[2])
    v_far.start()
    s_line.finish()
    s_go = Spread(wires, to, s_all, s_z.at[chip])
    s_go.start()
    keeps.append(local(s_z.at[chip], s_all.at[0]))
    q_go.relay()
    p_sum.finish()
    keeps.append(local(p_lead.at[2], p_all.at[pl.ds(0, p_cut)]))
    keeps.append(local(p_tail.at[2], p_all.at[pl.ds(p_cut, p_tail.shape[1])]))
    c_go.finish()
    v_far.arrive()
    vec_ref[...] = v_own[5] + v_in[4]
    s_go.relay()
    f_go.finish()
    g_go.finish()
    q_go.finish()
    s_go.finish()
    for copy in keeps:
        copy.wait()
    wires.drain()


def reduce_all(
    late, lead, tail, normed_all, d_triple_t, joined, joined_peer, hidden, d_middle, w, feeds,
    gain, vec_two, fc1_bias_grad,
):
    depth, small, width = late.shape
    rows = hidden.shape[0]
    slots = SLOTS // 4
    images = rows - slots
    mid = depth // 2
    own = d_triple_t.shape[0]
    skip_rows = joined.shape[1]
    skip_chunk = (skip_rows // 4 + 15) // 16 * 16
    pair = depth // 2 * (skip_rows // 4)
    half = rows // 2
    cut = (small // 2 + 15) // 16 * 16
    v = lambda *shape: pltpu.VMEM(shape, BF16)
    ends = depth - 1
    scratch = [
        v(depth, small, 8 * rows), v(8 * rows, width), v(depth, small, 8 * rows), v(8 * rows, width),
        v(8 * slots, width), v(depth, 2, small, 8 * slots), v(8, small, 4 * slots),
        v(depth, small, width), v(ends, small, width), v(ends, small, width),
        v(4, small, width), v(2, cut, width), v(2, small - cut, width), v(cut, width), v(small - cut, width),
        v(depth, small, width), v(ends, small, width), v(ends, small, width),
        v(width, own), v(depth, small, own), v(ends, small, own), v(ends, small, own),
        v(4, 2, pair, width), v(2, 2, pair, width), v(2, pair, width),
        v(depth, skip_chunk, width), v(ends, skip_chunk, width), v(ends, skip_chunk, width),
        v(2, 2, half, width), v(2, 2, half, width), v(2, half, width),
        v(3, cut, width), v(3, small - cut, width), v(2, cut, width), v(2, small - cut, width),
        v(rows, width), v(rows, width), v(slots, 2 * width),
        pltpu.VMEM((rows, width), F32), pltpu.VMEM((rows, width), F32),
        v(*joined.shape), v(*joined.shape),
        pltpu.VMEM((6, 16, width), F32), pltpu.VMEM((5, 16, width), F32),
        pltpu.SemaphoreType.DMA((128,)), pltpu.SemaphoreType.DMA((128,)), pltpu.SemaphoreType.DMA((128,)),
    ]
    hbm = pl.BlockSpec(memory_space=pl.ANY)
    vmem = pl.BlockSpec(memory_space=pltpu.VMEM)
    f = lambda *shape: jax.ShapeDtypeStruct(shape, F32)
    b = lambda *shape: jax.ShapeDtypeStruct(shape, BF16)
    return pl.pallas_call(
        reduce_kernel,
        in_specs=[hbm] * 27 + [vmem] * 3,
        out_specs=[hbm] * 8 + [vmem],
        out_shape=[
            b(small, width),
            b(4, small, width),
            b(4, small, width),
            b(4, small, own),
            b(4, skip_chunk, width),
            b(4, slots, 2 * width),
            f(images, width),
            f(images, width),
            f(16, width),
        ],
        scratch_shapes=scratch,
        compiler_params=pltpu.CompilerParams(
            vmem_limit_bytes=VMEM_LIMIT, collective_id=0, has_side_effects=True
        ),
        cost_estimate=cost(1e10, 1e8),
        name="reduce_all",
    )(
        late, lead, tail, normed_all, d_triple_t, joined, joined_peer, hidden, d_middle, w, *feeds,
        gain, vec_two, fc1_bias_grad,
    )


def ends_of(place, index, depth):
    chip, core = index // 2, index % 2
    to = {k: (index, flip(place, k)) for k in (1, 2, 3)}
    return to, (index + 1 - 2 * core, place), (index + 2, place), (index - 2, place)


def line_of(place, index, depth):
    chip = index // 2
    return [((chip + i) % depth * 2 + c, place) for i in range(1, depth) for c in (0, 1)]


def arrive_by_core(wires, core):
    for c in range(2):

        @pl.when(core == c)
        def _():
            wires[2 * c].arrive()
            wires[2 * c + 1].arrive()


class Hop:
    def __init__(self, wires, depth, chip, up_to, down_to, t, src_up, src_down, dst_up, dst_down):
        last = depth - 1
        self.up = wires.copy(src_up, dst_up, up_to, (chip < last) & (chip >= t))
        self.down = wires.copy(src_down, dst_down, down_to, (chip > 0) & (chip <= last - t))
        self.from_up = (chip > 0) & (chip - 1 >= t)
        self.from_down = (chip < last) & (chip + 1 <= last - t)

    def start(self):
        pl.when(self.up.when)(self.up.start)
        pl.when(self.down.when)(self.down.start)

    def arrive(self):
        pl.when(self.from_up)(self.up.arrive)
        pl.when(self.from_down)(self.down.arrive)


def greet(devices, chip=None, depth=0, up_to=None, down_to=None):
    barrier = pltpu.get_barrier_semaphore()
    for device in devices:
        pl.semaphore_signal(barrier, inc=1, device_id=device, device_id_type=MESH)
    if chip is None:
        pl.semaphore_wait(barrier, len(devices))
        return

    @pl.when(chip < depth - 1)
    def _():
        pl.semaphore_signal(barrier, inc=1, device_id=up_to, device_id_type=MESH)

    @pl.when(chip > 0)
    def _():
        pl.semaphore_signal(barrier, inc=1, device_id=down_to, device_id_type=MESH)

    pl.semaphore_wait(
        barrier, len(devices) + jnp.minimum(chip, 1) + jnp.minimum(depth - 1 - chip, 1)
    )


class Locals:
    def __init__(self, sems):
        self.sems, self.taken = sems, 0

    def copy(self, src, dst):
        self.taken += 1
        assert self.taken <= self.sems.shape[0]
        return pltpu.make_async_copy(src, dst, self.sems.at[self.taken - 1])

    def start(self, src, dst):
        copy = self.copy(src, dst)
        copy.start()
        return copy


def own_slots(cond_ref, pad_ref, place, slots):
    pad_ref[...] = jnp.zeros(pad_ref.shape, BF16)
    pad_ref[0 : cond_ref.shape[0]] = cond_ref[...]
    return pad_ref[pl.ds(pl.multiple_of(place * slots, 16), slots)]


def start_kernel(
    window,
    length_ref,
    x_ref,
    x_cond_ref,
    s_ref,
    s_cond_ref,
    cot_ref,
    cot_cond_ref,
    w_ref,
    bias_ref,
    gain_ref,
    shift_ref,
    qkv_w_hbm,
    hidden_ref,
    normed_hbm,
    heads_ref,
    qkv_ref,
    joined_hbm,
    peer_hbm,
    cot_all,
    cot_z,
    lse_ref,
    ctx_hbm,
    rest_hbm,
    cot_zz,
    pad_ref,
    x_all,
    s_all,
    normed_all,
    joined_ref,
    qkv_w_ref,
    vt_ref,
    ot_ref,
    go_ref,
    rest_ref,
    send_sems,
    recv_sems,
    local_sems,
):
    images, width = x_ref.shape
    slots = x_all.shape[0] - images
    place, index = lax.axis_index("seq"), lax.axis_index("batch")
    core = index % 2
    chip = index // 2
    depth = joined_hbm.shape[0]
    to, other, up_to, down_to = ends_of(place, index, depth)
    greet([to[1], to[2], to[3], other], chip, depth, up_to, down_to)
    wires, moves = Wires(send_sems, recv_sems), Locals(local_sems)
    w_load = moves.start(qkv_w_hbm, qkv_w_ref)
    cot_all[:images] = cot_ref[...]
    cot_all[images:] = own_slots(cot_cond_ref, pad_ref, place, slots)
    cot_go = Hop(
        wires, depth, chip, up_to, down_to, 0, cot_all, cot_all, cot_z.at[0], cot_z.at[1]
    )
    cot_go.start()
    for ref, cond, whole in ((x_ref, x_cond_ref, x_all), (s_ref, s_cond_ref, s_all)):
        whole[:images] = ref[...]
        whole[images:] = own_slots(cond, pad_ref, place, slots)
    hidden = (
        dot(x_all[...], w_ref[:width]) + dot(s_all[...], w_ref[width:]) + bias_ref[...].reshape(1, -1)
    )
    hidden_ref[...] = hidden
    scaled, _ = normalize(hidden)
    normed_all[0] = (
        scaled * gain_ref[...].reshape(1, -1) + shift_ref[...].reshape(1, -1)
    ).astype(BF16)
    spread = Spread(wires, to, normed_all)
    spread.start()

    size = joined_ref.shape[2]
    per = width // size
    for which, whole in enumerate((x_all, s_all)):
        flat = turned(whole[...])
        for i in range(per):
            block = which * per + i
            joined_ref[block // 2, block % 2] = flat[i * size : (i + 1) * size]
    swap = wires.copy(joined_ref.at[:, 1 - core], peer_hbm, other)
    swap.start()
    keep = moves.start(joined_ref.at[:, core], joined_hbm)
    heads = qkv_ref.shape[0]
    width_own = heads * HEAD_DIM
    real = lax.broadcasted_iota(jnp.int32, (width, LANES), 1) < HEAD_DIM

    def weights(which):
        first = place * width_own + which * width
        start = jnp.minimum(first // LANES * LANES, 3 * width - window)
        value = qkv_w_ref[:, pl.ds(pl.multiple_of(start, LANES), window)].astype(F32)
        value = pltpu.roll(value, lax.rem(window - (first - start), window), 1)
        for head in range(heads):
            shifted = value if head == 0 else pltpu.roll(value, window - head * HEAD_DIM, 1)
            at = (3 * head + which) * LANES
            heads_ref[:, at : at + LANES] = jnp.where(real, shifted[:, :LANES], 0.0).astype(BF16)

    rows = normed_all.shape[1]
    lane = lax.broadcasted_iota(jnp.int32, (1, LANES), 1)
    one = jnp.where(lane == HEAD_DIM, 1.0, 0.0)
    slot = lax.broadcasted_iota(jnp.int32, (slots, LANES), 0)
    lanes = lax.broadcasted_iota(jnp.int32, (slots, LANES), 1)

    def project(part):
        hidden_key = flip(place, part) * slots + slot > length_ref[0]
        bias = jnp.where(hidden_key & (lanes == HEAD_DIM), -1e30, 0.0)
        base = part * rows
        for head in range(heads):
            triple = dot(
                normed_all[part], heads_ref[:, 3 * head * LANES : 3 * (head + 1) * LANES]
            )
            qkv_ref[head, base : base + rows, :LANES] = (triple[:, :LANES] + one).astype(BF16)
            key = triple[:, LANES : 2 * LANES]
            qkv_ref[head, base : base + images, LANES : 2 * LANES] = key[:images].astype(BF16)
            qkv_ref[head, base + images : base + rows, LANES : 2 * LANES] = (
                key[images:] + bias
            ).astype(BF16)
            qkv_ref[head, base : base + rows, 2 * LANES :] = triple[:, 2 * LANES :].astype(BF16)

    w_load.wait()
    weights(0)
    spread.relay()
    weights(1)
    weights(2)
    project(0)
    spread.near[1].arrive()
    project(1)
    spread.far[1].arrive()
    project(2)
    spread.lead.arrive()
    spread.tail.arrive()
    project(3)
    out = moves.start(normed_all, normed_hbm)
    cot_go.arrive()
    cot_on = Hop(
        wires, depth, chip, up_to, down_to, 1, cot_z.at[0], cot_z.at[1], cot_zz.at[0], cot_zz.at[1]
    )
    cot_on.start()

    total = 4 * rows
    step = 3 * LANES
    go, keeps = [], []
    for head in range(heads):
        vt_ref[...] = turned(qkv_ref[head, :, 2 * LANES :])
        for first in range(0, total, step):
            span = slice(first, first + step)
            scores = dot_nt(qkv_ref[head, :, LANES : 2 * LANES], qkv_ref[head, span, :LANES])
            peak = jnp.max(scores, axis=0, keepdims=True)
            shifted = jnp.exp2((scores - peak) * SCALE2)
            sums = jnp.sum(shifted, axis=0, keepdims=True)
            mixed = dot(vt_ref[...], shifted.astype(BF16)) / sums
            ot_ref[head * HEAD_DIM : (head + 1) * HEAD_DIM, span] = mixed[:HEAD_DIM]
            lse_ref[head, :, span] = peak * SCALE2 + jnp.log2(sums)
        if head % 2 == 1:
            half = pl.ds((head - 1) * HEAD_DIM, 2 * HEAD_DIM)
            for part in (3, 1, 2, 0):
                go_ref[part, half] = ot_ref[half, part * rows : part * rows + images].astype(BF16)
                if part:
                    go.append(wires.copy(go_ref.at[part, half], ctx_hbm.at[part, half], to[part]))
                    go[-1].start()
                else:
                    keeps.append(moves.start(go_ref.at[0, half], ctx_hbm.at[0, half]))
    for part in (3, 1, 2, 0):
        rest_ref[part] = split_lanes(ot_ref[:, part * rows : (part + 1) * rows])[1]
        if part:
            go.append(wires.copy(rest_ref.at[part], rest_hbm.at[part], to[part]))
            go[-1].start()
        else:
            keeps.append(moves.start(rest_ref.at[0], rest_hbm.at[0]))
    swap.arrive()
    cot_on.arrive()
    for wire in go:
        wire.arrive()
    for copy in keeps + [keep, out]:
        copy.wait()
    wires.drain()


def start_stage(depth, length, x, x_cond, s, s_cond, cot, cot_cond, w, bias, gain, shift, qkv_w):
    images, width = x.shape
    slots = SLOTS // 4
    rows = images + slots
    heads = HEADS // 4
    own = heads * HEAD_DIM
    window = (max(p * own % LANES for p in range(4)) + own + LANES - 1) // LANES * LANES
    block = 2 * width // (2 * depth)
    vmem, hbm = pl.BlockSpec(memory_space=pltpu.VMEM), pl.BlockSpec(memory_space=pl.ANY)
    b = lambda *shape: jax.ShapeDtypeStruct(shape, BF16)
    v = lambda *shape: pltpu.VMEM(shape, BF16)
    return pl.pallas_call(
        functools.partial(start_kernel, window),
        in_specs=[pl.BlockSpec(memory_space=pltpu.SMEM)] + [vmem] * 10 + [hbm],
        out_specs=[vmem, hbm, vmem, vmem, hbm, hbm, vmem, hbm, vmem, hbm, hbm, hbm],
        out_shape=[
            jax.ShapeDtypeStruct((rows, width), F32),
            b(4, rows, width),
            b(width, heads * 3 * LANES),
            b(heads, 4 * rows, 3 * LANES),
            b(depth, block, rows),
            b(depth, block, rows),
            b(rows, width),
            b(2, rows, width),
            jax.ShapeDtypeStruct((heads, 1, 4 * rows), F32),
            b(4, own, images),
            b(4, (own // 4 + 15) // 16 * 16, LANES),
            b(2, rows, width),
        ],
        scratch_shapes=[
            v(SLOTS, width), v(rows, width), v(rows, width), v(4, rows, width),
            v(depth, 2, block, rows), v(width, 3 * width),
            v(LANES, 4 * rows), pltpu.VMEM((own, 4 * rows), F32), v(4, own, images),
            v(4, (own // 4 + 15) // 16 * 16, LANES),
            pltpu.SemaphoreType.DMA((32,)), pltpu.SemaphoreType.DMA((32,)), pltpu.SemaphoreType.DMA((16,)),
        ],
        compiler_params=pltpu.CompilerParams(
            vmem_limit_bytes=VMEM_LIMIT, collective_id=1, has_side_effects=True
        ),
        cost_estimate=cost(12 * rows * width * width, 12 * width * width),
        name="start_stage",
    )(length, x, x_cond, s, s_cond, cot, cot_cond, w, bias, gain, shift, qkv_w)


def split_lanes(value):
    size = value.shape[0] // 4
    cut = value.shape[1] - 32
    rest = jnp.concatenate([value[i * size : (i + 1) * size, cut:] for i in range(4)], 1)
    room = (size + 15) // 16 * 16
    rest = jnp.concatenate([rest, jnp.zeros((room - size, 4 * 32), F32)], 0)
    return value[:, :cut].astype(BF16), rest.astype(BF16)


def join_lanes(main, rest):
    size = main.shape[0] // 4
    rest = rest.astype(F32)
    rest = jnp.concatenate([rest[:size, i * 32 : (i + 1) * 32] for i in range(4)], 0)
    return jnp.concatenate([main.astype(F32), rest], 1)


def both(own_t, peer_t, own, peer):
    rows = own_t.shape[-1]
    cut = rows // 256 * 256
    total = dot(own_t[:, :cut], own[:cut]) + dot(peer_t[:, :cut], peer[:cut])
    ends_t = jnp.concatenate([own_t[:, cut:], peer_t[:, cut:]], 1)
    return total + dot(ends_t, jnp.concatenate([own[cut:], peer[cut:]], 0))


def middle_kernel(
    ctx_t_ref,
    ctx_rest_ref,
    hidden_ref,
    cot_ref,
    proj_ref,
    proj_bias_ref,
    gain_ref,
    shift_ref,
    fc2_bias_ref,
    fc1_bias_ref,
    cot_zz,
    fc1_hbm,
    fc2_hbm,
    out_hbm,
    c_all,
    d_middle_ref,
    late_hbm,
    d_ctx_hbm,
    d_rest_hbm,
    vec_ref,
    fc1_vec_ref,
    normed_x,
    normed_cond_x,
    d_pre_go,
    active_go,
    active_cond_go,
    active_near,
    active_cond_near,
    cot_far,
    fc1_ref,
    fc2_ref,
    bias_ref,
    normed_ref,
    middle_ref,
    acc_out,
    acc_back,
    normed_t,
    ctx_two,
    ctx_peer,
    active_t,
    active_pack,
    d_pre,
    d_branch_ref,
    d_branch_peer,
    d_go,
    d_rest,
    proj_stage,
    c_own,
    send_sems,
    recv_sems,
    local_sems,
):
    rows, width = cot_ref.shape
    slots = c_own.shape[0]
    images = rows - slots
    depth, _, small, _ = ctx_two.shape
    chunk = fc1_ref.shape[2]
    own = ctx_t_ref.shape[1]
    quarter = chunk // 8
    place, index = lax.axis_index("seq"), lax.axis_index("batch")
    chip, core = index // 2, index % 2
    to, other, up_to, down_to = ends_of(place, index, depth)
    moves = Locals(local_sems)

    def load(i):
        span = pl.ds(pl.multiple_of((chip + AWAY[i]) % depth * chunk, LANES), chunk)
        return (
            moves.start(fc1_hbm.at[:, span], fc1_ref.at[i % 2]),
            moves.start(fc2_hbm.at[span], fc2_ref.at[i % 2]),
        )

    loads = [load(0), load(1)]
    greet([to[1], to[2], to[3], other] + line_of(place, index, depth))
    wires = Wires(send_sems, recv_sems)
    hop = Hop(
        wires, depth, chip, up_to, down_to, 2, cot_zz.at[0], cot_zz.at[1], cot_far, cot_far
    )
    hop.start()
    for f in range(4):
        bias_ref[f : f + 1] = fc1_bias_ref[f * chunk : (f + 1) * chunk].reshape(1, -1)

    branch = proj_bias_ref[...].reshape(1, -1) + hidden_ref[...]
    for k in range(4):
        at = pl.ds(pl.multiple_of(flip(place, k) * own, 16), own)
        context_t = join_lanes(ctx_t_ref[k], ctx_rest_ref[k])
        branch += dot(context_t.T.astype(BF16), proj_ref[at, :])
        for i in range(2):
            ctx_two[flip(place, k), i] = context_t[i * small : (i + 1) * small].astype(BF16)
    ctx_swap = wires.copy(ctx_two.at[:, 1 - core], ctx_peer, other)
    ctx_swap.start()
    middle_ref[...] = branch
    scaled, _ = normalize(branch)
    gain = gain_ref[...].reshape(1, -1)
    normed = scaled * gain + shift_ref[...].reshape(1, -1)
    normed_ref[...] = normed.astype(BF16)
    normed_t[...] = normed[:images].T.astype(BF16)
    normed_go = Spread(wires, to, normed_x, normed_t)
    normed_go.start()
    keeps = [
        moves.start(normed_t, normed_x.at[0]),
        moves.start(normed_ref.at[pl.ds(images, slots)], normed_cond_x.at[0]),
    ]
    cond_go = [
        wires.copy(normed_ref.at[pl.ds(images, slots)], normed_cond_x.at[k], to[k]) for k in (1, 2, 3)
    ]
    for wire in cond_go:
        wire.start()

    near = []
    for i in range(4):
        f = (chip + AWAY[i]) % depth
        for copy in loads[i]:
            copy.wait()
        fc1, fc2 = fc1_ref.at[i % 2], fc2_ref.at[i % 2]
        before = dot(normed_ref[...], fc1[...]) + bias_ref[pl.ds(f, 1)]
        cdf = 0.5 + 0.5 * lax.erf(before * math.sqrt(0.5))
        active = before * cdf
        slope = cdf + before * (jnp.exp(-0.5 * before * before) * (1.0 / math.sqrt(2.0 * math.pi)))
        d_before = dot_nt(cot_ref[...], fc2[...]) * slope
        fc1_vec_ref[pl.ds(f, 1)] = jnp.sum(d_before, axis=0, keepdims=True)
        d_pre[i] = d_before.astype(BF16)
        keeps.append(moves.start(d_pre.at[i], d_pre_go.at[f]))
        flat = active.T
        for c in range(2):
            for j in range(4):
                piece = flat[(c * 4 + j) * quarter : (c * 4 + j + 1) * quarter]
                active_t[i, c, j] = piece[:, :images].astype(BF16)
            active_pack[i, c] = jnp.concatenate(
                [flat[(c * 4 + j) * quarter : (c * 4 + j + 1) * quarter, images:] for j in range(4)], 1
            ).astype(BF16)
        if i < 2:
            for c in range(2):
                device = (f * 2 + c, place)
                near.append(
                    wires.by_core(core, active_t.at[i, c], active_near.at[i, core], device)
                )
                near.append(
                    wires.by_core(core, active_pack.at[i, c], active_cond_near.at[i, core], device)
                )
            for wire in near[4 * i :]:
                wire.start()
        else:
            keeps.append(moves.start(active_t.at[i], active_go.at[i - 2]))
            keeps.append(moves.start(active_pack.at[i], active_cond_go.at[i - 2]))
        forward = dot(active.astype(BF16), fc2[...])
        backward = dot_nt(d_pre[i], fc1[...])
        if i == 0:
            acc_out[...] = forward
            acc_back[...] = backward
        else:
            acc_out[...] += forward
            acc_back[...] += backward
        if i + 2 < 4:
            loads.append(load(i + 2))
        if i == 1:
            normed_go.relay()

    middle = middle_ref[...]
    scaled, factor = normalize(middle)
    upstream = acc_back[...]
    cot = cot_ref[...].astype(F32)
    d_middle = cot + norm_back(upstream, scaled, factor, gain)
    d_middle_ref[...] = d_middle
    d_branch_ref[...] = d_middle.astype(BF16)
    branch_swap = wires.copy(d_branch_ref, d_branch_peer, other)
    branch_swap.start()
    go = []
    for k in (3, 1, 2, 0):
        at = pl.ds(pl.multiple_of(flip(place, k) * own, 16), own)
        d_go[k], d_rest[k] = split_lanes(dot_nt(d_branch_ref[...], proj_ref[at, :]))
        for src, dst in ((d_go, d_ctx_hbm), (d_rest, d_rest_hbm)):
            if k:
                go.append(wires.copy(src.at[k], dst.at[k], to[k]))
                go[-1].start()
            else:
                keeps.append(moves.start(src.at[0], dst.at[0]))
    acc_out[...] = middle + acc_out[...] + fc2_bias_ref[...].reshape(1, -1)
    keeps.append(moves.start(acc_out.at[pl.ds(0, images)], out_hbm))
    c_own[...] = acc_out[images:].astype(BF16)
    c_go = [wires.copy(c_own, c_all.at[k], to[k]) for k in (3, 1, 2)]
    keeps.append(moves.start(c_own, c_all.at[0]))
    for wire in c_go:
        wire.start()
    vec_ref[0:1] = jnp.sum(upstream * scaled, axis=0, keepdims=True)
    vec_ref[1:2] = jnp.sum(upstream, axis=0, keepdims=True)
    vec_ref[2:3] = jnp.sum(d_middle, axis=0, keepdims=True)
    vec_ref[3:4] = jnp.sum(cot, axis=0, keepdims=True)
    vec_ref[4:] = jnp.zeros((4, width), F32)
    ctx_swap.arrive()
    branch_swap.arrive()
    proj_stage[...] = (
        both(
            ctx_two[:, core].reshape(depth * small, rows),
            ctx_peer[...].reshape(depth * small, rows),
            d_branch_ref[...],
            d_branch_peer[...],
        )
        .astype(BF16)
        .reshape(depth, small, width)
    )
    keeps.append(moves.start(proj_stage, late_hbm))
    for wire in c_go + cond_go + go:
        wire.arrive()
    hop.arrive()
    for i in range(2):
        arrive_by_core(near[4 * i : 4 * i + 4], core)
    normed_go.finish()
    for copy in keeps:
        copy.wait()
    wires.drain()


def middle_stage(
    depth, ctx_t, ctx_rest, hidden, cot, proj, proj_bias, gain, shift, fc2_bias, fc1_bias, cot_zz, fc1, fc2
):
    rows, width = hidden.shape
    slots = SLOTS // 4
    images = rows - slots
    ff = fc1.shape[1]
    small = width // (2 * depth)
    own = ctx_t.shape[1]
    chunk = ff // 4
    quarter = chunk // 8
    vmem, hbm = pl.BlockSpec(memory_space=pltpu.VMEM), pl.BlockSpec(memory_space=pl.ANY)
    f = lambda *shape: jax.ShapeDtypeStruct(shape, F32)
    b = lambda *shape: jax.ShapeDtypeStruct(shape, BF16)
    v = lambda *shape: pltpu.VMEM(shape, BF16)
    vf = lambda *shape: pltpu.VMEM(shape, F32)
    return pl.pallas_call(
        middle_kernel,
        in_specs=[vmem] * 10 + [hbm] * 3,
        out_specs=[hbm, hbm, vmem, hbm, hbm, hbm, vmem, vmem] + [hbm] * 8,
        out_shape=[
            f(images, width),
            b(4, slots, width),
            f(rows, width),
            b(depth, small, width),
            b(4, rows, own - 32),
            b(4, (rows // 4 + 15) // 16 * 16, LANES),
            f(8, width),
            f(4, chunk),
            b(4, width, images),
            b(4, slots, width),
            b(4, rows, chunk),
            b(2, 2, 4, quarter, images),
            b(2, 2, quarter, 4 * slots),
            b(2, 2, 4, quarter, images),
            b(2, 2, quarter, 4 * slots),
            b(rows, width),
        ],
        scratch_shapes=[
            v(2, width, chunk), v(2, chunk, width), vf(4, chunk),
            v(rows, width), vf(rows, width), vf(rows, width), vf(rows, width),
            v(width, images),
            v(depth, 2, small, rows), v(depth, small, rows),
            v(4, 2, 4, quarter, images), v(4, 2, quarter, 4 * slots),
            v(4, rows, chunk),
            v(rows, width), v(rows, width),
            v(4, rows, own - 32),
            v(4, (rows // 4 + 15) // 16 * 16, LANES),
            v(depth, small, width),
            v(slots, width),
            pltpu.SemaphoreType.DMA((48,)), pltpu.SemaphoreType.DMA((48,)), pltpu.SemaphoreType.DMA((48,)),
        ],
        compiler_params=pltpu.CompilerParams(
            vmem_limit_bytes=VMEM_LIMIT, collective_id=3, has_side_effects=True
        ),
        cost_estimate=cost(8 * rows * width * ff, 8 * width * ff),
        name="middle_stage",
    )(ctx_t, ctx_rest, hidden, cot, proj, proj_bias, gain, shift, fc2_bias, fc1_bias, cot_zz, fc1, fc2)


def attend_back_send_kernel(
    d_ref, d_rest_ref, qkv_ref, lse_ref, w_ref,
    normed_x, normed_cond_x, d_pre_go, active_go, active_cond_go, cot_hbm, cot_z, cot_zz, cot_far,
    dt_ref, lead_ref, tail_ref,
    normed_peer, normed_cond_peer, d_pre_x, active_x, active_cond_x, cot_peer,
    dot_all, dt_all, d_all, dk_ref, dv_ref, send_sems, recv_sems,
):
    head = pl.program_id(0)
    depth = lax.axis_size("batch") // 2
    place, index = lax.axis_index("seq"), lax.axis_index("batch")
    chip, core = index // 2, index % 2
    to, other, _, _ = ends_of(place, index, depth)
    wires = Wires(send_sems, recv_sems)
    links = [wires.copy(d_pre_go.at[flip(place, k)], d_pre_x.at[k - 1], to[k]) for k in (3, 1, 2)]
    far = []
    for c in range(2):
        device = ((chip + AWAY[2]) % depth * 2 + c, place)
        far.append(wires.by_core(core, active_go.at[0, c], active_x.at[0, core], device))
        far.append(wires.by_core(core, active_cond_go.at[0, c], active_cond_x.at[0, core], device))
    links += [
        wires.copy(active_go.at[1, 1 - core], active_x.at[1, core], other),
        wires.copy(active_cond_go.at[1, 1 - core], active_cond_x.at[1, core], other),
        wires.copy(normed_x.at[:, :, 1 - core], normed_peer, other),
        wires.copy(normed_cond_x, normed_cond_peer, other),
        wires.copy(cot_hbm, cot_peer.at[0], other),
        wires.copy(cot_z, cot_peer.at[pl.ds(1, 2)], other),
        wires.copy(cot_zz, cot_peer.at[pl.ds(3, 2)], other),
        wires.copy(cot_far, cot_peer.at[5], other),
    ]
    @pl.when(head == 0)
    def _():
        greet([to[1], to[2], to[3], other] + line_of(place, index, depth))
        for wire in far + links:
            wire.start()

    total = qkv_ref.shape[1]
    rows = total // 4
    half = rows // 2
    own = dot_all.shape[0]

    @pl.when(head == 0)
    def _():
        for part in range(4):
            dot_all[:, pl.ds(part * rows, rows)] = join_lanes(d_ref[part], d_rest_ref[part]).T

    base = pl.multiple_of(head * HEAD_DIM, 8)
    upstream_t = jnp.concatenate(
        [dot_all[pl.ds(base, HEAD_DIM), :], jnp.zeros((LANES - HEAD_DIM, total), F32)], 0
    )
    upstream = upstream_t.T.astype(BF16)
    upstream_t = upstream_t.astype(BF16)
    key = qkv_ref[0, :, LANES : 2 * LANES]
    key_t = turned(key)
    value = qkv_ref[0, :, 2 * LANES :]
    lane = pl.multiple_of(head * 3 * LANES, LANES)
    step = 3 * LANES
    for start in range(0, total, step):
        query = qkv_ref[0, pl.ds(start, step), :LANES]
        probs = jnp.exp2(dot_nt(key, query) * SCALE2 - lse_ref[0, :, pl.ds(start, step)])
        d_probs = dot(value, upstream_t[:, start : start + step])
        delta = jnp.sum(probs * d_probs, axis=0, keepdims=True)
        d_raw = (probs * (d_probs - delta)).astype(BF16)
        d_value = dot(probs.astype(BF16), upstream[start : start + step])
        d_key = dot(d_raw, query)
        if start == 0:
            dv_ref[...] = d_value
            dk_ref[...] = d_key
        else:
            dv_ref[...] += d_value
            dk_ref[...] += d_key
        d_query = dot(key_t, d_raw) * SCALE
        dt_all[pl.ds(base, HEAD_DIM), pl.ds(start, step)] = d_query[:HEAD_DIM]
        d_all[pl.ds(start, step), pl.ds(lane, LANES)] = d_query.T.astype(BF16)
    d_key = dk_ref[...] * SCALE
    d_value = dv_ref[...]
    dt_all[pl.ds(pl.multiple_of(own + base, 8), HEAD_DIM)] = d_key.T[:HEAD_DIM]
    dt_all[pl.ds(pl.multiple_of(2 * own + base, 8), HEAD_DIM)] = d_value.T[:HEAD_DIM]
    d_all[:, pl.ds(pl.multiple_of(lane + LANES, LANES), LANES)] = d_key.astype(BF16)
    d_all[:, pl.ds(pl.multiple_of(lane + 2 * LANES, LANES), LANES)] = d_value.astype(BF16)

    @pl.when(head == pl.num_programs(0) - 1)
    def _():
        for part in (3, 1, 2, 0):
            update = dot_nt(d_all[pl.ds(part * rows, rows)], w_ref[...])
            lead_ref[part] = update[:half].astype(BF16)
            tail_ref[part] = update[half:].astype(BF16)
        dt_ref[...] = dt_all[...].astype(BF16)

    @pl.when(head == pl.num_programs(0) - 1)
    def _():
        for wire in links:
            wire.arrive()
        arrive_by_core(far, core)
        wires.drain()


def attend_back_send(
    d_context, d_rest, qkv, lse, w_heads, normed_x, normed_cond_x, d_pre_go, active_go, active_cond_go,
    cot, cot_z, cot_zz, cot_far,
):
    heads, total, _ = qkv.shape
    width = w_heads.shape[0]
    rows = total // 4
    own = heads * HEAD_DIM
    whole = lambda *shape: pl.BlockSpec(shape, lambda h: (0,) * len(shape))
    hbm = pl.BlockSpec(memory_space=pl.ANY)
    b = lambda *shape: jax.ShapeDtypeStruct(shape, BF16)
    v = lambda *shape: pltpu.VMEM(shape, BF16)
    shape = normed_x.shape
    return pl.pallas_call(
        attend_back_send_kernel,
        grid=(heads,),
        in_specs=[
            whole(*d_context.shape),
            whole(*d_rest.shape),
            pl.BlockSpec((1, total, 3 * LANES), lambda h: (h, 0, 0)),
            pl.BlockSpec((1, 1, total), lambda h: (h, 0, 0)),
            whole(*w_heads.shape),
        ]
        + [hbm] * 9,
        out_specs=[
            whole(3 * own, total),
            whole(4, rows // 2, width),
            whole(4, rows // 2, width),
        ]
        + [hbm] * 6,
        out_shape=[
            b(3 * own, total),
            b(4, rows // 2, width),
            b(4, rows // 2, width),
            b(shape[0], shape[1], *shape[3:]),
            b(*normed_cond_x.shape),
            b(3, *d_pre_go.shape[1:]),
            b(*active_go.shape),
            b(*active_cond_go.shape),
            b(6, *cot.shape),
        ],
        scratch_shapes=[
            pltpu.VMEM((own, total), F32),
            pltpu.VMEM((3 * own, total), F32),
            pltpu.VMEM((total, heads * 3 * LANES), BF16),
            pltpu.VMEM((total, LANES), F32),
            pltpu.VMEM((total, LANES), F32),
            pltpu.SemaphoreType.DMA((48,)),
            pltpu.SemaphoreType.DMA((48,)),
        ],
        compiler_params=pltpu.CompilerParams(
            vmem_limit_bytes=VMEM_LIMIT, collective_id=4, has_side_effects=True
        ),
        cost_estimate=cost(
            2 * heads * total * (width * 3 * LANES + 10 * LANES * total), 12 * total * width
        ),
        name="attend_back_send",
    )(
        d_context, d_rest, qkv, lse, w_heads, normed_x, normed_cond_x, d_pre_go, active_go, active_cond_go,
        cot, cot_z, cot_zz, cot_far,
    )


def finish_kernel(
    p_hbm, f_hbm, g_hbm, q_hbm, s_hbm, c_hbm, out_c_hbm, vec_ref, out_hbm, din_hbm, dskip_hbm,
    g_fc2_hbm, g_proj_hbm, g_first_hbm, g_heads_hbm, g_skip_hbm,
    o_out, o_din, o_dskip, o_out_cond, o_din_cond, o_dskip_cond,
    v0, v1, v2, v3, v4, v5, v6, fc1_vec_ref,
    p_in, f_in, g_in, q_in, s_in, c_in, out_c_in, p_st, f_st, g_st, q_st, s_st, cond_st, rows_st, sems,
):
    width = out_hbm.shape[1]
    place, index = lax.axis_index("seq"), lax.axis_index("batch")
    batch = lax.axis_size("batch")
    moves = Locals(sems)
    loads = [
        moves.start(src, dst)
        for src, dst in (
            (f_hbm, f_in), (g_hbm, g_in), (q_hbm, q_in), (s_hbm, s_in), (p_hbm, p_in),
            (c_hbm, c_in),
            (out_c_hbm, out_c_in),
        )
    ]
    rows_in = [
        moves.start(src, rows_st.at[i]) for i, src in enumerate((out_hbm, din_hbm, dskip_hbm))
    ]
    done = []
    for i, dst in enumerate((o_out, o_din, o_dskip)):
        rows_in[i].wait()
        done.append(moves.start(rows_st.at[i], dst.at[:, 0]))
    loads[0].wait()
    for j in range(4):
        f_st[:, j * width : (j + 1) * width] = f_in[flip(place, j)].astype(F32)
    done.append(moves.start(f_st, g_first_hbm))
    loads[1].wait()
    small = g_in.shape[1]
    for j in range(4):
        g_st[j * small : (j + 1) * small] = g_in[flip(place, j)].astype(F32)
    done.append(moves.start(g_st, g_fc2_hbm))
    loads[2].wait()
    size = q_in.shape[2] // 3
    for j in range(4):
        value = q_in[flip(place, j)].astype(F32)
        for which in range(3):
            at = (which * 4 + j) * size
            q_st[:, at : at + size] = value[:, which * size : (which + 1) * size]
    done.append(moves.start(q_st, g_heads_hbm))
    loads[3].wait()
    size = s_st.shape[0] // 4
    for j in range(4):
        s_st[j * size : (j + 1) * size] = s_in[flip(place, j), :size].astype(F32)
    done.append(moves.start(s_st, g_skip_hbm))
    for copy in loads[4:]:
        copy.wait()
    p_st[...] = p_in[...].astype(F32)
    done.append(moves.start(p_st, g_proj_hbm))
    slots = c_in.shape[1]
    for j in range(4):
        span = slice(j * slots, (j + 1) * slots)
        piece = c_in[flip(place, j)].astype(F32)
        cond_st[0, span] = out_c_in[flip(place, j)].astype(F32)
        cond_st[1, span] = piece[:, :width]
        cond_st[2, span] = piece[:, width:]
    conds = o_out_cond.shape[0]
    for i, ref in enumerate((o_out_cond, o_din_cond, o_dskip_cond)):
        ref[:, 0] = cond_st[i, :conds]
    share = width // batch
    vectors = vec_ref[...]
    rolled = pltpu.roll(vectors, lax.rem(width - index * share, width), 1)
    for row, ref in zip((0, 1, 2, 5, 3, 4, 6), (v0, v1, v2, v3, v4, v5, v6)):
        ref[...] = rolled[row, :share]
    share = 4 * width // batch
    per = width // share
    vector = vec_ref[pl.ds(8 + index // per, 1)]
    vector = pltpu.roll(vector, lax.rem(width - index % per * share, width), 1)
    fc1_vec_ref[...] = vector[0, :share]
    for copy in done:
        copy.wait()


def finish_stage(batch, conds, slots_of, out_c, vec, out, d_image, d_skip):
    p_all, f_all, g_all, q_all, s_all, c_all = slots_of
    images, width = out.shape
    small = f_all.shape[1]
    skip_rows = 2 * width // batch
    large = 4 * width // batch
    slots = c_all.shape[1]
    vmem, hbm = pl.BlockSpec(memory_space=pltpu.VMEM), pl.BlockSpec(memory_space=pl.ANY)
    f = lambda *shape: jax.ShapeDtypeStruct(shape, F32)
    like = lambda a: pltpu.VMEM(a.shape, a.dtype)
    vf = lambda *shape: pltpu.VMEM(shape, F32)
    return pl.pallas_call(
        finish_kernel,
        in_specs=[hbm] * 7 + [vmem] + [hbm] * 3,
        out_specs=[hbm] * 8 + [vmem] * 11,
        out_shape=[
            f(large, width), f(small, width), f(small, 4 * width), f(small, 4 * q_all.shape[2]),
            f(skip_rows, width), f(images, 1, width), f(images, 1, width), f(images, 1, width),
            f(conds, 1, width), f(conds, 1, width), f(conds, 1, width),
        ]
        + [f(width // batch)] * 7
        + [f(large)],
        scratch_shapes=[
            like(p_all), like(f_all), like(g_all), like(q_all), like(s_all), like(c_all), like(out_c),
            vf(small, width), vf(small, 4 * width), vf(large, width), vf(small, 4 * q_all.shape[2]),
            vf(skip_rows, width), vf(3, 4 * slots, width), vf(3, images, width),
            pltpu.SemaphoreType.DMA((24,)),
        ],
        compiler_params=params(),
        cost_estimate=cost(1e6, 2e7),
        name="finish_stage",
    )(*slots_of, out_c, vec, out, d_image, d_skip)


def per_device(
    batch,
    parts,
    image_in,
    cond_in,
    skip_image,
    skip_cond,
    caption_len,
    skip_weight,
    skip_bias,
    first_gain,
    first_bias,
    qkv_weight,
    proj_weight,
    proj_bias,
    second_gain,
    second_bias,
    fc1_weight,
    fc1_bias,
    fc2_weight,
    fc2_bias,
    grad_image,
    grad_cond,
):
    conds = cond_in.shape[0]
    width = image_in.shape[2]
    images = image_in.shape[0]
    ff = fc1_weight.shape[1]
    slots = SLOTS // parts
    rows = slots + images
    total = rows * parts
    heads = HEADS // parts
    depth = batch // 2
    place = lax.axis_index("seq")
    index = lax.axis_index("batch")
    core, chip = index % 2, index // 2
    where = jnp.stack([core, place]).astype(jnp.int32)

    fast = parts == 4 and depth == 4 and (ff // parts) % LANES == 0
    if fast:
        (
            hidden, normed_all, w_heads, qkv, joined, joined_peer, cot, cot_z, lse, ctx_t, ctx_rest,
            cot_zz,
        ) = start_stage(
            depth, caption_len, image_in[:, 0], cond_in[:, 0], skip_image[:, 0], skip_cond[:, 0],
            grad_image[:, 0], grad_cond[:, 0], skip_weight, skip_bias, first_gain, first_bias,
            qkv_weight,
        )
        normed_all = normed_all.reshape(total, width)
        (
            out, out_c, d_middle, late, d_ctx, d_rest, vec_two, fc1_vec, normed_x, normed_cond_x, d_pre_go,
            active_go, active_cond_go, active_near, active_cond_near, cot_far,
        ) = middle_stage(
            depth, ctx_t, ctx_rest, hidden, cot, proj_weight, proj_bias, second_gain, second_bias, fc2_bias,
            fc1_bias, cot_zz, fc1_weight, fc2_weight,
        )
        normed_x = normed_x.reshape(4, depth, 2, width // batch, images)
        (
            d_triple_t, lead, tail, normed_peer, normed_cond_peer, d_pre_x, active_x, active_cond_x,
            cot_peer,
        ) = attend_back_send(
            d_ctx, d_rest, qkv, lse, w_heads, normed_x, normed_cond_x, d_pre_go, active_go,
            active_cond_go, cot, cot_z, cot_zz, cot_far,
        )
        feeds = (
            normed_x, normed_peer, normed_cond_x, normed_cond_peer, d_pre_go, d_pre_x, active_go,
            active_near, active_x, active_cond_go, active_cond_near, active_cond_x, cot, cot_z,
            cot_zz, cot_far, cot_peer,
        )
        *slots_of, d_image, d_skip, vec = reduce_all(
            late, lead, tail, normed_all, d_triple_t, joined, joined_peer, hidden, d_middle,
            skip_weight, feeds, first_gain, vec_two, fc1_vec,
        )
        (
            wgrad_fc2, wgrad_proj, wgrad_fc1, wgrad_qkv, wgrad_skip, out_image, d_image, d_skip,
            out_cond, d_cond, d_skip_cond, *vec,
        ) = finish_stage(batch, conds, slots_of, out_c, vec, out, d_image, d_skip)
        return (
            out_image, out_cond, d_image, d_cond, d_skip, d_skip_cond, wgrad_skip, vec[0],
            vec[1], vec[2], wgrad_qkv, wgrad_proj, vec[3], vec[4], vec[5], wgrad_fc1, vec[7],
            wgrad_fc2, vec[6],
        )

    def own_rows(cond, image):
        padded = jnp.pad(cond[:, 0], ((0, SLOTS - conds), (0, 0)))
        lead = lax.dynamic_slice_in_dim(padded, place * slots, slots, 0)
        return jnp.concatenate([lead, image[:, 0]], 0)

    x = own_rows(cond_in, image_in)
    s = own_rows(skip_cond, skip_image)
    cot = own_rows(grad_cond, grad_image)

    hidden, normed, joined_t = pre(
        x, s, skip_weight, skip_bias[None], first_gain[None], first_bias[None]
    )
    normed_all = jnp.concatenate(everywhere(normed, parts), 0)
    own = heads * HEAD_DIM
    w_heads = heads_weight(where[1:], qkv_weight, heads)
    order = place ^ jnp.arange(parts, dtype=jnp.int32)
    position = order[:, None] * slots + jnp.arange(rows, dtype=jnp.int32)[None]
    valid = (jnp.arange(rows)[None] >= slots) | (position <= caption_len[0])
    kbias = jnp.where(
        (jnp.arange(LANES) == HEAD_DIM)[None] & ~valid.reshape(total, 1), F32(-1e30), F32(0)
    )
    qkv, lse, *ctx_parts = attend(parts, normed_all, w_heads, kbias)
    context = [ctx_parts[0]] + [across(ctx_parts[k], parts, k) for k in range(1, parts)]

    zero = jnp.zeros_like(proj_bias)
    vecs = jnp.stack([proj_bias, second_gain, second_bias, fc2_bias, zero, zero, zero, zero])
    (
        out,
        d_middle,
        d_branch,
        active_t,
        d_pre,
        normed2_t,
        ctx_t,
        vec_two,
        fc1_bias_grad,
        *d_ctx_parts,
    ) = mlp(
        parts,
        where[1:],
        context,
        hidden,
        cot,
        proj_weight,
        vecs,
        fc1_weight,
        fc1_bias[None],
        fc2_weight,
    )
    d_context = [d_ctx_parts[0]] + [across(d_ctx_parts[k], parts, k) for k in range(1, parts)]

    def by_core(turned_rows):
        blocks = turned_rows.reshape(depth, 2, -1, rows)
        send = lax.dynamic_index_in_dim(blocks, 1 - core, 1, keepdims=False)
        return blocks, other_core(send, batch)

    active_b, active_p = by_core(active_t)
    normed2_b, normed2_p = by_core(normed2_t)
    ctx_b, ctx_p = by_core(ctx_t)
    joined_b, joined_p = by_core(joined_t)
    cot_p, d_pre_p, d_branch_p = (other_core(v, batch) for v in (cot, d_pre, d_branch))
    late = pair_grads(
        where, [(active_b, active_p, cot, cot_p), (ctx_b, ctx_p, d_branch, d_branch_p)]
    )
    by_columns = (ff // parts) % LANES == 0
    if by_columns:
        first = column_grads(where, parts, normed2_b, normed2_p, d_pre, d_pre_p)
        late, first, d_context = lax.optimization_barrier((late, first, d_context))
        middle = depth // 2
    if by_columns:
        first = jnp.concatenate(
            [
                scattered(first[:, :middle], parts, bits_of(parts)),
                scattered(first[:, middle:], parts, bits_of(parts)[::-1]),
            ],
            0,
        )
    if not by_columns:
        first = pair_grads(where, [(normed2_b, normed2_p, d_pre, d_pre_p)])
    def all_conds(lead):
        pieces = [lead] + [across(lead, parts, k) for k in range(1, parts)]
        full = jnp.zeros((SLOTS, lead.shape[1]), F32)
        for k in range(parts):
            full = lax.dynamic_update_slice_in_dim(
                full, pieces[k].astype(F32), (place ^ k) * slots, 0
            )
        return full[:conds, None]

    d_triple_t, d_lead, d_tail = attend_back(parts, d_context, qkv, lse, w_heads)
    d_lead = scattered(d_lead, parts, bits_of(parts))
    d_tail = scattered(d_tail, parts, bits_of(parts)[::-1])
    heads_grad = heads_grads(normed_all, d_triple_t).reshape(depth, 2, -1, 3 * own)
    heads_grad = plus(
        lax.dynamic_index_in_dim(heads_grad, core, 1, keepdims=False),
        other_core(lax.dynamic_index_in_dim(heads_grad, 1 - core, 1, keepdims=False), batch),
    )
    heads_grad = everywhere(down_the_line(heads_grad, batch, chip), parts)
    wgrad_qkv = put_heads(where[1:], heads_grad)

    d_in, d_skip, d_low, vec_one = post(
        d_lead, d_tail, hidden, d_middle, first_gain[None], skip_weight
    )
    d_low_p = other_core(d_low, batch)
    last = pair_grads(where, [(joined_b, joined_p, d_low, d_low_p)])

    late = down_the_line(late, batch, chip)
    first = down_the_line(first, batch, chip)
    late = summed(late, parts)
    if by_columns:
        fc1_cols = everywhere(first, parts)
        wgrad_fc1 = put_columns(where[1:], fc1_cols)
    else:
        wgrad_fc1 = summed(first, parts).astype(F32)

    vectors = [
        vec_one[0],
        vec_one[1],
        vec_one[2],
        vec_two[2],
        vec_two[0],
        vec_two[1],
        fc1_bias_grad[0],
        vec_two[3],
    ]
    sizes = [v.shape[0] // batch for v in vectors]
    packed = jnp.concatenate([v.reshape(batch, -1) for v in vectors], 1)
    packed = packed.reshape(depth, 2, -1)
    packed = lax.dynamic_index_in_dim(packed, core, 1, keepdims=False) + other_core(
        lax.dynamic_index_in_dim(packed, 1 - core, 1, keepdims=False), batch
    )
    packed = jnp.pad(packed, ((0, 0), (0, 16 * width - packed.shape[1]))).reshape(depth, 16, width)
    last = jnp.concatenate([last, packed.astype(BF16)], 1)
    last = summed(down_the_line(last, batch, chip), parts)
    skip_rows = 2 * width // batch
    wgrad_skip = last[:skip_rows].astype(F32)
    flat = last[skip_rows:].reshape(-1).astype(F32)
    vector_out, at = [], 0
    for size in sizes:
        vector_out.append(flat[at : at + size])
        at += size
    fc2_rows = ff // batch
    wgrad_fc2 = late[:fc2_rows].astype(F32)
    wgrad_proj = late[fc2_rows:].astype(F32)

    out_cond = all_conds(out[:slots].astype(BF16))
    d_cond = all_conds(jnp.concatenate([d_in[:slots], d_skip[:slots]], 1).astype(BF16))
    return (
        out[slots:, None],
        out_cond,
        d_in[slots:, None],
        d_cond[:, :, :width],
        d_skip[slots:, None],
        d_cond[:, :, width:],
        wgrad_skip,
        vector_out[0],
        vector_out[1],
        vector_out[2],
        wgrad_qkv,
        wgrad_proj,
        vector_out[3],
        vector_out[4],
        vector_out[5],
        wgrad_fc1,
        vector_out[6],
        wgrad_fc2,
        vector_out[7],
    )


def solution(mesh):
    tokens, conds, shared = P("seq", "batch", None), P(None, "batch", None), P()
    return jax.shard_map(
        functools.partial(per_device, mesh.shape["batch"], mesh.shape["seq"]),
        mesh=mesh,
        in_specs=(tokens, conds, tokens, conds, P("batch")) + (shared,) * 13 + (tokens, conds),
        out_specs=(tokens, conds) * 3
        + (
            P("batch", None),
            P("batch"),
            P("batch"),
            P("batch"),
            P("batch", None),
            P("batch", None),
            P("batch"),
            P("batch"),
            P("batch"),
            P("batch", None),
            P("batch"),
            P("batch", None),
            P("batch"),
        ),
        check_vma=False,
    )
```

```python
import functools
import math

import jax
import jax.numpy as jnp
from jax import lax
from jax.experimental import pallas as pl
from jax.experimental.pallas import tpu as pltpu
from jax.sharding import PartitionSpec as P

HEADS = 16
HEAD_DIM = 72
LANES = 128
SLOTS = 128
F32 = jnp.float32
BF16 = jnp.bfloat16
VMEM_LIMIT = 60 * 1024 * 1024
SCALE = 1.0 / math.sqrt(HEAD_DIM)
SCALE2 = SCALE * math.log2(math.e)


def dot(left, right):
    return jnp.dot(left, right, preferred_element_type=F32)


def dot_nt(left, right):
    return lax.dot_general(left, right, (((1,), (1,)), ((), ())), preferred_element_type=F32)


def dot_tn(left, right):
    return lax.dot_general(left, right, (((0,), (0,)), ((), ())), preferred_element_type=F32)


def params():
    return pltpu.CompilerParams(vmem_limit_bytes=VMEM_LIMIT)


def cost(flops, nbytes):
    return pl.CostEstimate(flops=int(flops), bytes_accessed=int(nbytes), transcendentals=0)


def turned(value):
    return value.astype(F32).T.astype(BF16)


def normalize(values):
    centre = values - jnp.mean(values, axis=-1, keepdims=True)
    factor = lax.rsqrt(jnp.mean(centre * centre, axis=-1, keepdims=True) + 1e-5)
    return centre * factor, factor


def norm_back(upstream, scaled, factor, gain):
    inner = upstream * gain
    centred = inner - jnp.mean(inner, axis=-1, keepdims=True)
    return factor * (centred - scaled * jnp.mean(inner * scaled, axis=-1, keepdims=True))


def pre_kernel(x_ref, s_ref, w_ref, bias_ref, gain_ref, shift_ref, hidden_ref, normed_ref, turn_ref):
    width = x_ref.shape[1]
    hidden = dot(x_ref[...], w_ref[:width]) + dot(s_ref[...], w_ref[width:]) + bias_ref[...]
    hidden_ref[...] = hidden
    scaled, _ = normalize(hidden)
    normed_ref[...] = (scaled * gain_ref[...] + shift_ref[...]).astype(BF16)
    turn_ref[:width] = turned(x_ref[...])
    turn_ref[width:] = turned(s_ref[...])


def pre(x, s, w, bias, gain, shift):
    rows, width = x.shape
    return pl.pallas_call(
        pre_kernel,
        out_shape=(
            jax.ShapeDtypeStruct((rows, width), F32),
            jax.ShapeDtypeStruct((rows, width), BF16),
            jax.ShapeDtypeStruct((2 * width, rows), BF16),
        ),
        compiler_params=params(),
        cost_estimate=cost(4 * rows * width * width, 4 * width * width + 12 * rows * width),
        name="input_linear",
    )(x, s, w, bias, gain, shift)


def heads_weight_kernel(window, place_ref, w_ref, out_ref):
    heads = out_ref.shape[0]
    width = w_ref.shape[0]
    own = heads * HEAD_DIM
    keep = lax.broadcasted_iota(jnp.int32, (width, LANES), 1) < HEAD_DIM
    place = place_ref[0]
    for which in range(3):
        first = place * own + which * width
        start = jnp.minimum(first // LANES * LANES, 3 * width - window)
        value = w_ref[:, pl.ds(pl.multiple_of(start, LANES), window)].astype(F32)
        value = pltpu.roll(value, lax.rem(window - (first - start), window), 1)
        for head in range(heads):
            turned_back = value if head == 0 else pltpu.roll(value, window - head * HEAD_DIM, 1)
            out_ref[head, :, which * LANES : (which + 1) * LANES] = jnp.where(
                keep, turned_back[:, :LANES], 0.0
            ).astype(BF16)


def heads_weight(place, w, heads):
    width = w.shape[0]
    own = heads * HEAD_DIM
    offsets = [p * own % LANES for p in range(HEADS // heads)]
    window = (max(offsets) + own + LANES - 1) // LANES * LANES
    return pl.pallas_call(
        functools.partial(heads_weight_kernel, window),
        in_specs=[
            pl.BlockSpec(memory_space=pltpu.SMEM),
            pl.BlockSpec(memory_space=pltpu.VMEM),
        ],
        out_shape=jax.ShapeDtypeStruct((heads, width, 3 * LANES), BF16),
        compiler_params=params(),
        cost_estimate=cost(1e6, 2 * w.size + 6 * heads * width * LANES),
        name="heads_weight",
    )(place, w)


def attend_kernel(parts, normed_ref, w_ref, kbias_ref, qkv_ref, lse_ref, *rest):
    ctx_refs, (vt_ref, ot_ref) = rest[:parts], rest[parts:]
    head = pl.program_id(0)
    total = normed_ref.shape[0]
    rows = total // parts
    lane = lax.broadcasted_iota(jnp.int32, (1, LANES), 1)
    one = jnp.where(lane == HEAD_DIM, 1.0, 0.0)
    for part in range(parts):
        span = pl.ds(part * rows, rows)
        triple = dot(normed_ref[span], w_ref[0])
        qkv_ref[0, span, :LANES] = (triple[:, :LANES] + one).astype(BF16)
        qkv_ref[0, span, LANES : 2 * LANES] = (
            triple[:, LANES : 2 * LANES] + kbias_ref[span]
        ).astype(BF16)
        qkv_ref[0, span, 2 * LANES :] = triple[:, 2 * LANES :].astype(BF16)
        vt_ref[:, span] = turned(qkv_ref[0, span, 2 * LANES :])
    step = 3 * LANES if total % (3 * LANES) == 0 else LANES
    for start in range(0, total, step):
        query = qkv_ref[0, pl.ds(start, step), :LANES]
        scores = dot_nt(qkv_ref[0, :, LANES : 2 * LANES], query)
        peak = jnp.max(scores, axis=0, keepdims=True)
        shifted = jnp.exp2((scores - peak) * SCALE2)
        sums = jnp.sum(shifted, axis=0, keepdims=True)
        mixed = dot(vt_ref[...], shifted.astype(BF16)) / sums
        ot_ref[pl.ds(pl.multiple_of(head * HEAD_DIM, 8), HEAD_DIM), pl.ds(start, step)] = mixed[
            :HEAD_DIM
        ]
        lse_ref[0, :, pl.ds(start, step)] = peak * SCALE2 + jnp.log2(sums)

    @pl.when(head == pl.num_programs(0) - 1)
    def _():
        for part in range(parts):
            ctx_refs[part][...] = ot_ref[:, pl.ds(part * rows, rows)].T.astype(BF16)


def attend(parts, normed_all, w_heads, kbias):
    total, width = normed_all.shape
    heads = w_heads.shape[0]
    rows = total // parts
    own = heads * HEAD_DIM
    return pl.pallas_call(
        functools.partial(attend_kernel, parts),
        grid=(heads,),
        in_specs=[
            pl.BlockSpec((total, width), lambda h: (0, 0)),
            pl.BlockSpec((1, width, 3 * LANES), lambda h: (h, 0, 0)),
            pl.BlockSpec((total, LANES), lambda h: (0, 0)),
        ],
        out_specs=[
            pl.BlockSpec((1, total, 3 * LANES), lambda h: (h, 0, 0)),
            pl.BlockSpec((1, 1, total), lambda h: (h, 0, 0)),
        ]
        + [pl.BlockSpec((rows, own), lambda h: (0, 0))] * parts,
        out_shape=[
            jax.ShapeDtypeStruct((heads, total, 3 * LANES), BF16),
            jax.ShapeDtypeStruct((heads, 1, total), F32),
        ]
        + [jax.ShapeDtypeStruct((rows, own), BF16)] * parts,
        scratch_shapes=[pltpu.VMEM((LANES, total), BF16), pltpu.VMEM((own, total), F32)],
        compiler_params=params(),
        cost_estimate=cost(
            2 * heads * total * (width * 3 * LANES + 4 * LANES * total), 6 * total * width
        ),
        name="attend",
    )(normed_all, w_heads, kbias)


def attend_back_kernel(parts, *refs):
    d_refs = refs[:parts]
    (qkv_ref, lse_ref, w_ref, dt_ref, lead_ref, tail_ref) = refs[parts : parts + 6]
    (dot_all, dt_all, acc, dq_ref, dk_ref, dv_ref) = refs[parts + 6 :]
    head = pl.program_id(0)
    heads = pl.num_programs(0)
    total = qkv_ref.shape[1]
    rows = total // parts
    half = rows // 2
    own = dot_all.shape[0]

    @pl.when(head == 0)
    def _():
        for part in range(parts):
            dot_all[:, pl.ds(part * rows, rows)] = d_refs[part][...].astype(F32).T

    base = pl.multiple_of(head * HEAD_DIM, 8)
    upstream_t = jnp.concatenate(
        [dot_all[pl.ds(base, HEAD_DIM), :], jnp.zeros((LANES - HEAD_DIM, total), F32)], 0
    )
    upstream = upstream_t.T.astype(BF16)
    upstream_t = upstream_t.astype(BF16)
    key = qkv_ref[0, :, LANES : 2 * LANES]
    key_t = turned(key)
    value = qkv_ref[0, :, 2 * LANES :]
    step = 3 * LANES if total % (3 * LANES) == 0 else LANES
    for start in range(0, total, step):
        query = qkv_ref[0, pl.ds(start, step), :LANES]
        probs = jnp.exp2(dot_nt(key, query) * SCALE2 - lse_ref[0, :, pl.ds(start, step)])
        d_probs = dot(value, upstream_t[:, start : start + step])
        delta = jnp.sum(probs * d_probs, axis=0, keepdims=True)
        d_raw = (probs * (d_probs - delta) * SCALE).astype(BF16)
        d_value = dot(probs.astype(BF16), upstream[start : start + step])
        d_key = dot(d_raw, query)
        if start == 0:
            dv_ref[...] = d_value
            dk_ref[...] = d_key
        else:
            dv_ref[...] += d_value
            dk_ref[...] += d_key
        d_query = dot(key_t, d_raw)
        dt_all[pl.ds(base, HEAD_DIM), pl.ds(start, step)] = d_query[:HEAD_DIM]
        dq_ref[pl.ds(start, step)] = d_query.T
    dt_all[pl.ds(pl.multiple_of(own + base, 8), HEAD_DIM)] = dk_ref[...].T[:HEAD_DIM]
    dt_all[pl.ds(pl.multiple_of(2 * own + base, 8), HEAD_DIM)] = dv_ref[...].T[:HEAD_DIM]
    for part in range(parts):
        span = pl.ds(part * rows, rows)
        update = (
            dot_nt(dq_ref[span].astype(BF16), w_ref[0, :, :LANES])
            + dot_nt(dk_ref[span].astype(BF16), w_ref[0, :, LANES : 2 * LANES])
            + dot_nt(dv_ref[span].astype(BF16), w_ref[0, :, 2 * LANES :])
        )

        @pl.when(head == 0)
        def _():
            acc[span] = update

        @pl.when(head > 0)
        def _():
            acc[span] += update

    @pl.when(head == heads - 1)
    def _():
        dt_ref[...] = dt_all[...].astype(BF16)
        for part in range(parts):
            lead_ref[part] = acc[pl.ds(part * rows, half)].astype(BF16)
            tail_ref[part] = acc[pl.ds(part * rows + half, half)].astype(BF16)


def attend_back(parts, d_context, qkv, lse, w_heads):
    heads, total, _ = qkv.shape
    width = w_heads.shape[1]
    rows = total // parts
    own = heads * HEAD_DIM
    whole = lambda *shape: pl.BlockSpec(shape, lambda h: (0,) * len(shape))
    return pl.pallas_call(
        functools.partial(attend_back_kernel, parts),
        grid=(heads,),
        in_specs=[whole(rows, own)] * parts
        + [
            pl.BlockSpec((1, total, 3 * LANES), lambda h: (h, 0, 0)),
            pl.BlockSpec((1, 1, total), lambda h: (h, 0, 0)),
            pl.BlockSpec((1, width, 3 * LANES), lambda h: (h, 0, 0)),
        ],
        out_specs=[
            whole(3 * own, total),
            whole(parts, rows // 2, width),
            whole(parts, rows // 2, width),
        ],
        out_shape=[
            jax.ShapeDtypeStruct((3 * own, total), BF16),
            jax.ShapeDtypeStruct((parts, rows // 2, width), BF16),
            jax.ShapeDtypeStruct((parts, rows // 2, width), BF16),
        ],
        scratch_shapes=[
            pltpu.VMEM((own, total), F32),
            pltpu.VMEM((3 * own, total), F32),
            pltpu.VMEM((total, width), F32),
            pltpu.VMEM((total, LANES), F32),
            pltpu.VMEM((total, LANES), F32),
            pltpu.VMEM((total, LANES), F32),
        ],
        compiler_params=params(),
        cost_estimate=cost(
            2 * heads * total * (width * 3 * LANES + 10 * LANES * total), 12 * total * width
        ),
        name="attend_back",
    )(*d_context, qkv, lse, w_heads)


def mlp_kernel(parts, place_ref, *refs):
    ctx_refs = refs[:parts]
    (
        hidden_ref,
        cot_ref,
        proj_ref,
        vec_ref,
        fc1_ref,
        fc1_bias_ref,
        fc2_ref,
        out_ref,
        d_middle_ref,
        d_branch_ref,
        active_t_ref,
        d_pre_ref,
        normed_t_ref,
        ctx_t_ref,
        vec_out_ref,
        fc1_bias_out_ref,
    ) = refs[parts : parts + 16]
    d_ctx_refs = refs[parts + 16 : 2 * parts + 16]
    middle_ref, normed_ref, acc_out, acc_back, turn_ref = refs[2 * parts + 16 :]
    step = pl.program_id(0)
    place = place_ref[0]
    own = ctx_refs[0].shape[1]

    @pl.when(step == 0)
    def _():
        branch = vec_ref[0:1] + hidden_ref[...]
        for part in range(parts):
            at = pl.ds(pl.multiple_of((place ^ part) * own, 8), own)
            branch += dot(ctx_refs[part][...], proj_ref[at, :])
            turn_ref[at] = ctx_refs[part][...].astype(F32).T
        ctx_t_ref[...] = turn_ref[...].astype(BF16)
        middle_ref[...] = branch
        scaled, _ = normalize(branch)
        normed = (scaled * vec_ref[1:2] + vec_ref[2:3]).astype(BF16)
        normed_ref[...] = normed
        normed_t_ref[...] = turned(normed)

    before = dot(normed_ref[...], fc1_ref[...]) + fc1_bias_ref[...]
    cdf = 0.5 + 0.5 * lax.erf(before * math.sqrt(0.5))
    active = (before * cdf).astype(BF16)
    slope = cdf + before * (jnp.exp(-0.5 * before * before) * (1.0 / math.sqrt(2.0 * math.pi)))
    d_before = dot_nt(cot_ref[...], fc2_ref[...]) * slope
    fc1_bias_out_ref[...] = jnp.sum(d_before, axis=0, keepdims=True)
    d_low = d_before.astype(BF16)
    d_pre_ref[...] = d_low
    active_t_ref[...] = turned(active)
    forward = dot(active, fc2_ref[...])
    backward = dot_nt(d_low, fc1_ref[...])

    @pl.when(step == 0)
    def _():
        acc_out[...] = forward
        acc_back[...] = backward

    @pl.when(step > 0)
    def _():
        acc_out[...] += forward
        acc_back[...] += backward

    @pl.when(step == pl.num_programs(0) - 1)
    def _():
        middle = middle_ref[...]
        out_ref[...] = middle + acc_out[...] + vec_ref[3:4]
        scaled, factor = normalize(middle)
        upstream = acc_back[...]
        cot = cot_ref[...].astype(F32)
        d_middle = cot + norm_back(upstream, scaled, factor, vec_ref[1:2])
        d_middle_ref[...] = d_middle
        d_branch = d_middle.astype(BF16)
        d_branch_ref[...] = d_branch
        vec_out_ref[0:1] = jnp.sum(upstream * scaled, axis=0, keepdims=True)
        vec_out_ref[1:2] = jnp.sum(upstream, axis=0, keepdims=True)
        vec_out_ref[2:3] = jnp.sum(d_middle, axis=0, keepdims=True)
        vec_out_ref[3:4] = jnp.sum(cot, axis=0, keepdims=True)
        vec_out_ref[4:] = jnp.zeros((4, vec_out_ref.shape[1]), F32)
        for part in range(parts):
            at = pl.ds(pl.multiple_of((place ^ part) * own, 8), own)
            d_ctx_refs[part][...] = dot_nt(d_branch, proj_ref[at, :]).astype(BF16)


def mlp(parts, place, context, hidden, cot, proj, vecs, fc1, fc1_bias, fc2):
    rows, width = hidden.shape
    ff = fc1.shape[1]
    own = context[0].shape[1]
    chunk = width
    whole = lambda *shape: pl.BlockSpec(shape, lambda i, p: (0,) * len(shape))
    return pl.pallas_call(
        functools.partial(mlp_kernel, parts),
        grid_spec=pltpu.PrefetchScalarGridSpec(
            num_scalar_prefetch=1,
            grid=(ff // chunk,),
            in_specs=[whole(rows, own)] * parts
            + [
                whole(rows, width),
                whole(rows, width),
                whole(width, width),
                whole(8, width),
                pl.BlockSpec((width, chunk), lambda i, p: (0, i)),
                pl.BlockSpec((1, chunk), lambda i, p: (0, i)),
                pl.BlockSpec((chunk, width), lambda i, p: (i, 0)),
            ],
            out_specs=[
                whole(rows, width),
                whole(rows, width),
                whole(rows, width),
                pl.BlockSpec((chunk, rows), lambda i, p: (i, 0)),
                pl.BlockSpec((rows, chunk), lambda i, p: (0, i)),
                whole(width, rows),
                whole(width, rows),
                whole(8, width),
                pl.BlockSpec((1, chunk), lambda i, p: (0, i)),
            ]
            + [whole(rows, own)] * parts,
            scratch_shapes=[
                pltpu.VMEM((rows, width), F32),
                pltpu.VMEM((rows, width), BF16),
                pltpu.VMEM((rows, width), F32),
                pltpu.VMEM((rows, width), F32),
                pltpu.VMEM((width, rows), F32),
            ],
        ),
        out_shape=[
            jax.ShapeDtypeStruct((rows, width), F32),
            jax.ShapeDtypeStruct((rows, width), F32),
            jax.ShapeDtypeStruct((rows, width), BF16),
            jax.ShapeDtypeStruct((ff, rows), BF16),
            jax.ShapeDtypeStruct((rows, ff), BF16),
            jax.ShapeDtypeStruct((width, rows), BF16),
            jax.ShapeDtypeStruct((width, rows), BF16),
            jax.ShapeDtypeStruct((8, width), F32),
            jax.ShapeDtypeStruct((1, ff), F32),
        ]
        + [jax.ShapeDtypeStruct((rows, own), BF16)] * parts,
        compiler_params=params(),
        cost_estimate=cost(8 * rows * width * ff, 4 * width * ff + 24 * rows * width),
        name="feed_forward",
    )(place, *context, hidden, cot, proj, vecs, fc1, fc1_bias, fc2)


def post_kernel(lead_ref, tail_ref, hidden_ref, d_middle_ref, gain_ref, w_ref, din_ref, dskip_ref, low_ref, vec_ref):
    width = hidden_ref.shape[1]
    upstream = jnp.concatenate([lead_ref[...].astype(F32), tail_ref[...].astype(F32)], 0)
    scaled, factor = normalize(hidden_ref[...])
    d_hidden = d_middle_ref[...] + norm_back(upstream, scaled, factor, gain_ref[...])
    low = d_hidden.astype(BF16)
    low_ref[...] = low
    vec_ref[0:1] = jnp.sum(d_hidden, axis=0, keepdims=True)
    vec_ref[1:2] = jnp.sum(upstream * scaled, axis=0, keepdims=True)
    vec_ref[2:3] = jnp.sum(upstream, axis=0, keepdims=True)
    vec_ref[3:] = jnp.zeros((5, width), F32)
    din_ref[...] = dot_nt(low, w_ref[:width])
    dskip_ref[...] = dot_nt(low, w_ref[width:])


def post(lead, tail, hidden, d_middle, gain, w):
    rows, width = hidden.shape
    return pl.pallas_call(
        post_kernel,
        out_shape=(
            jax.ShapeDtypeStruct((rows, width), F32),
            jax.ShapeDtypeStruct((rows, width), F32),
            jax.ShapeDtypeStruct((rows, width), BF16),
            jax.ShapeDtypeStruct((8, width), F32),
        ),
        compiler_params=params(),
        cost_estimate=cost(4 * rows * width * width, 4 * width * width + 20 * rows * width),
        name="input_back",
    )(lead, tail, hidden, d_middle, gain, w)


def pair_kernel(count, where_ref, *refs):
    out_ref = refs[4 * count]
    at = 0
    for index in range(count):
        own_t, peer_t, own, peer = refs[4 * index : 4 * index + 4]
        size = own_t.shape[2]
        out_ref[0, pl.ds(at, size)] = (
            dot(own_t[0, 0], own[...]) + dot(peer_t[0], peer[...])
        ).astype(BF16)
        at += size


def pair_grads(where, groups):
    depth = groups[0][0].shape[0]
    width = groups[0][2].shape[1]
    in_specs, operands, height, flops = [], [], 0, 0
    for own_t, peer_t, own, peer in groups:
        size, rows = own_t.shape[2:]
        in_specs += [
            pl.BlockSpec((1, 1, size, rows), lambda z, w: (z, w[0], 0, 0)),
            pl.BlockSpec((1, size, rows), lambda z, w: (z, 0, 0)),
            pl.BlockSpec((rows, width), lambda z, w: (0, 0)),
            pl.BlockSpec((rows, width), lambda z, w: (0, 0)),
        ]
        operands += [own_t, peer_t, own, peer]
        height += size
        flops += 4 * depth * size * rows * width
    return pl.pallas_call(
        functools.partial(pair_kernel, len(groups)),
        grid_spec=pltpu.PrefetchScalarGridSpec(
            num_scalar_prefetch=1,
            grid=(depth,),
            in_specs=in_specs,
            out_specs=pl.BlockSpec((1, height, width), lambda z, w: (z, 0, 0)),
        ),
        out_shape=jax.ShapeDtypeStruct((depth, height, width), BF16),
        compiler_params=params(),
        cost_estimate=cost(flops, 4 * depth * height * width),
        name="pair_grads",
    )(where, *operands)


def column_kernel(where_ref, own_t, peer_t, own, peer, out_ref):
    for z in range(own_t.shape[0]):
        out_ref[0, z] = (dot(own_t[z, 0], own[...]) + dot(peer_t[z], peer[...])).astype(BF16)


def column_grads(where, parts, own_t, peer_t, own, peer):
    depth, _, size, rows = own_t.shape
    width = own.shape[1] // parts
    return pl.pallas_call(
        column_kernel,
        grid_spec=pltpu.PrefetchScalarGridSpec(
            num_scalar_prefetch=1,
            grid=(parts,),
            in_specs=[
                pl.BlockSpec((depth, 1, size, rows), lambda k, w: (0, w[0], 0, 0)),
                pl.BlockSpec((depth, size, rows), lambda k, w: (0, 0, 0)),
                pl.BlockSpec((rows, width), lambda k, w: (0, k ^ w[1])),
                pl.BlockSpec((rows, width), lambda k, w: (0, k ^ w[1])),
            ],
            out_specs=pl.BlockSpec((1, depth, size, width), lambda k, w: (k, 0, 0, 0)),
        ),
        out_shape=jax.ShapeDtypeStruct((parts, depth, size, width), BF16),
        compiler_params=params(),
        cost_estimate=cost(
            4 * parts * depth * size * rows * width, 4 * parts * depth * size * width
        ),
        name="column_grads",
    )(where, own_t, peer_t, own, peer)


def heads_kernel(normed_ref, dt_ref, out_ref):
    out_ref[...] = lax.dot_general(
        normed_ref[...], dt_ref[...], (((0,), (1,)), ((), ())), preferred_element_type=F32
    ).astype(BF16)


def heads_grads(normed_all, d_triple_t):
    total, width = normed_all.shape
    wide = d_triple_t.shape[0]
    return pl.pallas_call(
        heads_kernel,
        out_shape=jax.ShapeDtypeStruct((width, wide), BF16),
        compiler_params=params(),
        cost_estimate=cost(2 * total * width * wide, 2 * total * (width + wide)),
        name="heads_grads",
    )(normed_all, d_triple_t)


def columns_kernel(place_ref, *refs):
    out_ref = refs[-1]
    size = refs[0].shape[1]
    for k in range(len(refs) - 1):
        at = pl.multiple_of((place_ref[0] ^ k) * size, LANES)
        out_ref[:, pl.ds(at, size)] = refs[k][...].astype(F32)


def put_columns(place, pieces):
    height, size = pieces[0].shape
    count = len(pieces)
    return pl.pallas_call(
        columns_kernel,
        in_specs=[pl.BlockSpec(memory_space=pltpu.SMEM)]
        + [pl.BlockSpec(memory_space=pltpu.VMEM)] * count,
        out_shape=jax.ShapeDtypeStruct((height, count * size), F32),
        compiler_params=params(),
        cost_estimate=cost(1e6, 6 * count * height * size),
        name="put_columns",
    )(place, *pieces)


def head_columns_kernel(place_ref, *refs):
    out_ref = refs[-1]
    count = len(refs) - 1
    size = refs[0].shape[1] // 3
    for j in range(count):
        value = refs[0][...]
        for k in range(1, count):
            value = jnp.where((place_ref[0] ^ k) == j, refs[k][...], value)
        value = value.astype(F32)
        for which in range(3):
            at = (which * count + j) * size
            out_ref[:, at : at + size] = value[:, which * size : (which + 1) * size]


def put_heads(place, pieces):
    height, size = pieces[0].shape
    count = len(pieces)
    return pl.pallas_call(
        head_columns_kernel,
        in_specs=[pl.BlockSpec(memory_space=pltpu.SMEM)]
        + [pl.BlockSpec(memory_space=pltpu.VMEM)] * count,
        out_shape=jax.ShapeDtypeStruct((height, count * size), F32),
        compiler_params=params(),
        cost_estimate=cost(1e6, 6 * count * height * size),
        name="put_heads",
    )(place, *pieces)


def across(value, size, bit):
    return lax.ppermute(value, "seq", [(i, i ^ bit) for i in range(size)])


def other_core(value, size):
    return lax.ppermute(value, "batch", [(i, i ^ 1) for i in range(size)])


def plus(*terms):
    total = terms[0].astype(F32)
    for term in terms[1:]:
        total = total + term.astype(F32)
    return total.astype(BF16)


def bits_of(size):
    return [1 << i for i in range(size.bit_length() - 1)]


def everywhere(value, size):
    if size != 4:
        return [value] + [across(value, size, k) for k in range(1, size)]
    half = value.shape[0] // 2
    near, far = across(value, size, 1), across(value, size, 2)
    lead, tail = across(near[:half], size, 2), across(far[half:], size, 1)
    return [value, near, far, jnp.concatenate([lead, tail], 0)]


def scattered(value, size, bits):
    left = list(range(size))
    for bit in bits:
        keep = [i for i, k in enumerate(left) if not k & bit]
        send = [i for i, k in enumerate(left) if k & bit]
        pick = lambda which: jnp.concatenate([value[i : i + 1] for i in which], 0)
        value = plus(pick(keep), across(pick(send), size, bit))
        left = [left[i] for i in keep]
    return value[0]


def summed(value, size):
    half = (value.shape[0] // 2 + 7) // 8 * 8
    bits = bits_of(size)
    done = []
    for piece, order in ((value[:half], bits), (value[half:], bits[::-1])):
        for bit in order:
            piece = plus(piece, across(piece, size, bit))
        done.append(piece)
    return jnp.concatenate(done, 0)


def down_the_line(value, size, at):
    depth = value.shape[0]
    pick = lambda index: lax.dynamic_index_in_dim(
        value, jnp.clip(index, 0, depth - 1), 0, keepdims=False
    )
    up = down = None
    for t in range(depth - 1):
        send_up = pick(depth - 1 - t + at)
        send_down = pick(t - (depth - 1 - at))
        if t:
            send_up, send_down = plus(send_up, up), plus(send_down, down)
        up = lax.ppermute(
            send_up,
            "batch",
            [(2 * z + c, 2 * z + 2 + c) for z in range(depth - 1) if z <= t for c in (0, 1)],
        )
        down = lax.ppermute(
            send_down,
            "batch",
            [
                (2 * z + c, 2 * z - 2 + c)
                for z in range(1, depth)
                if z >= depth - 1 - t
                for c in (0, 1)
            ],
        )
    return plus(pick(at), up, down)


MESH = pl.DeviceIdType.MESH
AWAY = (1, 3, 2, 0)


def flip(value, k):
    if k == 0:
        return value
    if k == 1:
        return value + 1 - 2 * (value % 2)
    if k == 2:
        return value + 2 - 4 * (value // 2)
    return 3 - value


def add_rows(into, other):
    if len(into.shape) > 2:
        for i in range(into.shape[0]):
            add_rows(into.at[i], other.at[i])
        return
    tile = 16

    def body(i, carry):
        at = pl.ds(pl.multiple_of(i * tile, tile), tile)
        into[at] = (into[at].astype(F32) + other[at].astype(F32)).astype(BF16)
        return carry

    lax.fori_loop(0, into.shape[0] // tile, body, 0)


class Wires:
    def __init__(self, send_sems, recv_sems):
        self.send_sems, self.recv_sems, self.made = send_sems, recv_sems, []
        self.limit = send_sems.shape[0]

    def copy(self, src, dst, device, when=None):
        index = len(self.made)
        assert index < self.limit
        made = Wire(
            pltpu.make_async_remote_copy(
                src_ref=src,
                dst_ref=dst,
                send_sem=self.send_sems.at[index],
                recv_sem=self.recv_sems.at[index],
                device_id=device,
                device_id_type=MESH,
            ),
            when,
        )
        self.made.append(made)
        return made

    def by_core(self, core, src, dst, device, when=None):
        index = len(self.made)
        assert index + 1 < self.limit
        self.made.append(None)
        pick = lambda which: pltpu.make_async_remote_copy(
            src_ref=src,
            dst_ref=dst,
            send_sem=self.send_sems.at[index],
            recv_sem=self.recv_sems.at[index + which],
            device_id=device,
            device_id_type=MESH,
        )
        made = Wire(pick(core), when)
        made.arrive = lambda: [pick(which).wait_recv() for which in (0, 1)]
        self.made.append(made)
        return made

    def drain(self):
        for wire in [w for w in self.made if w is not None]:
            if wire.when is None:
                wire.copy.wait_send()
            else:
                pl.when(wire.when)(wire.copy.wait_send)


class Wire:
    def __init__(self, copy, when):
        self.copy, self.when = copy, when
        self.start, self.arrive = copy.start, copy.wait_recv


class Line:
    def __init__(self, wires, depth, chip, up_to, down_to, own, up_in, down_in, begun=False):
        self.depth, self.chip, self.own, self.begun = depth, chip, own, begun
        self.up_in, self.down_in = up_in, down_in
        last = depth - 1
        self.up = {
            d: wires.copy(
                own(d),
                up_in.at[d - 1],
                up_to,
                (chip < d) & (chip > 0) if begun and d == last else chip < d,
            )
            for d in range(1, depth)
        }
        self.down = {
            d: wires.copy(
                own(d),
                down_in.at[d],
                down_to,
                (chip > d) & (chip < last) if begun and d == 0 else chip > d,
            )
            for d in range(last)
        }

    def hop(self, t):
        last = self.depth - 1
        for d in range(1, self.depth):
            z = d - (last - t)
            if 0 <= z < d:

                @pl.when(self.chip == z)
                def _():
                    if z > 0 and not (self.begun and t == 1):
                        self.up[d].arrive()
                        add_rows(self.own(d), self.up_in.at[d - 1])
                    self.up[d].start()

                @pl.when(self.chip == last - z)
                def _():
                    if z > 0 and not (self.begun and t == 1):
                        self.down[last - d].arrive()
                        add_rows(self.own(last - d), self.down_in.at[last - d])
                    self.down[last - d].start()

    def finish(self):
        for d in range(self.depth):

            @pl.when(self.chip == d)
            def _():
                if d > 0:
                    self.up[d].arrive()
                    add_rows(self.own(d), self.up_in.at[d - 1])
                if d < self.depth - 1:
                    self.down[d].arrive()
                    add_rows(self.own(d), self.down_in.at[d])


class Square:
    def __init__(self, wires, to, own, in_one, in_two, src=None, begun=False):
        self.own, self.in_one, self.in_two = own, in_one, in_two
        src = src or own
        self.one, self.two = [], []
        for h, (f, g) in enumerate(((1, 2), (2, 1))):
            if not begun:
                self.one.append(
                    (
                        wires.copy(src(h, 3), in_one[h].at[1], to[f]),
                        wires.copy(src(h, f), in_one[h].at[0], to[f]),
                    )
                )
        for h, (f, g) in enumerate(((1, 2), (2, 1))):
            self.two.append(wires.copy(own(h, g), in_two[h], to[g]))

    def start(self):
        for i in range(2):
            for h in range(2):
                self.one[h][i].start()

    def middle(self):
        for h, g in ((0, 2), (1, 1)):
            self.one[h][0].arrive()
            add_rows(self.own(h, g), self.in_one[h].at[1])
            self.two[h].start()
        for h in range(2):
            self.one[h][1].arrive()
            add_rows(self.own(h, 0), self.in_one[h].at[0])

    def finish(self):
        for h in range(2):
            self.two[h].arrive()
            add_rows(self.own(h, 0), self.in_two[h])


class Spread:
    def __init__(self, wires, to, slots, src=None, cut=None):
        rows = slots.shape[1]
        cut = (rows // 2 + 15) // 16 * 16 if cut is None else cut
        src = slots.at[0] if src is None else src
        lead, tail = pl.ds(0, cut), pl.ds(cut, rows - cut)
        self.near = [wires.copy(src.at[p], slots.at[1, p], to[1]) for p in (lead, tail)]
        self.far = [wires.copy(src.at[p], slots.at[2, p], to[2]) for p in (tail, lead)]
        self.lead = wires.copy(slots.at[1, lead], slots.at[3, lead], to[2])
        self.tail = wires.copy(slots.at[2, tail], slots.at[3, tail], to[1])

    def start(self):
        for i in range(2):
            self.near[i].start()
            self.far[i].start()

    def relay(self):
        self.near[0].arrive()
        self.lead.start()
        self.far[0].arrive()
        self.tail.start()

    def finish(self):
        self.near[1].arrive()
        self.far[1].arrive()
        self.lead.arrive()
        self.tail.arrive()


class Pair:
    def __init__(self, wires, to, halves, ins):
        self.halves, self.ins, self.wires, self.to, self.step = halves, ins, wires, to, 0
        self.sent = [
            [wires.copy(halves[h][i], ins[h].at[i], to[(1, 2)[(h + i) % 2]]) for h in range(2)]
            for i in range(2)
        ]

    def start(self):
        for wire in self.sent[0]:
            wire.start()

    def middle(self):
        for h in range(2):
            self.sent[0][h].arrive()
            one, two = self.halves[h][0], self.halves[h][1]
            two[...] = (one[...].astype(F32) + self.ins[h][0].astype(F32)).astype(BF16)
            self.sent[1][h].start()

    def finish(self):
        for h in range(2):
            self.sent[1][h].arrive()
            two, three = self.halves[h][1], self.halves[h][2]
            three[...] = (two[...].astype(F32) + self.ins[h][1].astype(F32)).astype(BF16)


def reduce_kernel(
    late_hbm,
    lead_hbm,
    tail_hbm,
    normed_hbm,
    dt_hbm,
    joined_hbm,
    joined_peer_hbm,
    hidden_hbm,
    d_middle_hbm,
    w_hbm,
    normed_x,
    normed_peer,
    normed_cond_x,
    normed_cond_peer,
    d_pre_own,
    d_pre_x,
    active_x,
    active_cond_x,
    cot_hbm,
    cot_z,
    cot_zz,
    cot_far,
    cot_peer,
    gain_ref,
    vec_two_ref,
    fc1_bias_ref,
    p_all,
    f_all,
    g_all,
    q_all,
    s_all,
    c_all,
    din_hbm,
    dskip_hbm,
    vec_ref,
    left_one,
    right_one,
    left_two,
    right_two,
    cond_rows,
    cond_flat,
    active_cond,
    f_own,
    f_up,
    f_down,
    g_own,
    g_lead_one,
    g_tail_one,
    g_lead_two,
    g_tail_two,
    l_own,
    l_up,
    l_down,
    q_own,
    q_sum,
    q_up,
    q_down,
    s_own,
    s_one,
    s_two,
    s_z,
    s_up,
    s_down,
    d_own,
    d_one,
    d_two,
    p_lead,
    p_tail,
    p_lead_in,
    p_tail_in,
    low_ref,
    low_peer,
    c_own,
    hidden_ref,
    d_middle_ref,
    joined_ref,
    joined_peer_ref,
    v_own,
    v_in,
    send_sems,
    recv_sems,
    local_sems,
):
    rows, width = hidden_hbm.shape
    depth = f_own.shape[0]
    mid = depth // 2
    slots = c_own.shape[0]
    images = rows - slots
    place, index = lax.axis_index("seq"), lax.axis_index("batch")
    chip, core = index // 2, index % 2
    last = depth - 1
    to, other, up_to, down_to = ends_of(place, index, depth)
    greet([to[1], to[2], to[3], other], chip, depth, up_to, down_to)
    wires = Wires(send_sems, recv_sems)
    taken = [0]

    def local(src, dst):
        taken[0] += 1
        copy = pltpu.make_async_copy(src, dst, local_sems.at[taken[0] - 1])
        copy.start()
        return copy

    keeps = []

    d_hbm = (lead_hbm, tail_hbm)
    norm_sum = Square(
        wires,
        to,
        lambda h, k: d_own.at[h, (0, 1, 1, None)[k]],
        [d_one.at[h] for h in range(2)],
        [d_two.at[h] for h in range(2)],
        src=lambda h, k: d_hbm[h].at[k],
    )
    norm_sum.start()

    l_load = local(late_hbm, l_own)
    l_line = Line(wires, depth, chip, up_to, down_to, lambda d: l_own.at[d], l_up, l_down)

    img, cnd = pl.ds(0, images), pl.ds(images, slots)

    def cut(g):
        return pl.ds(pl.multiple_of(g * images, images), images)

    def end(g):
        return pl.ds(pl.multiple_of(8 * images + g * slots, slots), slots)

    loads_two, loads_able = [], []
    for i in range(depth):
        source = (chip + depth - AWAY[i]) % depth
        for c in range(2):
            g = source * 2 + c
            loads_two.append(local(active_x.at[i, c], left_two.at[:, :, cut(g)]))
            loads_two.append(local(active_cond_x.at[i, c], active_cond.at[g]))
    held = [cot_hbm, cot_z.at[0], cot_z.at[1], cot_zz.at[0], cot_zz.at[1], cot_far]
    for away, picks in ((0, (0, 0)), (1, (1, 2)), (2, (3, 4)), (3, (5, 5))):
        for which in range(2):
            if away == 0 and which == 1:
                continue
            z = chip - away if which == 0 else chip + away
            able = (z >= 0) & (z <= last)
            for ref, c in ((held[picks[which]], core), (cot_peer.at[picks[which]], 1 - core)):
                g = jnp.clip(z, 0, last) * 2 + c
                for src, dst in ((img, cut(g)), (cnd, end(g))):
                    sem = local_sems.at[taken[0]]
                    taken[0] += 1
                    copy = pltpu.make_async_copy(ref.at[src], right_two.at[dst], sem)
                    pl.when(able)(copy.start)
                    loads_able.append((able, copy))
    swaps_one = []
    d_pre_of = lambda k, part: d_pre_x.at[k - 1, part] if k else d_pre_own.at[part]
    for k in range(4):
        swaps_one.append(wires.copy(d_pre_of(k, img), right_one.at[cut(4 + k)], other))
        swaps_one.append(wires.copy(d_pre_of(k, cnd), right_one.at[end(4 + k)], other))
    for wire in swaps_one:
        wire.start()
    loads_one = []
    for k in range(4):
        for g, left, cond in (
            (k, normed_x.at[k, :, core], normed_cond_x.at[k]),
            (4 + k, normed_peer.at[k], normed_cond_peer.at[k]),
        ):
            loads_one.append(local(left, left_one.at[:, :, cut(g)]))
            loads_one.append(local(cond, cond_rows.at[pl.ds(g * slots, slots)]))
        loads_one.append(local(d_pre_of(k, img), right_one.at[cut(k)]))
        loads_one.append(local(d_pre_of(k, cnd), right_one.at[end(k)]))
    d_loads = [
        local(d_hbm[h].at[k], d_own.at[h, i]) for h, ks in ((0, (0, 2)), (1, (0, 1))) for i, k in enumerate(ks)
    ]
    p_cut = p_lead.shape[1]
    h_loads = [local(hidden_hbm, hidden_ref), local(d_middle_hbm, d_middle_ref)]
    j_loads = [local(joined_hbm, joined_ref), local(joined_peer_hbm, joined_peer_ref)]
    l_load.wait()
    l_line.hop(0)

    for copy in loads_two:
        copy.wait()
    for able, copy in loads_able:
        pl.when(able)(copy.wait)
    small = f_own.shape[1]
    for j in range(4):
        left_two[j, :, 8 * images :] = jnp.concatenate(
            [active_cond[g, :, j * slots : (j + 1) * slots] for g in range(8)], 1
        )
    g_own[...] = (
        dot(left_two[...].reshape(4 * small, 8 * rows), right_two[...])
        .astype(BF16)
        .reshape(4, small, width)
    )
    l_line.hop(1)
    g_cut = g_lead_one.shape[1]
    g_sum = Square(
        wires,
        to,
        lambda h, k: g_own.at[flip(place, k), (pl.ds(0, g_cut), pl.ds(g_cut, small - g_cut))[h]],
        (g_lead_one, g_tail_one),
        (g_lead_two, g_tail_two),
    )

    for copy in loads_one:
        copy.wait()
    flat = turned(cond_rows[...])
    for b in range(2 * depth):
        cond_flat[b // 2, b % 2] = flat[b * small : (b + 1) * small]
    for z in range(depth):
        left_one[z, :, 8 * images :] = cond_flat[z, core]
    for wire in swaps_one:
        wire.arrive()
    f_own[...] = (
        dot(left_one[...].reshape(depth * small, 8 * rows), right_one[...])
        .astype(BF16)
        .reshape(depth, small, width)
    )
    f_line = Line(wires, depth, chip, up_to, down_to, lambda d: f_own.at[d], f_up, f_down)
    f_line.hop(0)
    for copy in d_loads:
        copy.wait()
    norm_sum.middle()
    for t in range(2, last):
        l_line.hop(t)

    def heads_part(normed, dt):
        loads = [local(normed_hbm, normed), local(dt_hbm, dt)]
        for copy in loads:
            copy.wait()
        step = 3 * LANES
        for part in range(normed.shape[1] // step):
            grads = lax.dot_general(
                normed[:, part * step : (part + 1) * step],
                dt[...],
                (((0,), (1,)), ((), ())),
                preferred_element_type=F32,
            ).astype(BF16)
            q_own[pl.ds(part * step, step)] = grads

    pl.run_scoped(
        heads_part, pltpu.VMEM(normed_hbm.shape, BF16), pltpu.VMEM(dt_hbm.shape, BF16)
    )
    height = q_sum.shape[1]
    q_swap = [
        wires.copy(
            q_own.at[pl.ds(pl.multiple_of((2 * z + 1 - core) * height, 16), height)],
            q_sum.at[z],
            other,
        )
        for z in range(depth)
    ]
    for wire in q_swap:
        wire.start()

    norm_sum.finish()
    low_swap = wires.copy(low_ref, low_peer, other)
    v_swap = wires.copy(v_own.at[0], v_in.at[0], other)
    for copy in h_loads:
        copy.wait()
    upstream = jnp.concatenate([d_own[0, 0].astype(F32), d_own[1, 0].astype(F32)], 0)
    scaled, factor = normalize(hidden_ref[...])
    d_hidden = d_middle_ref[...] + norm_back(
        upstream, scaled, factor, gain_ref[...].reshape(1, -1)
    )
    low_ref[...] = d_hidden.astype(BF16)
    low_swap.start()
    l_line.finish()
    p_lead[0] = l_own[chip, :p_cut]
    p_tail[0] = l_own[chip, p_cut:]
    p_sum = Pair(
        wires,
        to,
        [[ref.at[i] for i in range(3)] for ref in (p_lead, p_tail)],
        (p_lead_in, p_tail_in),
    )
    p_sum.start()
    g_sum.start()
    v_own[0] = jnp.zeros(v_own.shape[1:], F32)
    v_own[0, 0:1] = jnp.sum(d_hidden, axis=0, keepdims=True)
    v_own[0, 1:2] = jnp.sum(upstream * scaled, axis=0, keepdims=True)
    v_own[0, 2:3] = jnp.sum(upstream, axis=0, keepdims=True)
    v_own[0, 3:7] = vec_two_ref[0:4]
    v_own[0, 8:12] = fc1_bias_ref[...]
    v_swap.start()
    f_line.hop(1)
    for z, wire in enumerate(q_swap):
        wire.arrive()
        add_rows(q_sum.at[z], q_own.at[pl.ds(pl.multiple_of((2 * z + core) * height, 16), height)])
    q_line = Line(wires, depth, chip, up_to, down_to, lambda d: q_sum.at[d], q_up, q_down)
    q_line.hop(0)

    for copy in j_loads:
        copy.wait()
    low_swap.arrive()
    block = joined_ref.shape[1]
    chunk = block // 4
    grads = both(
        joined_ref[...].reshape(depth * block, rows),
        joined_peer_ref[...].reshape(depth * block, rows),
        low_ref[...],
        low_peer[...],
    )
    for h in range(mid):
        for j in range(4):
            at = [(2 * h + i) * block + j * chunk for i in range(2)]
            piece = jnp.concatenate([grads[a : a + chunk] for a in at], 0)
            s_own[flip(place, j), h] = piece.astype(BF16)
    s_sum = Square(
        wires,
        to,
        lambda h, k: s_own.at[k, h],
        [s_one.at[h] for h in range(2)],
        [s_two.at[h] for h in range(2)],
    )
    s_sum.start()
    for t in range(2, last):
        f_line.hop(t)
    p_sum.middle()

    c_go = Spread(wires, to, c_all, c_own)

    def rows_part(which, out_hbm):
        def run(w, stage):
            copy = local(w_hbm.at[pl.ds(which * width, width)], w)
            copy.wait()
            stage[...] = dot_nt(low_ref[...], w[...])
            c_own[:, which * width : (which + 1) * width] = stage[images:].astype(BF16)
            local(stage.at[pl.ds(0, images)], out_hbm).wait()

        pl.run_scoped(run, pltpu.VMEM((width, width), BF16), pltpu.VMEM((rows, width), F32))

    rows_part(0, din_hbm)
    q_line.hop(1)
    g_sum.middle()
    rows_part(1, dskip_hbm)
    keeps.append(local(c_own, c_all.at[0]))
    for t in range(2, last):
        q_line.hop(t)

    v_swap.arrive()
    v_own[1] = v_own[0] + v_in[0]
    v_own[2] = v_own[1]
    v_own[3] = v_own[1]
    v_up = wires.copy(v_own.at[2], v_in.at[1], up_to, chip < last)
    v_down = wires.copy(v_own.at[3], v_in.at[2], down_to, chip > 0)
    s_sum.middle()
    g_sum.finish()
    f_line.finish()
    s_sum.finish()
    room = s_z.shape[1]
    for h in range(mid):
        value = s_own[0, h].astype(F32)
        for i in range(2):
            s_z[2 * h + i] = jnp.concatenate(
                [value[i * chunk : (i + 1) * chunk], jnp.zeros((room - chunk, width), F32)], 0
            ).astype(BF16)
    s_line = Line(wires, depth, chip, up_to, down_to, lambda d: s_z.at[d], s_up, s_down)
    s_line.hop(0)
    g_go = Spread(wires, to, g_all, g_own.at[place])
    g_go.start()
    f_go = Spread(wires, to, f_all, f_own.at[chip])
    f_go.start()
    c_go.start()
    keeps.append(local(g_own.at[place], g_all.at[0]))
    keeps.append(local(f_own.at[chip], f_all.at[0]))

    @pl.when(chip > 0)
    def _():
        v_up.arrive()
        v_own[2] = v_own[1] + v_in[1]

    @pl.when(chip < last)
    def _():
        v_up.start()

    @pl.when(chip < last)
    def _():
        v_down.arrive()
        v_own[3] = v_own[1] + v_in[2]

    @pl.when(chip > 0)
    def _():
        v_down.start()

    v_own[4] = v_own[2] + v_own[3] - v_own[1]
    v_near = wires.copy(v_own.at[4], v_in.at[3], to[1])
    v_near.start()
    s_line.hop(1)
    q_line.finish()
    q_go = Spread(wires, to, q_all, q_sum.at[chip])
    q_go.start()
    keeps.append(local(q_sum.at[chip], q_all.at[0]))
    for t in range(2, last):
        s_line.hop(t)
    c_go.relay()
    g_go.relay()
    f_go.relay()
    v_near.arrive()
    v_own[5] = v_own[4] + v_in[3]
    v_far = wires.copy(v_own.at[5], v_in.at[4], to[2])
    v_far.start()
    s_line.finish()
    s_go = Spread(wires, to, s_all, s_z.at[chip])
    s_go.start()
    keeps.append(local(s_z.at[chip], s_all.at[0]))
    q_go.relay()
    p_sum.finish()
    keeps.append(local(p_lead.at[2], p_all.at[pl.ds(0, p_cut)]))
    keeps.append(local(p_tail.at[2], p_all.at[pl.ds(p_cut, p_tail.shape[1])]))
    c_go.finish()
    v_far.arrive()
    vec_ref[...] = v_own[5] + v_in[4]
    s_go.relay()
    f_go.finish()
    g_go.finish()
    q_go.finish()
    s_go.finish()
    for copy in keeps:
        copy.wait()
    wires.drain()


def reduce_all(
    late, lead, tail, normed_all, d_triple_t, joined, joined_peer, hidden, d_middle, w, feeds,
    gain, vec_two, fc1_bias_grad,
):
    depth, small, width = late.shape
    rows = hidden.shape[0]
    slots = SLOTS // 4
    images = rows - slots
    mid = depth // 2
    own = d_triple_t.shape[0]
    skip_rows = joined.shape[1]
    skip_chunk = (skip_rows // 4 + 15) // 16 * 16
    pair = depth // 2 * (skip_rows // 4)
    half = rows // 2
    cut = (small // 2 + 15) // 16 * 16
    v = lambda *shape: pltpu.VMEM(shape, BF16)
    ends = depth - 1
    scratch = [
        v(depth, small, 8 * rows), v(8 * rows, width), v(depth, small, 8 * rows), v(8 * rows, width),
        v(8 * slots, width), v(depth, 2, small, 8 * slots), v(8, small, 4 * slots),
        v(depth, small, width), v(ends, small, width), v(ends, small, width),
        v(4, small, width), v(2, cut, width), v(2, small - cut, width), v(cut, width), v(small - cut, width),
        v(depth, small, width), v(ends, small, width), v(ends, small, width),
        v(width, own), v(depth, small, own), v(ends, small, own), v(ends, small, own),
        v(4, 2, pair, width), v(2, 2, pair, width), v(2, pair, width),
        v(depth, skip_chunk, width), v(ends, skip_chunk, width), v(ends, skip_chunk, width),
        v(2, 2, half, width), v(2, 2, half, width), v(2, half, width),
        v(3, cut, width), v(3, small - cut, width), v(2, cut, width), v(2, small - cut, width),
        v(rows, width), v(rows, width), v(slots, 2 * width),
        pltpu.VMEM((rows, width), F32), pltpu.VMEM((rows, width), F32),
        v(*joined.shape), v(*joined.shape),
        pltpu.VMEM((6, 16, width), F32), pltpu.VMEM((5, 16, width), F32),
        pltpu.SemaphoreType.DMA((128,)), pltpu.SemaphoreType.DMA((128,)), pltpu.SemaphoreType.DMA((128,)),
    ]
    hbm = pl.BlockSpec(memory_space=pl.ANY)
    vmem = pl.BlockSpec(memory_space=pltpu.VMEM)
    f = lambda *shape: jax.ShapeDtypeStruct(shape, F32)
    b = lambda *shape: jax.ShapeDtypeStruct(shape, BF16)
    return pl.pallas_call(
        reduce_kernel,
        in_specs=[hbm] * 23 + [vmem] * 3,
        out_specs=[hbm] * 8 + [vmem],
        out_shape=[
            b(small, width),
            b(4, small, width),
            b(4, small, width),
            b(4, small, own),
            b(4, skip_chunk, width),
            b(4, slots, 2 * width),
            f(images, width),
            f(images, width),
            f(16, width),
        ],
        scratch_shapes=scratch,
        compiler_params=pltpu.CompilerParams(
            vmem_limit_bytes=VMEM_LIMIT, collective_id=0, has_side_effects=True
        ),
        cost_estimate=cost(1e10, 1e8),
        name="reduce_all",
    )(
        late, lead, tail, normed_all, d_triple_t, joined, joined_peer, hidden, d_middle, w, *feeds,
        gain, vec_two, fc1_bias_grad,
    )


def ends_of(place, index, depth):
    chip, core = index // 2, index % 2
    to = {k: (index, flip(place, k)) for k in (1, 2, 3)}
    return to, (index + 1 - 2 * core, place), (index + 2, place), (index - 2, place)


def line_of(place, index, depth):
    chip = index // 2
    return [((chip + i) % depth * 2 + c, place) for i in range(1, depth) for c in (0, 1)]


def arrive_by_core(wires, core):
    for c in range(2):

        @pl.when(core == c)
        def _():
            wires[2 * c].arrive()
            wires[2 * c + 1].arrive()


class Hop:
    def __init__(self, wires, depth, chip, up_to, down_to, t, src_up, src_down, dst_up, dst_down):
        last = depth - 1
        self.up = wires.copy(src_up, dst_up, up_to, (chip < last) & (chip >= t))
        self.down = wires.copy(src_down, dst_down, down_to, (chip > 0) & (chip <= last - t))
        self.from_up = (chip > 0) & (chip - 1 >= t)
        self.from_down = (chip < last) & (chip + 1 <= last - t)

    def start(self):
        pl.when(self.up.when)(self.up.start)
        pl.when(self.down.when)(self.down.start)

    def arrive(self):
        pl.when(self.from_up)(self.up.arrive)
        pl.when(self.from_down)(self.down.arrive)


def greet(devices, chip=None, depth=0, up_to=None, down_to=None):
    barrier = pltpu.get_barrier_semaphore()
    for device in devices:
        pl.semaphore_signal(barrier, inc=1, device_id=device, device_id_type=MESH)
    if chip is None:
        pl.semaphore_wait(barrier, len(devices))
        return

    @pl.when(chip < depth - 1)
    def _():
        pl.semaphore_signal(barrier, inc=1, device_id=up_to, device_id_type=MESH)

    @pl.when(chip > 0)
    def _():
        pl.semaphore_signal(barrier, inc=1, device_id=down_to, device_id_type=MESH)

    pl.semaphore_wait(
        barrier, len(devices) + jnp.minimum(chip, 1) + jnp.minimum(depth - 1 - chip, 1)
    )


class Locals:
    def __init__(self, sems):
        self.sems, self.taken = sems, 0

    def copy(self, src, dst):
        self.taken += 1
        assert self.taken <= self.sems.shape[0]
        return pltpu.make_async_copy(src, dst, self.sems.at[self.taken - 1])

    def start(self, src, dst):
        copy = self.copy(src, dst)
        copy.start()
        return copy


def own_slots(cond_ref, pad_ref, place, slots):
    pad_ref[...] = jnp.zeros(pad_ref.shape, BF16)
    pad_ref[0 : cond_ref.shape[0]] = cond_ref[...]
    return pad_ref[pl.ds(pl.multiple_of(place * slots, 16), slots)]


def start_kernel(
    window,
    length_ref,
    x_ref,
    x_cond_ref,
    s_ref,
    s_cond_ref,
    cot_ref,
    cot_cond_ref,
    w_ref,
    bias_ref,
    gain_ref,
    shift_ref,
    qkv_w_hbm,
    hidden_ref,
    normed_hbm,
    heads_ref,
    qkv_ref,
    joined_hbm,
    peer_hbm,
    cot_all,
    cot_z,
    lse_ref,
    ctx_hbm,
    rest_hbm,
    cot_zz,
    pad_ref,
    x_all,
    s_all,
    normed_all,
    joined_ref,
    qkv_w_ref,
    vt_ref,
    ot_ref,
    go_ref,
    rest_ref,
    send_sems,
    recv_sems,
    local_sems,
):
    images, width = x_ref.shape
    slots = x_all.shape[0] - images
    place, index = lax.axis_index("seq"), lax.axis_index("batch")
    core = index % 2
    chip = index // 2
    depth = joined_hbm.shape[0]
    to, other, up_to, down_to = ends_of(place, index, depth)
    greet([to[1], to[2], to[3], other], chip, depth, up_to, down_to)
    wires, moves = Wires(send_sems, recv_sems), Locals(local_sems)
    w_load = moves.start(qkv_w_hbm, qkv_w_ref)
    cot_all[:images] = cot_ref[...]
    cot_all[images:] = own_slots(cot_cond_ref, pad_ref, place, slots)
    cot_go = Hop(
        wires, depth, chip, up_to, down_to, 0, cot_all, cot_all, cot_z.at[0], cot_z.at[1]
    )
    cot_go.start()
    for ref, cond, whole in ((x_ref, x_cond_ref, x_all), (s_ref, s_cond_ref, s_all)):
        whole[:images] = ref[...]
        whole[images:] = own_slots(cond, pad_ref, place, slots)
    hidden = (
        dot(x_all[...], w_ref[:width]) + dot(s_all[...], w_ref[width:]) + bias_ref[...].reshape(1, -1)
    )
    hidden_ref[...] = hidden
    scaled, _ = normalize(hidden)
    normed_all[0] = (
        scaled * gain_ref[...].reshape(1, -1) + shift_ref[...].reshape(1, -1)
    ).astype(BF16)
    spread = Spread(wires, to, normed_all)
    spread.start()

    size = joined_ref.shape[2]
    per = width // size
    for which, whole in enumerate((x_all, s_all)):
        flat = turned(whole[...])
        for i in range(per):
            block = which * per + i
            joined_ref[block // 2, block % 2] = flat[i * size : (i + 1) * size]
    swap = wires.copy(joined_ref.at[:, 1 - core], peer_hbm, other)
    swap.start()
    keep = moves.start(joined_ref.at[:, core], joined_hbm)
    heads = qkv_ref.shape[0]
    width_own = heads * HEAD_DIM
    real = lax.broadcasted_iota(jnp.int32, (width, LANES), 1) < HEAD_DIM

    def weights(which):
        first = place * width_own + which * width
        start = jnp.minimum(first // LANES * LANES, 3 * width - window)
        value = qkv_w_ref[:, pl.ds(pl.multiple_of(start, LANES), window)].astype(F32)
        value = pltpu.roll(value, lax.rem(window - (first - start), window), 1)
        for head in range(heads):
            shifted = value if head == 0 else pltpu.roll(value, window - head * HEAD_DIM, 1)
            at = (3 * head + which) * LANES
            heads_ref[:, at : at + LANES] = jnp.where(real, shifted[:, :LANES], 0.0).astype(BF16)

    rows = normed_all.shape[1]
    lane = lax.broadcasted_iota(jnp.int32, (1, LANES), 1)
    one = jnp.where(lane == HEAD_DIM, 1.0, 0.0)
    slot = lax.broadcasted_iota(jnp.int32, (slots, LANES), 0)
    lanes = lax.broadcasted_iota(jnp.int32, (slots, LANES), 1)

    def project(part):
        hidden_key = flip(place, part) * slots + slot > length_ref[0]
        bias = jnp.where(hidden_key & (lanes == HEAD_DIM), -1e30, 0.0)
        base = part * rows
        for head in range(heads):
            triple = dot(
                normed_all[part], heads_ref[:, 3 * head * LANES : 3 * (head + 1) * LANES]
            )
            qkv_ref[head, base : base + rows, :LANES] = (triple[:, :LANES] + one).astype(BF16)
            key = triple[:, LANES : 2 * LANES]
            qkv_ref[head, base : base + images, LANES : 2 * LANES] = key[:images].astype(BF16)
            qkv_ref[head, base + images : base + rows, LANES : 2 * LANES] = (
                key[images:] + bias
            ).astype(BF16)
            qkv_ref[head, base : base + rows, 2 * LANES :] = triple[:, 2 * LANES :].astype(BF16)

    w_load.wait()
    weights(0)
    spread.relay()
    weights(1)
    weights(2)
    project(0)
    spread.near[1].arrive()
    project(1)
    spread.far[1].arrive()
    project(2)
    spread.lead.arrive()
    spread.tail.arrive()
    project(3)
    out = moves.start(normed_all, normed_hbm)
    cot_go.arrive()
    cot_on = Hop(
        wires, depth, chip, up_to, down_to, 1, cot_z.at[0], cot_z.at[1], cot_zz.at[0], cot_zz.at[1]
    )
    cot_on.start()

    total = 4 * rows
    step = 3 * LANES
    go, keeps = [], []
    for head in range(heads):
        vt_ref[...] = turned(qkv_ref[head, :, 2 * LANES :])
        for first in range(0, total, step):
            span = slice(first, first + step)
            scores = dot_nt(qkv_ref[head, :, LANES : 2 * LANES], qkv_ref[head, span, :LANES])
            peak = jnp.max(scores, axis=0, keepdims=True)
            shifted = jnp.exp2((scores - peak) * SCALE2)
            sums = jnp.sum(shifted, axis=0, keepdims=True)
            mixed = dot(vt_ref[...], shifted.astype(BF16)) / sums
            ot_ref[head * HEAD_DIM : (head + 1) * HEAD_DIM, span] = mixed[:HEAD_DIM]
            lse_ref[head, :, span] = peak * SCALE2 + jnp.log2(sums)
        if head % 2 == 1:
            half = pl.ds((head - 1) * HEAD_DIM, 2 * HEAD_DIM)
            for part in (3, 1, 2, 0):
                go_ref[part, half] = ot_ref[half, part * rows : part * rows + images].astype(BF16)
                if part:
                    go.append(wires.copy(go_ref.at[part, half], ctx_hbm.at[part, half], to[part]))
                    go[-1].start()
                else:
                    keeps.append(moves.start(go_ref.at[0, half], ctx_hbm.at[0, half]))
    for part in (3, 1, 2, 0):
        rest_ref[part] = split_lanes(ot_ref[:, part * rows : (part + 1) * rows])[1]
        if part:
            go.append(wires.copy(rest_ref.at[part], rest_hbm.at[part], to[part]))
            go[-1].start()
        else:
            keeps.append(moves.start(rest_ref.at[0], rest_hbm.at[0]))
    swap.arrive()
    cot_on.arrive()
    for wire in go:
        wire.arrive()
    for copy in keeps + [keep, out]:
        copy.wait()
    wires.drain()


def start_stage(depth, length, x, x_cond, s, s_cond, cot, cot_cond, w, bias, gain, shift, qkv_w):
    images, width = x.shape
    slots = SLOTS // 4
    rows = images + slots
    heads = HEADS // 4
    own = heads * HEAD_DIM
    window = (max(p * own % LANES for p in range(4)) + own + LANES - 1) // LANES * LANES
    block = 2 * width // (2 * depth)
    vmem, hbm = pl.BlockSpec(memory_space=pltpu.VMEM), pl.BlockSpec(memory_space=pl.ANY)
    b = lambda *shape: jax.ShapeDtypeStruct(shape, BF16)
    v = lambda *shape: pltpu.VMEM(shape, BF16)
    return pl.pallas_call(
        functools.partial(start_kernel, window),
        in_specs=[pl.BlockSpec(memory_space=pltpu.SMEM)] + [vmem] * 10 + [hbm],
        out_specs=[vmem, hbm, vmem, vmem, hbm, hbm, vmem, hbm, vmem, hbm, hbm, hbm],
        out_shape=[
            jax.ShapeDtypeStruct((rows, width), F32),
            b(4, rows, width),
            b(width, heads * 3 * LANES),
            b(heads, 4 * rows, 3 * LANES),
            b(depth, block, rows),
            b(depth, block, rows),
            b(rows, width),
            b(2, rows, width),
            jax.ShapeDtypeStruct((heads, 1, 4 * rows), F32),
            b(4, own, images),
            b(4, (own // 4 + 15) // 16 * 16, LANES),
            b(2, rows, width),
        ],
        scratch_shapes=[
            v(SLOTS, width), v(rows, width), v(rows, width), v(4, rows, width),
            v(depth, 2, block, rows), v(width, 3 * width),
            v(LANES, 4 * rows), pltpu.VMEM((own, 4 * rows), F32), v(4, own, images),
            v(4, (own // 4 + 15) // 16 * 16, LANES),
            pltpu.SemaphoreType.DMA((32,)), pltpu.SemaphoreType.DMA((32,)), pltpu.SemaphoreType.DMA((16,)),
        ],
        compiler_params=pltpu.CompilerParams(
            vmem_limit_bytes=VMEM_LIMIT, collective_id=1, has_side_effects=True
        ),
        cost_estimate=cost(12 * rows * width * width, 12 * width * width),
        name="start_stage",
    )(length, x, x_cond, s, s_cond, cot, cot_cond, w, bias, gain, shift, qkv_w)


def split_lanes(value):
    size = value.shape[0] // 4
    cut = value.shape[1] - 32
    rest = jnp.concatenate([value[i * size : (i + 1) * size, cut:] for i in range(4)], 1)
    room = (size + 15) // 16 * 16
    rest = jnp.concatenate([rest, jnp.zeros((room - size, 4 * 32), F32)], 0)
    return value[:, :cut].astype(BF16), rest.astype(BF16)


def join_lanes(main, rest):
    size = main.shape[0] // 4
    rest = rest.astype(F32)
    rest = jnp.concatenate([rest[:size, i * 32 : (i + 1) * 32] for i in range(4)], 0)
    return jnp.concatenate([main.astype(F32), rest], 1)


def both(own_t, peer_t, own, peer):
    rows = own_t.shape[-1]
    cut = rows // 256 * 256
    total = dot(own_t[:, :cut], own[:cut]) + dot(peer_t[:, :cut], peer[:cut])
    ends_t = jnp.concatenate([own_t[:, cut:], peer_t[:, cut:]], 1)
    return total + dot(ends_t, jnp.concatenate([own[cut:], peer[cut:]], 0))


def middle_kernel(
    ctx_t_ref,
    ctx_rest_ref,
    hidden_ref,
    cot_ref,
    proj_ref,
    proj_bias_ref,
    gain_ref,
    shift_ref,
    fc2_bias_ref,
    fc1_bias_ref,
    lse_ref,
    cot_z,
    cot_zz,
    fc1_hbm,
    fc2_hbm,
    qkv_hbm,
    w_hbm,
    out_hbm,
    c_all,
    d_middle_ref,
    late_hbm,
    vec_ref,
    fc1_vec_ref,
    dt_ref,
    lead_ref,
    tail_ref,
    normed_x,
    normed_peer,
    normed_cond_x,
    normed_cond_peer,
    d_pre_own,
    d_pre_x,
    active_x,
    active_cond_x,
    cot_far,
    cot_peer,
    fc1_ref,
    fc2_ref,
    bias_ref,
    normed_ref,
    middle_ref,
    acc_out,
    acc_back,
    normed_t,
    ctx_two,
    ctx_peer,
    active_t,
    active_pack,
    d_pre,
    d_branch_ref,
    d_branch_peer,
    d_go,
    d_rest,
    d_in,
    d_rest_in,
    dot_all,
    dt_all,
    d_all,
    dk_ref,
    dv_ref,
    proj_stage,
    c_own,
    send_sems,
    recv_sems,
    local_sems,
):
    rows, width = cot_ref.shape
    slots = c_own.shape[0]
    images = rows - slots
    depth, _, small, _ = ctx_two.shape
    chunk = fc1_ref.shape[2]
    own = ctx_t_ref.shape[1]
    quarter = chunk // 8
    place, index = lax.axis_index("seq"), lax.axis_index("batch")
    chip, core = index // 2, index % 2
    to, other, up_to, down_to = ends_of(place, index, depth)
    moves = Locals(local_sems)

    def load(i):
        span = pl.ds(pl.multiple_of((chip + AWAY[i]) % depth * chunk, LANES), chunk)
        return (
            moves.start(fc1_hbm.at[:, span], fc1_ref.at[i % 2]),
            moves.start(fc2_hbm.at[span], fc2_ref.at[i % 2]),
        )

    loads = [load(0), load(1)]
    greet([to[1], to[2], to[3], other] + line_of(place, index, depth))
    wires = Wires(send_sems, recv_sems)
    hop = Hop(
        wires, depth, chip, up_to, down_to, 2, cot_zz.at[0], cot_zz.at[1], cot_far, cot_far
    )
    hop.start()
    for f in range(4):
        bias_ref[f : f + 1] = fc1_bias_ref[f * chunk : (f + 1) * chunk].reshape(1, -1)

    branch = proj_bias_ref[...].reshape(1, -1) + hidden_ref[...]
    for k in range(4):
        at = pl.ds(pl.multiple_of(flip(place, k) * own, 16), own)
        context_t = join_lanes(ctx_t_ref[k], ctx_rest_ref[k])
        branch += dot(context_t.T.astype(BF16), proj_ref[at, :])
        for i in range(2):
            ctx_two[flip(place, k), i] = context_t[i * small : (i + 1) * small].astype(BF16)
    ctx_swap = wires.copy(ctx_two.at[:, 1 - core], ctx_peer, other)
    ctx_swap.start()
    middle_ref[...] = branch
    scaled, _ = normalize(branch)
    gain = gain_ref[...].reshape(1, -1)
    normed = scaled * gain + shift_ref[...].reshape(1, -1)
    normed_ref[...] = normed.astype(BF16)
    normed_t[...] = normed[:images].T.astype(BF16).reshape(normed_t.shape)
    normed_go = Spread(wires, to, normed_x, normed_t, depth // 2)
    normed_go.start()
    keeps = [
        moves.start(normed_t, normed_x.at[0]),
        moves.start(normed_ref.at[pl.ds(images, slots)], normed_cond_x.at[0]),
    ]
    cond_go = [
        wires.copy(normed_ref.at[pl.ds(images, slots)], normed_cond_x.at[k], to[k]) for k in (1, 2, 3)
    ]
    for wire in cond_go:
        wire.start()

    near = []
    for i in range(4):
        f = (chip + AWAY[i]) % depth
        for copy in loads[i]:
            copy.wait()
        fc1, fc2 = fc1_ref.at[i % 2], fc2_ref.at[i % 2]
        before = dot(normed_ref[...], fc1[...]) + bias_ref[pl.ds(f, 1)]
        cdf = 0.5 + 0.5 * lax.erf(before * math.sqrt(0.5))
        active = before * cdf
        slope = cdf + before * (jnp.exp(-0.5 * before * before) * (1.0 / math.sqrt(2.0 * math.pi)))
        d_before = dot_nt(cot_ref[...], fc2[...]) * slope
        fc1_vec_ref[pl.ds(f, 1)] = jnp.sum(d_before, axis=0, keepdims=True)
        d_low = d_before.astype(BF16)
        d_pre[f] = d_low
        flat = active.T
        for c in range(2):
            for j in range(4):
                piece = flat[(c * 4 + j) * quarter : (c * 4 + j + 1) * quarter]
                active_t[i, c, j] = piece[:, :images].astype(BF16)
            active_pack[i, c] = jnp.concatenate(
                [flat[(c * 4 + j) * quarter : (c * 4 + j + 1) * quarter, images:] for j in range(4)], 1
            ).astype(BF16)
        if i < 3:
            for c in range(2):
                device = (f * 2 + c, place)
                near.append(wires.by_core(core, active_t.at[i, c], active_x.at[i, core], device))
                near.append(
                    wires.by_core(core, active_pack.at[i, c], active_cond_x.at[i, core], device)
                )
            for wire in near[4 * i :]:
                wire.start()
        else:
            keeps.append(moves.start(active_t.at[3, core], active_x.at[3, core]))
            keeps.append(moves.start(active_pack.at[3, core], active_cond_x.at[3, core]))
            late_go = [
                wires.copy(active_t.at[3, 1 - core], active_x.at[3, core], other),
                wires.copy(active_pack.at[3, 1 - core], active_cond_x.at[3, core], other),
            ]
        forward = dot(active.astype(BF16), fc2[...])
        backward = dot_nt(d_low, fc1[...])
        if i == 0:
            acc_out[...] = forward
            acc_back[...] = backward
        else:
            acc_out[...] += forward
            acc_back[...] += backward
        if i + 2 < 4:
            loads.append(load(i + 2))
        else:
            heads = range(0, 3) if i == 2 else range(3, 4)
            span = pl.ds(0, 9 * LANES) if i == 2 else pl.ds(9 * LANES, 3 * LANES)
            size = 9 * LANES if i == 2 else 3 * LANES
            qkv_loads = [
                moves.start(
                    qkv_hbm.at[h], fc1_ref.at[i % 2, :, pl.ds((h - heads[0]) * 3 * LANES, 3 * LANES)]
                )
                for h in heads
            ]
            qkv_loads.append(moves.start(w_hbm.at[:, span], fc2_ref.at[i % 2, :, pl.ds(0, size)]))
            loads.append(qkv_loads)
        if i == 1:
            normed_go.relay()

    middle = middle_ref[...]
    scaled, factor = normalize(middle)
    upstream = acc_back[...]
    cot = cot_ref[...].astype(F32)
    d_middle = cot + norm_back(upstream, scaled, factor, gain)
    d_middle_ref[...] = d_middle
    d_branch_ref[...] = d_middle.astype(BF16)
    branch_swap = wires.copy(d_branch_ref, d_branch_peer, other)
    branch_swap.start()
    go = []
    for k in (3, 1, 2, 0):
        at = pl.ds(pl.multiple_of(flip(place, k) * own, 16), own)
        d_go[k], d_rest[k] = split_lanes(dot_nt(d_branch_ref[...], proj_ref[at, :]))
        if k:
            for src, dst in ((d_go, d_in), (d_rest, d_rest_in)):
                go.append(wires.copy(src.at[k], dst.at[k], to[k]))
                go[-1].start()
        else:
            d_in[0], d_rest_in[0] = d_go[0], d_rest[0]
    acc_out[...] = middle + acc_out[...] + fc2_bias_ref[...].reshape(1, -1)
    keeps.append(moves.start(acc_out.at[pl.ds(0, images)], out_hbm))
    c_own[...] = acc_out[images:].astype(BF16)
    c_go = [wires.copy(c_own, c_all.at[k], to[k]) for k in (3, 1, 2)]
    keeps.append(moves.start(c_own, c_all.at[0]))
    vec_ref[0:1] = jnp.sum(upstream * scaled, axis=0, keepdims=True)
    vec_ref[1:2] = jnp.sum(upstream, axis=0, keepdims=True)
    vec_ref[2:3] = jnp.sum(d_middle, axis=0, keepdims=True)
    vec_ref[3:4] = jnp.sum(cot, axis=0, keepdims=True)
    vec_ref[4:] = jnp.zeros((4, width), F32)
    ctx_swap.arrive()
    branch_swap.arrive()
    proj_stage[...] = (
        both(
            ctx_two[:, core].reshape(depth * small, rows),
            ctx_peer[...].reshape(depth * small, rows),
            d_branch_ref[...],
            d_branch_peer[...],
        )
        .astype(BF16)
        .reshape(depth, small, width)
    )
    keeps.append(moves.start(proj_stage, late_hbm))
    for wire in go:
        wire.arrive()
    normed_go.finish()
    for wire in cond_go:
        wire.arrive()
    hop.arrive()
    keeps.append(moves.start(d_pre.at[place], d_pre_own))
    last_go = (
        [wires.copy(d_pre.at[flip(place, k)], d_pre_x.at[k - 1], to[k]) for k in (3, 1, 2)]
        + late_go
        + [
            wires.copy(normed_x.at[:, :, 1 - core], normed_peer, other),
            wires.copy(normed_cond_x, normed_cond_peer, other),
            wires.copy(cot_ref, cot_peer.at[0], other),
            wires.copy(cot_z, cot_peer.at[pl.ds(1, 2)], other),
            wires.copy(cot_zz, cot_peer.at[pl.ds(3, 2)], other),
            wires.copy(cot_far, cot_peer.at[5], other),
        ]
        + c_go
    )
    for copy in keeps:
        copy.wait()
    for wire in last_go:
        wire.start()

    total = 4 * rows
    half = rows // 2
    for part in range(4):
        dot_all[:, part * rows : (part + 1) * rows] = join_lanes(d_in[part], d_rest_in[part]).T
    for copy in loads[4] + loads[5]:
        copy.wait()
    step = 3 * LANES
    for head in range(4):
        slot, lane = (0, 3 * head * LANES) if head < 3 else (1, 0)
        base = head * HEAD_DIM
        upstream_t = jnp.concatenate(
            [dot_all[base : base + HEAD_DIM, :], jnp.zeros((LANES - HEAD_DIM, total), F32)], 0
        )
        upstream = upstream_t.T.astype(BF16)
        upstream_t = upstream_t.astype(BF16)
        key = fc1_ref[slot, :, lane + LANES : lane + 2 * LANES]
        key_t = turned(key)
        value = fc1_ref[slot, :, lane + 2 * LANES : lane + 3 * LANES]
        for start in range(0, total, step):
            span = slice(start, start + step)
            query = fc1_ref[slot, span, lane : lane + LANES]
            probs = jnp.exp2(dot_nt(key, query) * SCALE2 - lse_ref[head, :, span])
            d_probs = dot(value, upstream_t[:, span])
            delta = jnp.sum(probs * d_probs, axis=0, keepdims=True)
            d_raw = (probs * (d_probs - delta)).astype(BF16)
            d_value = dot(probs.astype(BF16), upstream[span])
            d_key = dot(d_raw, query)
            if start == 0:
                dv_ref[...] = d_value
                dk_ref[...] = d_key
            else:
                dv_ref[...] += d_value
                dk_ref[...] += d_key
            d_query = dot(key_t, d_raw) * SCALE
            dt_all[base : base + HEAD_DIM, span] = d_query[:HEAD_DIM]
            d_all[span, 3 * head * LANES : (3 * head + 1) * LANES] = d_query.T.astype(BF16)
        d_key = dk_ref[...] * SCALE
        d_value = dv_ref[...]
        dt_all[own + base : own + base + HEAD_DIM] = d_key.T[:HEAD_DIM]
        dt_all[2 * own + base : 2 * own + base + HEAD_DIM] = d_value.T[:HEAD_DIM]
        d_all[:, (3 * head + 1) * LANES : (3 * head + 2) * LANES] = d_key.astype(BF16)
        d_all[:, (3 * head + 2) * LANES : (3 * head + 3) * LANES] = d_value.astype(BF16)
    cut = 9 * LANES
    for part in (3, 1, 2, 0):
        span = slice(part * rows, (part + 1) * rows)
        update = dot_nt(d_all[span, :cut], fc2_ref[0]) + dot_nt(
            d_all[span, cut:], fc2_ref[1, :, : 3 * LANES]
        )
        lead_ref[part] = update[:half].astype(BF16)
        tail_ref[part] = update[half:].astype(BF16)
    dt_ref[...] = dt_all[...].astype(BF16)
    for i in range(3):
        arrive_by_core(near[4 * i : 4 * i + 4], core)
    for wire in last_go:
        wire.arrive()
    wires.drain()


def middle_stage(
    depth, ctx_t, ctx_rest, hidden, cot, proj, proj_bias, gain, shift, fc2_bias, fc1_bias, lse,
    cot_z, cot_zz, fc1, fc2, qkv, w_heads,
):
    rows, width = hidden.shape
    slots = SLOTS // 4
    images = rows - slots
    ff = fc1.shape[1]
    small = width // (2 * depth)
    own = ctx_t.shape[1]
    chunk = ff // 4
    quarter = chunk // 8
    vmem, hbm = pl.BlockSpec(memory_space=pltpu.VMEM), pl.BlockSpec(memory_space=pl.ANY)
    f = lambda *shape: jax.ShapeDtypeStruct(shape, F32)
    b = lambda *shape: jax.ShapeDtypeStruct(shape, BF16)
    v = lambda *shape: pltpu.VMEM(shape, BF16)
    vf = lambda *shape: pltpu.VMEM(shape, F32)
    return pl.pallas_call(
        middle_kernel,
        in_specs=[vmem] * 11 + [hbm] * 6,
        out_specs=[hbm, hbm, vmem, hbm] + [vmem] * 5 + [hbm] * 10,
        out_shape=[
            f(images, width),
            b(4, slots, width),
            f(rows, width),
            b(depth, small, width),
            f(8, width),
            f(4, chunk),
            b(3 * own, 4 * rows),
            b(4, rows // 2, width),
            b(4, rows // 2, width),
            b(4, depth, 2, small, images),
            b(4, depth, small, images),
            b(4, slots, width),
            b(4, slots, width),
            b(rows, chunk),
            b(3, rows, chunk),
            b(4, 2, 4, quarter, images),
            b(4, 2, quarter, 4 * slots),
            b(rows, width),
            b(6, rows, width),
        ],
        scratch_shapes=[
            v(2, width, chunk), v(2, chunk, width), vf(4, chunk),
            v(rows, width), vf(rows, width), vf(rows, width), vf(rows, width),
            v(depth, 2, small, images),
            v(depth, 2, small, rows), v(depth, small, rows),
            v(4, 2, 4, quarter, images), v(4, 2, quarter, 4 * slots),
            v(4, rows, chunk),
            v(rows, width), v(rows, width),
            v(4, rows, own - 32), v(4, (rows // 4 + 15) // 16 * 16, LANES),
            v(4, rows, own - 32), v(4, (rows // 4 + 15) // 16 * 16, LANES),
            vf(own, 4 * rows), vf(3 * own, 4 * rows), v(4 * rows, 12 * LANES),
            vf(4 * rows, LANES), vf(4 * rows, LANES),
            v(depth, small, width),
            v(slots, width),
            pltpu.SemaphoreType.DMA((64,)), pltpu.SemaphoreType.DMA((64,)), pltpu.SemaphoreType.DMA((64,)),
        ],
        compiler_params=pltpu.CompilerParams(
            vmem_limit_bytes=VMEM_LIMIT, collective_id=3, has_side_effects=True
        ),
        cost_estimate=cost(8 * rows * width * ff, 8 * width * ff),
        name="middle_stage",
    )(ctx_t, ctx_rest, hidden, cot, proj, proj_bias, gain, shift, fc2_bias, fc1_bias, lse, cot_z, cot_zz, fc1, fc2, qkv, w_heads)


def finish_kernel(
    p_hbm, f_hbm, g_hbm, q_hbm, s_hbm, c_hbm, out_c_hbm, vec_ref, out_hbm, din_hbm, dskip_hbm,
    g_fc2_hbm, g_proj_hbm, g_first_hbm, g_heads_hbm, g_skip_hbm,
    o_out, o_din, o_dskip, o_out_cond, o_din_cond, o_dskip_cond,
    v0, v1, v2, v3, v4, v5, v6, fc1_vec_ref,
    p_in, f_in, g_in, q_in, s_in, c_in, out_c_in, p_st, f_st, g_st, q_st, s_st, cond_st, rows_st, sems,
):
    width = out_hbm.shape[1]
    place, index = lax.axis_index("seq"), lax.axis_index("batch")
    batch = lax.axis_size("batch")
    moves = Locals(sems)
    loads = [
        moves.start(src, dst)
        for src, dst in (
            (f_hbm, f_in), (g_hbm, g_in), (q_hbm, q_in), (s_hbm, s_in), (p_hbm, p_in),
            (c_hbm, c_in),
            (out_c_hbm, out_c_in),
        )
    ]
    rows_in = [
        moves.start(src, rows_st.at[i]) for i, src in enumerate((out_hbm, din_hbm, dskip_hbm))
    ]
    done = []
    for i, dst in enumerate((o_out, o_din, o_dskip)):
        rows_in[i].wait()
        done.append(moves.start(rows_st.at[i], dst.at[:, 0]))
    loads[0].wait()
    for j in range(4):
        f_st[:, j * width : (j + 1) * width] = f_in[flip(place, j)].astype(F32)
    done.append(moves.start(f_st, g_first_hbm))
    loads[1].wait()
    small = g_in.shape[1]
    for j in range(4):
        g_st[j * small : (j + 1) * small] = g_in[flip(place, j)].astype(F32)
    done.append(moves.start(g_st, g_fc2_hbm))
    loads[2].wait()
    size = q_in.shape[2] // 3
    for j in range(4):
        value = q_in[flip(place, j)].astype(F32)
        for which in range(3):
            at = (which * 4 + j) * size
            q_st[:, at : at + size] = value[:, which * size : (which + 1) * size]
    done.append(moves.start(q_st, g_heads_hbm))
    loads[3].wait()
    size = s_st.shape[0] // 4
    for j in range(4):
        s_st[j * size : (j + 1) * size] = s_in[flip(place, j), :size].astype(F32)
    done.append(moves.start(s_st, g_skip_hbm))
    for copy in loads[4:]:
        copy.wait()
    p_st[...] = p_in[...].astype(F32)
    done.append(moves.start(p_st, g_proj_hbm))
    slots = c_in.shape[1]
    for j in range(4):
        span = slice(j * slots, (j + 1) * slots)
        piece = c_in[flip(place, j)].astype(F32)
        cond_st[0, span] = out_c_in[flip(place, j)].astype(F32)
        cond_st[1, span] = piece[:, :width]
        cond_st[2, span] = piece[:, width:]
    conds = o_out_cond.shape[0]
    for i, ref in enumerate((o_out_cond, o_din_cond, o_dskip_cond)):
        ref[:, 0] = cond_st[i, :conds]
    share = width // batch
    vectors = vec_ref[...]
    rolled = pltpu.roll(vectors, lax.rem(width - index * share, width), 1)
    for row, ref in zip((0, 1, 2, 5, 3, 4, 6), (v0, v1, v2, v3, v4, v5, v6)):
        ref[...] = rolled[row, :share]
    share = 4 * width // batch
    per = width // share
    vector = vec_ref[pl.ds(8 + index // per, 1)]
    vector = pltpu.roll(vector, lax.rem(width - index % per * share, width), 1)
    fc1_vec_ref[...] = vector[0, :share]
    for copy in done:
        copy.wait()


def finish_stage(batch, conds, slots_of, out_c, vec, out, d_image, d_skip):
    p_all, f_all, g_all, q_all, s_all, c_all = slots_of
    images, width = out.shape
    small = f_all.shape[1]
    skip_rows = 2 * width // batch
    large = 4 * width // batch
    slots = c_all.shape[1]
    vmem, hbm = pl.BlockSpec(memory_space=pltpu.VMEM), pl.BlockSpec(memory_space=pl.ANY)
    f = lambda *shape: jax.ShapeDtypeStruct(shape, F32)
    like = lambda a: pltpu.VMEM(a.shape, a.dtype)
    vf = lambda *shape: pltpu.VMEM(shape, F32)
    return pl.pallas_call(
        finish_kernel,
        in_specs=[hbm] * 7 + [vmem] + [hbm] * 3,
        out_specs=[hbm] * 8 + [vmem] * 11,
        out_shape=[
            f(large, width), f(small, width), f(small, 4 * width), f(small, 4 * q_all.shape[2]),
            f(skip_rows, width), f(images, 1, width), f(images, 1, width), f(images, 1, width),
            f(conds, 1, width), f(conds, 1, width), f(conds, 1, width),
        ]
        + [f(width // batch)] * 7
        + [f(large)],
        scratch_shapes=[
            like(p_all), like(f_all), like(g_all), like(q_all), like(s_all), like(c_all), like(out_c),
            vf(small, width), vf(small, 4 * width), vf(large, width), vf(small, 4 * q_all.shape[2]),
            vf(skip_rows, width), vf(3, 4 * slots, width), vf(3, images, width),
            pltpu.SemaphoreType.DMA((24,)),
        ],
        compiler_params=params(),
        cost_estimate=cost(1e6, 2e7),
        name="finish_stage",
    )(*slots_of, out_c, vec, out, d_image, d_skip)


def per_device(
    batch,
    parts,
    image_in,
    cond_in,
    skip_image,
    skip_cond,
    caption_len,
    skip_weight,
    skip_bias,
    first_gain,
    first_bias,
    qkv_weight,
    proj_weight,
    proj_bias,
    second_gain,
    second_bias,
    fc1_weight,
    fc1_bias,
    fc2_weight,
    fc2_bias,
    grad_image,
    grad_cond,
):
    conds = cond_in.shape[0]
    width = image_in.shape[2]
    images = image_in.shape[0]
    ff = fc1_weight.shape[1]
    slots = SLOTS // parts
    rows = slots + images
    total = rows * parts
    heads = HEADS // parts
    depth = batch // 2
    place = lax.axis_index("seq")
    index = lax.axis_index("batch")
    core, chip = index % 2, index // 2
    where = jnp.stack([core, place]).astype(jnp.int32)

    fast = parts == 4 and depth == 4 and (ff // parts) % LANES == 0
    if fast:
        (
            hidden, normed_all, w_heads, qkv, joined, joined_peer, cot, cot_z, lse, ctx_t, ctx_rest,
            cot_zz,
        ) = start_stage(
            depth, caption_len, image_in[:, 0], cond_in[:, 0], skip_image[:, 0], skip_cond[:, 0],
            grad_image[:, 0], grad_cond[:, 0], skip_weight, skip_bias, first_gain, first_bias,
            qkv_weight,
        )
        normed_all = normed_all.reshape(total, width)
        (
            out, out_c, d_middle, late, vec_two, fc1_vec, d_triple_t, lead, tail, normed_x,
            normed_peer, normed_cond_x, normed_cond_peer, d_pre_own, d_pre_x, active_x,
            active_cond_x, cot_far, cot_peer,
        ) = middle_stage(
            depth, ctx_t, ctx_rest, hidden, cot, proj_weight, proj_bias, second_gain, second_bias,
            fc2_bias, fc1_bias, lse, cot_z, cot_zz, fc1_weight, fc2_weight, qkv, w_heads,
        )
        feeds = (
            normed_x, normed_peer, normed_cond_x, normed_cond_peer, d_pre_own, d_pre_x, active_x,
            active_cond_x, cot, cot_z, cot_zz, cot_far, cot_peer,
        )
        *slots_of, d_image, d_skip, vec = reduce_all(
            late, lead, tail, normed_all, d_triple_t, joined, joined_peer, hidden, d_middle,
            skip_weight, feeds, first_gain, vec_two, fc1_vec,
        )
        (
            wgrad_fc2, wgrad_proj, wgrad_fc1, wgrad_qkv, wgrad_skip, out_image, d_image, d_skip,
            out_cond, d_cond, d_skip_cond, *vec,
        ) = finish_stage(batch, conds, slots_of, out_c, vec, out, d_image, d_skip)
        return (
            out_image, out_cond, d_image, d_cond, d_skip, d_skip_cond, wgrad_skip, vec[0],
            vec[1], vec[2], wgrad_qkv, wgrad_proj, vec[3], vec[4], vec[5], wgrad_fc1, vec[7],
            wgrad_fc2, vec[6],
        )

    def own_rows(cond, image):
        padded = jnp.pad(cond[:, 0], ((0, SLOTS - conds), (0, 0)))
        lead = lax.dynamic_slice_in_dim(padded, place * slots, slots, 0)
        return jnp.concatenate([lead, image[:, 0]], 0)

    x = own_rows(cond_in, image_in)
    s = own_rows(skip_cond, skip_image)
    cot = own_rows(grad_cond, grad_image)

    hidden, normed, joined_t = pre(
        x, s, skip_weight, skip_bias[None], first_gain[None], first_bias[None]
    )
    normed_all = jnp.concatenate(everywhere(normed, parts), 0)
    own = heads * HEAD_DIM
    w_heads = heads_weight(where[1:], qkv_weight, heads)
    order = place ^ jnp.arange(parts, dtype=jnp.int32)
    position = order[:, None] * slots + jnp.arange(rows, dtype=jnp.int32)[None]
    valid = (jnp.arange(rows)[None] >= slots) | (position <= caption_len[0])
    kbias = jnp.where(
        (jnp.arange(LANES) == HEAD_DIM)[None] & ~valid.reshape(total, 1), F32(-1e30), F32(0)
    )
    qkv, lse, *ctx_parts = attend(parts, normed_all, w_heads, kbias)
    context = [ctx_parts[0]] + [across(ctx_parts[k], parts, k) for k in range(1, parts)]

    zero = jnp.zeros_like(proj_bias)
    vecs = jnp.stack([proj_bias, second_gain, second_bias, fc2_bias, zero, zero, zero, zero])
    (
        out,
        d_middle,
        d_branch,
        active_t,
        d_pre,
        normed2_t,
        ctx_t,
        vec_two,
        fc1_bias_grad,
        *d_ctx_parts,
    ) = mlp(
        parts,
        where[1:],
        context,
        hidden,
        cot,
        proj_weight,
        vecs,
        fc1_weight,
        fc1_bias[None],
        fc2_weight,
    )
    d_context = [d_ctx_parts[0]] + [across(d_ctx_parts[k], parts, k) for k in range(1, parts)]

    def by_core(turned_rows):
        blocks = turned_rows.reshape(depth, 2, -1, rows)
        send = lax.dynamic_index_in_dim(blocks, 1 - core, 1, keepdims=False)
        return blocks, other_core(send, batch)

    active_b, active_p = by_core(active_t)
    normed2_b, normed2_p = by_core(normed2_t)
    ctx_b, ctx_p = by_core(ctx_t)
    joined_b, joined_p = by_core(joined_t)
    cot_p, d_pre_p, d_branch_p = (other_core(v, batch) for v in (cot, d_pre, d_branch))
    late = pair_grads(
        where, [(active_b, active_p, cot, cot_p), (ctx_b, ctx_p, d_branch, d_branch_p)]
    )
    by_columns = (ff // parts) % LANES == 0
    if by_columns:
        first = column_grads(where, parts, normed2_b, normed2_p, d_pre, d_pre_p)
        late, first, d_context = lax.optimization_barrier((late, first, d_context))
        middle = depth // 2
    if by_columns:
        first = jnp.concatenate(
            [
                scattered(first[:, :middle], parts, bits_of(parts)),
                scattered(first[:, middle:], parts, bits_of(parts)[::-1]),
            ],
            0,
        )
    if not by_columns:
        first = pair_grads(where, [(normed2_b, normed2_p, d_pre, d_pre_p)])
    def all_conds(lead):
        pieces = [lead] + [across(lead, parts, k) for k in range(1, parts)]
        full = jnp.zeros((SLOTS, lead.shape[1]), F32)
        for k in range(parts):
            full = lax.dynamic_update_slice_in_dim(
                full, pieces[k].astype(F32), (place ^ k) * slots, 0
            )
        return full[:conds, None]

    d_triple_t, d_lead, d_tail = attend_back(parts, d_context, qkv, lse, w_heads)
    d_lead = scattered(d_lead, parts, bits_of(parts))
    d_tail = scattered(d_tail, parts, bits_of(parts)[::-1])
    heads_grad = heads_grads(normed_all, d_triple_t).reshape(depth, 2, -1, 3 * own)
    heads_grad = plus(
        lax.dynamic_index_in_dim(heads_grad, core, 1, keepdims=False),
        other_core(lax.dynamic_index_in_dim(heads_grad, 1 - core, 1, keepdims=False), batch),
    )
    heads_grad = everywhere(down_the_line(heads_grad, batch, chip), parts)
    wgrad_qkv = put_heads(where[1:], heads_grad)

    d_in, d_skip, d_low, vec_one = post(
        d_lead, d_tail, hidden, d_middle, first_gain[None], skip_weight
    )
    d_low_p = other_core(d_low, batch)
    last = pair_grads(where, [(joined_b, joined_p, d_low, d_low_p)])

    late = down_the_line(late, batch, chip)
    first = down_the_line(first, batch, chip)
    late = summed(late, parts)
    if by_columns:
        fc1_cols = everywhere(first, parts)
        wgrad_fc1 = put_columns(where[1:], fc1_cols)
    else:
        wgrad_fc1 = summed(first, parts).astype(F32)

    vectors = [
        vec_one[0],
        vec_one[1],
        vec_one[2],
        vec_two[2],
        vec_two[0],
        vec_two[1],
        fc1_bias_grad[0],
        vec_two[3],
    ]
    sizes = [v.shape[0] // batch for v in vectors]
    packed = jnp.concatenate([v.reshape(batch, -1) for v in vectors], 1)
    packed = packed.reshape(depth, 2, -1)
    packed = lax.dynamic_index_in_dim(packed, core, 1, keepdims=False) + other_core(
        lax.dynamic_index_in_dim(packed, 1 - core, 1, keepdims=False), batch
    )
    packed = jnp.pad(packed, ((0, 0), (0, 16 * width - packed.shape[1]))).reshape(depth, 16, width)
    last = jnp.concatenate([last, packed.astype(BF16)], 1)
    last = summed(down_the_line(last, batch, chip), parts)
    skip_rows = 2 * width // batch
    wgrad_skip = last[:skip_rows].astype(F32)
    flat = last[skip_rows:].reshape(-1).astype(F32)
    vector_out, at = [], 0
    for size in sizes:
        vector_out.append(flat[at : at + size])
        at += size
    fc2_rows = ff // batch
    wgrad_fc2 = late[:fc2_rows].astype(F32)
    wgrad_proj = late[fc2_rows:].astype(F32)

    out_cond = all_conds(out[:slots].astype(BF16))
    d_cond = all_conds(jnp.concatenate([d_in[:slots], d_skip[:slots]], 1).astype(BF16))
    return (
        out[slots:, None],
        out_cond,
        d_in[slots:, None],
        d_cond[:, :, :width],
        d_skip[slots:, None],
        d_cond[:, :, width:],
        wgrad_skip,
        vector_out[0],
        vector_out[1],
        vector_out[2],
        wgrad_qkv,
        wgrad_proj,
        vector_out[3],
        vector_out[4],
        vector_out[5],
        wgrad_fc1,
        vector_out[6],
        wgrad_fc2,
        vector_out[7],
    )


def solution(mesh):
    tokens, conds, shared = P("seq", "batch", None), P(None, "batch", None), P()
    return jax.shard_map(
        functools.partial(per_device, mesh.shape["batch"], mesh.shape["seq"]),
        mesh=mesh,
        in_specs=(tokens, conds, tokens, conds, P("batch")) + (shared,) * 13 + (tokens, conds),
        out_specs=(tokens, conds) * 3
        + (
            P("batch", None),
            P("batch"),
            P("batch"),
            P("batch"),
            P("batch", None),
            P("batch", None),
            P("batch"),
            P("batch"),
            P("batch"),
            P("batch", None),
            P("batch"),
            P("batch", None),
            P("batch"),
        ),
        check_vma=False,
    )
```

```python
import functools
import math

import jax
import jax.numpy as jnp
from jax import lax
from jax.experimental import pallas as pl
from jax.experimental.pallas import tpu as pltpu
from jax.sharding import PartitionSpec as P

HEADS = 16
HEAD_DIM = 72
LANES = 128
SLOTS = 128
F32 = jnp.float32
BF16 = jnp.bfloat16
VMEM_LIMIT = 60 * 1024 * 1024
SCALE = 1.0 / math.sqrt(HEAD_DIM)
SCALE2 = SCALE * math.log2(math.e)


def dot(left, right):
    return jnp.dot(left, right, preferred_element_type=F32)


def dot_nt(left, right):
    return lax.dot_general(left, right, (((1,), (1,)), ((), ())), preferred_element_type=F32)


def dot_tn(left, right):
    return lax.dot_general(left, right, (((0,), (0,)), ((), ())), preferred_element_type=F32)


def params():
    return pltpu.CompilerParams(vmem_limit_bytes=VMEM_LIMIT)


def cost(flops, nbytes):
    return pl.CostEstimate(flops=int(flops), bytes_accessed=int(nbytes), transcendentals=0)


def turned(value):
    return value.astype(F32).T.astype(BF16)


def normalize(values):
    centre = values - jnp.mean(values, axis=-1, keepdims=True)
    factor = lax.rsqrt(jnp.mean(centre * centre, axis=-1, keepdims=True) + 1e-5)
    return centre * factor, factor


def norm_back(upstream, scaled, factor, gain):
    inner = upstream * gain
    centred = inner - jnp.mean(inner, axis=-1, keepdims=True)
    return factor * (centred - scaled * jnp.mean(inner * scaled, axis=-1, keepdims=True))


def pre_kernel(x_ref, s_ref, w_ref, bias_ref, gain_ref, shift_ref, hidden_ref, normed_ref, turn_ref):
    width = x_ref.shape[1]
    hidden = dot(x_ref[...], w_ref[:width]) + dot(s_ref[...], w_ref[width:]) + bias_ref[...]
    hidden_ref[...] = hidden
    scaled, _ = normalize(hidden)
    normed_ref[...] = (scaled * gain_ref[...] + shift_ref[...]).astype(BF16)
    turn_ref[:width] = turned(x_ref[...])
    turn_ref[width:] = turned(s_ref[...])


def pre(x, s, w, bias, gain, shift):
    rows, width = x.shape
    return pl.pallas_call(
        pre_kernel,
        out_shape=(
            jax.ShapeDtypeStruct((rows, width), F32),
            jax.ShapeDtypeStruct((rows, width), BF16),
            jax.ShapeDtypeStruct((2 * width, rows), BF16),
        ),
        compiler_params=params(),
        cost_estimate=cost(4 * rows * width * width, 4 * width * width + 12 * rows * width),
        name="input_linear",
    )(x, s, w, bias, gain, shift)


def heads_weight_kernel(window, place_ref, w_ref, out_ref):
    heads = out_ref.shape[0]
    width = w_ref.shape[0]
    own = heads * HEAD_DIM
    keep = lax.broadcasted_iota(jnp.int32, (width, LANES), 1) < HEAD_DIM
    place = place_ref[0]
    for which in range(3):
        first = place * own + which * width
        start = jnp.minimum(first // LANES * LANES, 3 * width - window)
        value = w_ref[:, pl.ds(pl.multiple_of(start, LANES), window)].astype(F32)
        value = pltpu.roll(value, lax.rem(window - (first - start), window), 1)
        for head in range(heads):
            turned_back = value if head == 0 else pltpu.roll(value, window - head * HEAD_DIM, 1)
            out_ref[head, :, which * LANES : (which + 1) * LANES] = jnp.where(
                keep, turned_back[:, :LANES], 0.0
            ).astype(BF16)


def heads_weight(place, w, heads):
    width = w.shape[0]
    own = heads * HEAD_DIM
    offsets = [p * own % LANES for p in range(HEADS // heads)]
    window = (max(offsets) + own + LANES - 1) // LANES * LANES
    return pl.pallas_call(
        functools.partial(heads_weight_kernel, window),
        in_specs=[
            pl.BlockSpec(memory_space=pltpu.SMEM),
            pl.BlockSpec(memory_space=pltpu.VMEM),
        ],
        out_shape=jax.ShapeDtypeStruct((heads, width, 3 * LANES), BF16),
        compiler_params=params(),
        cost_estimate=cost(1e6, 2 * w.size + 6 * heads * width * LANES),
        name="heads_weight",
    )(place, w)


def attend_kernel(parts, normed_ref, w_ref, kbias_ref, qkv_ref, lse_ref, *rest):
    ctx_refs, (vt_ref, ot_ref) = rest[:parts], rest[parts:]
    head = pl.program_id(0)
    total = normed_ref.shape[0]
    rows = total // parts
    lane = lax.broadcasted_iota(jnp.int32, (1, LANES), 1)
    one = jnp.where(lane == HEAD_DIM, 1.0, 0.0)
    for part in range(parts):
        span = pl.ds(part * rows, rows)
        triple = dot(normed_ref[span], w_ref[0])
        qkv_ref[0, span, :LANES] = (triple[:, :LANES] + one).astype(BF16)
        qkv_ref[0, span, LANES : 2 * LANES] = (
            triple[:, LANES : 2 * LANES] + kbias_ref[span]
        ).astype(BF16)
        qkv_ref[0, span, 2 * LANES :] = triple[:, 2 * LANES :].astype(BF16)
        vt_ref[:, span] = turned(qkv_ref[0, span, 2 * LANES :])
    step = 3 * LANES if total % (3 * LANES) == 0 else LANES
    for start in range(0, total, step):
        query = qkv_ref[0, pl.ds(start, step), :LANES]
        scores = dot_nt(qkv_ref[0, :, LANES : 2 * LANES], query)
        peak = jnp.max(scores, axis=0, keepdims=True)
        shifted = jnp.exp2((scores - peak) * SCALE2)
        sums = jnp.sum(shifted, axis=0, keepdims=True)
        mixed = dot(vt_ref[...], shifted.astype(BF16)) / sums
        ot_ref[pl.ds(pl.multiple_of(head * HEAD_DIM, 8), HEAD_DIM), pl.ds(start, step)] = mixed[
            :HEAD_DIM
        ]
        lse_ref[0, :, pl.ds(start, step)] = peak * SCALE2 + jnp.log2(sums)

    @pl.when(head == pl.num_programs(0) - 1)
    def _():
        for part in range(parts):
            ctx_refs[part][...] = ot_ref[:, pl.ds(part * rows, rows)].T.astype(BF16)


def attend(parts, normed_all, w_heads, kbias):
    total, width = normed_all.shape
    heads = w_heads.shape[0]
    rows = total // parts
    own = heads * HEAD_DIM
    return pl.pallas_call(
        functools.partial(attend_kernel, parts),
        grid=(heads,),
        in_specs=[
            pl.BlockSpec((total, width), lambda h: (0, 0)),
            pl.BlockSpec((1, width, 3 * LANES), lambda h: (h, 0, 0)),
            pl.BlockSpec((total, LANES), lambda h: (0, 0)),
        ],
        out_specs=[
            pl.BlockSpec((1, total, 3 * LANES), lambda h: (h, 0, 0)),
            pl.BlockSpec((1, 1, total), lambda h: (h, 0, 0)),
        ]
        + [pl.BlockSpec((rows, own), lambda h: (0, 0))] * parts,
        out_shape=[
            jax.ShapeDtypeStruct((heads, total, 3 * LANES), BF16),
            jax.ShapeDtypeStruct((heads, 1, total), F32),
        ]
        + [jax.ShapeDtypeStruct((rows, own), BF16)] * parts,
        scratch_shapes=[pltpu.VMEM((LANES, total), BF16), pltpu.VMEM((own, total), F32)],
        compiler_params=params(),
        cost_estimate=cost(
            2 * heads * total * (width * 3 * LANES + 4 * LANES * total), 6 * total * width
        ),
        name="attend",
    )(normed_all, w_heads, kbias)


def attend_back_kernel(parts, *refs):
    d_refs = refs[:parts]
    (qkv_ref, lse_ref, w_ref, dt_ref, lead_ref, tail_ref) = refs[parts : parts + 6]
    (dot_all, dt_all, acc, dq_ref, dk_ref, dv_ref) = refs[parts + 6 :]
    head = pl.program_id(0)
    heads = pl.num_programs(0)
    total = qkv_ref.shape[1]
    rows = total // parts
    half = rows // 2
    own = dot_all.shape[0]

    @pl.when(head == 0)
    def _():
        for part in range(parts):
            dot_all[:, pl.ds(part * rows, rows)] = d_refs[part][...].astype(F32).T

    base = pl.multiple_of(head * HEAD_DIM, 8)
    upstream_t = jnp.concatenate(
        [dot_all[pl.ds(base, HEAD_DIM), :], jnp.zeros((LANES - HEAD_DIM, total), F32)], 0
    )
    upstream = upstream_t.T.astype(BF16)
    upstream_t = upstream_t.astype(BF16)
    key = qkv_ref[0, :, LANES : 2 * LANES]
    key_t = turned(key)
    value = qkv_ref[0, :, 2 * LANES :]
    step = 3 * LANES if total % (3 * LANES) == 0 else LANES
    for start in range(0, total, step):
        query = qkv_ref[0, pl.ds(start, step), :LANES]
        probs = jnp.exp2(dot_nt(key, query) * SCALE2 - lse_ref[0, :, pl.ds(start, step)])
        d_probs = dot(value, upstream_t[:, start : start + step])
        delta = jnp.sum(probs * d_probs, axis=0, keepdims=True)
        d_raw = (probs * (d_probs - delta) * SCALE).astype(BF16)
        d_value = dot(probs.astype(BF16), upstream[start : start + step])
        d_key = dot(d_raw, query)
        if start == 0:
            dv_ref[...] = d_value
            dk_ref[...] = d_key
        else:
            dv_ref[...] += d_value
            dk_ref[...] += d_key
        d_query = dot(key_t, d_raw)
        dt_all[pl.ds(base, HEAD_DIM), pl.ds(start, step)] = d_query[:HEAD_DIM]
        dq_ref[pl.ds(start, step)] = d_query.T
    dt_all[pl.ds(pl.multiple_of(own + base, 8), HEAD_DIM)] = dk_ref[...].T[:HEAD_DIM]
    dt_all[pl.ds(pl.multiple_of(2 * own + base, 8), HEAD_DIM)] = dv_ref[...].T[:HEAD_DIM]
    for part in range(parts):
        span = pl.ds(part * rows, rows)
        update = (
            dot_nt(dq_ref[span].astype(BF16), w_ref[0, :, :LANES])
            + dot_nt(dk_ref[span].astype(BF16), w_ref[0, :, LANES : 2 * LANES])
            + dot_nt(dv_ref[span].astype(BF16), w_ref[0, :, 2 * LANES :])
        )

        @pl.when(head == 0)
        def _():
            acc[span] = update

        @pl.when(head > 0)
        def _():
            acc[span] += update

    @pl.when(head == heads - 1)
    def _():
        dt_ref[...] = dt_all[...].astype(BF16)
        for part in range(parts):
            lead_ref[part] = acc[pl.ds(part * rows, half)].astype(BF16)
            tail_ref[part] = acc[pl.ds(part * rows + half, half)].astype(BF16)


def attend_back(parts, d_context, qkv, lse, w_heads):
    heads, total, _ = qkv.shape
    width = w_heads.shape[1]
    rows = total // parts
    own = heads * HEAD_DIM
    whole = lambda *shape: pl.BlockSpec(shape, lambda h: (0,) * len(shape))
    return pl.pallas_call(
        functools.partial(attend_back_kernel, parts),
        grid=(heads,),
        in_specs=[whole(rows, own)] * parts
        + [
            pl.BlockSpec((1, total, 3 * LANES), lambda h: (h, 0, 0)),
            pl.BlockSpec((1, 1, total), lambda h: (h, 0, 0)),
            pl.BlockSpec((1, width, 3 * LANES), lambda h: (h, 0, 0)),
        ],
        out_specs=[
            whole(3 * own, total),
            whole(parts, rows // 2, width),
            whole(parts, rows // 2, width),
        ],
        out_shape=[
            jax.ShapeDtypeStruct((3 * own, total), BF16),
            jax.ShapeDtypeStruct((parts, rows // 2, width), BF16),
            jax.ShapeDtypeStruct((parts, rows // 2, width), BF16),
        ],
        scratch_shapes=[
            pltpu.VMEM((own, total), F32),
            pltpu.VMEM((3 * own, total), F32),
            pltpu.VMEM((total, width), F32),
            pltpu.VMEM((total, LANES), F32),
            pltpu.VMEM((total, LANES), F32),
            pltpu.VMEM((total, LANES), F32),
        ],
        compiler_params=params(),
        cost_estimate=cost(
            2 * heads * total * (width * 3 * LANES + 10 * LANES * total), 12 * total * width
        ),
        name="attend_back",
    )(*d_context, qkv, lse, w_heads)


def mlp_kernel(parts, place_ref, *refs):
    ctx_refs = refs[:parts]
    (
        hidden_ref,
        cot_ref,
        proj_ref,
        vec_ref,
        fc1_ref,
        fc1_bias_ref,
        fc2_ref,
        out_ref,
        d_middle_ref,
        d_branch_ref,
        active_t_ref,
        d_pre_ref,
        normed_t_ref,
        ctx_t_ref,
        vec_out_ref,
        fc1_bias_out_ref,
    ) = refs[parts : parts + 16]
    d_ctx_refs = refs[parts + 16 : 2 * parts + 16]
    middle_ref, normed_ref, acc_out, acc_back, turn_ref = refs[2 * parts + 16 :]
    step = pl.program_id(0)
    place = place_ref[0]
    own = ctx_refs[0].shape[1]

    @pl.when(step == 0)
    def _():
        branch = vec_ref[0:1] + hidden_ref[...]
        for part in range(parts):
            at = pl.ds(pl.multiple_of((place ^ part) * own, 8), own)
            branch += dot(ctx_refs[part][...], proj_ref[at, :])
            turn_ref[at] = ctx_refs[part][...].astype(F32).T
        ctx_t_ref[...] = turn_ref[...].astype(BF16)
        middle_ref[...] = branch
        scaled, _ = normalize(branch)
        normed = (scaled * vec_ref[1:2] + vec_ref[2:3]).astype(BF16)
        normed_ref[...] = normed
        normed_t_ref[...] = turned(normed)

    before = dot(normed_ref[...], fc1_ref[...]) + fc1_bias_ref[...]
    cdf = 0.5 + 0.5 * lax.erf(before * math.sqrt(0.5))
    active = (before * cdf).astype(BF16)
    slope = cdf + before * (jnp.exp(-0.5 * before * before) * (1.0 / math.sqrt(2.0 * math.pi)))
    d_before = dot_nt(cot_ref[...], fc2_ref[...]) * slope
    fc1_bias_out_ref[...] = jnp.sum(d_before, axis=0, keepdims=True)
    d_low = d_before.astype(BF16)
    d_pre_ref[...] = d_low
    active_t_ref[...] = turned(active)
    forward = dot(active, fc2_ref[...])
    backward = dot_nt(d_low, fc1_ref[...])

    @pl.when(step == 0)
    def _():
        acc_out[...] = forward
        acc_back[...] = backward

    @pl.when(step > 0)
    def _():
        acc_out[...] += forward
        acc_back[...] += backward

    @pl.when(step == pl.num_programs(0) - 1)
    def _():
        middle = middle_ref[...]
        out_ref[...] = middle + acc_out[...] + vec_ref[3:4]
        scaled, factor = normalize(middle)
        upstream = acc_back[...]
        cot = cot_ref[...].astype(F32)
        d_middle = cot + norm_back(upstream, scaled, factor, vec_ref[1:2])
        d_middle_ref[...] = d_middle
        d_branch = d_middle.astype(BF16)
        d_branch_ref[...] = d_branch
        vec_out_ref[0:1] = jnp.sum(upstream * scaled, axis=0, keepdims=True)
        vec_out_ref[1:2] = jnp.sum(upstream, axis=0, keepdims=True)
        vec_out_ref[2:3] = jnp.sum(d_middle, axis=0, keepdims=True)
        vec_out_ref[3:4] = jnp.sum(cot, axis=0, keepdims=True)
        vec_out_ref[4:] = jnp.zeros((4, vec_out_ref.shape[1]), F32)
        for part in range(parts):
            at = pl.ds(pl.multiple_of((place ^ part) * own, 8), own)
            d_ctx_refs[part][...] = dot_nt(d_branch, proj_ref[at, :]).astype(BF16)


def mlp(parts, place, context, hidden, cot, proj, vecs, fc1, fc1_bias, fc2):
    rows, width = hidden.shape
    ff = fc1.shape[1]
    own = context[0].shape[1]
    chunk = width
    whole = lambda *shape: pl.BlockSpec(shape, lambda i, p: (0,) * len(shape))
    return pl.pallas_call(
        functools.partial(mlp_kernel, parts),
        grid_spec=pltpu.PrefetchScalarGridSpec(
            num_scalar_prefetch=1,
            grid=(ff // chunk,),
            in_specs=[whole(rows, own)] * parts
            + [
                whole(rows, width),
                whole(rows, width),
                whole(width, width),
                whole(8, width),
                pl.BlockSpec((width, chunk), lambda i, p: (0, i)),
                pl.BlockSpec((1, chunk), lambda i, p: (0, i)),
                pl.BlockSpec((chunk, width), lambda i, p: (i, 0)),
            ],
            out_specs=[
                whole(rows, width),
                whole(rows, width),
                whole(rows, width),
                pl.BlockSpec((chunk, rows), lambda i, p: (i, 0)),
                pl.BlockSpec((rows, chunk), lambda i, p: (0, i)),
                whole(width, rows),
                whole(width, rows),
                whole(8, width),
                pl.BlockSpec((1, chunk), lambda i, p: (0, i)),
            ]
            + [whole(rows, own)] * parts,
            scratch_shapes=[
                pltpu.VMEM((rows, width), F32),
                pltpu.VMEM((rows, width), BF16),
                pltpu.VMEM((rows, width), F32),
                pltpu.VMEM((rows, width), F32),
                pltpu.VMEM((width, rows), F32),
            ],
        ),
        out_shape=[
            jax.ShapeDtypeStruct((rows, width), F32),
            jax.ShapeDtypeStruct((rows, width), F32),
            jax.ShapeDtypeStruct((rows, width), BF16),
            jax.ShapeDtypeStruct((ff, rows), BF16),
            jax.ShapeDtypeStruct((rows, ff), BF16),
            jax.ShapeDtypeStruct((width, rows), BF16),
            jax.ShapeDtypeStruct((width, rows), BF16),
            jax.ShapeDtypeStruct((8, width), F32),
            jax.ShapeDtypeStruct((1, ff), F32),
        ]
        + [jax.ShapeDtypeStruct((rows, own), BF16)] * parts,
        compiler_params=params(),
        cost_estimate=cost(8 * rows * width * ff, 4 * width * ff + 24 * rows * width),
        name="feed_forward",
    )(place, *context, hidden, cot, proj, vecs, fc1, fc1_bias, fc2)


def post_kernel(lead_ref, tail_ref, hidden_ref, d_middle_ref, gain_ref, w_ref, din_ref, dskip_ref, low_ref, vec_ref):
    width = hidden_ref.shape[1]
    upstream = jnp.concatenate([lead_ref[...].astype(F32), tail_ref[...].astype(F32)], 0)
    scaled, factor = normalize(hidden_ref[...])
    d_hidden = d_middle_ref[...] + norm_back(upstream, scaled, factor, gain_ref[...])
    low = d_hidden.astype(BF16)
    low_ref[...] = low
    vec_ref[0:1] = jnp.sum(d_hidden, axis=0, keepdims=True)
    vec_ref[1:2] = jnp.sum(upstream * scaled, axis=0, keepdims=True)
    vec_ref[2:3] = jnp.sum(upstream, axis=0, keepdims=True)
    vec_ref[3:] = jnp.zeros((5, width), F32)
    din_ref[...] = dot_nt(low, w_ref[:width])
    dskip_ref[...] = dot_nt(low, w_ref[width:])


def post(lead, tail, hidden, d_middle, gain, w):
    rows, width = hidden.shape
    return pl.pallas_call(
        post_kernel,
        out_shape=(
            jax.ShapeDtypeStruct((rows, width), F32),
            jax.ShapeDtypeStruct((rows, width), F32),
            jax.ShapeDtypeStruct((rows, width), BF16),
            jax.ShapeDtypeStruct((8, width), F32),
        ),
        compiler_params=params(),
        cost_estimate=cost(4 * rows * width * width, 4 * width * width + 20 * rows * width),
        name="input_back",
    )(lead, tail, hidden, d_middle, gain, w)


def pair_kernel(count, where_ref, *refs):
    out_ref = refs[4 * count]
    at = 0
    for index in range(count):
        own_t, peer_t, own, peer = refs[4 * index : 4 * index + 4]
        size = own_t.shape[2]
        out_ref[0, pl.ds(at, size)] = (
            dot(own_t[0, 0], own[...]) + dot(peer_t[0], peer[...])
        ).astype(BF16)
        at += size


def pair_grads(where, groups):
    depth = groups[0][0].shape[0]
    width = groups[0][2].shape[1]
    in_specs, operands, height, flops = [], [], 0, 0
    for own_t, peer_t, own, peer in groups:
        size, rows = own_t.shape[2:]
        in_specs += [
            pl.BlockSpec((1, 1, size, rows), lambda z, w: (z, w[0], 0, 0)),
            pl.BlockSpec((1, size, rows), lambda z, w: (z, 0, 0)),
            pl.BlockSpec((rows, width), lambda z, w: (0, 0)),
            pl.BlockSpec((rows, width), lambda z, w: (0, 0)),
        ]
        operands += [own_t, peer_t, own, peer]
        height += size
        flops += 4 * depth * size * rows * width
    return pl.pallas_call(
        functools.partial(pair_kernel, len(groups)),
        grid_spec=pltpu.PrefetchScalarGridSpec(
            num_scalar_prefetch=1,
            grid=(depth,),
            in_specs=in_specs,
            out_specs=pl.BlockSpec((1, height, width), lambda z, w: (z, 0, 0)),
        ),
        out_shape=jax.ShapeDtypeStruct((depth, height, width), BF16),
        compiler_params=params(),
        cost_estimate=cost(flops, 4 * depth * height * width),
        name="pair_grads",
    )(where, *operands)


def column_kernel(where_ref, own_t, peer_t, own, peer, out_ref):
    for z in range(own_t.shape[0]):
        out_ref[0, z] = (dot(own_t[z, 0], own[...]) + dot(peer_t[z], peer[...])).astype(BF16)


def column_grads(where, parts, own_t, peer_t, own, peer):
    depth, _, size, rows = own_t.shape
    width = own.shape[1] // parts
    return pl.pallas_call(
        column_kernel,
        grid_spec=pltpu.PrefetchScalarGridSpec(
            num_scalar_prefetch=1,
            grid=(parts,),
            in_specs=[
                pl.BlockSpec((depth, 1, size, rows), lambda k, w: (0, w[0], 0, 0)),
                pl.BlockSpec((depth, size, rows), lambda k, w: (0, 0, 0)),
                pl.BlockSpec((rows, width), lambda k, w: (0, k ^ w[1])),
                pl.BlockSpec((rows, width), lambda k, w: (0, k ^ w[1])),
            ],
            out_specs=pl.BlockSpec((1, depth, size, width), lambda k, w: (k, 0, 0, 0)),
        ),
        out_shape=jax.ShapeDtypeStruct((parts, depth, size, width), BF16),
        compiler_params=params(),
        cost_estimate=cost(
            4 * parts * depth * size * rows * width, 4 * parts * depth * size * width
        ),
        name="column_grads",
    )(where, own_t, peer_t, own, peer)


def heads_kernel(normed_ref, dt_ref, out_ref):
    out_ref[...] = lax.dot_general(
        normed_ref[...], dt_ref[...], (((0,), (1,)), ((), ())), preferred_element_type=F32
    ).astype(BF16)


def heads_grads(normed_all, d_triple_t):
    total, width = normed_all.shape
    wide = d_triple_t.shape[0]
    return pl.pallas_call(
        heads_kernel,
        out_shape=jax.ShapeDtypeStruct((width, wide), BF16),
        compiler_params=params(),
        cost_estimate=cost(2 * total * width * wide, 2 * total * (width + wide)),
        name="heads_grads",
    )(normed_all, d_triple_t)


def columns_kernel(place_ref, *refs):
    out_ref = refs[-1]
    size = refs[0].shape[1]
    for k in range(len(refs) - 1):
        at = pl.multiple_of((place_ref[0] ^ k) * size, LANES)
        out_ref[:, pl.ds(at, size)] = refs[k][...].astype(F32)


def put_columns(place, pieces):
    height, size = pieces[0].shape
    count = len(pieces)
    return pl.pallas_call(
        columns_kernel,
        in_specs=[pl.BlockSpec(memory_space=pltpu.SMEM)]
        + [pl.BlockSpec(memory_space=pltpu.VMEM)] * count,
        out_shape=jax.ShapeDtypeStruct((height, count * size), F32),
        compiler_params=params(),
        cost_estimate=cost(1e6, 6 * count * height * size),
        name="put_columns",
    )(place, *pieces)


def head_columns_kernel(place_ref, *refs):
    out_ref = refs[-1]
    count = len(refs) - 1
    size = refs[0].shape[1] // 3
    for j in range(count):
        value = refs[0][...]
        for k in range(1, count):
            value = jnp.where((place_ref[0] ^ k) == j, refs[k][...], value)
        value = value.astype(F32)
        for which in range(3):
            at = (which * count + j) * size
            out_ref[:, at : at + size] = value[:, which * size : (which + 1) * size]


def put_heads(place, pieces):
    height, size = pieces[0].shape
    count = len(pieces)
    return pl.pallas_call(
        head_columns_kernel,
        in_specs=[pl.BlockSpec(memory_space=pltpu.SMEM)]
        + [pl.BlockSpec(memory_space=pltpu.VMEM)] * count,
        out_shape=jax.ShapeDtypeStruct((height, count * size), F32),
        compiler_params=params(),
        cost_estimate=cost(1e6, 6 * count * height * size),
        name="put_heads",
    )(place, *pieces)


def across(value, size, bit):
    return lax.ppermute(value, "seq", [(i, i ^ bit) for i in range(size)])


def other_core(value, size):
    return lax.ppermute(value, "batch", [(i, i ^ 1) for i in range(size)])


def plus(*terms):
    total = terms[0].astype(F32)
    for term in terms[1:]:
        total = total + term.astype(F32)
    return total.astype(BF16)


def bits_of(size):
    return [1 << i for i in range(size.bit_length() - 1)]


def everywhere(value, size):
    if size != 4:
        return [value] + [across(value, size, k) for k in range(1, size)]
    half = value.shape[0] // 2
    near, far = across(value, size, 1), across(value, size, 2)
    lead, tail = across(near[:half], size, 2), across(far[half:], size, 1)
    return [value, near, far, jnp.concatenate([lead, tail], 0)]


def scattered(value, size, bits):
    left = list(range(size))
    for bit in bits:
        keep = [i for i, k in enumerate(left) if not k & bit]
        send = [i for i, k in enumerate(left) if k & bit]
        pick = lambda which: jnp.concatenate([value[i : i + 1] for i in which], 0)
        value = plus(pick(keep), across(pick(send), size, bit))
        left = [left[i] for i in keep]
    return value[0]


def summed(value, size):
    half = (value.shape[0] // 2 + 7) // 8 * 8
    bits = bits_of(size)
    done = []
    for piece, order in ((value[:half], bits), (value[half:], bits[::-1])):
        for bit in order:
            piece = plus(piece, across(piece, size, bit))
        done.append(piece)
    return jnp.concatenate(done, 0)


def down_the_line(value, size, at):
    depth = value.shape[0]
    pick = lambda index: lax.dynamic_index_in_dim(
        value, jnp.clip(index, 0, depth - 1), 0, keepdims=False
    )
    up = down = None
    for t in range(depth - 1):
        send_up = pick(depth - 1 - t + at)
        send_down = pick(t - (depth - 1 - at))
        if t:
            send_up, send_down = plus(send_up, up), plus(send_down, down)
        up = lax.ppermute(
            send_up,
            "batch",
            [(2 * z + c, 2 * z + 2 + c) for z in range(depth - 1) if z <= t for c in (0, 1)],
        )
        down = lax.ppermute(
            send_down,
            "batch",
            [
                (2 * z + c, 2 * z - 2 + c)
                for z in range(1, depth)
                if z >= depth - 1 - t
                for c in (0, 1)
            ],
        )
    return plus(pick(at), up, down)


MESH = pl.DeviceIdType.MESH
AWAY = (1, 3, 2, 0)


def flip(value, k):
    if k == 0:
        return value
    if k == 1:
        return value + 1 - 2 * (value % 2)
    if k == 2:
        return value + 2 - 4 * (value // 2)
    return 3 - value


def add_rows(into, other):
    if len(into.shape) > 2:
        for i in range(into.shape[0]):
            add_rows(into.at[i], other.at[i])
        return
    tile = 16

    def body(i, carry):
        at = pl.ds(pl.multiple_of(i * tile, tile), tile)
        into[at] = (into[at].astype(F32) + other[at].astype(F32)).astype(BF16)
        return carry

    lax.fori_loop(0, into.shape[0] // tile, body, 0)


class Wires:
    def __init__(self, send_sems, recv_sems):
        self.send_sems, self.recv_sems, self.made = send_sems, recv_sems, []
        self.limit = send_sems.shape[0]

    def copy(self, src, dst, device, when=None):
        index = len(self.made)
        assert index < self.limit
        made = Wire(
            pltpu.make_async_remote_copy(
                src_ref=src,
                dst_ref=dst,
                send_sem=self.send_sems.at[index],
                recv_sem=self.recv_sems.at[index],
                device_id=device,
                device_id_type=MESH,
            ),
            when,
        )
        self.made.append(made)
        return made

    def by_core(self, core, src, dst, device, when=None):
        index = len(self.made)
        assert index + 1 < self.limit
        self.made.append(None)
        pick = lambda which: pltpu.make_async_remote_copy(
            src_ref=src,
            dst_ref=dst,
            send_sem=self.send_sems.at[index],
            recv_sem=self.recv_sems.at[index + which],
            device_id=device,
            device_id_type=MESH,
        )
        made = Wire(pick(core), when)
        made.arrive = lambda: [pick(which).wait_recv() for which in (0, 1)]
        self.made.append(made)
        return made

    def drain(self):
        for wire in [w for w in self.made if w is not None]:
            if wire.when is None:
                wire.copy.wait_send()
            else:
                pl.when(wire.when)(wire.copy.wait_send)


class Wire:
    def __init__(self, copy, when):
        self.copy, self.when = copy, when
        self.start, self.arrive = copy.start, copy.wait_recv


class Line:
    def __init__(self, wires, depth, chip, up_to, down_to, own, up_in, down_in, begun=False):
        self.depth, self.chip, self.own, self.begun = depth, chip, own, begun
        self.up_in, self.down_in = up_in, down_in
        last = depth - 1
        self.up = {
            d: wires.copy(
                own(d),
                up_in.at[d - 1],
                up_to,
                (chip < d) & (chip > 0) if begun and d == last else chip < d,
            )
            for d in range(1, depth)
        }
        self.down = {
            d: wires.copy(
                own(d),
                down_in.at[d],
                down_to,
                (chip > d) & (chip < last) if begun and d == 0 else chip > d,
            )
            for d in range(last)
        }

    def hop(self, t):
        last = self.depth - 1
        for d in range(1, self.depth):
            z = d - (last - t)
            if 0 <= z < d:

                @pl.when(self.chip == z)
                def _():
                    if z > 0 and not (self.begun and t == 1):
                        self.up[d].arrive()
                        add_rows(self.own(d), self.up_in.at[d - 1])
                    self.up[d].start()

                @pl.when(self.chip == last - z)
                def _():
                    if z > 0 and not (self.begun and t == 1):
                        self.down[last - d].arrive()
                        add_rows(self.own(last - d), self.down_in.at[last - d])
                    self.down[last - d].start()

    def finish(self):
        for d in range(self.depth):

            @pl.when(self.chip == d)
            def _():
                if d > 0:
                    self.up[d].arrive()
                    add_rows(self.own(d), self.up_in.at[d - 1])
                if d < self.depth - 1:
                    self.down[d].arrive()
                    add_rows(self.own(d), self.down_in.at[d])


class Square:
    def __init__(self, wires, to, own, in_one, in_two, src=None, begun=False):
        self.own, self.in_one, self.in_two = own, in_one, in_two
        src = src or own
        self.one, self.two = [], []
        for h, (f, g) in enumerate(((1, 2), (2, 1))):
            if not begun:
                self.one.append(
                    (
                        wires.copy(src(h, 3), in_one[h].at[1], to[f]),
                        wires.copy(src(h, f), in_one[h].at[0], to[f]),
                    )
                )
        for h, (f, g) in enumerate(((1, 2), (2, 1))):
            self.two.append(wires.copy(own(h, g), in_two[h], to[g]))

    def start(self):
        for i in range(2):
            for h in range(2):
                self.one[h][i].start()

    def middle(self):
        for h, g in ((0, 2), (1, 1)):
            self.one[h][0].arrive()
            add_rows(self.own(h, g), self.in_one[h].at[1])
            self.two[h].start()
        for h in range(2):
            self.one[h][1].arrive()
            add_rows(self.own(h, 0), self.in_one[h].at[0])

    def finish(self):
        for h in range(2):
            self.two[h].arrive()
            add_rows(self.own(h, 0), self.in_two[h])


class Spread:
    def __init__(self, wires, to, slots, src=None, cut=None):
        rows = slots.shape[1]
        cut = (rows // 2 + 15) // 16 * 16 if cut is None else cut
        src = slots.at[0] if src is None else src
        lead, tail = pl.ds(0, cut), pl.ds(cut, rows - cut)
        self.near = [wires.copy(src.at[p], slots.at[1, p], to[1]) for p in (lead, tail)]
        self.far = [wires.copy(src.at[p], slots.at[2, p], to[2]) for p in (tail, lead)]
        self.lead = wires.copy(slots.at[1, lead], slots.at[3, lead], to[2])
        self.tail = wires.copy(slots.at[2, tail], slots.at[3, tail], to[1])

    def start(self):
        for i in range(2):
            self.near[i].start()
            self.far[i].start()

    def relay(self):
        self.near[0].arrive()
        self.lead.start()
        self.far[0].arrive()
        self.tail.start()

    def finish(self):
        self.near[1].arrive()
        self.far[1].arrive()
        self.lead.arrive()
        self.tail.arrive()


class Pair:
    def __init__(self, wires, to, halves, ins):
        self.halves, self.ins, self.wires, self.to, self.step = halves, ins, wires, to, 0
        self.sent = [
            [wires.copy(halves[h][i], ins[h].at[i], to[(1, 2)[(h + i) % 2]]) for h in range(2)]
            for i in range(2)
        ]

    def start(self):
        for wire in self.sent[0]:
            wire.start()

    def middle(self):
        for h in range(2):
            self.sent[0][h].arrive()
            one, two = self.halves[h][0], self.halves[h][1]
            two[...] = (one[...].astype(F32) + self.ins[h][0].astype(F32)).astype(BF16)
            self.sent[1][h].start()

    def finish(self):
        for h in range(2):
            self.sent[1][h].arrive()
            two, three = self.halves[h][1], self.halves[h][2]
            three[...] = (two[...].astype(F32) + self.ins[h][1].astype(F32)).astype(BF16)


def reduce_kernel(
    late_hbm,
    lead_hbm,
    tail_hbm,
    normed_hbm,
    dt_hbm,
    joined_hbm,
    joined_peer_hbm,
    hidden_hbm,
    d_middle_hbm,
    w_hbm,
    normed_x,
    normed_peer,
    normed_cond_x,
    normed_cond_peer,
    d_pre_own,
    d_pre_x,
    active_x,
    active_cond_x,
    cot_hbm,
    cot_z,
    cot_zz,
    cot_far,
    cot_peer,
    gain_ref,
    vec_two_ref,
    fc1_bias_ref,
    p_all,
    f_all,
    g_all,
    q_all,
    s_all,
    c_all,
    din_hbm,
    dskip_hbm,
    vec_ref,
    left_one,
    right_one,
    left_two,
    right_two,
    cond_rows,
    cond_flat,
    active_cond,
    f_own,
    f_up,
    f_down,
    g_own,
    g_lead_one,
    g_tail_one,
    g_lead_two,
    g_tail_two,
    l_own,
    l_up,
    l_down,
    q_own,
    q_sum,
    q_up,
    q_down,
    s_own,
    s_one,
    s_two,
    s_z,
    s_up,
    s_down,
    d_own,
    d_one,
    d_two,
    p_lead,
    p_tail,
    p_lead_in,
    p_tail_in,
    low_ref,
    low_peer,
    c_own,
    c_in,
    rows_ref,
    hidden_ref,
    d_middle_ref,
    joined_ref,
    joined_peer_ref,
    v_own,
    v_in,
    send_sems,
    recv_sems,
    local_sems,
):
    rows, width = hidden_hbm.shape
    depth = f_own.shape[0]
    mid = depth // 2
    slots = c_own.shape[1]
    images = rows - slots
    place, index = lax.axis_index("seq"), lax.axis_index("batch")
    chip, core = index // 2, index % 2
    last = depth - 1
    to, other, up_to, down_to = ends_of(place, index, depth)
    greet([to[1], to[2], to[3], other], chip, depth, up_to, down_to)
    wires = Wires(send_sems, recv_sems)
    taken = [0]

    def local(src, dst):
        taken[0] += 1
        copy = pltpu.make_async_copy(src, dst, local_sems.at[taken[0] - 1])
        copy.start()
        return copy

    keeps = []

    d_hbm = (lead_hbm, tail_hbm)
    norm_sum = Square(
        wires,
        to,
        lambda h, k: d_own.at[h, (0, 1, 1, None)[k]],
        [d_one.at[h] for h in range(2)],
        [d_two.at[h] for h in range(2)],
        src=lambda h, k: d_hbm[h].at[k],
    )
    norm_sum.start()

    l_load = local(late_hbm, l_own)
    l_line = Line(wires, depth, chip, up_to, down_to, lambda d: l_own.at[d], l_up, l_down)

    img, cnd = pl.ds(0, images), pl.ds(images, slots)

    def cut(g):
        return pl.ds(pl.multiple_of(g * images, images), images)

    def end(g):
        return pl.ds(pl.multiple_of(8 * images + g * slots, slots), slots)

    loads_two, loads_able = [], []
    for i in range(depth):
        source = (chip + depth - AWAY[i]) % depth
        for c in range(2):
            g = source * 2 + c
            loads_two.append(local(active_x.at[i, c], left_two.at[:, :, cut(g)]))
            loads_two.append(local(active_cond_x.at[i, c], active_cond.at[g]))
    held = [cot_hbm, cot_z.at[0], cot_z.at[1], cot_zz.at[0], cot_zz.at[1], cot_far]
    for away, picks in ((0, (0, 0)), (1, (1, 2)), (2, (3, 4)), (3, (5, 5))):
        for which in range(2):
            if away == 0 and which == 1:
                continue
            z = chip - away if which == 0 else chip + away
            able = (z >= 0) & (z <= last)
            for ref, c in ((held[picks[which]], core), (cot_peer.at[picks[which]], 1 - core)):
                g = jnp.clip(z, 0, last) * 2 + c
                for src, dst in ((img, cut(g)), (cnd, end(g))):
                    sem = local_sems.at[taken[0]]
                    taken[0] += 1
                    copy = pltpu.make_async_copy(ref.at[src], right_two.at[dst], sem)
                    pl.when(able)(copy.start)
                    loads_able.append((able, copy))
    swaps_one = []
    d_pre_of = lambda k, part: d_pre_x.at[k - 1, part] if k else d_pre_own.at[part]
    for k in range(4):
        swaps_one.append(wires.copy(d_pre_of(k, img), right_one.at[cut(4 + k)], other))
        swaps_one.append(wires.copy(d_pre_of(k, cnd), right_one.at[end(4 + k)], other))
    for wire in swaps_one:
        wire.start()
    loads_one = []
    for k in range(4):
        for g, left, cond in (
            (k, normed_x.at[k, :, core], normed_cond_x.at[k]),
            (4 + k, normed_peer.at[k], normed_cond_peer.at[k]),
        ):
            loads_one.append(local(left, left_one.at[:, :, cut(g)]))
            loads_one.append(local(cond, cond_rows.at[pl.ds(g * slots, slots)]))
        loads_one.append(local(d_pre_of(k, img), right_one.at[cut(k)]))
        loads_one.append(local(d_pre_of(k, cnd), right_one.at[end(k)]))
    d_loads = [
        local(d_hbm[h].at[k], d_own.at[h, i]) for h, ks in ((0, (0, 2)), (1, (0, 1))) for i, k in enumerate(ks)
    ]
    p_cut = p_lead.shape[1]
    h_loads = [local(hidden_hbm, hidden_ref), local(d_middle_hbm, d_middle_ref)]
    j_loads = [local(joined_hbm, joined_ref), local(joined_peer_hbm, joined_peer_ref)]
    l_load.wait()
    l_line.hop(0)

    for copy in loads_two:
        copy.wait()
    for able, copy in loads_able:
        pl.when(able)(copy.wait)
    small = f_own.shape[1]
    for j in range(4):
        left_two[j, :, 8 * images :] = jnp.concatenate(
            [active_cond[g, :, j * slots : (j + 1) * slots] for g in range(8)], 1
        )
    g_own[...] = (
        dot(left_two[...].reshape(4 * small, 8 * rows), right_two[...])
        .astype(BF16)
        .reshape(4, small, width)
    )
    l_line.hop(1)
    g_cut = g_lead_one.shape[1]
    g_sum = Square(
        wires,
        to,
        lambda h, k: g_own.at[flip(place, k), (pl.ds(0, g_cut), pl.ds(g_cut, small - g_cut))[h]],
        (g_lead_one, g_tail_one),
        (g_lead_two, g_tail_two),
    )

    for copy in loads_one:
        copy.wait()
    flat = turned(cond_rows[...])
    for b in range(2 * depth):
        cond_flat[b // 2, b % 2] = flat[b * small : (b + 1) * small]
    for z in range(depth):
        left_one[z, :, 8 * images :] = cond_flat[z, core]
    for wire in swaps_one:
        wire.arrive()
    f_own[...] = (
        dot(left_one[...].reshape(depth * small, 8 * rows), right_one[...])
        .astype(BF16)
        .reshape(depth, small, width)
    )
    f_line = Line(wires, depth, chip, up_to, down_to, lambda d: f_own.at[d], f_up, f_down)
    f_line.hop(0)
    for copy in d_loads:
        copy.wait()
    norm_sum.middle()
    for t in range(2, last):
        l_line.hop(t)

    def heads_part(normed, dt):
        loads = [local(normed_hbm, normed), local(dt_hbm, dt)]
        for copy in loads:
            copy.wait()
        step = 3 * LANES
        for part in range(normed.shape[1] // step):
            grads = lax.dot_general(
                normed[:, part * step : (part + 1) * step],
                dt[...],
                (((0,), (1,)), ((), ())),
                preferred_element_type=F32,
            ).astype(BF16)
            q_own[pl.ds(part * step, step)] = grads

    pl.run_scoped(
        heads_part, pltpu.VMEM(normed_hbm.shape, BF16), pltpu.VMEM(dt_hbm.shape, BF16)
    )
    height = q_sum.shape[1]
    q_swap = [
        wires.copy(
            q_own.at[pl.ds(pl.multiple_of((2 * z + 1 - core) * height, 16), height)],
            q_sum.at[z],
            other,
        )
        for z in range(depth)
    ]
    for wire in q_swap:
        wire.start()

    norm_sum.finish()
    low_swap = wires.copy(low_ref, low_peer, other)
    v_swap = wires.copy(v_own.at[0], v_in.at[0], other)
    for copy in h_loads:
        copy.wait()
    upstream = jnp.concatenate([d_own[0, 0].astype(F32), d_own[1, 0].astype(F32)], 0)
    scaled, factor = normalize(hidden_ref[...])
    d_hidden = d_middle_ref[...] + norm_back(
        upstream, scaled, factor, gain_ref[...].reshape(1, -1)
    )
    low_ref[...] = d_hidden.astype(BF16)
    low_swap.start()
    c_src = low_ref.at[pl.ds(images, slots)]
    c_go = Spread(wires, to, c_in, c_src)
    c_go.start()
    l_line.finish()
    p_lead[0] = l_own[chip, :p_cut]
    p_tail[0] = l_own[chip, p_cut:]
    p_sum = Pair(
        wires,
        to,
        [[ref.at[i] for i in range(3)] for ref in (p_lead, p_tail)],
        (p_lead_in, p_tail_in),
    )
    p_sum.start()
    g_sum.start()
    v_own[0] = jnp.zeros(v_own.shape[1:], F32)
    v_own[0, 0:1] = jnp.sum(d_hidden, axis=0, keepdims=True)
    v_own[0, 1:2] = jnp.sum(upstream * scaled, axis=0, keepdims=True)
    v_own[0, 2:3] = jnp.sum(upstream, axis=0, keepdims=True)
    v_own[0, 3:7] = vec_two_ref[0:4]
    v_own[0, 8:12] = fc1_bias_ref[...]
    v_swap.start()
    f_line.hop(1)
    for z, wire in enumerate(q_swap):
        wire.arrive()
        add_rows(q_sum.at[z], q_own.at[pl.ds(pl.multiple_of((2 * z + core) * height, 16), height)])
    q_line = Line(wires, depth, chip, up_to, down_to, lambda d: q_sum.at[d], q_up, q_down)
    q_line.hop(0)
    c_go.relay()

    for copy in j_loads:
        copy.wait()
    low_swap.arrive()
    block = joined_ref.shape[1]
    chunk = block // 4
    grads = both(
        joined_ref[...].reshape(depth * block, rows),
        joined_peer_ref[...].reshape(depth * block, rows),
        low_ref[...],
        low_peer[...],
    )
    for h in range(mid):
        for j in range(4):
            at = [(2 * h + i) * block + j * chunk for i in range(2)]
            piece = jnp.concatenate([grads[a : a + chunk] for a in at], 0)
            s_own[flip(place, j), h] = piece.astype(BF16)
    s_sum = Square(
        wires,
        to,
        lambda h, k: s_own.at[k, h],
        [s_one.at[h] for h in range(2)],
        [s_two.at[h] for h in range(2)],
    )
    s_sum.start()
    for t in range(2, last):
        f_line.hop(t)
    p_sum.middle()

    c_go.finish()
    rows_ref[:images] = low_ref[:images]
    rows_ref[images : images + slots] = low_ref[images:]
    for k in range(1, 4):
        rows_ref[images + k * slots : images + (k + 1) * slots] = c_in[k]

    def rows_part(which, out_hbm):
        def run(w, stage):
            copy = local(w_hbm.at[pl.ds(which * width, width)], w)
            copy.wait()
            stage[...] = dot_nt(rows_ref[...], w[...])
            for k in range(4):
                c_own[k, :, which * width : (which + 1) * width] = stage[
                    images + k * slots : images + (k + 1) * slots
                ].astype(BF16)
            local(stage.at[pl.ds(0, images)], out_hbm).wait()

        pl.run_scoped(
            run, pltpu.VMEM((width, width), BF16), pltpu.VMEM((images + 4 * slots, width), F32)
        )

    rows_part(0, din_hbm)
    q_line.hop(1)
    g_sum.middle()
    rows_part(1, dskip_hbm)
    keeps.append(local(c_own, c_all))
    for t in range(2, last):
        q_line.hop(t)

    v_swap.arrive()
    v_own[1] = v_own[0] + v_in[0]
    v_own[2] = v_own[1]
    v_own[3] = v_own[1]
    v_up = wires.copy(v_own.at[2], v_in.at[1], up_to, chip < last)
    v_down = wires.copy(v_own.at[3], v_in.at[2], down_to, chip > 0)
    s_sum.middle()
    g_sum.finish()
    f_line.finish()
    s_sum.finish()
    room = s_z.shape[1]
    for h in range(mid):
        value = s_own[0, h].astype(F32)
        for i in range(2):
            s_z[2 * h + i] = jnp.concatenate(
                [value[i * chunk : (i + 1) * chunk], jnp.zeros((room - chunk, width), F32)], 0
            ).astype(BF16)
    s_line = Line(wires, depth, chip, up_to, down_to, lambda d: s_z.at[d], s_up, s_down)
    s_line.hop(0)
    g_go = Spread(wires, to, g_all, g_own.at[place])
    g_go.start()
    f_go = Spread(wires, to, f_all, f_own.at[chip])
    f_go.start()
    keeps.append(local(g_own.at[place], g_all.at[0]))
    keeps.append(local(f_own.at[chip], f_all.at[0]))

    @pl.when(chip > 0)
    def _():
        v_up.arrive()
        v_own[2] = v_own[1] + v_in[1]

    @pl.when(chip < last)
    def _():
        v_up.start()

    @pl.when(chip < last)
    def _():
        v_down.arrive()
        v_own[3] = v_own[1] + v_in[2]

    @pl.when(chip > 0)
    def _():
        v_down.start()

    v_own[4] = v_own[2] + v_own[3] - v_own[1]
    v_near = wires.copy(v_own.at[4], v_in.at[3], to[1])
    v_near.start()
    s_line.hop(1)
    q_line.finish()
    q_go = Spread(wires, to, q_all, q_sum.at[chip])
    q_go.start()
    keeps.append(local(q_sum.at[chip], q_all.at[0]))
    for t in range(2, last):
        s_line.hop(t)
    g_go.relay()
    f_go.relay()
    v_near.arrive()
    v_own[5] = v_own[4] + v_in[3]
    v_far = wires.copy(v_own.at[5], v_in.at[4], to[2])
    v_far.start()
    s_line.finish()
    s_go = Spread(wires, to, s_all, s_z.at[chip])
    s_go.start()
    keeps.append(local(s_z.at[chip], s_all.at[0]))
    q_go.relay()
    p_sum.finish()
    keeps.append(local(p_lead.at[2], p_all.at[pl.ds(0, p_cut)]))
    keeps.append(local(p_tail.at[2], p_all.at[pl.ds(p_cut, p_tail.shape[1])]))
    v_far.arrive()
    vec_ref[...] = v_own[5] + v_in[4]
    s_go.relay()
    f_go.finish()
    g_go.finish()
    q_go.finish()
    s_go.finish()
    for copy in keeps:
        copy.wait()
    wires.drain()


def reduce_all(
    late, lead, tail, normed_all, d_triple_t, joined, joined_peer, hidden, d_middle, w, feeds,
    gain, vec_two, fc1_bias_grad,
):
    depth, small, width = late.shape
    rows = hidden.shape[0]
    slots = SLOTS // 4
    images = rows - slots
    mid = depth // 2
    own = d_triple_t.shape[0]
    skip_rows = joined.shape[1]
    skip_chunk = (skip_rows // 4 + 15) // 16 * 16
    pair = depth // 2 * (skip_rows // 4)
    half = rows // 2
    cut = (small // 2 + 15) // 16 * 16
    v = lambda *shape: pltpu.VMEM(shape, BF16)
    ends = depth - 1
    scratch = [
        v(depth, small, 8 * rows), v(8 * rows, width), v(depth, small, 8 * rows), v(8 * rows, width),
        v(8 * slots, width), v(depth, 2, small, 8 * slots), v(8, small, 4 * slots),
        v(depth, small, width), v(ends, small, width), v(ends, small, width),
        v(4, small, width), v(2, cut, width), v(2, small - cut, width), v(cut, width), v(small - cut, width),
        v(depth, small, width), v(ends, small, width), v(ends, small, width),
        v(width, own), v(depth, small, own), v(ends, small, own), v(ends, small, own),
        v(4, 2, pair, width), v(2, 2, pair, width), v(2, pair, width),
        v(depth, skip_chunk, width), v(ends, skip_chunk, width), v(ends, skip_chunk, width),
        v(2, 2, half, width), v(2, 2, half, width), v(2, half, width),
        v(3, cut, width), v(3, small - cut, width), v(2, cut, width), v(2, small - cut, width),
        v(rows, width), v(rows, width), v(4, slots, 2 * width),
        v(4, slots, width), v(images + 4 * slots, width),
        pltpu.VMEM((rows, width), F32), pltpu.VMEM((rows, width), F32),
        v(*joined.shape), v(*joined.shape),
        pltpu.VMEM((6, 16, width), F32), pltpu.VMEM((5, 16, width), F32),
        pltpu.SemaphoreType.DMA((128,)), pltpu.SemaphoreType.DMA((128,)), pltpu.SemaphoreType.DMA((128,)),
    ]
    hbm = pl.BlockSpec(memory_space=pl.ANY)
    vmem = pl.BlockSpec(memory_space=pltpu.VMEM)
    f = lambda *shape: jax.ShapeDtypeStruct(shape, F32)
    b = lambda *shape: jax.ShapeDtypeStruct(shape, BF16)
    return pl.pallas_call(
        reduce_kernel,
        in_specs=[hbm] * 23 + [vmem] * 3,
        out_specs=[hbm] * 8 + [vmem],
        out_shape=[
            b(small, width),
            b(4, small, width),
            b(4, small, width),
            b(4, small, own),
            b(4, skip_chunk, width),
            b(4, slots, 2 * width),
            f(images, width),
            f(images, width),
            f(16, width),
        ],
        scratch_shapes=scratch,
        compiler_params=pltpu.CompilerParams(
            vmem_limit_bytes=VMEM_LIMIT, collective_id=0, has_side_effects=True
        ),
        cost_estimate=cost(1e10, 1e8),
        name="reduce_all",
    )(
        late, lead, tail, normed_all, d_triple_t, joined, joined_peer, hidden, d_middle, w, *feeds,
        gain, vec_two, fc1_bias_grad,
    )


def ends_of(place, index, depth):
    chip, core = index // 2, index % 2
    to = {k: (index, flip(place, k)) for k in (1, 2, 3)}
    return to, (index + 1 - 2 * core, place), (index + 2, place), (index - 2, place)


def line_of(place, index, depth):
    chip = index // 2
    return [((chip + i) % depth * 2 + c, place) for i in range(1, depth) for c in (0, 1)]


def arrive_by_core(wires, core):
    for c in range(2):

        @pl.when(core == c)
        def _():
            wires[2 * c].arrive()
            wires[2 * c + 1].arrive()


class Hop:
    def __init__(self, wires, depth, chip, up_to, down_to, t, src_up, src_down, dst_up, dst_down):
        last = depth - 1
        self.up = wires.copy(src_up, dst_up, up_to, (chip < last) & (chip >= t))
        self.down = wires.copy(src_down, dst_down, down_to, (chip > 0) & (chip <= last - t))
        self.from_up = (chip > 0) & (chip - 1 >= t)
        self.from_down = (chip < last) & (chip + 1 <= last - t)

    def start(self):
        pl.when(self.up.when)(self.up.start)
        pl.when(self.down.when)(self.down.start)

    def arrive(self):
        pl.when(self.from_up)(self.up.arrive)
        pl.when(self.from_down)(self.down.arrive)


def greet(devices, chip=None, depth=0, up_to=None, down_to=None):
    barrier = pltpu.get_barrier_semaphore()
    for device in devices:
        pl.semaphore_signal(barrier, inc=1, device_id=device, device_id_type=MESH)
    if chip is None:
        pl.semaphore_wait(barrier, len(devices))
        return

    @pl.when(chip < depth - 1)
    def _():
        pl.semaphore_signal(barrier, inc=1, device_id=up_to, device_id_type=MESH)

    @pl.when(chip > 0)
    def _():
        pl.semaphore_signal(barrier, inc=1, device_id=down_to, device_id_type=MESH)

    pl.semaphore_wait(
        barrier, len(devices) + jnp.minimum(chip, 1) + jnp.minimum(depth - 1 - chip, 1)
    )


class Locals:
    def __init__(self, sems):
        self.sems, self.taken = sems, 0

    def copy(self, src, dst):
        self.taken += 1
        assert self.taken <= self.sems.shape[0]
        return pltpu.make_async_copy(src, dst, self.sems.at[self.taken - 1])

    def start(self, src, dst):
        copy = self.copy(src, dst)
        copy.start()
        return copy


def own_slots(cond_ref, pad_ref, place, slots):
    pad_ref[...] = jnp.zeros(pad_ref.shape, BF16)
    pad_ref[0 : cond_ref.shape[0]] = cond_ref[...]
    return pad_ref[pl.ds(pl.multiple_of(place * slots, 16), slots)]


def start_kernel(
    window,
    length_ref,
    x_ref,
    x_cond_ref,
    s_ref,
    s_cond_ref,
    cot_ref,
    cot_cond_ref,
    bias_ref,
    gain_ref,
    shift_ref,
    w_hbm,
    qkv_w_hbm,
    hidden_ref,
    normed_hbm,
    heads_ref,
    qkv_ref,
    joined_hbm,
    peer_hbm,
    cot_all,
    cot_z,
    lse_ref,
    ctx_hbm,
    rest_hbm,
    cot_zz,
    pad_ref,
    x_all,
    s_all,
    normed_all,
    joined_ref,
    w_ref,
    qkv_w_ref,
    vt_ref,
    ot_ref,
    go_ref,
    rest_ref,
    send_sems,
    recv_sems,
    local_sems,
):
    images, width = x_ref.shape
    slots = x_all.shape[0] - images
    place, index = lax.axis_index("seq"), lax.axis_index("batch")
    core = index % 2
    chip = index // 2
    depth = joined_hbm.shape[0]
    to, other, up_to, down_to = ends_of(place, index, depth)
    wires, moves = Wires(send_sems, recv_sems), Locals(local_sems)
    loads = [
        moves.start(w_hbm.at[span], w_ref.at[span]) for span in (pl.ds(0, width), pl.ds(width, width))
    ]
    w_load = moves.start(qkv_w_hbm, qkv_w_ref)
    greet([to[1], to[2], to[3], other], chip, depth, up_to, down_to)
    cot_all[:images] = cot_ref[...]
    cot_all[images:] = own_slots(cot_cond_ref, pad_ref, place, slots)
    cot_go = Hop(
        wires, depth, chip, up_to, down_to, 0, cot_all, cot_all, cot_z.at[0], cot_z.at[1]
    )
    cot_go.start()
    for ref, cond, whole in ((x_ref, x_cond_ref, x_all), (s_ref, s_cond_ref, s_all)):
        whole[:images] = ref[...]
        whole[images:] = own_slots(cond, pad_ref, place, slots)
    spread = Spread(wires, to, normed_all)
    half = x_all.shape[0] // 2
    loads[0].wait()
    for i in range(2):
        span = slice(i * half, (i + 1) * half)
        hidden = dot(x_all[span], w_ref[:width])
        if i == 0:
            loads[1].wait()
        hidden += dot(s_all[span], w_ref[width:]) + bias_ref[...].reshape(1, -1)
        hidden_ref[span] = hidden
        scaled, _ = normalize(hidden)
        normed_all[0, span] = (
            scaled * gain_ref[...].reshape(1, -1) + shift_ref[...].reshape(1, -1)
        ).astype(BF16)
        spread.near[i].start()
        spread.far[1 - i].start()
    size = joined_ref.shape[2]
    per = width // size
    for which, whole in enumerate((x_all, s_all)):
        flat = turned(whole[...])
        for i in range(per):
            block = which * per + i
            joined_ref[block // 2, block % 2] = flat[i * size : (i + 1) * size]
    swap = wires.copy(joined_ref.at[:, 1 - core], peer_hbm, other)
    swap.start()
    keep = moves.start(joined_ref.at[:, core], joined_hbm)
    heads = qkv_ref.shape[0]
    width_own = heads * HEAD_DIM
    real = lax.broadcasted_iota(jnp.int32, (width, LANES), 1) < HEAD_DIM

    def weights(which):
        first = place * width_own + which * width
        start = jnp.minimum(first // LANES * LANES, 3 * width - window)
        value = qkv_w_ref[:, pl.ds(pl.multiple_of(start, LANES), window)].astype(F32)
        value = pltpu.roll(value, lax.rem(window - (first - start), window), 1)
        for head in range(heads):
            shifted = value if head == 0 else pltpu.roll(value, window - head * HEAD_DIM, 1)
            at = (3 * head + which) * LANES
            heads_ref[:, at : at + LANES] = jnp.where(real, shifted[:, :LANES], 0.0).astype(BF16)

    rows = normed_all.shape[1]
    lane = lax.broadcasted_iota(jnp.int32, (1, LANES), 1)
    one = jnp.where(lane == HEAD_DIM, 1.0, 0.0)
    slot = lax.broadcasted_iota(jnp.int32, (slots, LANES), 0)
    lanes = lax.broadcasted_iota(jnp.int32, (slots, LANES), 1)

    def project(part):
        hidden_key = flip(place, part) * slots + slot > length_ref[0]
        bias = jnp.where(hidden_key & (lanes == HEAD_DIM), -1e30, 0.0)
        base = part * rows
        for head in range(heads):
            triple = dot(
                normed_all[part], heads_ref[:, 3 * head * LANES : 3 * (head + 1) * LANES]
            )
            qkv_ref[head, base : base + rows, :LANES] = (triple[:, :LANES] + one).astype(BF16)
            key = triple[:, LANES : 2 * LANES]
            qkv_ref[head, base : base + images, LANES : 2 * LANES] = key[:images].astype(BF16)
            qkv_ref[head, base + images : base + rows, LANES : 2 * LANES] = (
                key[images:] + bias
            ).astype(BF16)
            qkv_ref[head, base : base + rows, 2 * LANES :] = triple[:, 2 * LANES :].astype(BF16)

    w_load.wait()
    weights(0)
    spread.relay()
    weights(1)
    weights(2)
    project(0)
    spread.near[1].arrive()
    project(1)
    spread.far[1].arrive()
    project(2)
    spread.lead.arrive()
    spread.tail.arrive()
    project(3)
    out = moves.start(normed_all, normed_hbm)
    cot_go.arrive()
    cot_on = Hop(
        wires, depth, chip, up_to, down_to, 1, cot_z.at[0], cot_z.at[1], cot_zz.at[0], cot_zz.at[1]
    )
    cot_on.start()

    total = 4 * rows
    step = 3 * LANES
    go, keeps = [], []
    sent = 0
    for head in range(heads):
        vt_ref[...] = turned(qkv_ref[head, :, 2 * LANES :])
        for first in range(0, total, step):
            span = slice(first, first + step)
            scores = dot_nt(qkv_ref[head, :, LANES : 2 * LANES], qkv_ref[head, span, :LANES])
            peak = jnp.max(scores, axis=0, keepdims=True)
            shifted = jnp.exp2((scores - peak) * SCALE2)
            sums = jnp.sum(shifted, axis=0, keepdims=True)
            mixed = dot(vt_ref[...], shifted.astype(BF16)) / sums
            ot_ref[head * HEAD_DIM : (head + 1) * HEAD_DIM, span] = mixed[:HEAD_DIM]
            lse_ref[head, :, span] = peak * SCALE2 + jnp.log2(sums)
        done = (head + 1) * HEAD_DIM if head == heads - 1 else (head + 1) * HEAD_DIM // 16 * 16
        if head:
            half = pl.ds(sent, done - sent)
            for part in (3, 1, 2, 0):
                go_ref[part, half] = ot_ref[half, part * rows : part * rows + images].astype(BF16)
                if part:
                    go.append(wires.copy(go_ref.at[part, half], ctx_hbm.at[part, half], to[part]))
                    go[-1].start()
                else:
                    keeps.append(moves.start(go_ref.at[0, half], ctx_hbm.at[0, half]))
            sent = done
    for part in (3, 1, 2, 0):
        rest_ref[part] = split_lanes(ot_ref[:, part * rows : (part + 1) * rows])[1]
        if part:
            go.append(wires.copy(rest_ref.at[part], rest_hbm.at[part], to[part]))
            go[-1].start()
        else:
            keeps.append(moves.start(rest_ref.at[0], rest_hbm.at[0]))
    swap.arrive()
    cot_on.arrive()
    for wire in go:
        wire.arrive()
    for copy in keeps + [keep, out]:
        copy.wait()
    wires.drain()


def start_stage(depth, length, x, x_cond, s, s_cond, cot, cot_cond, w, bias, gain, shift, qkv_w):
    images, width = x.shape
    slots = SLOTS // 4
    rows = images + slots
    heads = HEADS // 4
    own = heads * HEAD_DIM
    window = (max(p * own % LANES for p in range(4)) + own + LANES - 1) // LANES * LANES
    block = 2 * width // (2 * depth)
    vmem, hbm = pl.BlockSpec(memory_space=pltpu.VMEM), pl.BlockSpec(memory_space=pl.ANY)
    b = lambda *shape: jax.ShapeDtypeStruct(shape, BF16)
    v = lambda *shape: pltpu.VMEM(shape, BF16)
    return pl.pallas_call(
        functools.partial(start_kernel, window),
        in_specs=[pl.BlockSpec(memory_space=pltpu.SMEM)] + [vmem] * 9 + [hbm] * 2,
        out_specs=[vmem, hbm, vmem, vmem, hbm, hbm, vmem, hbm, vmem, hbm, hbm, hbm],
        out_shape=[
            jax.ShapeDtypeStruct((rows, width), F32),
            b(4, rows, width),
            b(width, heads * 3 * LANES),
            b(heads, 4 * rows, 3 * LANES),
            b(depth, block, rows),
            b(depth, block, rows),
            b(rows, width),
            b(2, rows, width),
            jax.ShapeDtypeStruct((heads, 1, 4 * rows), F32),
            b(4, own, images),
            b(4, (own // 4 + 15) // 16 * 16, LANES),
            b(2, rows, width),
        ],
        scratch_shapes=[
            v(SLOTS, width), v(rows, width), v(rows, width), v(4, rows, width),
            v(depth, 2, block, rows), v(2 * width, width), v(width, 3 * width),
            v(LANES, 4 * rows), pltpu.VMEM((own, 4 * rows), F32), v(4, own, images),
            v(4, (own // 4 + 15) // 16 * 16, LANES),
            pltpu.SemaphoreType.DMA((32,)), pltpu.SemaphoreType.DMA((32,)), pltpu.SemaphoreType.DMA((16,)),
        ],
        compiler_params=pltpu.CompilerParams(
            vmem_limit_bytes=VMEM_LIMIT, collective_id=1, has_side_effects=True
        ),
        cost_estimate=cost(12 * rows * width * width, 12 * width * width),
        name="start_stage",
    )(length, x, x_cond, s, s_cond, cot, cot_cond, bias, gain, shift, w, qkv_w)


def split_lanes(value):
    size = value.shape[0] // 4
    cut = value.shape[1] - 32
    rest = jnp.concatenate([value[i * size : (i + 1) * size, cut:] for i in range(4)], 1)
    room = (size + 15) // 16 * 16
    rest = jnp.concatenate([rest, jnp.zeros((room - size, 4 * 32), F32)], 0)
    return value[:, :cut].astype(BF16), rest.astype(BF16)


def join_lanes(main, rest):
    size = main.shape[0] // 4
    rest = rest.astype(F32)
    rest = jnp.concatenate([rest[:size, i * 32 : (i + 1) * 32] for i in range(4)], 0)
    return jnp.concatenate([main.astype(F32), rest], 1)


def both(own_t, peer_t, own, peer):
    rows = own_t.shape[-1]
    cut = rows // 256 * 256
    total = dot(own_t[:, :cut], own[:cut]) + dot(peer_t[:, :cut], peer[:cut])
    ends_t = jnp.concatenate([own_t[:, cut:], peer_t[:, cut:]], 1)
    return total + dot(ends_t, jnp.concatenate([own[cut:], peer[cut:]], 0))


def middle_kernel(
    ctx_t_ref,
    ctx_rest_ref,
    hidden_ref,
    cot_ref,
    proj_bias_ref,
    gain_ref,
    shift_ref,
    fc2_bias_ref,
    fc1_bias_ref,
    lse_ref,
    cot_z,
    cot_zz,
    proj_hbm,
    fc1_hbm,
    fc2_hbm,
    qkv_hbm,
    w_hbm,
    out_hbm,
    c_all,
    d_middle_ref,
    late_hbm,
    vec_ref,
    fc1_vec_ref,
    dt_ref,
    lead_ref,
    tail_ref,
    normed_x,
    normed_peer,
    normed_cond_x,
    normed_cond_peer,
    d_pre_own,
    d_pre_x,
    active_x,
    active_cond_x,
    cot_far,
    cot_peer,
    proj_ref,
    fc1_ref,
    fc2_ref,
    bias_ref,
    normed_ref,
    middle_ref,
    acc_out,
    acc_back,
    normed_t,
    ctx_two,
    ctx_peer,
    active_t,
    active_pack,
    d_pre,
    d_branch_ref,
    d_branch_peer,
    d_go,
    d_rest,
    d_in,
    d_rest_in,
    dot_all,
    dt_all,
    d_all,
    dk_ref,
    dv_ref,
    proj_stage,
    c_own,
    send_sems,
    recv_sems,
    local_sems,
):
    rows, width = cot_ref.shape
    slots = c_own.shape[0]
    images = rows - slots
    depth, _, small, _ = ctx_two.shape
    chunk = fc1_ref.shape[2]
    own = ctx_t_ref.shape[1]
    quarter = chunk // 8
    place, index = lax.axis_index("seq"), lax.axis_index("batch")
    chip, core = index // 2, index % 2
    to, other, up_to, down_to = ends_of(place, index, depth)
    moves = Locals(local_sems)

    def load(i):
        span = pl.ds(pl.multiple_of((chip + AWAY[i]) % depth * chunk, LANES), chunk)
        return (
            moves.start(fc1_hbm.at[:, span], fc1_ref.at[i % 2]),
            moves.start(fc2_hbm.at[span], fc2_ref.at[i % 2]),
        )

    proj_load = moves.start(proj_hbm, proj_ref)
    loads = [load(0), load(1)]
    greet([to[1], to[2], to[3], other] + line_of(place, index, depth))
    wires = Wires(send_sems, recv_sems)
    hop = Hop(
        wires, depth, chip, up_to, down_to, 2, cot_zz.at[0], cot_zz.at[1], cot_far, cot_far
    )
    hop.start()
    for f in range(4):
        bias_ref[f : f + 1] = fc1_bias_ref[f * chunk : (f + 1) * chunk].reshape(1, -1)

    branch = proj_bias_ref[...].reshape(1, -1) + hidden_ref[...]
    proj_load.wait()
    for k in range(4):
        at = pl.ds(pl.multiple_of(flip(place, k) * own, 16), own)
        context_t = join_lanes(ctx_t_ref[k], ctx_rest_ref[k])
        branch += dot(context_t.T.astype(BF16), proj_ref[at, :])
        for i in range(2):
            ctx_two[flip(place, k), i] = context_t[i * small : (i + 1) * small].astype(BF16)
    ctx_swap = wires.copy(ctx_two.at[:, 1 - core], ctx_peer, other)
    ctx_swap.start()
    middle_ref[...] = branch
    scaled, _ = normalize(branch)
    gain = gain_ref[...].reshape(1, -1)
    normed = scaled * gain + shift_ref[...].reshape(1, -1)
    normed_ref[...] = normed.astype(BF16)
    normed_t[...] = normed[:images].T.astype(BF16).reshape(normed_t.shape)
    normed_go = Spread(wires, to, normed_x, normed_t, depth // 2)
    normed_go.start()
    keeps = [
        moves.start(normed_t, normed_x.at[0]),
        moves.start(normed_ref.at[pl.ds(images, slots)], normed_cond_x.at[0]),
    ]
    cond_go = [
        wires.copy(normed_ref.at[pl.ds(images, slots)], normed_cond_x.at[k], to[k]) for k in (1, 2, 3)
    ]
    for wire in cond_go:
        wire.start()

    near = []
    for i in range(4):
        f = (chip + AWAY[i]) % depth
        for copy in loads[i]:
            copy.wait()
        fc1, fc2 = fc1_ref.at[i % 2], fc2_ref.at[i % 2]
        before = dot(normed_ref[...], fc1[...]) + bias_ref[pl.ds(f, 1)]
        cdf = 0.5 + 0.5 * lax.erf(before * math.sqrt(0.5))
        active = before * cdf
        slope = cdf + before * (jnp.exp(-0.5 * before * before) * (1.0 / math.sqrt(2.0 * math.pi)))
        d_before = dot_nt(cot_ref[...], fc2[...]) * slope
        fc1_vec_ref[pl.ds(f, 1)] = jnp.sum(d_before, axis=0, keepdims=True)
        d_low = d_before.astype(BF16)
        d_pre[f] = d_low
        flat = active.T
        for c in range(2):
            for j in range(4):
                piece = flat[(c * 4 + j) * quarter : (c * 4 + j + 1) * quarter]
                active_t[i, c, j] = piece[:, :images].astype(BF16)
            active_pack[i, c] = jnp.concatenate(
                [flat[(c * 4 + j) * quarter : (c * 4 + j + 1) * quarter, images:] for j in range(4)], 1
            ).astype(BF16)
        if i < 3:
            for c in range(2):
                device = (f * 2 + c, place)
                near.append(wires.by_core(core, active_t.at[i, c], active_x.at[i, core], device))
                near.append(
                    wires.by_core(core, active_pack.at[i, c], active_cond_x.at[i, core], device)
                )
            for wire in near[4 * i :]:
                wire.start()
        else:
            keeps.append(moves.start(active_t.at[3, core], active_x.at[3, core]))
            keeps.append(moves.start(active_pack.at[3, core], active_cond_x.at[3, core]))
            late_go = [
                wires.copy(active_t.at[3, 1 - core], active_x.at[3, core], other),
                wires.copy(active_pack.at[3, 1 - core], active_cond_x.at[3, core], other),
            ]
        forward = dot(active.astype(BF16), fc2[...])
        backward = dot_nt(d_low, fc1[...])
        if i == 0:
            acc_out[...] = forward
            acc_back[...] = backward
        else:
            acc_out[...] += forward
            acc_back[...] += backward
        if i + 2 < 4:
            loads.append(load(i + 2))
        else:
            heads = range(0, 3) if i == 2 else range(3, 4)
            span = pl.ds(0, 9 * LANES) if i == 2 else pl.ds(9 * LANES, 3 * LANES)
            size = 9 * LANES if i == 2 else 3 * LANES
            qkv_loads = [
                moves.start(
                    qkv_hbm.at[h], fc1_ref.at[i % 2, :, pl.ds((h - heads[0]) * 3 * LANES, 3 * LANES)]
                )
                for h in heads
            ]
            qkv_loads.append(moves.start(w_hbm.at[:, span], fc2_ref.at[i % 2, :, pl.ds(0, size)]))
            loads.append(qkv_loads)
        if i == 1:
            normed_go.relay()

    middle = middle_ref[...]
    scaled, factor = normalize(middle)
    upstream = acc_back[...]
    cot = cot_ref[...].astype(F32)
    d_middle = cot + norm_back(upstream, scaled, factor, gain)
    d_middle_ref[...] = d_middle
    d_branch_ref[...] = d_middle.astype(BF16)
    branch_swap = wires.copy(d_branch_ref, d_branch_peer, other)
    branch_swap.start()
    go, go_on = [], []
    for k in (3, 1, 2, 0):
        at = pl.ds(pl.multiple_of(flip(place, k) * own, 16), own)
        main, d_rest[k] = split_lanes(dot_nt(d_branch_ref[...], proj_ref[at, :]))
        d_go[0, k], d_go[1, k] = main[:, :LANES], main[:, LANES:]
        if k:
            go.append(wires.copy(d_go.at[0, k], d_in.at[0, k], to[k]))
            go[-1].start()
            for src, dst in ((d_go.at[1], d_in.at[1]), (d_rest, d_rest_in)):
                go_on.append(wires.copy(src.at[k], dst.at[k], to[k]))
        else:
            d_in[0, 0], d_in[1, 0], d_rest_in[0] = d_go[0, 0], d_go[1, 0], d_rest[0]
    for wire in go_on:
        wire.start()
    acc_out[...] = middle + acc_out[...] + fc2_bias_ref[...].reshape(1, -1)
    keeps.append(moves.start(acc_out.at[pl.ds(0, images)], out_hbm))
    c_own[...] = acc_out[images:].astype(BF16)
    c_go = [wires.copy(c_own, c_all.at[k], to[k]) for k in (3, 1, 2)]
    keeps.append(moves.start(c_own, c_all.at[0]))
    vec_ref[0:1] = jnp.sum(upstream * scaled, axis=0, keepdims=True)
    vec_ref[1:2] = jnp.sum(upstream, axis=0, keepdims=True)
    vec_ref[2:3] = jnp.sum(d_middle, axis=0, keepdims=True)
    vec_ref[3:4] = jnp.sum(cot, axis=0, keepdims=True)
    vec_ref[4:] = jnp.zeros((4, width), F32)
    ctx_swap.arrive()
    branch_swap.arrive()
    proj_stage[...] = (
        both(
            ctx_two[:, core].reshape(depth * small, rows),
            ctx_peer[...].reshape(depth * small, rows),
            d_branch_ref[...],
            d_branch_peer[...],
        )
        .astype(BF16)
        .reshape(depth, small, width)
    )
    keeps.append(moves.start(proj_stage, late_hbm))
    for wire in go:
        wire.arrive()
    normed_go.finish()
    for wire in cond_go:
        wire.arrive()
    hop.arrive()
    keeps.append(moves.start(d_pre.at[place], d_pre_own))
    last_go = (
        [wires.copy(d_pre.at[flip(place, k)], d_pre_x.at[k - 1], to[k]) for k in (3, 1, 2)]
        + late_go
        + [
            wires.copy(normed_x.at[:, :, 1 - core], normed_peer, other),
            wires.copy(normed_cond_x, normed_cond_peer, other),
            wires.copy(cot_ref, cot_peer.at[0], other),
            wires.copy(cot_z, cot_peer.at[pl.ds(1, 2)], other),
            wires.copy(cot_zz, cot_peer.at[pl.ds(3, 2)], other),
            wires.copy(cot_far, cot_peer.at[5], other),
        ]
        + c_go
    )
    for copy in keeps:
        copy.wait()
    for wire in last_go:
        wire.start()

    total = 4 * rows
    half = rows // 2
    for part in range(4):
        dot_all[:LANES, part * rows : (part + 1) * rows] = d_in[0, part].astype(F32).T
    for copy in loads[4] + loads[5]:
        copy.wait()
    step = 3 * LANES
    for head in range(4):
        slot, lane = (0, 3 * head * LANES) if head < 3 else (1, 0)
        base = head * HEAD_DIM
        if head == 1:
            for wire in go_on:
                wire.arrive()
            for part in range(4):
                dot_all[LANES:, part * rows : (part + 1) * rows] = join_lanes(
                    d_in[1, part], d_rest_in[part]
                ).T
        upstream_t = jnp.concatenate(
            [dot_all[base : base + HEAD_DIM, :], jnp.zeros((LANES - HEAD_DIM, total), F32)], 0
        )
        upstream = upstream_t.T.astype(BF16)
        upstream_t = upstream_t.astype(BF16)
        key = fc1_ref[slot, :, lane + LANES : lane + 2 * LANES]
        key_t = turned(key)
        value = fc1_ref[slot, :, lane + 2 * LANES : lane + 3 * LANES]
        for start in range(0, total, step):
            span = slice(start, start + step)
            query = fc1_ref[slot, span, lane : lane + LANES]
            probs = jnp.exp2(dot_nt(key, query) * SCALE2 - lse_ref[head, :, span])
            d_probs = dot(value, upstream_t[:, span])
            delta = jnp.sum(probs * d_probs, axis=0, keepdims=True)
            d_raw = (probs * (d_probs - delta)).astype(BF16)
            d_value = dot(probs.astype(BF16), upstream[span])
            d_key = dot(d_raw, query)
            if start == 0:
                dv_ref[...] = d_value
                dk_ref[...] = d_key
            else:
                dv_ref[...] += d_value
                dk_ref[...] += d_key
            d_query = dot(key_t, d_raw) * SCALE
            dt_all[base : base + HEAD_DIM, span] = d_query[:HEAD_DIM]
            d_all[span, 3 * head * LANES : (3 * head + 1) * LANES] = d_query.T.astype(BF16)
        d_key = dk_ref[...] * SCALE
        d_value = dv_ref[...]
        dt_all[own + base : own + base + HEAD_DIM] = d_key.T[:HEAD_DIM]
        dt_all[2 * own + base : 2 * own + base + HEAD_DIM] = d_value.T[:HEAD_DIM]
        d_all[:, (3 * head + 1) * LANES : (3 * head + 2) * LANES] = d_key.astype(BF16)
        d_all[:, (3 * head + 2) * LANES : (3 * head + 3) * LANES] = d_value.astype(BF16)
    cut = 9 * LANES
    for part in (3, 1, 2, 0):
        span = slice(part * rows, (part + 1) * rows)
        update = dot_nt(d_all[span, :cut], fc2_ref[0]) + dot_nt(
            d_all[span, cut:], fc2_ref[1, :, : 3 * LANES]
        )
        lead_ref[part] = update[:half].astype(BF16)
        tail_ref[part] = update[half:].astype(BF16)
    dt_ref[...] = dt_all[...].astype(BF16)
    for i in range(3):
        arrive_by_core(near[4 * i : 4 * i + 4], core)
    for wire in last_go:
        wire.arrive()
    wires.drain()


def middle_stage(
    depth, ctx_t, ctx_rest, hidden, cot, proj, proj_bias, gain, shift, fc2_bias, fc1_bias, lse,
    cot_z, cot_zz, fc1, fc2, qkv, w_heads,
):
    rows, width = hidden.shape
    slots = SLOTS // 4
    images = rows - slots
    ff = fc1.shape[1]
    small = width // (2 * depth)
    own = ctx_t.shape[1]
    chunk = ff // 4
    quarter = chunk // 8
    vmem, hbm = pl.BlockSpec(memory_space=pltpu.VMEM), pl.BlockSpec(memory_space=pl.ANY)
    f = lambda *shape: jax.ShapeDtypeStruct(shape, F32)
    b = lambda *shape: jax.ShapeDtypeStruct(shape, BF16)
    v = lambda *shape: pltpu.VMEM(shape, BF16)
    vf = lambda *shape: pltpu.VMEM(shape, F32)
    return pl.pallas_call(
        middle_kernel,
        in_specs=[vmem] * 10 + [hbm] * 7,
        out_specs=[hbm, hbm, vmem, hbm] + [vmem] * 5 + [hbm] * 10,
        out_shape=[
            f(images, width),
            b(4, slots, width),
            f(rows, width),
            b(depth, small, width),
            f(8, width),
            f(4, chunk),
            b(3 * own, 4 * rows),
            b(4, rows // 2, width),
            b(4, rows // 2, width),
            b(4, depth, 2, small, images),
            b(4, depth, small, images),
            b(4, slots, width),
            b(4, slots, width),
            b(rows, chunk),
            b(3, rows, chunk),
            b(4, 2, 4, quarter, images),
            b(4, 2, quarter, 4 * slots),
            b(rows, width),
            b(6, rows, width),
        ],
        scratch_shapes=[
            v(width, width), v(2, width, chunk), v(2, chunk, width), vf(4, chunk),
            v(rows, width), vf(rows, width), vf(rows, width), vf(rows, width),
            v(depth, 2, small, images),
            v(depth, 2, small, rows), v(depth, small, rows),
            v(4, 2, 4, quarter, images), v(4, 2, quarter, 4 * slots),
            v(4, rows, chunk),
            v(rows, width), v(rows, width),
            v(2, 4, rows, LANES), v(4, (rows // 4 + 15) // 16 * 16, LANES),
            v(2, 4, rows, LANES), v(4, (rows // 4 + 15) // 16 * 16, LANES),
            vf(own, 4 * rows), vf(3 * own, 4 * rows), v(4 * rows, 12 * LANES),
            vf(4 * rows, LANES), vf(4 * rows, LANES),
            v(depth, small, width),
            v(slots, width),
            pltpu.SemaphoreType.DMA((64,)), pltpu.SemaphoreType.DMA((64,)), pltpu.SemaphoreType.DMA((64,)),
        ],
        compiler_params=pltpu.CompilerParams(
            vmem_limit_bytes=VMEM_LIMIT, collective_id=3, has_side_effects=True
        ),
        cost_estimate=cost(8 * rows * width * ff, 8 * width * ff),
        name="middle_stage",
    )(ctx_t, ctx_rest, hidden, cot, proj_bias, gain, shift, fc2_bias, fc1_bias, lse, cot_z, cot_zz, proj, fc1, fc2, qkv, w_heads)


def finish_kernel(
    p_hbm, f_hbm, g_hbm, q_hbm, s_hbm, c_hbm, out_c_hbm, vec_ref, out_hbm, din_hbm, dskip_hbm,
    g_fc2_hbm, g_proj_hbm, g_first_hbm, g_heads_hbm, g_skip_hbm,
    o_out, o_din, o_dskip, o_out_cond, o_din_cond, o_dskip_cond,
    v0, v1, v2, v3, v4, v5, v6, fc1_vec_ref,
    p_in, f_in, g_in, q_in, s_in, c_in, out_c_in, p_st, f_st, g_st, q_st, s_st, cond_st, rows_st, sems,
):
    width = out_hbm.shape[1]
    place, index = lax.axis_index("seq"), lax.axis_index("batch")
    batch = lax.axis_size("batch")
    moves = Locals(sems)
    loads = [
        moves.start(src, dst)
        for src, dst in (
            (f_hbm, f_in), (g_hbm, g_in), (q_hbm, q_in), (s_hbm, s_in), (p_hbm, p_in),
            (c_hbm, c_in),
            (out_c_hbm, out_c_in),
        )
    ]
    rows_in = [
        moves.start(src, rows_st.at[i]) for i, src in enumerate((out_hbm, din_hbm, dskip_hbm))
    ]
    done = []
    for i, dst in enumerate((o_out, o_din, o_dskip)):
        rows_in[i].wait()
        done.append(moves.start(rows_st.at[i], dst.at[:, 0]))
    loads[0].wait()
    for j in range(4):
        f_st[:, j * width : (j + 1) * width] = f_in[flip(place, j)].astype(F32)
    done.append(moves.start(f_st, g_first_hbm))
    loads[1].wait()
    small = g_in.shape[1]
    for j in range(4):
        g_st[j * small : (j + 1) * small] = g_in[flip(place, j)].astype(F32)
    done.append(moves.start(g_st, g_fc2_hbm))
    loads[2].wait()
    size = q_in.shape[2] // 3
    for j in range(4):
        value = q_in[flip(place, j)].astype(F32)
        for which in range(3):
            at = (which * 4 + j) * size
            q_st[:, at : at + size] = value[:, which * size : (which + 1) * size]
    done.append(moves.start(q_st, g_heads_hbm))
    loads[3].wait()
    size = s_st.shape[0] // 4
    for j in range(4):
        s_st[j * size : (j + 1) * size] = s_in[flip(place, j), :size].astype(F32)
    done.append(moves.start(s_st, g_skip_hbm))
    for copy in loads[4:]:
        copy.wait()
    p_st[...] = p_in[...].astype(F32)
    done.append(moves.start(p_st, g_proj_hbm))
    slots = c_in.shape[1]
    for j in range(4):
        span = slice(j * slots, (j + 1) * slots)
        piece = c_in[flip(place, j)].astype(F32)
        cond_st[0, span] = out_c_in[flip(place, j)].astype(F32)
        cond_st[1, span] = piece[:, :width]
        cond_st[2, span] = piece[:, width:]
    conds = o_out_cond.shape[0]
    for i, ref in enumerate((o_out_cond, o_din_cond, o_dskip_cond)):
        ref[:, 0] = cond_st[i, :conds]
    share = width // batch
    vectors = vec_ref[...]
    rolled = pltpu.roll(vectors, lax.rem(width - index * share, width), 1)
    for row, ref in zip((0, 1, 2, 5, 3, 4, 6), (v0, v1, v2, v3, v4, v5, v6)):
        ref[...] = rolled[row, :share]
    share = 4 * width // batch
    per = width // share
    vector = vec_ref[pl.ds(8 + index // per, 1)]
    vector = pltpu.roll(vector, lax.rem(width - index % per * share, width), 1)
    fc1_vec_ref[...] = vector[0, :share]
    for copy in done:
        copy.wait()


def finish_stage(batch, conds, slots_of, out_c, vec, out, d_image, d_skip):
    p_all, f_all, g_all, q_all, s_all, c_all = slots_of
    images, width = out.shape
    small = f_all.shape[1]
    skip_rows = 2 * width // batch
    large = 4 * width // batch
    slots = c_all.shape[1]
    vmem, hbm = pl.BlockSpec(memory_space=pltpu.VMEM), pl.BlockSpec(memory_space=pl.ANY)
    f = lambda *shape: jax.ShapeDtypeStruct(shape, F32)
    like = lambda a: pltpu.VMEM(a.shape, a.dtype)
    vf = lambda *shape: pltpu.VMEM(shape, F32)
    return pl.pallas_call(
        finish_kernel,
        in_specs=[hbm] * 7 + [vmem] + [hbm] * 3,
        out_specs=[hbm] * 8 + [vmem] * 11,
        out_shape=[
            f(large, width), f(small, width), f(small, 4 * width), f(small, 4 * q_all.shape[2]),
            f(skip_rows, width), f(images, 1, width), f(images, 1, width), f(images, 1, width),
            f(conds, 1, width), f(conds, 1, width), f(conds, 1, width),
        ]
        + [f(width // batch)] * 7
        + [f(large)],
        scratch_shapes=[
            like(p_all), like(f_all), like(g_all), like(q_all), like(s_all), like(c_all), like(out_c),
            vf(small, width), vf(small, 4 * width), vf(large, width), vf(small, 4 * q_all.shape[2]),
            vf(skip_rows, width), vf(3, 4 * slots, width), vf(3, images, width),
            pltpu.SemaphoreType.DMA((24,)),
        ],
        compiler_params=params(),
        cost_estimate=cost(1e6, 2e7),
        name="finish_stage",
    )(*slots_of, out_c, vec, out, d_image, d_skip)


def per_device(
    batch,
    parts,
    image_in,
    cond_in,
    skip_image,
    skip_cond,
    caption_len,
    skip_weight,
    skip_bias,
    first_gain,
    first_bias,
    qkv_weight,
    proj_weight,
    proj_bias,
    second_gain,
    second_bias,
    fc1_weight,
    fc1_bias,
    fc2_weight,
    fc2_bias,
    grad_image,
    grad_cond,
):
    conds = cond_in.shape[0]
    width = image_in.shape[2]
    images = image_in.shape[0]
    ff = fc1_weight.shape[1]
    slots = SLOTS // parts
    rows = slots + images
    total = rows * parts
    heads = HEADS // parts
    depth = batch // 2
    place = lax.axis_index("seq")
    index = lax.axis_index("batch")
    core, chip = index % 2, index // 2
    where = jnp.stack([core, place]).astype(jnp.int32)

    fast = parts == 4 and depth == 4 and (ff // parts) % LANES == 0
    if fast:
        (
            hidden, normed_all, w_heads, qkv, joined, joined_peer, cot, cot_z, lse, ctx_t, ctx_rest,
            cot_zz,
        ) = start_stage(
            depth, caption_len, image_in[:, 0], cond_in[:, 0], skip_image[:, 0], skip_cond[:, 0],
            grad_image[:, 0], grad_cond[:, 0], skip_weight, skip_bias, first_gain, first_bias,
            qkv_weight,
        )
        normed_all = normed_all.reshape(total, width)
        (
            out, out_c, d_middle, late, vec_two, fc1_vec, d_triple_t, lead, tail, normed_x,
            normed_peer, normed_cond_x, normed_cond_peer, d_pre_own, d_pre_x, active_x,
            active_cond_x, cot_far, cot_peer,
        ) = middle_stage(
            depth, ctx_t, ctx_rest, hidden, cot, proj_weight, proj_bias, second_gain, second_bias,
            fc2_bias, fc1_bias, lse, cot_z, cot_zz, fc1_weight, fc2_weight, qkv, w_heads,
        )
        feeds = (
            normed_x, normed_peer, normed_cond_x, normed_cond_peer, d_pre_own, d_pre_x, active_x,
            active_cond_x, cot, cot_z, cot_zz, cot_far, cot_peer,
        )
        *slots_of, d_image, d_skip, vec = reduce_all(
            late, lead, tail, normed_all, d_triple_t, joined, joined_peer, hidden, d_middle,
            skip_weight, feeds, first_gain, vec_two, fc1_vec,
        )
        (
            wgrad_fc2, wgrad_proj, wgrad_fc1, wgrad_qkv, wgrad_skip, out_image, d_image, d_skip,
            out_cond, d_cond, d_skip_cond, *vec,
        ) = finish_stage(batch, conds, slots_of, out_c, vec, out, d_image, d_skip)
        return (
            out_image, out_cond, d_image, d_cond, d_skip, d_skip_cond, wgrad_skip, vec[0],
            vec[1], vec[2], wgrad_qkv, wgrad_proj, vec[3], vec[4], vec[5], wgrad_fc1, vec[7],
            wgrad_fc2, vec[6],
        )

    def own_rows(cond, image):
        padded = jnp.pad(cond[:, 0], ((0, SLOTS - conds), (0, 0)))
        lead = lax.dynamic_slice_in_dim(padded, place * slots, slots, 0)
        return jnp.concatenate([lead, image[:, 0]], 0)

    x = own_rows(cond_in, image_in)
    s = own_rows(skip_cond, skip_image)
    cot = own_rows(grad_cond, grad_image)

    hidden, normed, joined_t = pre(
        x, s, skip_weight, skip_bias[None], first_gain[None], first_bias[None]
    )
    normed_all = jnp.concatenate(everywhere(normed, parts), 0)
    own = heads * HEAD_DIM
    w_heads = heads_weight(where[1:], qkv_weight, heads)
    order = place ^ jnp.arange(parts, dtype=jnp.int32)
    position = order[:, None] * slots + jnp.arange(rows, dtype=jnp.int32)[None]
    valid = (jnp.arange(rows)[None] >= slots) | (position <= caption_len[0])
    kbias = jnp.where(
        (jnp.arange(LANES) == HEAD_DIM)[None] & ~valid.reshape(total, 1), F32(-1e30), F32(0)
    )
    qkv, lse, *ctx_parts = attend(parts, normed_all, w_heads, kbias)
    context = [ctx_parts[0]] + [across(ctx_parts[k], parts, k) for k in range(1, parts)]

    zero = jnp.zeros_like(proj_bias)
    vecs = jnp.stack([proj_bias, second_gain, second_bias, fc2_bias, zero, zero, zero, zero])
    (
        out,
        d_middle,
        d_branch,
        active_t,
        d_pre,
        normed2_t,
        ctx_t,
        vec_two,
        fc1_bias_grad,
        *d_ctx_parts,
    ) = mlp(
        parts,
        where[1:],
        context,
        hidden,
        cot,
        proj_weight,
        vecs,
        fc1_weight,
        fc1_bias[None],
        fc2_weight,
    )
    d_context = [d_ctx_parts[0]] + [across(d_ctx_parts[k], parts, k) for k in range(1, parts)]

    def by_core(turned_rows):
        blocks = turned_rows.reshape(depth, 2, -1, rows)
        send = lax.dynamic_index_in_dim(blocks, 1 - core, 1, keepdims=False)
        return blocks, other_core(send, batch)

    active_b, active_p = by_core(active_t)
    normed2_b, normed2_p = by_core(normed2_t)
    ctx_b, ctx_p = by_core(ctx_t)
    joined_b, joined_p = by_core(joined_t)
    cot_p, d_pre_p, d_branch_p = (other_core(v, batch) for v in (cot, d_pre, d_branch))
    late = pair_grads(
        where, [(active_b, active_p, cot, cot_p), (ctx_b, ctx_p, d_branch, d_branch_p)]
    )
    by_columns = (ff // parts) % LANES == 0
    if by_columns:
        first = column_grads(where, parts, normed2_b, normed2_p, d_pre, d_pre_p)
        late, first, d_context = lax.optimization_barrier((late, first, d_context))
        middle = depth // 2
    if by_columns:
        first = jnp.concatenate(
            [
                scattered(first[:, :middle], parts, bits_of(parts)),
                scattered(first[:, middle:], parts, bits_of(parts)[::-1]),
            ],
            0,
        )
    if not by_columns:
        first = pair_grads(where, [(normed2_b, normed2_p, d_pre, d_pre_p)])
    def all_conds(lead):
        pieces = [lead] + [across(lead, parts, k) for k in range(1, parts)]
        full = jnp.zeros((SLOTS, lead.shape[1]), F32)
        for k in range(parts):
            full = lax.dynamic_update_slice_in_dim(
                full, pieces[k].astype(F32), (place ^ k) * slots, 0
            )
        return full[:conds, None]

    d_triple_t, d_lead, d_tail = attend_back(parts, d_context, qkv, lse, w_heads)
    d_lead = scattered(d_lead, parts, bits_of(parts))
    d_tail = scattered(d_tail, parts, bits_of(parts)[::-1])
    heads_grad = heads_grads(normed_all, d_triple_t).reshape(depth, 2, -1, 3 * own)
    heads_grad = plus(
        lax.dynamic_index_in_dim(heads_grad, core, 1, keepdims=False),
        other_core(lax.dynamic_index_in_dim(heads_grad, 1 - core, 1, keepdims=False), batch),
    )
    heads_grad = everywhere(down_the_line(heads_grad, batch, chip), parts)
    wgrad_qkv = put_heads(where[1:], heads_grad)

    d_in, d_skip, d_low, vec_one = post(
        d_lead, d_tail, hidden, d_middle, first_gain[None], skip_weight
    )
    d_low_p = other_core(d_low, batch)
    last = pair_grads(where, [(joined_b, joined_p, d_low, d_low_p)])

    late = down_the_line(late, batch, chip)
    first = down_the_line(first, batch, chip)
    late = summed(late, parts)
    if by_columns:
        fc1_cols = everywhere(first, parts)
        wgrad_fc1 = put_columns(where[1:], fc1_cols)
    else:
        wgrad_fc1 = summed(first, parts).astype(F32)

    vectors = [
        vec_one[0],
        vec_one[1],
        vec_one[2],
        vec_two[2],
        vec_two[0],
        vec_two[1],
        fc1_bias_grad[0],
        vec_two[3],
    ]
    sizes = [v.shape[0] // batch for v in vectors]
    packed = jnp.concatenate([v.reshape(batch, -1) for v in vectors], 1)
    packed = packed.reshape(depth, 2, -1)
    packed = lax.dynamic_index_in_dim(packed, core, 1, keepdims=False) + other_core(
        lax.dynamic_index_in_dim(packed, 1 - core, 1, keepdims=False), batch
    )
    packed = jnp.pad(packed, ((0, 0), (0, 16 * width - packed.shape[1]))).reshape(depth, 16, width)
    last = jnp.concatenate([last, packed.astype(BF16)], 1)
    last = summed(down_the_line(last, batch, chip), parts)
    skip_rows = 2 * width // batch
    wgrad_skip = last[:skip_rows].astype(F32)
    flat = last[skip_rows:].reshape(-1).astype(F32)
    vector_out, at = [], 0
    for size in sizes:
        vector_out.append(flat[at : at + size])
        at += size
    fc2_rows = ff // batch
    wgrad_fc2 = late[:fc2_rows].astype(F32)
    wgrad_proj = late[fc2_rows:].astype(F32)

    out_cond = all_conds(out[:slots].astype(BF16))
    d_cond = all_conds(jnp.concatenate([d_in[:slots], d_skip[:slots]], 1).astype(BF16))
    return (
        out[slots:, None],
        out_cond,
        d_in[slots:, None],
        d_cond[:, :, :width],
        d_skip[slots:, None],
        d_cond[:, :, width:],
        wgrad_skip,
        vector_out[0],
        vector_out[1],
        vector_out[2],
        wgrad_qkv,
        wgrad_proj,
        vector_out[3],
        vector_out[4],
        vector_out[5],
        wgrad_fc1,
        vector_out[6],
        wgrad_fc2,
        vector_out[7],
    )


def solution(mesh):
    tokens, conds, shared = P("seq", "batch", None), P(None, "batch", None), P()
    return jax.shard_map(
        functools.partial(per_device, mesh.shape["batch"], mesh.shape["seq"]),
        mesh=mesh,
        in_specs=(tokens, conds, tokens, conds, P("batch")) + (shared,) * 13 + (tokens, conds),
        out_specs=(tokens, conds) * 3
        + (
            P("batch", None),
            P("batch"),
            P("batch"),
            P("batch"),
            P("batch", None),
            P("batch", None),
            P("batch"),
            P("batch"),
            P("batch"),
            P("batch", None),
            P("batch"),
            P("batch", None),
            P("batch"),
        ),
        check_vma=False,
    )
```

```python
import functools
import math

import jax
import jax.numpy as jnp
from jax import lax
from jax.experimental import pallas as pl
from jax.experimental.pallas import tpu as pltpu
from jax.sharding import PartitionSpec as P

HEADS = 16
HEAD_DIM = 72
LANES = 128
SLOTS = 128
F32 = jnp.float32
BF16 = jnp.bfloat16
VMEM_LIMIT = 60 * 1024 * 1024
SCALE = 1.0 / math.sqrt(HEAD_DIM)
SCALE2 = SCALE * math.log2(math.e)


def dot(left, right):
    return jnp.dot(left, right, preferred_element_type=F32)


def dot_nt(left, right):
    return lax.dot_general(left, right, (((1,), (1,)), ((), ())), preferred_element_type=F32)


def dot_tn(left, right):
    return lax.dot_general(left, right, (((0,), (0,)), ((), ())), preferred_element_type=F32)


def params():
    return pltpu.CompilerParams(vmem_limit_bytes=VMEM_LIMIT)


def cost(flops, nbytes):
    return pl.CostEstimate(flops=int(flops), bytes_accessed=int(nbytes), transcendentals=0)


def turned(value):
    return value.astype(F32).T.astype(BF16)


def normalize(values):
    centre = values - jnp.mean(values, axis=-1, keepdims=True)
    factor = lax.rsqrt(jnp.mean(centre * centre, axis=-1, keepdims=True) + 1e-5)
    return centre * factor, factor


def norm_back(upstream, scaled, factor, gain):
    inner = upstream * gain
    centred = inner - jnp.mean(inner, axis=-1, keepdims=True)
    return factor * (centred - scaled * jnp.mean(inner * scaled, axis=-1, keepdims=True))


def pre_kernel(x_ref, s_ref, w_ref, bias_ref, gain_ref, shift_ref, hidden_ref, normed_ref, turn_ref):
    width = x_ref.shape[1]
    hidden = dot(x_ref[...], w_ref[:width]) + dot(s_ref[...], w_ref[width:]) + bias_ref[...]
    hidden_ref[...] = hidden
    scaled, _ = normalize(hidden)
    normed_ref[...] = (scaled * gain_ref[...] + shift_ref[...]).astype(BF16)
    turn_ref[:width] = turned(x_ref[...])
    turn_ref[width:] = turned(s_ref[...])


def pre(x, s, w, bias, gain, shift):
    rows, width = x.shape
    return pl.pallas_call(
        pre_kernel,
        out_shape=(
            jax.ShapeDtypeStruct((rows, width), F32),
            jax.ShapeDtypeStruct((rows, width), BF16),
            jax.ShapeDtypeStruct((2 * width, rows), BF16),
        ),
        compiler_params=params(),
        cost_estimate=cost(4 * rows * width * width, 4 * width * width + 12 * rows * width),
        name="input_linear",
    )(x, s, w, bias, gain, shift)


def heads_weight_kernel(window, place_ref, w_ref, out_ref):
    heads = out_ref.shape[0]
    width = w_ref.shape[0]
    own = heads * HEAD_DIM
    keep = lax.broadcasted_iota(jnp.int32, (width, LANES), 1) < HEAD_DIM
    place = place_ref[0]
    for which in range(3):
        first = place * own + which * width
        start = jnp.minimum(first // LANES * LANES, 3 * width - window)
        value = w_ref[:, pl.ds(pl.multiple_of(start, LANES), window)].astype(F32)
        value = pltpu.roll(value, lax.rem(window - (first - start), window), 1)
        for head in range(heads):
            turned_back = value if head == 0 else pltpu.roll(value, window - head * HEAD_DIM, 1)
            out_ref[head, :, which * LANES : (which + 1) * LANES] = jnp.where(
                keep, turned_back[:, :LANES], 0.0
            ).astype(BF16)


def heads_weight(place, w, heads):
    width = w.shape[0]
    own = heads * HEAD_DIM
    offsets = [p * own % LANES for p in range(HEADS // heads)]
    window = (max(offsets) + own + LANES - 1) // LANES * LANES
    return pl.pallas_call(
        functools.partial(heads_weight_kernel, window),
        in_specs=[
            pl.BlockSpec(memory_space=pltpu.SMEM),
            pl.BlockSpec(memory_space=pltpu.VMEM),
        ],
        out_shape=jax.ShapeDtypeStruct((heads, width, 3 * LANES), BF16),
        compiler_params=params(),
        cost_estimate=cost(1e6, 2 * w.size + 6 * heads * width * LANES),
        name="heads_weight",
    )(place, w)


def attend_kernel(parts, normed_ref, w_ref, kbias_ref, qkv_ref, lse_ref, *rest):
    ctx_refs, (vt_ref, ot_ref) = rest[:parts], rest[parts:]
    head = pl.program_id(0)
    total = normed_ref.shape[0]
    rows = total // parts
    lane = lax.broadcasted_iota(jnp.int32, (1, LANES), 1)
    one = jnp.where(lane == HEAD_DIM, 1.0, 0.0)
    for part in range(parts):
        span = pl.ds(part * rows, rows)
        triple = dot(normed_ref[span], w_ref[0])
        qkv_ref[0, span, :LANES] = (triple[:, :LANES] + one).astype(BF16)
        qkv_ref[0, span, LANES : 2 * LANES] = (
            triple[:, LANES : 2 * LANES] + kbias_ref[span]
        ).astype(BF16)
        qkv_ref[0, span, 2 * LANES :] = triple[:, 2 * LANES :].astype(BF16)
        vt_ref[:, span] = turned(qkv_ref[0, span, 2 * LANES :])
    step = 3 * LANES if total % (3 * LANES) == 0 else LANES
    for start in range(0, total, step):
        query = qkv_ref[0, pl.ds(start, step), :LANES]
        scores = dot_nt(qkv_ref[0, :, LANES : 2 * LANES], query)
        peak = jnp.max(scores, axis=0, keepdims=True)
        shifted = jnp.exp2((scores - peak) * SCALE2)
        sums = jnp.sum(shifted, axis=0, keepdims=True)
        mixed = dot(vt_ref[...], shifted.astype(BF16)) / sums
        ot_ref[pl.ds(pl.multiple_of(head * HEAD_DIM, 8), HEAD_DIM), pl.ds(start, step)] = mixed[
            :HEAD_DIM
        ]
        lse_ref[0, :, pl.ds(start, step)] = peak * SCALE2 + jnp.log2(sums)

    @pl.when(head == pl.num_programs(0) - 1)
    def _():
        for part in range(parts):
            ctx_refs[part][...] = ot_ref[:, pl.ds(part * rows, rows)].T.astype(BF16)


def attend(parts, normed_all, w_heads, kbias):
    total, width = normed_all.shape
    heads = w_heads.shape[0]
    rows = total // parts
    own = heads * HEAD_DIM
    return pl.pallas_call(
        functools.partial(attend_kernel, parts),
        grid=(heads,),
        in_specs=[
            pl.BlockSpec((total, width), lambda h: (0, 0)),
            pl.BlockSpec((1, width, 3 * LANES), lambda h: (h, 0, 0)),
            pl.BlockSpec((total, LANES), lambda h: (0, 0)),
        ],
        out_specs=[
            pl.BlockSpec((1, total, 3 * LANES), lambda h: (h, 0, 0)),
            pl.BlockSpec((1, 1, total), lambda h: (h, 0, 0)),
        ]
        + [pl.BlockSpec((rows, own), lambda h: (0, 0))] * parts,
        out_shape=[
            jax.ShapeDtypeStruct((heads, total, 3 * LANES), BF16),
            jax.ShapeDtypeStruct((heads, 1, total), F32),
        ]
        + [jax.ShapeDtypeStruct((rows, own), BF16)] * parts,
        scratch_shapes=[pltpu.VMEM((LANES, total), BF16), pltpu.VMEM((own, total), F32)],
        compiler_params=params(),
        cost_estimate=cost(
            2 * heads * total * (width * 3 * LANES + 4 * LANES * total), 6 * total * width
        ),
        name="attend",
    )(normed_all, w_heads, kbias)


def attend_back_kernel(parts, *refs):
    d_refs = refs[:parts]
    (qkv_ref, lse_ref, w_ref, dt_ref, lead_ref, tail_ref) = refs[parts : parts + 6]
    (dot_all, dt_all, acc, dq_ref, dk_ref, dv_ref) = refs[parts + 6 :]
    head = pl.program_id(0)
    heads = pl.num_programs(0)
    total = qkv_ref.shape[1]
    rows = total // parts
    half = rows // 2
    own = dot_all.shape[0]

    @pl.when(head == 0)
    def _():
        for part in range(parts):
            dot_all[:, pl.ds(part * rows, rows)] = d_refs[part][...].astype(F32).T

    base = pl.multiple_of(head * HEAD_DIM, 8)
    upstream_t = jnp.concatenate(
        [dot_all[pl.ds(base, HEAD_DIM), :], jnp.zeros((LANES - HEAD_DIM, total), F32)], 0
    )
    upstream = upstream_t.T.astype(BF16)
    upstream_t = upstream_t.astype(BF16)
    key = qkv_ref[0, :, LANES : 2 * LANES]
    key_t = turned(key)
    value = qkv_ref[0, :, 2 * LANES :]
    step = 3 * LANES if total % (3 * LANES) == 0 else LANES
    for start in range(0, total, step):
        query = qkv_ref[0, pl.ds(start, step), :LANES]
        probs = jnp.exp2(dot_nt(key, query) * SCALE2 - lse_ref[0, :, pl.ds(start, step)])
        d_probs = dot(value, upstream_t[:, start : start + step])
        delta = jnp.sum(probs * d_probs, axis=0, keepdims=True)
        d_raw = (probs * (d_probs - delta) * SCALE).astype(BF16)
        d_value = dot(probs.astype(BF16), upstream[start : start + step])
        d_key = dot(d_raw, query)
        if start == 0:
            dv_ref[...] = d_value
            dk_ref[...] = d_key
        else:
            dv_ref[...] += d_value
            dk_ref[...] += d_key
        d_query = dot(key_t, d_raw)
        dt_all[pl.ds(base, HEAD_DIM), pl.ds(start, step)] = d_query[:HEAD_DIM]
        dq_ref[pl.ds(start, step)] = d_query.T
    dt_all[pl.ds(pl.multiple_of(own + base, 8), HEAD_DIM)] = dk_ref[...].T[:HEAD_DIM]
    dt_all[pl.ds(pl.multiple_of(2 * own + base, 8), HEAD_DIM)] = dv_ref[...].T[:HEAD_DIM]
    for part in range(parts):
        span = pl.ds(part * rows, rows)
        update = (
            dot_nt(dq_ref[span].astype(BF16), w_ref[0, :, :LANES])
            + dot_nt(dk_ref[span].astype(BF16), w_ref[0, :, LANES : 2 * LANES])
            + dot_nt(dv_ref[span].astype(BF16), w_ref[0, :, 2 * LANES :])
        )

        @pl.when(head == 0)
        def _():
            acc[span] = update

        @pl.when(head > 0)
        def _():
            acc[span] += update

    @pl.when(head == heads - 1)
    def _():
        dt_ref[...] = dt_all[...].astype(BF16)
        for part in range(parts):
            lead_ref[part] = acc[pl.ds(part * rows, half)].astype(BF16)
            tail_ref[part] = acc[pl.ds(part * rows + half, half)].astype(BF16)


def attend_back(parts, d_context, qkv, lse, w_heads):
    heads, total, _ = qkv.shape
    width = w_heads.shape[1]
    rows = total // parts
    own = heads * HEAD_DIM
    whole = lambda *shape: pl.BlockSpec(shape, lambda h: (0,) * len(shape))
    return pl.pallas_call(
        functools.partial(attend_back_kernel, parts),
        grid=(heads,),
        in_specs=[whole(rows, own)] * parts
        + [
            pl.BlockSpec((1, total, 3 * LANES), lambda h: (h, 0, 0)),
            pl.BlockSpec((1, 1, total), lambda h: (h, 0, 0)),
            pl.BlockSpec((1, width, 3 * LANES), lambda h: (h, 0, 0)),
        ],
        out_specs=[
            whole(3 * own, total),
            whole(parts, rows // 2, width),
            whole(parts, rows // 2, width),
        ],
        out_shape=[
            jax.ShapeDtypeStruct((3 * own, total), BF16),
            jax.ShapeDtypeStruct((parts, rows // 2, width), BF16),
            jax.ShapeDtypeStruct((parts, rows // 2, width), BF16),
        ],
        scratch_shapes=[
            pltpu.VMEM((own, total), F32),
            pltpu.VMEM((3 * own, total), F32),
            pltpu.VMEM((total, width), F32),
            pltpu.VMEM((total, LANES), F32),
            pltpu.VMEM((total, LANES), F32),
            pltpu.VMEM((total, LANES), F32),
        ],
        compiler_params=params(),
        cost_estimate=cost(
            2 * heads * total * (width * 3 * LANES + 10 * LANES * total), 12 * total * width
        ),
        name="attend_back",
    )(*d_context, qkv, lse, w_heads)


def mlp_kernel(parts, place_ref, *refs):
    ctx_refs = refs[:parts]
    (
        hidden_ref,
        cot_ref,
        proj_ref,
        vec_ref,
        fc1_ref,
        fc1_bias_ref,
        fc2_ref,
        out_ref,
        d_middle_ref,
        d_branch_ref,
        active_t_ref,
        d_pre_ref,
        normed_t_ref,
        ctx_t_ref,
        vec_out_ref,
        fc1_bias_out_ref,
    ) = refs[parts : parts + 16]
    d_ctx_refs = refs[parts + 16 : 2 * parts + 16]
    middle_ref, normed_ref, acc_out, acc_back, turn_ref = refs[2 * parts + 16 :]
    step = pl.program_id(0)
    place = place_ref[0]
    own = ctx_refs[0].shape[1]

    @pl.when(step == 0)
    def _():
        branch = vec_ref[0:1] + hidden_ref[...]
        for part in range(parts):
            at = pl.ds(pl.multiple_of((place ^ part) * own, 8), own)
            branch += dot(ctx_refs[part][...], proj_ref[at, :])
            turn_ref[at] = ctx_refs[part][...].astype(F32).T
        ctx_t_ref[...] = turn_ref[...].astype(BF16)
        middle_ref[...] = branch
        scaled, _ = normalize(branch)
        normed = (scaled * vec_ref[1:2] + vec_ref[2:3]).astype(BF16)
        normed_ref[...] = normed
        normed_t_ref[...] = turned(normed)

    before = dot(normed_ref[...], fc1_ref[...]) + fc1_bias_ref[...]
    cdf = 0.5 + 0.5 * lax.erf(before * math.sqrt(0.5))
    active = (before * cdf).astype(BF16)
    slope = cdf + before * (jnp.exp(-0.5 * before * before) * (1.0 / math.sqrt(2.0 * math.pi)))
    d_before = dot_nt(cot_ref[...], fc2_ref[...]) * slope
    fc1_bias_out_ref[...] = jnp.sum(d_before, axis=0, keepdims=True)
    d_low = d_before.astype(BF16)
    d_pre_ref[...] = d_low
    active_t_ref[...] = turned(active)
    forward = dot(active, fc2_ref[...])
    backward = dot_nt(d_low, fc1_ref[...])

    @pl.when(step == 0)
    def _():
        acc_out[...] = forward
        acc_back[...] = backward

    @pl.when(step > 0)
    def _():
        acc_out[...] += forward
        acc_back[...] += backward

    @pl.when(step == pl.num_programs(0) - 1)
    def _():
        middle = middle_ref[...]
        out_ref[...] = middle + acc_out[...] + vec_ref[3:4]
        scaled, factor = normalize(middle)
        upstream = acc_back[...]
        cot = cot_ref[...].astype(F32)
        d_middle = cot + norm_back(upstream, scaled, factor, vec_ref[1:2])
        d_middle_ref[...] = d_middle
        d_branch = d_middle.astype(BF16)
        d_branch_ref[...] = d_branch
        vec_out_ref[0:1] = jnp.sum(upstream * scaled, axis=0, keepdims=True)
        vec_out_ref[1:2] = jnp.sum(upstream, axis=0, keepdims=True)
        vec_out_ref[2:3] = jnp.sum(d_middle, axis=0, keepdims=True)
        vec_out_ref[3:4] = jnp.sum(cot, axis=0, keepdims=True)
        vec_out_ref[4:] = jnp.zeros((4, vec_out_ref.shape[1]), F32)
        for part in range(parts):
            at = pl.ds(pl.multiple_of((place ^ part) * own, 8), own)
            d_ctx_refs[part][...] = dot_nt(d_branch, proj_ref[at, :]).astype(BF16)


def mlp(parts, place, context, hidden, cot, proj, vecs, fc1, fc1_bias, fc2):
    rows, width = hidden.shape
    ff = fc1.shape[1]
    own = context[0].shape[1]
    chunk = width
    whole = lambda *shape: pl.BlockSpec(shape, lambda i, p: (0,) * len(shape))
    return pl.pallas_call(
        functools.partial(mlp_kernel, parts),
        grid_spec=pltpu.PrefetchScalarGridSpec(
            num_scalar_prefetch=1,
            grid=(ff // chunk,),
            in_specs=[whole(rows, own)] * parts
            + [
                whole(rows, width),
                whole(rows, width),
                whole(width, width),
                whole(8, width),
                pl.BlockSpec((width, chunk), lambda i, p: (0, i)),
                pl.BlockSpec((1, chunk), lambda i, p: (0, i)),
                pl.BlockSpec((chunk, width), lambda i, p: (i, 0)),
            ],
            out_specs=[
                whole(rows, width),
                whole(rows, width),
                whole(rows, width),
                pl.BlockSpec((chunk, rows), lambda i, p: (i, 0)),
                pl.BlockSpec((rows, chunk), lambda i, p: (0, i)),
                whole(width, rows),
                whole(width, rows),
                whole(8, width),
                pl.BlockSpec((1, chunk), lambda i, p: (0, i)),
            ]
            + [whole(rows, own)] * parts,
            scratch_shapes=[
                pltpu.VMEM((rows, width), F32),
                pltpu.VMEM((rows, width), BF16),
                pltpu.VMEM((rows, width), F32),
                pltpu.VMEM((rows, width), F32),
                pltpu.VMEM((width, rows), F32),
            ],
        ),
        out_shape=[
            jax.ShapeDtypeStruct((rows, width), F32),
            jax.ShapeDtypeStruct((rows, width), F32),
            jax.ShapeDtypeStruct((rows, width), BF16),
            jax.ShapeDtypeStruct((ff, rows), BF16),
            jax.ShapeDtypeStruct((rows, ff), BF16),
            jax.ShapeDtypeStruct((width, rows), BF16),
            jax.ShapeDtypeStruct((width, rows), BF16),
            jax.ShapeDtypeStruct((8, width), F32),
            jax.ShapeDtypeStruct((1, ff), F32),
        ]
        + [jax.ShapeDtypeStruct((rows, own), BF16)] * parts,
        compiler_params=params(),
        cost_estimate=cost(8 * rows * width * ff, 4 * width * ff + 24 * rows * width),
        name="feed_forward",
    )(place, *context, hidden, cot, proj, vecs, fc1, fc1_bias, fc2)


def post_kernel(lead_ref, tail_ref, hidden_ref, d_middle_ref, gain_ref, w_ref, din_ref, dskip_ref, low_ref, vec_ref):
    width = hidden_ref.shape[1]
    upstream = jnp.concatenate([lead_ref[...].astype(F32), tail_ref[...].astype(F32)], 0)
    scaled, factor = normalize(hidden_ref[...])
    d_hidden = d_middle_ref[...] + norm_back(upstream, scaled, factor, gain_ref[...])
    low = d_hidden.astype(BF16)
    low_ref[...] = low
    vec_ref[0:1] = jnp.sum(d_hidden, axis=0, keepdims=True)
    vec_ref[1:2] = jnp.sum(upstream * scaled, axis=0, keepdims=True)
    vec_ref[2:3] = jnp.sum(upstream, axis=0, keepdims=True)
    vec_ref[3:] = jnp.zeros((5, width), F32)
    din_ref[...] = dot_nt(low, w_ref[:width])
    dskip_ref[...] = dot_nt(low, w_ref[width:])


def post(lead, tail, hidden, d_middle, gain, w):
    rows, width = hidden.shape
    return pl.pallas_call(
        post_kernel,
        out_shape=(
            jax.ShapeDtypeStruct((rows, width), F32),
            jax.ShapeDtypeStruct((rows, width), F32),
            jax.ShapeDtypeStruct((rows, width), BF16),
            jax.ShapeDtypeStruct((8, width), F32),
        ),
        compiler_params=params(),
        cost_estimate=cost(4 * rows * width * width, 4 * width * width + 20 * rows * width),
        name="input_back",
    )(lead, tail, hidden, d_middle, gain, w)


def pair_kernel(count, where_ref, *refs):
    out_ref = refs[4 * count]
    at = 0
    for index in range(count):
        own_t, peer_t, own, peer = refs[4 * index : 4 * index + 4]
        size = own_t.shape[2]
        out_ref[0, pl.ds(at, size)] = (
            dot(own_t[0, 0], own[...]) + dot(peer_t[0], peer[...])
        ).astype(BF16)
        at += size


def pair_grads(where, groups):
    depth = groups[0][0].shape[0]
    width = groups[0][2].shape[1]
    in_specs, operands, height, flops = [], [], 0, 0
    for own_t, peer_t, own, peer in groups:
        size, rows = own_t.shape[2:]
        in_specs += [
            pl.BlockSpec((1, 1, size, rows), lambda z, w: (z, w[0], 0, 0)),
            pl.BlockSpec((1, size, rows), lambda z, w: (z, 0, 0)),
            pl.BlockSpec((rows, width), lambda z, w: (0, 0)),
            pl.BlockSpec((rows, width), lambda z, w: (0, 0)),
        ]
        operands += [own_t, peer_t, own, peer]
        height += size
        flops += 4 * depth * size * rows * width
    return pl.pallas_call(
        functools.partial(pair_kernel, len(groups)),
        grid_spec=pltpu.PrefetchScalarGridSpec(
            num_scalar_prefetch=1,
            grid=(depth,),
            in_specs=in_specs,
            out_specs=pl.BlockSpec((1, height, width), lambda z, w: (z, 0, 0)),
        ),
        out_shape=jax.ShapeDtypeStruct((depth, height, width), BF16),
        compiler_params=params(),
        cost_estimate=cost(flops, 4 * depth * height * width),
        name="pair_grads",
    )(where, *operands)


def column_kernel(where_ref, own_t, peer_t, own, peer, out_ref):
    for z in range(own_t.shape[0]):
        out_ref[0, z] = (dot(own_t[z, 0], own[...]) + dot(peer_t[z], peer[...])).astype(BF16)


def column_grads(where, parts, own_t, peer_t, own, peer):
    depth, _, size, rows = own_t.shape
    width = own.shape[1] // parts
    return pl.pallas_call(
        column_kernel,
        grid_spec=pltpu.PrefetchScalarGridSpec(
            num_scalar_prefetch=1,
            grid=(parts,),
            in_specs=[
                pl.BlockSpec((depth, 1, size, rows), lambda k, w: (0, w[0], 0, 0)),
                pl.BlockSpec((depth, size, rows), lambda k, w: (0, 0, 0)),
                pl.BlockSpec((rows, width), lambda k, w: (0, k ^ w[1])),
                pl.BlockSpec((rows, width), lambda k, w: (0, k ^ w[1])),
            ],
            out_specs=pl.BlockSpec((1, depth, size, width), lambda k, w: (k, 0, 0, 0)),
        ),
        out_shape=jax.ShapeDtypeStruct((parts, depth, size, width), BF16),
        compiler_params=params(),
        cost_estimate=cost(
            4 * parts * depth * size * rows * width, 4 * parts * depth * size * width
        ),
        name="column_grads",
    )(where, own_t, peer_t, own, peer)


def heads_kernel(normed_ref, dt_ref, out_ref):
    out_ref[...] = lax.dot_general(
        normed_ref[...], dt_ref[...], (((0,), (1,)), ((), ())), preferred_element_type=F32
    ).astype(BF16)


def heads_grads(normed_all, d_triple_t):
    total, width = normed_all.shape
    wide = d_triple_t.shape[0]
    return pl.pallas_call(
        heads_kernel,
        out_shape=jax.ShapeDtypeStruct((width, wide), BF16),
        compiler_params=params(),
        cost_estimate=cost(2 * total * width * wide, 2 * total * (width + wide)),
        name="heads_grads",
    )(normed_all, d_triple_t)


def columns_kernel(place_ref, *refs):
    out_ref = refs[-1]
    size = refs[0].shape[1]
    for k in range(len(refs) - 1):
        at = pl.multiple_of((place_ref[0] ^ k) * size, LANES)
        out_ref[:, pl.ds(at, size)] = refs[k][...].astype(F32)


def put_columns(place, pieces):
    height, size = pieces[0].shape
    count = len(pieces)
    return pl.pallas_call(
        columns_kernel,
        in_specs=[pl.BlockSpec(memory_space=pltpu.SMEM)]
        + [pl.BlockSpec(memory_space=pltpu.VMEM)] * count,
        out_shape=jax.ShapeDtypeStruct((height, count * size), F32),
        compiler_params=params(),
        cost_estimate=cost(1e6, 6 * count * height * size),
        name="put_columns",
    )(place, *pieces)


def head_columns_kernel(place_ref, *refs):
    out_ref = refs[-1]
    count = len(refs) - 1
    size = refs[0].shape[1] // 3
    for j in range(count):
        value = refs[0][...]
        for k in range(1, count):
            value = jnp.where((place_ref[0] ^ k) == j, refs[k][...], value)
        value = value.astype(F32)
        for which in range(3):
            at = (which * count + j) * size
            out_ref[:, at : at + size] = value[:, which * size : (which + 1) * size]


def put_heads(place, pieces):
    height, size = pieces[0].shape
    count = len(pieces)
    return pl.pallas_call(
        head_columns_kernel,
        in_specs=[pl.BlockSpec(memory_space=pltpu.SMEM)]
        + [pl.BlockSpec(memory_space=pltpu.VMEM)] * count,
        out_shape=jax.ShapeDtypeStruct((height, count * size), F32),
        compiler_params=params(),
        cost_estimate=cost(1e6, 6 * count * height * size),
        name="put_heads",
    )(place, *pieces)


def across(value, size, bit):
    return lax.ppermute(value, "seq", [(i, i ^ bit) for i in range(size)])


def other_core(value, size):
    return lax.ppermute(value, "batch", [(i, i ^ 1) for i in range(size)])


def plus(*terms):
    total = terms[0].astype(F32)
    for term in terms[1:]:
        total = total + term.astype(F32)
    return total.astype(BF16)


def bits_of(size):
    return [1 << i for i in range(size.bit_length() - 1)]


def everywhere(value, size):
    if size != 4:
        return [value] + [across(value, size, k) for k in range(1, size)]
    half = value.shape[0] // 2
    near, far = across(value, size, 1), across(value, size, 2)
    lead, tail = across(near[:half], size, 2), across(far[half:], size, 1)
    return [value, near, far, jnp.concatenate([lead, tail], 0)]


def scattered(value, size, bits):
    left = list(range(size))
    for bit in bits:
        keep = [i for i, k in enumerate(left) if not k & bit]
        send = [i for i, k in enumerate(left) if k & bit]
        pick = lambda which: jnp.concatenate([value[i : i + 1] for i in which], 0)
        value = plus(pick(keep), across(pick(send), size, bit))
        left = [left[i] for i in keep]
    return value[0]


def summed(value, size):
    half = (value.shape[0] // 2 + 7) // 8 * 8
    bits = bits_of(size)
    done = []
    for piece, order in ((value[:half], bits), (value[half:], bits[::-1])):
        for bit in order:
            piece = plus(piece, across(piece, size, bit))
        done.append(piece)
    return jnp.concatenate(done, 0)


def down_the_line(value, size, at):
    depth = value.shape[0]
    pick = lambda index: lax.dynamic_index_in_dim(
        value, jnp.clip(index, 0, depth - 1), 0, keepdims=False
    )
    up = down = None
    for t in range(depth - 1):
        send_up = pick(depth - 1 - t + at)
        send_down = pick(t - (depth - 1 - at))
        if t:
            send_up, send_down = plus(send_up, up), plus(send_down, down)
        up = lax.ppermute(
            send_up,
            "batch",
            [(2 * z + c, 2 * z + 2 + c) for z in range(depth - 1) if z <= t for c in (0, 1)],
        )
        down = lax.ppermute(
            send_down,
            "batch",
            [
                (2 * z + c, 2 * z - 2 + c)
                for z in range(1, depth)
                if z >= depth - 1 - t
                for c in (0, 1)
            ],
        )
    return plus(pick(at), up, down)


MESH = pl.DeviceIdType.MESH
AWAY = (1, 3, 2, 0)


def flip(value, k):
    if k == 0:
        return value
    if k == 1:
        return value + 1 - 2 * (value % 2)
    if k == 2:
        return value + 2 - 4 * (value // 2)
    return 3 - value


def add_rows(into, other):
    if len(into.shape) > 2:
        for i in range(into.shape[0]):
            add_rows(into.at[i], other.at[i])
        return
    tile = 16

    def body(i, carry):
        at = pl.ds(pl.multiple_of(i * tile, tile), tile)
        into[at] = (into[at].astype(F32) + other[at].astype(F32)).astype(BF16)
        return carry

    lax.fori_loop(0, into.shape[0] // tile, body, 0)


class Wires:
    def __init__(self, send_sems, recv_sems):
        self.send_sems, self.recv_sems, self.made = send_sems, recv_sems, []
        self.limit = send_sems.shape[0]

    def copy(self, src, dst, device, when=None):
        index = len(self.made)
        assert index < self.limit
        made = Wire(
            pltpu.make_async_remote_copy(
                src_ref=src,
                dst_ref=dst,
                send_sem=self.send_sems.at[index],
                recv_sem=self.recv_sems.at[index],
                device_id=device,
                device_id_type=MESH,
            ),
            when,
        )
        self.made.append(made)
        return made

    def by_core(self, core, src, dst, device, when=None):
        index = len(self.made)
        assert index + 1 < self.limit
        self.made.append(None)
        pick = lambda which: pltpu.make_async_remote_copy(
            src_ref=src,
            dst_ref=dst,
            send_sem=self.send_sems.at[index],
            recv_sem=self.recv_sems.at[index + which],
            device_id=device,
            device_id_type=MESH,
        )
        made = Wire(pick(core), when)
        made.arrive = lambda: [pick(which).wait_recv() for which in (0, 1)]
        self.made.append(made)
        return made

    def drain(self):
        for wire in [w for w in self.made if w is not None]:
            if wire.when is None:
                wire.copy.wait_send()
            else:
                pl.when(wire.when)(wire.copy.wait_send)


class Wire:
    def __init__(self, copy, when):
        self.copy, self.when = copy, when
        self.start, self.arrive = copy.start, copy.wait_recv


class Line:
    def __init__(self, wires, depth, chip, up_to, down_to, own, up_in, down_in, begun=False):
        self.depth, self.chip, self.own, self.begun = depth, chip, own, begun
        self.up_in, self.down_in = up_in, down_in
        last = depth - 1
        self.up = {
            d: wires.copy(
                own(d),
                up_in.at[d - 1],
                up_to,
                (chip < d) & (chip > 0) if begun and d == last else chip < d,
            )
            for d in range(1, depth)
        }
        self.down = {
            d: wires.copy(
                own(d),
                down_in.at[d],
                down_to,
                (chip > d) & (chip < last) if begun and d == 0 else chip > d,
            )
            for d in range(last)
        }

    def hop(self, t):
        last = self.depth - 1
        for d in range(1, self.depth):
            z = d - (last - t)
            if 0 <= z < d:

                @pl.when(self.chip == z)
                def _():
                    if z > 0 and not (self.begun and t == 1):
                        self.up[d].arrive()
                        add_rows(self.own(d), self.up_in.at[d - 1])
                    self.up[d].start()

                @pl.when(self.chip == last - z)
                def _():
                    if z > 0 and not (self.begun and t == 1):
                        self.down[last - d].arrive()
                        add_rows(self.own(last - d), self.down_in.at[last - d])
                    self.down[last - d].start()

    def finish(self):
        for d in range(self.depth):

            @pl.when(self.chip == d)
            def _():
                if d > 0:
                    self.up[d].arrive()
                    add_rows(self.own(d), self.up_in.at[d - 1])
                if d < self.depth - 1:
                    self.down[d].arrive()
                    add_rows(self.own(d), self.down_in.at[d])


class Square:
    def __init__(self, wires, to, own, in_one, in_two, src=None, begun=False):
        self.own, self.in_one, self.in_two = own, in_one, in_two
        src = src or own
        self.one, self.two = [], []
        for h, (f, g) in enumerate(((1, 2), (2, 1))):
            if not begun:
                self.one.append(
                    (
                        wires.copy(src(h, 3), in_one[h].at[1], to[f]),
                        wires.copy(src(h, f), in_one[h].at[0], to[f]),
                    )
                )
        for h, (f, g) in enumerate(((1, 2), (2, 1))):
            self.two.append(wires.copy(own(h, g), in_two[h], to[g]))

    def start(self):
        for i in range(2):
            for h in range(2):
                self.one[h][i].start()

    def middle(self):
        for h, g in ((0, 2), (1, 1)):
            self.one[h][0].arrive()
            add_rows(self.own(h, g), self.in_one[h].at[1])
            self.two[h].start()
        for h in range(2):
            self.one[h][1].arrive()
            add_rows(self.own(h, 0), self.in_one[h].at[0])

    def finish(self):
        for h in range(2):
            self.two[h].arrive()
            add_rows(self.own(h, 0), self.in_two[h])


class Spread:
    def __init__(self, wires, to, slots, src=None, cut=None):
        rows = slots.shape[1]
        cut = (rows // 2 + 15) // 16 * 16 if cut is None else cut
        src = slots.at[0] if src is None else src
        lead, tail = pl.ds(0, cut), pl.ds(cut, rows - cut)
        self.near = [wires.copy(src.at[p], slots.at[1, p], to[1]) for p in (lead, tail)]
        self.far = [wires.copy(src.at[p], slots.at[2, p], to[2]) for p in (tail, lead)]
        self.lead = wires.copy(slots.at[1, lead], slots.at[3, lead], to[2])
        self.tail = wires.copy(slots.at[2, tail], slots.at[3, tail], to[1])

    def start(self):
        for i in range(2):
            self.near[i].start()
            self.far[i].start()

    def relay(self):
        self.near[0].arrive()
        self.lead.start()
        self.far[0].arrive()
        self.tail.start()

    def finish(self):
        self.near[1].arrive()
        self.far[1].arrive()
        self.lead.arrive()
        self.tail.arrive()


class Pair:
    def __init__(self, wires, to, halves, ins):
        self.halves, self.ins, self.wires, self.to, self.step = halves, ins, wires, to, 0
        self.sent = [
            [wires.copy(halves[h][i], ins[h].at[i], to[(1, 2)[(h + i) % 2]]) for h in range(2)]
            for i in range(2)
        ]

    def start(self):
        for wire in self.sent[0]:
            wire.start()

    def middle(self):
        for h in range(2):
            self.sent[0][h].arrive()
            one, two = self.halves[h][0], self.halves[h][1]
            two[...] = (one[...].astype(F32) + self.ins[h][0].astype(F32)).astype(BF16)
            self.sent[1][h].start()

    def finish(self):
        for h in range(2):
            self.sent[1][h].arrive()
            two, three = self.halves[h][1], self.halves[h][2]
            three[...] = (two[...].astype(F32) + self.ins[h][1].astype(F32)).astype(BF16)


def reduce_kernel(
    late_hbm,
    lead_hbm,
    tail_hbm,
    normed_hbm,
    dt_hbm,
    joined_hbm,
    joined_peer_hbm,
    hidden_hbm,
    d_middle_hbm,
    w_hbm,
    normed_x,
    normed_peer,
    normed_cond_x,
    normed_cond_peer,
    d_pre_own,
    d_pre_x,
    active_x,
    active_cond_x,
    cot_hbm,
    cot_z,
    cot_zz,
    cot_far,
    cot_peer,
    gain_ref,
    vec_two_ref,
    fc1_bias_ref,
    p_all,
    f_all,
    g_all,
    q_all,
    s_all,
    c_all,
    din_hbm,
    dskip_hbm,
    vec_ref,
    left_one,
    right_one,
    left_two,
    right_two,
    cond_rows,
    cond_flat,
    active_cond,
    f_own,
    f_up,
    f_down,
    g_own,
    g_lead_one,
    g_tail_one,
    g_lead_two,
    g_tail_two,
    l_own,
    l_up,
    l_down,
    q_own,
    q_sum,
    q_up,
    q_down,
    s_own,
    s_one,
    s_two,
    s_z,
    s_up,
    s_down,
    d_own,
    d_one,
    d_two,
    p_lead,
    p_tail,
    p_lead_in,
    p_tail_in,
    low_ref,
    low_peer,
    c_own,
    c_in,
    rows_ref,
    hidden_ref,
    d_middle_ref,
    joined_ref,
    joined_peer_ref,
    v_own,
    v_in,
    send_sems,
    recv_sems,
    local_sems,
):
    rows, width = hidden_hbm.shape
    depth = f_own.shape[0]
    mid = depth // 2
    slots = c_own.shape[1]
    images = rows - slots
    place, index = lax.axis_index("seq"), lax.axis_index("batch")
    chip, core = index // 2, index % 2
    last = depth - 1
    to, other, up_to, down_to = ends_of(place, index, depth)
    greet([to[1], to[2], to[3], other], chip, depth, up_to, down_to)
    wires = Wires(send_sems, recv_sems)
    taken = [0]

    def local(src, dst):
        taken[0] += 1
        copy = pltpu.make_async_copy(src, dst, local_sems.at[taken[0] - 1])
        copy.start()
        return copy

    keeps = []

    d_hbm = (lead_hbm, tail_hbm)
    norm_sum = Square(
        wires,
        to,
        lambda h, k: d_own.at[h, (0, 1, 1, None)[k]],
        [d_one.at[h] for h in range(2)],
        [d_two.at[h] for h in range(2)],
        src=lambda h, k: d_hbm[h].at[k],
    )
    norm_sum.start()

    l_load = local(late_hbm, l_own)
    l_line = Line(wires, depth, chip, up_to, down_to, lambda d: l_own.at[d], l_up, l_down)

    img, cnd = pl.ds(0, images), pl.ds(images, slots)

    def cut(g):
        return pl.ds(pl.multiple_of(g * images, images), images)

    def end(g):
        return pl.ds(pl.multiple_of(8 * images + g * slots, slots), slots)

    loads_two, loads_able = [], []
    for i in range(depth):
        source = (chip + depth - AWAY[i]) % depth
        for c in range(2):
            g = source * 2 + c
            loads_two.append(local(active_x.at[i, c], left_two.at[:, :, cut(g)]))
            loads_two.append(local(active_cond_x.at[i, c], active_cond.at[g]))
    held = [cot_hbm, cot_z.at[0], cot_z.at[1], cot_zz.at[0], cot_zz.at[1], cot_far]
    for away, picks in ((0, (0, 0)), (1, (1, 2)), (2, (3, 4)), (3, (5, 5))):
        for which in range(2):
            if away == 0 and which == 1:
                continue
            z = chip - away if which == 0 else chip + away
            able = (z >= 0) & (z <= last)
            for ref, c in ((held[picks[which]], core), (cot_peer.at[picks[which]], 1 - core)):
                g = jnp.clip(z, 0, last) * 2 + c
                for src, dst in ((img, cut(g)), (cnd, end(g))):
                    sem = local_sems.at[taken[0]]
                    taken[0] += 1
                    copy = pltpu.make_async_copy(ref.at[src], right_two.at[dst], sem)
                    pl.when(able)(copy.start)
                    loads_able.append((able, copy))
    swaps_one = []
    d_pre_of = lambda k, part: d_pre_x.at[k - 1, part] if k else d_pre_own.at[part]
    for k in range(4):
        swaps_one.append(wires.copy(d_pre_of(k, img), right_one.at[cut(4 + k)], other))
        swaps_one.append(wires.copy(d_pre_of(k, cnd), right_one.at[end(4 + k)], other))
    for wire in swaps_one:
        wire.start()
    loads_one = []
    for k in range(4):
        for g, left, cond in (
            (k, normed_x.at[k, :, core], normed_cond_x.at[k]),
            (4 + k, normed_peer.at[k], normed_cond_peer.at[k]),
        ):
            loads_one.append(local(left, left_one.at[:, :, cut(g)]))
            loads_one.append(local(cond, cond_rows.at[pl.ds(g * slots, slots)]))
        loads_one.append(local(d_pre_of(k, img), right_one.at[cut(k)]))
        loads_one.append(local(d_pre_of(k, cnd), right_one.at[end(k)]))
    d_loads = [
        local(d_hbm[h].at[k], d_own.at[h, i]) for h, ks in ((0, (0, 2)), (1, (0, 1))) for i, k in enumerate(ks)
    ]
    p_cut = p_lead.shape[1]
    h_loads = [local(hidden_hbm, hidden_ref), local(d_middle_hbm, d_middle_ref)]
    j_loads = [local(joined_hbm, joined_ref), local(joined_peer_hbm, joined_peer_ref)]
    l_load.wait()
    l_line.hop(0)

    for copy in loads_two:
        copy.wait()
    for able, copy in loads_able:
        pl.when(able)(copy.wait)
    small = f_own.shape[1]
    for j in range(4):
        left_two[j, :, 8 * images :] = jnp.concatenate(
            [active_cond[g, :, j * slots : (j + 1) * slots] for g in range(8)], 1
        )
    g_own[...] = (
        dot(left_two[...].reshape(4 * small, 8 * rows), right_two[...])
        .astype(BF16)
        .reshape(4, small, width)
    )
    l_line.hop(1)
    g_cut = g_lead_one.shape[1]
    g_sum = Square(
        wires,
        to,
        lambda h, k: g_own.at[flip(place, k), (pl.ds(0, g_cut), pl.ds(g_cut, small - g_cut))[h]],
        (g_lead_one, g_tail_one),
        (g_lead_two, g_tail_two),
    )

    for copy in loads_one:
        copy.wait()
    flat = turned(cond_rows[...])
    for b in range(2 * depth):
        cond_flat[b // 2, b % 2] = flat[b * small : (b + 1) * small]
    for z in range(depth):
        left_one[z, :, 8 * images :] = cond_flat[z, core]
    for wire in swaps_one:
        wire.arrive()
    f_own[...] = (
        dot(left_one[...].reshape(depth * small, 8 * rows), right_one[...])
        .astype(BF16)
        .reshape(depth, small, width)
    )
    f_line = Line(wires, depth, chip, up_to, down_to, lambda d: f_own.at[d], f_up, f_down)
    f_line.hop(0)
    for copy in d_loads:
        copy.wait()
    norm_sum.middle()
    for t in range(2, last):
        l_line.hop(t)

    def heads_part(normed, dt):
        loads = [local(normed_hbm, normed), local(dt_hbm, dt)]
        for copy in loads:
            copy.wait()
        step = 3 * LANES
        for part in range(normed.shape[1] // step):
            grads = lax.dot_general(
                normed[:, part * step : (part + 1) * step],
                dt[...],
                (((0,), (1,)), ((), ())),
                preferred_element_type=F32,
            ).astype(BF16)
            q_own[pl.ds(part * step, step)] = grads

    pl.run_scoped(
        heads_part, pltpu.VMEM(normed_hbm.shape, BF16), pltpu.VMEM(dt_hbm.shape, BF16)
    )
    height = q_sum.shape[1]
    q_swap = [
        wires.copy(
            q_own.at[pl.ds(pl.multiple_of((2 * z + 1 - core) * height, 16), height)],
            q_sum.at[z],
            other,
        )
        for z in range(depth)
    ]
    for wire in q_swap:
        wire.start()

    norm_sum.finish()
    low_swap = wires.copy(low_ref, low_peer, other)
    v_swap = wires.copy(v_own.at[0], v_in.at[0], other)
    for copy in h_loads:
        copy.wait()
    upstream = jnp.concatenate([d_own[0, 0].astype(F32), d_own[1, 0].astype(F32)], 0)
    scaled, factor = normalize(hidden_ref[...])
    d_hidden = d_middle_ref[...] + norm_back(
        upstream, scaled, factor, gain_ref[...].reshape(1, -1)
    )
    low_ref[...] = d_hidden.astype(BF16)
    low_swap.start()
    c_src = low_ref.at[pl.ds(images, slots)]
    c_go = Spread(wires, to, c_in, c_src)
    c_go.start()
    l_line.finish()
    p_lead[0] = l_own[chip, :p_cut]
    p_tail[0] = l_own[chip, p_cut:]
    p_sum = Pair(
        wires,
        to,
        [[ref.at[i] for i in range(3)] for ref in (p_lead, p_tail)],
        (p_lead_in, p_tail_in),
    )
    p_sum.start()
    g_sum.start()
    v_own[0] = jnp.zeros(v_own.shape[1:], F32)
    v_own[0, 0:1] = jnp.sum(d_hidden, axis=0, keepdims=True)
    v_own[0, 1:2] = jnp.sum(upstream * scaled, axis=0, keepdims=True)
    v_own[0, 2:3] = jnp.sum(upstream, axis=0, keepdims=True)
    v_own[0, 3:7] = vec_two_ref[0:4]
    v_own[0, 8:12] = fc1_bias_ref[...]
    v_swap.start()
    f_line.hop(1)
    for z, wire in enumerate(q_swap):
        wire.arrive()
        add_rows(q_sum.at[z], q_own.at[pl.ds(pl.multiple_of((2 * z + core) * height, 16), height)])
    q_line = Line(wires, depth, chip, up_to, down_to, lambda d: q_sum.at[d], q_up, q_down)
    q_line.hop(0)
    c_go.relay()

    for copy in j_loads:
        copy.wait()
    low_swap.arrive()
    block = joined_ref.shape[1]
    chunk = block // 4
    grads = both(
        joined_ref[...].reshape(depth * block, rows),
        joined_peer_ref[...].reshape(depth * block, rows),
        low_ref[...],
        low_peer[...],
    )
    for h in range(mid):
        for j in range(4):
            at = [(2 * h + i) * block + j * chunk for i in range(2)]
            piece = jnp.concatenate([grads[a : a + chunk] for a in at], 0)
            s_own[flip(place, j), h] = piece.astype(BF16)
    s_sum = Square(
        wires,
        to,
        lambda h, k: s_own.at[k, h],
        [s_one.at[h] for h in range(2)],
        [s_two.at[h] for h in range(2)],
    )
    s_sum.start()
    for t in range(2, last):
        f_line.hop(t)
    p_sum.middle()

    c_go.finish()
    rows_ref[:images] = low_ref[:images]
    rows_ref[images : images + slots] = low_ref[images:]
    for k in range(1, 4):
        rows_ref[images + k * slots : images + (k + 1) * slots] = c_in[k]

    def rows_part(which, out_hbm):
        def run(w, stage):
            copy = local(w_hbm.at[pl.ds(which * width, width)], w)
            copy.wait()
            stage[...] = dot_nt(rows_ref[...], w[...])
            for k in range(4):
                c_own[k, :, which * width : (which + 1) * width] = stage[
                    images + k * slots : images + (k + 1) * slots
                ].astype(BF16)
            local(stage.at[pl.ds(0, images)], out_hbm).wait()

        pl.run_scoped(
            run, pltpu.VMEM((width, width), BF16), pltpu.VMEM((images + 4 * slots, width), F32)
        )

    rows_part(0, din_hbm)
    q_line.hop(1)
    g_sum.middle()
    rows_part(1, dskip_hbm)
    keeps.append(local(c_own, c_all))
    for t in range(2, last):
        q_line.hop(t)

    v_swap.arrive()
    v_own[1] = v_own[0] + v_in[0]
    v_own[2] = v_own[1]
    v_own[3] = v_own[1]
    v_up = wires.copy(v_own.at[2], v_in.at[1], up_to, chip < last)
    v_down = wires.copy(v_own.at[3], v_in.at[2], down_to, chip > 0)
    s_sum.middle()
    g_sum.finish()
    f_line.finish()
    s_sum.finish()
    room = s_z.shape[1]
    for h in range(mid):
        value = s_own[0, h].astype(F32)
        for i in range(2):
            s_z[2 * h + i] = jnp.concatenate(
                [value[i * chunk : (i + 1) * chunk], jnp.zeros((room - chunk, width), F32)], 0
            ).astype(BF16)
    s_line = Line(wires, depth, chip, up_to, down_to, lambda d: s_z.at[d], s_up, s_down)
    s_line.hop(0)
    g_go = Spread(wires, to, g_all, g_own.at[place])
    g_go.start()
    f_go = Spread(wires, to, f_all, f_own.at[chip])
    f_go.start()
    keeps.append(local(g_own.at[place], g_all.at[0]))
    keeps.append(local(f_own.at[chip], f_all.at[0]))

    @pl.when(chip > 0)
    def _():
        v_up.arrive()
        v_own[2] = v_own[1] + v_in[1]

    @pl.when(chip < last)
    def _():
        v_up.start()

    @pl.when(chip < last)
    def _():
        v_down.arrive()
        v_own[3] = v_own[1] + v_in[2]

    @pl.when(chip > 0)
    def _():
        v_down.start()

    v_own[4] = v_own[2] + v_own[3] - v_own[1]
    v_near = wires.copy(v_own.at[4], v_in.at[3], to[1])
    v_near.start()
    s_line.hop(1)
    q_line.finish()
    q_go = Spread(wires, to, q_all, q_sum.at[chip])
    q_go.start()
    keeps.append(local(q_sum.at[chip], q_all.at[0]))
    for t in range(2, last):
        s_line.hop(t)
    g_go.relay()
    f_go.relay()
    v_near.arrive()
    v_own[5] = v_own[4] + v_in[3]
    v_far = wires.copy(v_own.at[5], v_in.at[4], to[2])
    v_far.start()
    s_line.finish()
    s_go = Spread(wires, to, s_all, s_z.at[chip])
    s_go.start()
    keeps.append(local(s_z.at[chip], s_all.at[0]))
    q_go.relay()
    p_sum.finish()
    keeps.append(local(p_lead.at[2], p_all.at[pl.ds(0, p_cut)]))
    keeps.append(local(p_tail.at[2], p_all.at[pl.ds(p_cut, p_tail.shape[1])]))
    v_far.arrive()
    vec_ref[...] = v_own[5] + v_in[4]
    s_go.relay()
    f_go.finish()
    g_go.finish()
    q_go.finish()
    s_go.finish()
    for copy in keeps:
        copy.wait()
    wires.drain()


def reduce_all(
    late, lead, tail, normed_all, d_triple_t, joined, joined_peer, hidden, d_middle, w, feeds,
    gain, vec_two, fc1_bias_grad,
):
    depth, small, width = late.shape
    rows = hidden.shape[0]
    slots = SLOTS // 4
    images = rows - slots
    mid = depth // 2
    own = d_triple_t.shape[0]
    skip_rows = joined.shape[1]
    skip_chunk = (skip_rows // 4 + 15) // 16 * 16
    pair = depth // 2 * (skip_rows // 4)
    half = rows // 2
    cut = (small // 2 + 15) // 16 * 16
    v = lambda *shape: pltpu.VMEM(shape, BF16)
    ends = depth - 1
    scratch = [
        v(depth, small, 8 * rows), v(8 * rows, width), v(depth, small, 8 * rows), v(8 * rows, width),
        v(8 * slots, width), v(depth, 2, small, 8 * slots), v(8, small, 4 * slots),
        v(depth, small, width), v(ends, small, width), v(ends, small, width),
        v(4, small, width), v(2, cut, width), v(2, small - cut, width), v(cut, width), v(small - cut, width),
        v(depth, small, width), v(ends, small, width), v(ends, small, width),
        v(width, own), v(depth, small, own), v(ends, small, own), v(ends, small, own),
        v(4, 2, pair, width), v(2, 2, pair, width), v(2, pair, width),
        v(depth, skip_chunk, width), v(ends, skip_chunk, width), v(ends, skip_chunk, width),
        v(2, 2, half, width), v(2, 2, half, width), v(2, half, width),
        v(3, cut, width), v(3, small - cut, width), v(2, cut, width), v(2, small - cut, width),
        v(rows, width), v(rows, width), v(4, slots, 2 * width),
        v(4, slots, width), v(images + 4 * slots, width),
        pltpu.VMEM((rows, width), F32), pltpu.VMEM((rows, width), F32),
        v(*joined.shape), v(*joined.shape),
        pltpu.VMEM((6, 16, width), F32), pltpu.VMEM((5, 16, width), F32),
        pltpu.SemaphoreType.DMA((128,)), pltpu.SemaphoreType.DMA((128,)), pltpu.SemaphoreType.DMA((128,)),
    ]
    hbm = pl.BlockSpec(memory_space=pl.ANY)
    vmem = pl.BlockSpec(memory_space=pltpu.VMEM)
    f = lambda *shape: jax.ShapeDtypeStruct(shape, F32)
    b = lambda *shape: jax.ShapeDtypeStruct(shape, BF16)
    return pl.pallas_call(
        reduce_kernel,
        in_specs=[hbm] * 23 + [vmem] * 3,
        out_specs=[hbm] * 8 + [vmem],
        out_shape=[
            b(small, width),
            b(4, small, width),
            b(4, small, width),
            b(4, small, own),
            b(4, skip_chunk, width),
            b(4, slots, 2 * width),
            f(images, width),
            f(images, width),
            f(16, width),
        ],
        scratch_shapes=scratch,
        compiler_params=pltpu.CompilerParams(
            vmem_limit_bytes=VMEM_LIMIT, collective_id=0, has_side_effects=True
        ),
        cost_estimate=cost(1e10, 1e8),
        name="reduce_all",
    )(
        late, lead, tail, normed_all, d_triple_t, joined, joined_peer, hidden, d_middle, w, *feeds,
        gain, vec_two, fc1_bias_grad,
    )


def ends_of(place, index, depth):
    chip, core = index // 2, index % 2
    to = {k: (index, flip(place, k)) for k in (1, 2, 3)}
    return to, (index + 1 - 2 * core, place), (index + 2, place), (index - 2, place)


def line_of(place, index, depth):
    chip = index // 2
    return [((chip + i) % depth * 2 + c, place) for i in range(1, depth) for c in (0, 1)]


def arrive_by_core(wires, core):
    for c in range(2):

        @pl.when(core == c)
        def _():
            wires[2 * c].arrive()
            wires[2 * c + 1].arrive()


class Hop:
    def __init__(self, wires, depth, chip, up_to, down_to, t, src_up, src_down, dst_up, dst_down):
        last = depth - 1
        self.up = wires.copy(src_up, dst_up, up_to, (chip < last) & (chip >= t))
        self.down = wires.copy(src_down, dst_down, down_to, (chip > 0) & (chip <= last - t))
        self.from_up = (chip > 0) & (chip - 1 >= t)
        self.from_down = (chip < last) & (chip + 1 <= last - t)

    def start(self):
        pl.when(self.up.when)(self.up.start)
        pl.when(self.down.when)(self.down.start)

    def arrive(self):
        pl.when(self.from_up)(self.up.arrive)
        pl.when(self.from_down)(self.down.arrive)


def greet(devices, chip=None, depth=0, up_to=None, down_to=None):
    barrier = pltpu.get_barrier_semaphore()
    for device in devices:
        pl.semaphore_signal(barrier, inc=1, device_id=device, device_id_type=MESH)
    if chip is None:
        pl.semaphore_wait(barrier, len(devices))
        return

    @pl.when(chip < depth - 1)
    def _():
        pl.semaphore_signal(barrier, inc=1, device_id=up_to, device_id_type=MESH)

    @pl.when(chip > 0)
    def _():
        pl.semaphore_signal(barrier, inc=1, device_id=down_to, device_id_type=MESH)

    pl.semaphore_wait(
        barrier, len(devices) + jnp.minimum(chip, 1) + jnp.minimum(depth - 1 - chip, 1)
    )


class Locals:
    def __init__(self, sems):
        self.sems, self.taken = sems, 0

    def copy(self, src, dst):
        self.taken += 1
        assert self.taken <= self.sems.shape[0]
        return pltpu.make_async_copy(src, dst, self.sems.at[self.taken - 1])

    def start(self, src, dst):
        copy = self.copy(src, dst)
        copy.start()
        return copy


def own_slots(cond_ref, pad_ref, place, slots):
    pad_ref[...] = jnp.zeros(pad_ref.shape, BF16)
    pad_ref[0 : cond_ref.shape[0]] = cond_ref[...]
    return pad_ref[pl.ds(pl.multiple_of(place * slots, 16), slots)]


def start_kernel(
    window,
    length_ref,
    x_ref,
    x_cond_ref,
    s_ref,
    s_cond_ref,
    cot_ref,
    cot_cond_ref,
    bias_ref,
    gain_ref,
    shift_ref,
    w_hbm,
    qkv_w_hbm,
    hidden_ref,
    normed_hbm,
    heads_ref,
    qkv_ref,
    joined_hbm,
    peer_hbm,
    cot_all,
    cot_z,
    lse_ref,
    ctx_hbm,
    rest_hbm,
    cot_zz,
    pad_ref,
    x_all,
    s_all,
    normed_all,
    joined_ref,
    w_ref,
    qkv_w_ref,
    vt_ref,
    ot_ref,
    go_ref,
    rest_ref,
    send_sems,
    recv_sems,
    local_sems,
):
    images, width = x_ref.shape
    slots = x_all.shape[0] - images
    place, index = lax.axis_index("seq"), lax.axis_index("batch")
    core = index % 2
    chip = index // 2
    depth = joined_hbm.shape[0]
    to, other, up_to, down_to = ends_of(place, index, depth)
    wires, moves = Wires(send_sems, recv_sems), Locals(local_sems)
    loads = [
        moves.start(w_hbm.at[span], w_ref.at[span]) for span in (pl.ds(0, width), pl.ds(width, width))
    ]
    w_load = moves.start(qkv_w_hbm, qkv_w_ref)
    greet([to[1], to[2], to[3], other], chip, depth, up_to, down_to)
    cot_all[:images] = cot_ref[...]
    cot_all[images:] = own_slots(cot_cond_ref, pad_ref, place, slots)
    cot_go = Hop(
        wires, depth, chip, up_to, down_to, 0, cot_all, cot_all, cot_z.at[0], cot_z.at[1]
    )
    cot_go.start()
    for ref, cond, whole in ((x_ref, x_cond_ref, x_all), (s_ref, s_cond_ref, s_all)):
        whole[:images] = ref[...]
        whole[images:] = own_slots(cond, pad_ref, place, slots)
    spread = Spread(wires, to, normed_all)
    half = x_all.shape[0] // 2
    loads[0].wait()
    for i in range(2):
        span = slice(i * half, (i + 1) * half)
        hidden = dot(x_all[span], w_ref[:width])
        if i == 0:
            loads[1].wait()
        hidden += dot(s_all[span], w_ref[width:]) + bias_ref[...].reshape(1, -1)
        hidden_ref[span] = hidden
        scaled, _ = normalize(hidden)
        normed_all[0, span] = (
            scaled * gain_ref[...].reshape(1, -1) + shift_ref[...].reshape(1, -1)
        ).astype(BF16)
        spread.near[i].start()
        spread.far[1 - i].start()
    size = joined_ref.shape[2]
    per = width // size
    for which, whole in enumerate((x_all, s_all)):
        flat = turned(whole[...])
        for i in range(per):
            block = which * per + i
            joined_ref[block // 2, block % 2] = flat[i * size : (i + 1) * size]
    swap = wires.copy(joined_ref.at[:, 1 - core], peer_hbm, other)
    swap.start()
    keep = moves.start(joined_ref.at[:, core], joined_hbm)
    heads = qkv_ref.shape[0]
    width_own = heads * HEAD_DIM
    real = lax.broadcasted_iota(jnp.int32, (width, LANES), 1) < HEAD_DIM

    def weights(which):
        first = place * width_own + which * width
        start = jnp.minimum(first // LANES * LANES, 3 * width - window)
        value = qkv_w_ref[:, pl.ds(pl.multiple_of(start, LANES), window)].astype(F32)
        value = pltpu.roll(value, lax.rem(window - (first - start), window), 1)
        for head in range(heads):
            shifted = value if head == 0 else pltpu.roll(value, window - head * HEAD_DIM, 1)
            at = (3 * head + which) * LANES
            heads_ref[:, at : at + LANES] = jnp.where(real, shifted[:, :LANES], 0.0).astype(BF16)

    rows = normed_all.shape[1]
    lane = lax.broadcasted_iota(jnp.int32, (1, LANES), 1)
    one = jnp.where(lane == HEAD_DIM, 1.0, 0.0)
    slot = lax.broadcasted_iota(jnp.int32, (slots, LANES), 0)
    lanes = lax.broadcasted_iota(jnp.int32, (slots, LANES), 1)

    def project(part):
        hidden_key = flip(place, part) * slots + slot > length_ref[0]
        bias = jnp.where(hidden_key & (lanes == HEAD_DIM), -1e30, 0.0)
        base = part * rows
        for head in range(heads):
            triple = dot(
                normed_all[part], heads_ref[:, 3 * head * LANES : 3 * (head + 1) * LANES]
            )
            qkv_ref[head, base : base + rows, :LANES] = (triple[:, :LANES] + one).astype(BF16)
            key = triple[:, LANES : 2 * LANES]
            qkv_ref[head, base : base + images, LANES : 2 * LANES] = key[:images].astype(BF16)
            qkv_ref[head, base + images : base + rows, LANES : 2 * LANES] = (
                key[images:] + bias
            ).astype(BF16)
            qkv_ref[head, base : base + rows, 2 * LANES :] = triple[:, 2 * LANES :].astype(BF16)

    w_load.wait()
    weights(0)
    spread.relay()
    weights(1)
    weights(2)
    project(0)
    spread.near[1].arrive()
    project(1)
    spread.far[1].arrive()
    project(2)
    spread.lead.arrive()
    spread.tail.arrive()
    project(3)
    out = moves.start(normed_all, normed_hbm)
    cot_go.arrive()
    cot_on = Hop(
        wires, depth, chip, up_to, down_to, 1, cot_z.at[0], cot_z.at[1], cot_zz.at[0], cot_zz.at[1]
    )
    cot_on.start()

    total = 4 * rows
    step = 3 * LANES
    go, keeps = [], []
    sent = 0
    for head in range(heads):
        vt_ref[...] = turned(qkv_ref[head, :, 2 * LANES :])
        for first in range(0, total, step):
            span = slice(first, first + step)
            scores = dot_nt(qkv_ref[head, :, LANES : 2 * LANES], qkv_ref[head, span, :LANES])
            peak = jnp.max(scores, axis=0, keepdims=True)
            shifted = jnp.exp2((scores - peak) * SCALE2)
            sums = jnp.sum(shifted, axis=0, keepdims=True)
            mixed = dot(vt_ref[...], shifted.astype(BF16)) / sums
            ot_ref[head * HEAD_DIM : (head + 1) * HEAD_DIM, span] = mixed[:HEAD_DIM]
            lse_ref[head, :, span] = peak * SCALE2 + jnp.log2(sums)
        done = (head + 1) * HEAD_DIM if head == heads - 1 else (head + 1) * HEAD_DIM // 16 * 16
        if head:
            half = pl.ds(sent, done - sent)
            for part in (3, 1, 2, 0):
                go_ref[part, half] = ot_ref[half, part * rows : part * rows + images].astype(BF16)
                if part:
                    go.append(wires.copy(go_ref.at[part, half], ctx_hbm.at[part, half], to[part]))
                    go[-1].start()
                else:
                    keeps.append(moves.start(go_ref.at[0, half], ctx_hbm.at[0, half]))
            sent = done
    for part in (3, 1, 2, 0):
        rest_ref[part] = split_lanes(ot_ref[:, part * rows : (part + 1) * rows])[1]
        if part:
            go.append(wires.copy(rest_ref.at[part], rest_hbm.at[part], to[part]))
            go[-1].start()
        else:
            keeps.append(moves.start(rest_ref.at[0], rest_hbm.at[0]))
    swap.arrive()
    cot_on.arrive()
    for wire in go:
        wire.arrive()
    for copy in keeps + [keep, out]:
        copy.wait()
    wires.drain()


def start_stage(depth, length, x, x_cond, s, s_cond, cot, cot_cond, w, bias, gain, shift, qkv_w):
    images, width = x.shape
    slots = SLOTS // 4
    rows = images + slots
    heads = HEADS // 4
    own = heads * HEAD_DIM
    window = (max(p * own % LANES for p in range(4)) + own + LANES - 1) // LANES * LANES
    block = 2 * width // (2 * depth)
    vmem, hbm = pl.BlockSpec(memory_space=pltpu.VMEM), pl.BlockSpec(memory_space=pl.ANY)
    b = lambda *shape: jax.ShapeDtypeStruct(shape, BF16)
    v = lambda *shape: pltpu.VMEM(shape, BF16)
    return pl.pallas_call(
        functools.partial(start_kernel, window),
        in_specs=[pl.BlockSpec(memory_space=pltpu.SMEM)] + [vmem] * 9 + [hbm] * 2,
        out_specs=[vmem, hbm, vmem, vmem, hbm, hbm, vmem, hbm, vmem, hbm, hbm, hbm],
        out_shape=[
            jax.ShapeDtypeStruct((rows, width), F32),
            b(4, rows, width),
            b(width, heads * 3 * LANES),
            b(heads, 4 * rows, 3 * LANES),
            b(depth, block, rows),
            b(depth, block, rows),
            b(rows, width),
            b(2, rows, width),
            jax.ShapeDtypeStruct((heads, 1, 4 * rows), F32),
            b(4, own, images),
            b(4, (own // 4 + 15) // 16 * 16, LANES),
            b(2, rows, width),
        ],
        scratch_shapes=[
            v(SLOTS, width), v(rows, width), v(rows, width), v(4, rows, width),
            v(depth, 2, block, rows), v(2 * width, width), v(width, 3 * width),
            v(LANES, 4 * rows), pltpu.VMEM((own, 4 * rows), F32), v(4, own, images),
            v(4, (own // 4 + 15) // 16 * 16, LANES),
            pltpu.SemaphoreType.DMA((32,)), pltpu.SemaphoreType.DMA((32,)), pltpu.SemaphoreType.DMA((16,)),
        ],
        compiler_params=pltpu.CompilerParams(
            vmem_limit_bytes=VMEM_LIMIT, collective_id=1, has_side_effects=True
        ),
        cost_estimate=cost(12 * rows * width * width, 12 * width * width),
        name="start_stage",
    )(length, x, x_cond, s, s_cond, cot, cot_cond, bias, gain, shift, w, qkv_w)


def split_lanes(value):
    size = value.shape[0] // 4
    cut = value.shape[1] - 32
    rest = jnp.concatenate([value[i * size : (i + 1) * size, cut:] for i in range(4)], 1)
    room = (size + 15) // 16 * 16
    rest = jnp.concatenate([rest, jnp.zeros((room - size, 4 * 32), F32)], 0)
    return value[:, :cut].astype(BF16), rest.astype(BF16)


def join_lanes(main, rest):
    size = main.shape[0] // 4
    rest = rest.astype(F32)
    rest = jnp.concatenate([rest[:size, i * 32 : (i + 1) * 32] for i in range(4)], 0)
    return jnp.concatenate([main.astype(F32), rest], 1)


def both(own_t, peer_t, own, peer):
    rows = own_t.shape[-1]
    cut = rows // 256 * 256
    total = dot(own_t[:, :cut], own[:cut]) + dot(peer_t[:, :cut], peer[:cut])
    ends_t = jnp.concatenate([own_t[:, cut:], peer_t[:, cut:]], 1)
    return total + dot(ends_t, jnp.concatenate([own[cut:], peer[cut:]], 0))


def middle_kernel(
    ctx_t_ref,
    ctx_rest_ref,
    hidden_ref,
    cot_ref,
    proj_bias_ref,
    gain_ref,
    shift_ref,
    fc2_bias_ref,
    fc1_bias_ref,
    lse_ref,
    cot_z,
    cot_zz,
    proj_hbm,
    fc1_hbm,
    fc2_hbm,
    qkv_hbm,
    w_hbm,
    out_hbm,
    c_all,
    d_middle_ref,
    late_hbm,
    vec_ref,
    fc1_vec_ref,
    dt_ref,
    lead_ref,
    tail_ref,
    normed_x,
    normed_peer,
    normed_cond_x,
    normed_cond_peer,
    d_pre_own,
    d_pre_x,
    active_x,
    active_cond_x,
    cot_far,
    cot_peer,
    proj_ref,
    fc1_ref,
    fc2_ref,
    bias_ref,
    normed_ref,
    middle_ref,
    acc_out,
    acc_back,
    normed_t,
    ctx_two,
    ctx_peer,
    active_t,
    active_pack,
    d_pre,
    d_branch_ref,
    d_branch_peer,
    d_go,
    d_rest,
    d_in,
    d_rest_in,
    dot_all,
    dt_all,
    d_all,
    dk_ref,
    dv_ref,
    proj_stage,
    c_own,
    send_sems,
    recv_sems,
    local_sems,
):
    rows, width = cot_ref.shape
    slots = c_own.shape[0]
    images = rows - slots
    depth, _, small, _ = ctx_two.shape
    chunk = fc1_ref.shape[2]
    own = ctx_t_ref.shape[1]
    quarter = chunk // 8
    place, index = lax.axis_index("seq"), lax.axis_index("batch")
    chip, core = index // 2, index % 2
    to, other, up_to, down_to = ends_of(place, index, depth)
    moves = Locals(local_sems)

    def load(i):
        span = pl.ds(pl.multiple_of((chip + AWAY[i]) % depth * chunk, LANES), chunk)
        return (
            moves.start(fc1_hbm.at[:, span], fc1_ref.at[i % 2]),
            moves.start(fc2_hbm.at[span], fc2_ref.at[i % 2]),
        )

    proj_load = moves.start(proj_hbm, proj_ref)
    loads = [load(0), load(1)]
    greet([to[1], to[2], to[3], other] + line_of(place, index, depth))
    wires = Wires(send_sems, recv_sems)
    hop = Hop(
        wires, depth, chip, up_to, down_to, 2, cot_zz.at[0], cot_zz.at[1], cot_far, cot_far
    )
    hop.start()
    for f in range(4):
        bias_ref[f : f + 1] = fc1_bias_ref[f * chunk : (f + 1) * chunk].reshape(1, -1)

    branch = proj_bias_ref[...].reshape(1, -1) + hidden_ref[...]
    proj_load.wait()
    for k in range(4):
        at = pl.ds(pl.multiple_of(flip(place, k) * own, 16), own)
        context_t = join_lanes(ctx_t_ref[k], ctx_rest_ref[k])
        branch += dot(context_t.T.astype(BF16), proj_ref[at, :])
        for i in range(2):
            ctx_two[flip(place, k), i] = context_t[i * small : (i + 1) * small].astype(BF16)
    ctx_swap = wires.copy(ctx_two.at[:, 1 - core], ctx_peer, other)
    ctx_swap.start()
    middle_ref[...] = branch
    scaled, _ = normalize(branch)
    gain = gain_ref[...].reshape(1, -1)
    normed = scaled * gain + shift_ref[...].reshape(1, -1)
    normed_ref[...] = normed.astype(BF16)
    normed_t[...] = normed[:images].T.astype(BF16).reshape(normed_t.shape)
    normed_go = Spread(wires, to, normed_x, normed_t, depth // 2)
    normed_go.start()
    keeps = [
        moves.start(normed_t, normed_x.at[0]),
        moves.start(normed_ref.at[pl.ds(images, slots)], normed_cond_x.at[0]),
    ]
    cond_go = [
        wires.copy(normed_ref.at[pl.ds(images, slots)], normed_cond_x.at[k], to[k]) for k in (1, 2, 3)
    ]
    for wire in cond_go:
        wire.start()

    near = []
    for i in range(4):
        f = (chip + AWAY[i]) % depth
        for copy in loads[i]:
            copy.wait()
        fc1, fc2 = fc1_ref.at[i % 2], fc2_ref.at[i % 2]
        before = dot(normed_ref[...], fc1[...]) + bias_ref[pl.ds(f, 1)]
        cdf = 0.5 + 0.5 * lax.erf(before * math.sqrt(0.5))
        active = before * cdf
        slope = cdf + before * (jnp.exp(-0.5 * before * before) * (1.0 / math.sqrt(2.0 * math.pi)))
        d_before = dot_nt(cot_ref[...], fc2[...]) * slope
        fc1_vec_ref[pl.ds(f, 1)] = jnp.sum(d_before, axis=0, keepdims=True)
        d_low = d_before.astype(BF16)
        d_pre[f] = d_low
        flat = active.T
        for c in range(2):
            for j in range(4):
                piece = flat[(c * 4 + j) * quarter : (c * 4 + j + 1) * quarter]
                active_t[i, c, j] = piece[:, :images].astype(BF16)
            active_pack[i, c] = jnp.concatenate(
                [flat[(c * 4 + j) * quarter : (c * 4 + j + 1) * quarter, images:] for j in range(4)], 1
            ).astype(BF16)
        if i < 3:
            for c in range(2):
                device = (f * 2 + c, place)
                near.append(wires.by_core(core, active_t.at[i, c], active_x.at[i, core], device))
                near.append(
                    wires.by_core(core, active_pack.at[i, c], active_cond_x.at[i, core], device)
                )
            for wire in near[4 * i :]:
                wire.start()
        else:
            keeps.append(moves.start(active_t.at[3, core], active_x.at[3, core]))
            keeps.append(moves.start(active_pack.at[3, core], active_cond_x.at[3, core]))
            late_go = [
                wires.copy(active_t.at[3, 1 - core], active_x.at[3, core], other),
                wires.copy(active_pack.at[3, 1 - core], active_cond_x.at[3, core], other),
            ]
        forward = dot(active.astype(BF16), fc2[...])
        backward = dot_nt(d_low, fc1[...])
        if i == 0:
            acc_out[...] = forward
            acc_back[...] = backward
        else:
            acc_out[...] += forward
            acc_back[...] += backward
        if i + 2 < 4:
            loads.append(load(i + 2))
        else:
            heads = range(0, 3) if i == 2 else range(3, 4)
            span = pl.ds(0, 9 * LANES) if i == 2 else pl.ds(9 * LANES, 3 * LANES)
            size = 9 * LANES if i == 2 else 3 * LANES
            qkv_loads = [
                moves.start(
                    qkv_hbm.at[h], fc1_ref.at[i % 2, :, pl.ds((h - heads[0]) * 3 * LANES, 3 * LANES)]
                )
                for h in heads
            ]
            qkv_loads.append(moves.start(w_hbm.at[:, span], fc2_ref.at[i % 2, :, pl.ds(0, size)]))
            loads.append(qkv_loads)
        if i == 1:
            normed_go.relay()

    middle = middle_ref[...]
    scaled, factor = normalize(middle)
    upstream = acc_back[...]
    cot = cot_ref[...].astype(F32)
    d_middle = cot + norm_back(upstream, scaled, factor, gain)
    d_middle_ref[...] = d_middle
    d_branch_ref[...] = d_middle.astype(BF16)
    branch_swap = wires.copy(d_branch_ref, d_branch_peer, other)
    branch_swap.start()
    go, go_on = [], []
    for k in (3, 1, 2, 0):
        at = pl.ds(pl.multiple_of(flip(place, k) * own, 16), own)
        main, d_rest[k] = split_lanes(dot_nt(d_branch_ref[...], proj_ref[at, :]))
        d_go[0, k], d_go[1, k] = main[:, :LANES], main[:, LANES:]
        if k:
            go.append(wires.copy(d_go.at[0, k], d_in.at[0, k], to[k]))
            go[-1].start()
            for src, dst in ((d_go.at[1], d_in.at[1]), (d_rest, d_rest_in)):
                go_on.append(wires.copy(src.at[k], dst.at[k], to[k]))
        else:
            d_in[0, 0], d_in[1, 0], d_rest_in[0] = d_go[0, 0], d_go[1, 0], d_rest[0]
    for wire in go_on:
        wire.start()
    acc_out[...] = middle + acc_out[...] + fc2_bias_ref[...].reshape(1, -1)
    keeps.append(moves.start(acc_out.at[pl.ds(0, images)], out_hbm))
    c_own[...] = acc_out[images:].astype(BF16)
    c_go = [wires.copy(c_own, c_all.at[k], to[k]) for k in (3, 1, 2)]
    keeps.append(moves.start(c_own, c_all.at[0]))
    vec_ref[0:1] = jnp.sum(upstream * scaled, axis=0, keepdims=True)
    vec_ref[1:2] = jnp.sum(upstream, axis=0, keepdims=True)
    vec_ref[2:3] = jnp.sum(d_middle, axis=0, keepdims=True)
    vec_ref[3:4] = jnp.sum(cot, axis=0, keepdims=True)
    vec_ref[4:] = jnp.zeros((4, width), F32)
    for wire in go:
        wire.arrive()
    normed_go.finish()
    for wire in cond_go:
        wire.arrive()
    hop.arrive()
    keeps.append(moves.start(d_pre.at[place], d_pre_own))
    last_go = (
        [wires.copy(d_pre.at[flip(place, k)], d_pre_x.at[k - 1], to[k]) for k in (3, 1, 2)]
        + late_go
        + [
            wires.copy(normed_x.at[:, :, 1 - core], normed_peer, other),
            wires.copy(normed_cond_x, normed_cond_peer, other),
            wires.copy(cot_ref, cot_peer.at[0], other),
            wires.copy(cot_z, cot_peer.at[pl.ds(1, 2)], other),
            wires.copy(cot_zz, cot_peer.at[pl.ds(3, 2)], other),
            wires.copy(cot_far, cot_peer.at[5], other),
        ]
        + c_go
    )
    for copy in keeps:
        copy.wait()
    for wire in last_go:
        wire.start()

    total = 4 * rows
    half = rows // 2
    for part in range(4):
        dot_all[:LANES, part * rows : (part + 1) * rows] = d_in[0, part].astype(F32).T
    for copy in loads[4] + loads[5]:
        copy.wait()
    step = 3 * LANES
    for head in range(4):
        slot, lane = (0, 3 * head * LANES) if head < 3 else (1, 0)
        base = head * HEAD_DIM
        if head == 1:
            for wire in go_on:
                wire.arrive()
            for part in range(4):
                dot_all[LANES:, part * rows : (part + 1) * rows] = join_lanes(
                    d_in[1, part], d_rest_in[part]
                ).T
        upstream_t = jnp.concatenate(
            [dot_all[base : base + HEAD_DIM, :], jnp.zeros((LANES - HEAD_DIM, total), F32)], 0
        )
        upstream = upstream_t.T.astype(BF16)
        upstream_t = upstream_t.astype(BF16)
        key = fc1_ref[slot, :, lane + LANES : lane + 2 * LANES]
        key_t = turned(key)
        value = fc1_ref[slot, :, lane + 2 * LANES : lane + 3 * LANES]
        for start in range(0, total, step):
            span = slice(start, start + step)
            query = fc1_ref[slot, span, lane : lane + LANES]
            probs = jnp.exp2(dot_nt(key, query) * SCALE2 - lse_ref[head, :, span])
            d_probs = dot(value, upstream_t[:, span])
            delta = jnp.sum(probs * d_probs, axis=0, keepdims=True)
            d_raw = (probs * (d_probs - delta)).astype(BF16)
            d_value = dot(probs.astype(BF16), upstream[span])
            d_key = dot(d_raw, query)
            if start == 0:
                dv_ref[...] = d_value
                dk_ref[...] = d_key
            else:
                dv_ref[...] += d_value
                dk_ref[...] += d_key
            d_query = dot(key_t, d_raw) * SCALE
            dt_all[base : base + HEAD_DIM, span] = d_query[:HEAD_DIM]
            d_all[span, 3 * head * LANES : (3 * head + 1) * LANES] = d_query.T.astype(BF16)
        d_key = dk_ref[...] * SCALE
        d_value = dv_ref[...]
        dt_all[own + base : own + base + HEAD_DIM] = d_key.T[:HEAD_DIM]
        dt_all[2 * own + base : 2 * own + base + HEAD_DIM] = d_value.T[:HEAD_DIM]
        d_all[:, (3 * head + 1) * LANES : (3 * head + 2) * LANES] = d_key.astype(BF16)
        d_all[:, (3 * head + 2) * LANES : (3 * head + 3) * LANES] = d_value.astype(BF16)
    cut = 9 * LANES
    for part in (3, 1, 2, 0):
        span = slice(part * rows, (part + 1) * rows)
        update = dot_nt(d_all[span, :cut], fc2_ref[0]) + dot_nt(
            d_all[span, cut:], fc2_ref[1, :, : 3 * LANES]
        )
        lead_ref[part] = update[:half].astype(BF16)
        tail_ref[part] = update[half:].astype(BF16)
    dt_ref[...] = dt_all[...].astype(BF16)
    ctx_swap.arrive()
    branch_swap.arrive()
    proj_stage[...] = (
        both(
            ctx_two[:, core].reshape(depth * small, rows),
            ctx_peer[...].reshape(depth * small, rows),
            d_branch_ref[...],
            d_branch_peer[...],
        )
        .astype(BF16)
        .reshape(depth, small, width)
    )
    proj_out = moves.start(proj_stage, late_hbm)
    for i in range(3):
        arrive_by_core(near[4 * i : 4 * i + 4], core)
    for wire in last_go:
        wire.arrive()
    proj_out.wait()
    wires.drain()


def middle_stage(
    depth, ctx_t, ctx_rest, hidden, cot, proj, proj_bias, gain, shift, fc2_bias, fc1_bias, lse,
    cot_z, cot_zz, fc1, fc2, qkv, w_heads,
):
    rows, width = hidden.shape
    slots = SLOTS // 4
    images = rows - slots
    ff = fc1.shape[1]
    small = width // (2 * depth)
    own = ctx_t.shape[1]
    chunk = ff // 4
    quarter = chunk // 8
    vmem, hbm = pl.BlockSpec(memory_space=pltpu.VMEM), pl.BlockSpec(memory_space=pl.ANY)
    f = lambda *shape: jax.ShapeDtypeStruct(shape, F32)
    b = lambda *shape: jax.ShapeDtypeStruct(shape, BF16)
    v = lambda *shape: pltpu.VMEM(shape, BF16)
    vf = lambda *shape: pltpu.VMEM(shape, F32)
    return pl.pallas_call(
        middle_kernel,
        in_specs=[vmem] * 10 + [hbm] * 7,
        out_specs=[hbm, hbm, vmem, hbm] + [vmem] * 5 + [hbm] * 10,
        out_shape=[
            f(images, width),
            b(4, slots, width),
            f(rows, width),
            b(depth, small, width),
            f(8, width),
            f(4, chunk),
            b(3 * own, 4 * rows),
            b(4, rows // 2, width),
            b(4, rows // 2, width),
            b(4, depth, 2, small, images),
            b(4, depth, small, images),
            b(4, slots, width),
            b(4, slots, width),
            b(rows, chunk),
            b(3, rows, chunk),
            b(4, 2, 4, quarter, images),
            b(4, 2, quarter, 4 * slots),
            b(rows, width),
            b(6, rows, width),
        ],
        scratch_shapes=[
            v(width, width), v(2, width, chunk), v(2, chunk, width), vf(4, chunk),
            v(rows, width), vf(rows, width), vf(rows, width), vf(rows, width),
            v(depth, 2, small, images),
            v(depth, 2, small, rows), v(depth, small, rows),
            v(4, 2, 4, quarter, images), v(4, 2, quarter, 4 * slots),
            v(4, rows, chunk),
            v(rows, width), v(rows, width),
            v(2, 4, rows, LANES), v(4, (rows // 4 + 15) // 16 * 16, LANES),
            v(2, 4, rows, LANES), v(4, (rows // 4 + 15) // 16 * 16, LANES),
            vf(own, 4 * rows), vf(3 * own, 4 * rows), v(4 * rows, 12 * LANES),
            vf(4 * rows, LANES), vf(4 * rows, LANES),
            v(depth, small, width),
            v(slots, width),
            pltpu.SemaphoreType.DMA((64,)), pltpu.SemaphoreType.DMA((64,)), pltpu.SemaphoreType.DMA((64,)),
        ],
        compiler_params=pltpu.CompilerParams(
            vmem_limit_bytes=VMEM_LIMIT, collective_id=3, has_side_effects=True
        ),
        cost_estimate=cost(8 * rows * width * ff, 8 * width * ff),
        name="middle_stage",
    )(ctx_t, ctx_rest, hidden, cot, proj_bias, gain, shift, fc2_bias, fc1_bias, lse, cot_z, cot_zz, proj, fc1, fc2, qkv, w_heads)


def finish_kernel(
    p_hbm, f_hbm, g_hbm, q_hbm, s_hbm, c_hbm, out_c_hbm, vec_ref, out_hbm, din_hbm, dskip_hbm,
    g_fc2_hbm, g_proj_hbm, g_first_hbm, g_heads_hbm, g_skip_hbm,
    o_out, o_din, o_dskip, o_out_cond, o_din_cond, o_dskip_cond,
    v0, v1, v2, v3, v4, v5, v6, fc1_vec_ref,
    p_in, f_in, g_in, q_in, s_in, c_in, out_c_in, p_st, f_st, g_st, q_st, s_st, cond_st, rows_st, sems,
):
    width = out_hbm.shape[1]
    place, index = lax.axis_index("seq"), lax.axis_index("batch")
    batch = lax.axis_size("batch")
    moves = Locals(sems)
    loads = [
        moves.start(src, dst)
        for src, dst in (
            (f_hbm, f_in), (g_hbm, g_in), (q_hbm, q_in), (s_hbm, s_in), (p_hbm, p_in),
            (c_hbm, c_in),
            (out_c_hbm, out_c_in),
        )
    ]
    rows_in = [
        moves.start(src, rows_st.at[i]) for i, src in enumerate((out_hbm, din_hbm, dskip_hbm))
    ]
    done = []
    for i, dst in enumerate((o_out, o_din, o_dskip)):
        rows_in[i].wait()
        done.append(moves.start(rows_st.at[i], dst.at[:, 0]))
    loads[0].wait()
    for j in range(4):
        f_st[:, j * width : (j + 1) * width] = f_in[flip(place, j)].astype(F32)
    done.append(moves.start(f_st, g_first_hbm))
    loads[1].wait()
    small = g_in.shape[1]
    for j in range(4):
        g_st[j * small : (j + 1) * small] = g_in[flip(place, j)].astype(F32)
    done.append(moves.start(g_st, g_fc2_hbm))
    loads[2].wait()
    size = q_in.shape[2] // 3
    for j in range(4):
        value = q_in[flip(place, j)].astype(F32)
        for which in range(3):
            at = (which * 4 + j) * size
            q_st[:, at : at + size] = value[:, which * size : (which + 1) * size]
    done.append(moves.start(q_st, g_heads_hbm))
    loads[3].wait()
    size = s_st.shape[0] // 4
    for j in range(4):
        s_st[j * size : (j + 1) * size] = s_in[flip(place, j), :size].astype(F32)
    done.append(moves.start(s_st, g_skip_hbm))
    for copy in loads[4:]:
        copy.wait()
    p_st[...] = p_in[...].astype(F32)
    done.append(moves.start(p_st, g_proj_hbm))
    slots = c_in.shape[1]
    for j in range(4):
        span = slice(j * slots, (j + 1) * slots)
        piece = c_in[flip(place, j)].astype(F32)
        cond_st[0, span] = out_c_in[flip(place, j)].astype(F32)
        cond_st[1, span] = piece[:, :width]
        cond_st[2, span] = piece[:, width:]
    conds = o_out_cond.shape[0]
    for i, ref in enumerate((o_out_cond, o_din_cond, o_dskip_cond)):
        ref[:, 0] = cond_st[i, :conds]
    share = width // batch
    vectors = vec_ref[...]
    rolled = pltpu.roll(vectors, lax.rem(width - index * share, width), 1)
    for row, ref in zip((0, 1, 2, 5, 3, 4, 6), (v0, v1, v2, v3, v4, v5, v6)):
        ref[...] = rolled[row, :share]
    share = 4 * width // batch
    per = width // share
    vector = vec_ref[pl.ds(8 + index // per, 1)]
    vector = pltpu.roll(vector, lax.rem(width - index % per * share, width), 1)
    fc1_vec_ref[...] = vector[0, :share]
    for copy in done:
        copy.wait()


def finish_stage(batch, conds, slots_of, out_c, vec, out, d_image, d_skip):
    p_all, f_all, g_all, q_all, s_all, c_all = slots_of
    images, width = out.shape
    small = f_all.shape[1]
    skip_rows = 2 * width // batch
    large = 4 * width // batch
    slots = c_all.shape[1]
    vmem, hbm = pl.BlockSpec(memory_space=pltpu.VMEM), pl.BlockSpec(memory_space=pl.ANY)
    f = lambda *shape: jax.ShapeDtypeStruct(shape, F32)
    like = lambda a: pltpu.VMEM(a.shape, a.dtype)
    vf = lambda *shape: pltpu.VMEM(shape, F32)
    return pl.pallas_call(
        finish_kernel,
        in_specs=[hbm] * 7 + [vmem] + [hbm] * 3,
        out_specs=[hbm] * 8 + [vmem] * 11,
        out_shape=[
            f(large, width), f(small, width), f(small, 4 * width), f(small, 4 * q_all.shape[2]),
            f(skip_rows, width), f(images, 1, width), f(images, 1, width), f(images, 1, width),
            f(conds, 1, width), f(conds, 1, width), f(conds, 1, width),
        ]
        + [f(width // batch)] * 7
        + [f(large)],
        scratch_shapes=[
            like(p_all), like(f_all), like(g_all), like(q_all), like(s_all), like(c_all), like(out_c),
            vf(small, width), vf(small, 4 * width), vf(large, width), vf(small, 4 * q_all.shape[2]),
            vf(skip_rows, width), vf(3, 4 * slots, width), vf(3, images, width),
            pltpu.SemaphoreType.DMA((24,)),
        ],
        compiler_params=params(),
        cost_estimate=cost(1e6, 2e7),
        name="finish_stage",
    )(*slots_of, out_c, vec, out, d_image, d_skip)


def per_device(
    batch,
    parts,
    image_in,
    cond_in,
    skip_image,
    skip_cond,
    caption_len,
    skip_weight,
    skip_bias,
    first_gain,
    first_bias,
    qkv_weight,
    proj_weight,
    proj_bias,
    second_gain,
    second_bias,
    fc1_weight,
    fc1_bias,
    fc2_weight,
    fc2_bias,
    grad_image,
    grad_cond,
):
    conds = cond_in.shape[0]
    width = image_in.shape[2]
    images = image_in.shape[0]
    ff = fc1_weight.shape[1]
    slots = SLOTS // parts
    rows = slots + images
    total = rows * parts
    heads = HEADS // parts
    depth = batch // 2
    place = lax.axis_index("seq")
    index = lax.axis_index("batch")
    core, chip = index % 2, index // 2
    where = jnp.stack([core, place]).astype(jnp.int32)

    fast = parts == 4 and depth == 4 and (ff // parts) % LANES == 0
    if fast:
        (
            hidden, normed_all, w_heads, qkv, joined, joined_peer, cot, cot_z, lse, ctx_t, ctx_rest,
            cot_zz,
        ) = start_stage(
            depth, caption_len, image_in[:, 0], cond_in[:, 0], skip_image[:, 0], skip_cond[:, 0],
            grad_image[:, 0], grad_cond[:, 0], skip_weight, skip_bias, first_gain, first_bias,
            qkv_weight,
        )
        normed_all = normed_all.reshape(total, width)
        (
            out, out_c, d_middle, late, vec_two, fc1_vec, d_triple_t, lead, tail, normed_x,
            normed_peer, normed_cond_x, normed_cond_peer, d_pre_own, d_pre_x, active_x,
            active_cond_x, cot_far, cot_peer,
        ) = middle_stage(
            depth, ctx_t, ctx_rest, hidden, cot, proj_weight, proj_bias, second_gain, second_bias,
            fc2_bias, fc1_bias, lse, cot_z, cot_zz, fc1_weight, fc2_weight, qkv, w_heads,
        )
        feeds = (
            normed_x, normed_peer, normed_cond_x, normed_cond_peer, d_pre_own, d_pre_x, active_x,
            active_cond_x, cot, cot_z, cot_zz, cot_far, cot_peer,
        )
        *slots_of, d_image, d_skip, vec = reduce_all(
            late, lead, tail, normed_all, d_triple_t, joined, joined_peer, hidden, d_middle,
            skip_weight, feeds, first_gain, vec_two, fc1_vec,
        )
        (
            wgrad_fc2, wgrad_proj, wgrad_fc1, wgrad_qkv, wgrad_skip, out_image, d_image, d_skip,
            out_cond, d_cond, d_skip_cond, *vec,
        ) = finish_stage(batch, conds, slots_of, out_c, vec, out, d_image, d_skip)
        return (
            out_image, out_cond, d_image, d_cond, d_skip, d_skip_cond, wgrad_skip, vec[0],
            vec[1], vec[2], wgrad_qkv, wgrad_proj, vec[3], vec[4], vec[5], wgrad_fc1, vec[7],
            wgrad_fc2, vec[6],
        )

    def own_rows(cond, image):
        padded = jnp.pad(cond[:, 0], ((0, SLOTS - conds), (0, 0)))
        lead = lax.dynamic_slice_in_dim(padded, place * slots, slots, 0)
        return jnp.concatenate([lead, image[:, 0]], 0)

    x = own_rows(cond_in, image_in)
    s = own_rows(skip_cond, skip_image)
    cot = own_rows(grad_cond, grad_image)

    hidden, normed, joined_t = pre(
        x, s, skip_weight, skip_bias[None], first_gain[None], first_bias[None]
    )
    normed_all = jnp.concatenate(everywhere(normed, parts), 0)
    own = heads * HEAD_DIM
    w_heads = heads_weight(where[1:], qkv_weight, heads)
    order = place ^ jnp.arange(parts, dtype=jnp.int32)
    position = order[:, None] * slots + jnp.arange(rows, dtype=jnp.int32)[None]
    valid = (jnp.arange(rows)[None] >= slots) | (position <= caption_len[0])
    kbias = jnp.where(
        (jnp.arange(LANES) == HEAD_DIM)[None] & ~valid.reshape(total, 1), F32(-1e30), F32(0)
    )
    qkv, lse, *ctx_parts = attend(parts, normed_all, w_heads, kbias)
    context = [ctx_parts[0]] + [across(ctx_parts[k], parts, k) for k in range(1, parts)]

    zero = jnp.zeros_like(proj_bias)
    vecs = jnp.stack([proj_bias, second_gain, second_bias, fc2_bias, zero, zero, zero, zero])
    (
        out,
        d_middle,
        d_branch,
        active_t,
        d_pre,
        normed2_t,
        ctx_t,
        vec_two,
        fc1_bias_grad,
        *d_ctx_parts,
    ) = mlp(
        parts,
        where[1:],
        context,
        hidden,
        cot,
        proj_weight,
        vecs,
        fc1_weight,
        fc1_bias[None],
        fc2_weight,
    )
    d_context = [d_ctx_parts[0]] + [across(d_ctx_parts[k], parts, k) for k in range(1, parts)]

    def by_core(turned_rows):
        blocks = turned_rows.reshape(depth, 2, -1, rows)
        send = lax.dynamic_index_in_dim(blocks, 1 - core, 1, keepdims=False)
        return blocks, other_core(send, batch)

    active_b, active_p = by_core(active_t)
    normed2_b, normed2_p = by_core(normed2_t)
    ctx_b, ctx_p = by_core(ctx_t)
    joined_b, joined_p = by_core(joined_t)
    cot_p, d_pre_p, d_branch_p = (other_core(v, batch) for v in (cot, d_pre, d_branch))
    late = pair_grads(
        where, [(active_b, active_p, cot, cot_p), (ctx_b, ctx_p, d_branch, d_branch_p)]
    )
    by_columns = (ff // parts) % LANES == 0
    if by_columns:
        first = column_grads(where, parts, normed2_b, normed2_p, d_pre, d_pre_p)
        late, first, d_context = lax.optimization_barrier((late, first, d_context))
        middle = depth // 2
    if by_columns:
        first = jnp.concatenate(
            [
                scattered(first[:, :middle], parts, bits_of(parts)),
                scattered(first[:, middle:], parts, bits_of(parts)[::-1]),
            ],
            0,
        )
    if not by_columns:
        first = pair_grads(where, [(normed2_b, normed2_p, d_pre, d_pre_p)])
    def all_conds(lead):
        pieces = [lead] + [across(lead, parts, k) for k in range(1, parts)]
        full = jnp.zeros((SLOTS, lead.shape[1]), F32)
        for k in range(parts):
            full = lax.dynamic_update_slice_in_dim(
                full, pieces[k].astype(F32), (place ^ k) * slots, 0
            )
        return full[:conds, None]

    d_triple_t, d_lead, d_tail = attend_back(parts, d_context, qkv, lse, w_heads)
    d_lead = scattered(d_lead, parts, bits_of(parts))
    d_tail = scattered(d_tail, parts, bits_of(parts)[::-1])
    heads_grad = heads_grads(normed_all, d_triple_t).reshape(depth, 2, -1, 3 * own)
    heads_grad = plus(
        lax.dynamic_index_in_dim(heads_grad, core, 1, keepdims=False),
        other_core(lax.dynamic_index_in_dim(heads_grad, 1 - core, 1, keepdims=False), batch),
    )
    heads_grad = everywhere(down_the_line(heads_grad, batch, chip), parts)
    wgrad_qkv = put_heads(where[1:], heads_grad)

    d_in, d_skip, d_low, vec_one = post(
        d_lead, d_tail, hidden, d_middle, first_gain[None], skip_weight
    )
    d_low_p = other_core(d_low, batch)
    last = pair_grads(where, [(joined_b, joined_p, d_low, d_low_p)])

    late = down_the_line(late, batch, chip)
    first = down_the_line(first, batch, chip)
    late = summed(late, parts)
    if by_columns:
        fc1_cols = everywhere(first, parts)
        wgrad_fc1 = put_columns(where[1:], fc1_cols)
    else:
        wgrad_fc1 = summed(first, parts).astype(F32)

    vectors = [
        vec_one[0],
        vec_one[1],
        vec_one[2],
        vec_two[2],
        vec_two[0],
        vec_two[1],
        fc1_bias_grad[0],
        vec_two[3],
    ]
    sizes = [v.shape[0] // batch for v in vectors]
    packed = jnp.concatenate([v.reshape(batch, -1) for v in vectors], 1)
    packed = packed.reshape(depth, 2, -1)
    packed = lax.dynamic_index_in_dim(packed, core, 1, keepdims=False) + other_core(
        lax.dynamic_index_in_dim(packed, 1 - core, 1, keepdims=False), batch
    )
    packed = jnp.pad(packed, ((0, 0), (0, 16 * width - packed.shape[1]))).reshape(depth, 16, width)
    last = jnp.concatenate([last, packed.astype(BF16)], 1)
    last = summed(down_the_line(last, batch, chip), parts)
    skip_rows = 2 * width // batch
    wgrad_skip = last[:skip_rows].astype(F32)
    flat = last[skip_rows:].reshape(-1).astype(F32)
    vector_out, at = [], 0
    for size in sizes:
        vector_out.append(flat[at : at + size])
        at += size
    fc2_rows = ff // batch
    wgrad_fc2 = late[:fc2_rows].astype(F32)
    wgrad_proj = late[fc2_rows:].astype(F32)

    out_cond = all_conds(out[:slots].astype(BF16))
    d_cond = all_conds(jnp.concatenate([d_in[:slots], d_skip[:slots]], 1).astype(BF16))
    return (
        out[slots:, None],
        out_cond,
        d_in[slots:, None],
        d_cond[:, :, :width],
        d_skip[slots:, None],
        d_cond[:, :, width:],
        wgrad_skip,
        vector_out[0],
        vector_out[1],
        vector_out[2],
        wgrad_qkv,
        wgrad_proj,
        vector_out[3],
        vector_out[4],
        vector_out[5],
        wgrad_fc1,
        vector_out[6],
        wgrad_fc2,
        vector_out[7],
    )


def solution(mesh):
    tokens, conds, shared = P("seq", "batch", None), P(None, "batch", None), P()
    return jax.shard_map(
        functools.partial(per_device, mesh.shape["batch"], mesh.shape["seq"]),
        mesh=mesh,
        in_specs=(tokens, conds, tokens, conds, P("batch")) + (shared,) * 13 + (tokens, conds),
        out_specs=(tokens, conds) * 3
        + (
            P("batch", None),
            P("batch"),
            P("batch"),
            P("batch"),
            P("batch", None),
            P("batch", None),
            P("batch"),
            P("batch"),
            P("batch"),
            P("batch", None),
            P("batch"),
            P("batch", None),
            P("batch"),
        ),
        check_vma=False,
    )
```
